32 devices in a mesh: dp: 8 (over z, y), mp: 4 (over x, core).
Axes of the slice: x: 2, y: 2, z: 4, core: 2. Of those that a mesh axis runs over, the one named last changes fastest.
Arguments:
- char_states: bfloat16 [32768, 16, 256], P(('dp', 'mp')), may hold values from -6 to 6
- word_states: bfloat16 [32768, 512], P(('dp', 'mp')), may hold values from -6 to 6
- char_counts: int32 [32768], P(('dp', 'mp')), may hold values from 1 to 16
- language_group: int32 [32], P('dp'), may hold values from 0 to 7
- output_grad: bfloat16 [32768, 512], P(('dp', 'mp')), may hold values from -6 to 6
- char_norm_gain: float32 [256], P(('dp', 'mp')), may hold values from 0.25 to 1.75
- char_norm_bias: float32 [256], P(('dp', 'mp')), may hold values from -1.5 to 1.5
- char_qkv: float32 [256, 768], P(('dp', 'mp')), may hold values from -0.375 to 0.375
- char_out: float32 [256, 256], P(('dp', 'mp')), may hold values from -1 to 1
- char_mlp_gain: float32 [256], P(('dp', 'mp')), may hold values from 0.25 to 1.75
- char_mlp_bias: float32 [256], P(('dp', 'mp')), may hold values from -1.5 to 1.5
- char_up: float32 [256, 1024], P(('dp', 'mp')), may hold values from -0.375 to 0.375
- char_down: float32 [1024, 256], P(('dp', 'mp')), may hold values from -0.1875 to 0.1875
- pool_query: float32 [256], P(('dp', 'mp')), may hold values from -5 to 5
- char_proj: float32 [256, 512], P(('dp', 'mp')), may hold values from -0.75 to 0.75
- language_table: float32 [8, 512], P(None, ('dp', 'mp')), may hold values from -3 to 3
- word_norm_gain: float32 [512], P(('dp', 'mp')), may hold values from 0.25 to 1.75
- word_norm_bias: float32 [512], P(('dp', 'mp')), may hold values from -1.5 to 1.5
- word_qkv: float32 [3, 512, 512], P(None, 'dp', 'mp'), may hold values from -0.25 to 0.25
- word_out: float32 [512, 512], P('mp', 'dp'), may hold values from -2 to 2
- word_mlp_gain: float32 [512], P(('dp', 'mp')), may hold values from 0.25 to 1.75
- word_mlp_bias: float32 [512], P(('dp', 'mp')), may hold values from -1.5 to 1.5
- word_up: float32 [512, 2048], P('dp', 'mp'), may hold values from -0.25 to 0.25
- word_down: float32 [2048, 512], P('mp', 'dp'), may hold values from -0.125 to 0.125
Outputs:
- layer_output: bfloat16 [32768, 512], P(('dp', 'mp'))
- grad_chars: bfloat16 [32768, 16, 256], P(('dp', 'mp'))
- grad_words: bfloat16 [32768, 512], P(('dp', 'mp'))
- grad_char_norm_gain: float32 [256], P(('dp', 'mp'))
- grad_char_norm_bias: float32 [256], P(('dp', 'mp'))
- grad_char_qkv: float32 [256, 768], P(('dp', 'mp'))
- grad_char_out: float32 [256, 256], P(('dp', 'mp'))
- grad_char_mlp_gain: float32 [256], P(('dp', 'mp'))
- grad_char_mlp_bias: float32 [256], P(('dp', 'mp'))
- grad_char_up: float32 [256, 1024], P(('dp', 'mp'))
- grad_char_down: float32 [1024, 256], P(('dp', 'mp'))
- grad_pool_query: float32 [256], P(('dp', 'mp'))
- grad_char_proj: float32 [256, 512], P(('dp', 'mp'))
- grad_language_table: float32 [8, 512], P(None, ('dp', 'mp'))
- grad_word_norm_gain: float32 [512], P(('dp', 'mp'))
- grad_word_norm_bias: float32 [512], P(('dp', 'mp'))
- grad_word_qkv: float32 [3, 512, 512], P(None, 'dp', 'mp')
- grad_word_out: float32 [512, 512], P('mp', 'dp')
- grad_word_mlp_gain: float32 [512], P(('dp', 'mp'))
- grad_word_mlp_bias: float32 [512], P(('dp', 'mp'))
- grad_word_up: float32 [512, 2048], P('dp', 'mp')
- grad_word_down: float32 [2048, 512], P('mp', 'dp')
The draws below stay inside these ranges and needn't reach their ends.
All inputs are finite; a program needn't handle non-finite values.
Results may differ from the reference program's by a relative error of at most 0.03.
The reference program's roundings to bfloat16 on the way count: a program that leaves them out, or rounds other values in their place, can miss the bound.
Values may be sent and summed in bfloat16 or wider, within the bound.
A program may use at most 640 MiB of HBM per device.

```python
import jax
import jax.numpy as jnp
from jax import lax

D = 512
HEADS = 8
HEAD = 64
FF = 2048
C = 256
CHAR_HEADS = 4
CF = 1024
CHARS = 16
LANGS = 8
LEN = 1024
SEQS = 32
WORDS = 32768


def set_ends(entries, key, smallest, top_value):
    longest = entries.shape.index(max(entries.shape))
    spots = []
    for shift in (0, 1):
        where = [jax.random.randint(jax.random.fold_in(key, axis), (), 0, length) for axis, length in enumerate(entries.shape)]
        where[longest] = (where[longest] + shift) % entries.shape[longest]
        spots.append(tuple(where))
    return entries.at[spots[0]].set(smallest).at[spots[1]].set(top_value)


def shard_levels(own_key, extent, split, smallest, top_value):
    factor_of, own = 1.0, jax.random.fold_in(own_key, 6)
    for dim, shards_of in split:
        draws = jnp.exp(jax.random.uniform(jax.random.fold_in(own, dim), (shards_of,), jnp.float32, smallest / len(split), top_value / len(split)))
        factor_of = factor_of * jnp.repeat(draws, extent[dim] // shards_of).reshape([-1 if axis == dim else 1 for axis in range(len(extent))])
    return factor_of


def noise(own_key, shape, scale, limit, split=(), held_as=jnp.bfloat16):
    array = jax.random.normal(own_key, shape, jnp.float32) * scale
    if len(split) > 0:
        array = shard_levels(own_key, shape, split, -0.22, 0.18) * array
    return jnp.clip(array, min=-limit, max=limit).astype(held_as)


def setup_inputs(seed: int = 0) -> dict:
    keys = jax.random.split(jax.random.key(seed), 25)
    return {
        "char_states": noise(keys[0], (WORDS, CHARS, C), 1.0, 6.0, ((0, 32),)),
        "word_states": noise(keys[1], (WORDS, D), 1.0, 6.0, ((0, 32),)),
        "char_counts": set_ends(jax.random.randint(keys[2], (WORDS,), 1, CHARS + 1), jax.random.fold_in(keys[2], 1), 1, CHARS).astype(jnp.int32),
        "language_group": set_ends(jax.random.randint(keys[3], (SEQS,), 0, LANGS), jax.random.fold_in(keys[3], 1), 0, LANGS - 1).astype(jnp.int32),
        "output_grad": noise(keys[4], (WORDS, D), 1.0, 6.0, ((0, 32),)),
        "char_norm_gain": jnp.clip(1.0 + 0.15 * jax.random.normal(keys[5], (C,), jnp.float32), 0.25, 1.75),
        "char_norm_bias": noise(keys[6], (C,), 0.3, 1.5, ((0, 32),), jnp.float32),
        "char_qkv": noise(keys[7], (C, 3 * C), C ** -0.5, 0.375, ((0, 32),), jnp.float32),
        "char_out": noise(keys[8], (C, C), (C // 8) ** -0.5, 1.0, ((0, 32),), jnp.float32),
        "char_mlp_gain": jnp.clip(1.0 + 0.15 * jax.random.normal(keys[9], (C,), jnp.float32), 0.25, 1.75),
        "char_mlp_bias": noise(keys[10], (C,), 0.3, 1.5, ((0, 32),), jnp.float32),
        "char_up": noise(keys[11], (C, CF), C ** -0.5, 0.375, ((0, 32),), jnp.float32),
        "char_down": noise(keys[12], (CF, C), CF ** -0.5, 0.1875, ((0, 32),), jnp.float32),
        "pool_query": noise(keys[13], (C,), 1.0, 5.0, ((0, 32),), jnp.float32),
        "char_proj": noise(keys[14], (C, D), (C // 4) ** -0.5, 0.75, ((0, 32),), jnp.float32),
        "language_table": noise(keys[15], (LANGS, D), 0.5, 3.0, ((1, 32),), jnp.float32),
        "word_norm_gain": jnp.clip(1.0 + 0.15 * jax.random.normal(keys[16], (D,), jnp.float32), 0.25, 1.75),
        "word_norm_bias": noise(keys[17], (D,), 0.3, 1.5, ((0, 32),), jnp.float32),
        "word_qkv": noise(keys[18], (3, D, D), D ** -0.5, 0.25, ((1, 8), (2, 4)), jnp.float32),
        "word_out": noise(keys[19], (D, D), (D // 64) ** -0.5, 2.0, ((0, 4), (1, 8)), jnp.float32),
        "word_mlp_gain": jnp.clip(1.0 + 0.15 * jax.random.normal(keys[20], (D,), jnp.float32), 0.25, 1.75),
        "word_mlp_bias": noise(keys[21], (D,), 0.3, 1.5, ((0, 32),), jnp.float32),
        "word_up": noise(keys[22], (D, FF), D ** -0.5, 0.25, ((0, 8), (1, 4)), jnp.float32),
        "word_down": noise(keys[23], (FF, D), FF ** -0.5, 0.125, ((0, 4), (1, 8)), jnp.float32),
    }


NORM_EPS = 1e-05
NEG_FILL = -1000000000.0

@jax.custom_vjp
def low(v):
    return lax.optimization_barrier(v.astype(jnp.bfloat16)).astype(jnp.float32)

@jax.custom_vjp
def low_back(v):
    return v

def low_keep(v):
    return (low(v), None)

def low_pass(kept, grad):
    return (grad,)

def back_keep(v):
    return (v, None)

def back_low(kept, grad):
    return (low(grad),)
low.defvjp(low_keep, low_pass)
low_back.defvjp(back_keep, back_low)

def matmul(first_arg, second_arg):
    return jnp.dot(first_arg, second_arg, precision=lax.Precision.HIGHEST, preferred_element_type=jnp.float32)

def high_sum(pattern, first_arg, second_arg):
    return jnp.einsum(pattern, first_arg, second_arg, precision=lax.Precision.HIGHEST, preferred_element_type=jnp.float32)

def normalize(values, gain_value, bias_value):
    centred = values - lax.optimization_barrier(jnp.mean(values, axis=-1, keepdims=True))
    spread = lax.optimization_barrier(jnp.mean(centred * centred, axis=-1, keepdims=True))
    return centred * lax.rsqrt(spread + NORM_EPS) * gain_value + bias_value

def masked_softmax(scores, allowed):
    masked = jnp.where(allowed, scores, NEG_FILL)
    row_max = lax.optimization_barrier(jnp.max(masked, axis=-1, keepdims=True))
    powers = jnp.exp(masked - row_max)
    return powers / lax.optimization_barrier(jnp.sum(powers, axis=-1, keepdims=True))

def attention(packed, allowed, head_count):
    batch_size, length, triple = packed.shape
    model_width = triple // 3
    head_grid = packed.reshape(batch_size, length, 3, head_count, model_width // head_count)
    score_scale = (model_width // head_count) ** (-0.5)
    scores = low_back(high_sum('bqhd,bkhd->bhqk', head_grid[:, :, 0], head_grid[:, :, 1]) * score_scale)
    attn_probs = masked_softmax(scores, allowed)
    attn_mixed = high_sum('bhqk,bkhd->bqhd', low(attn_probs), head_grid[:, :, 2])
    return low_back(low(attn_mixed)).reshape(batch_size * length, model_width)

def one_sequence(params, chars_seq, words_seq, allowed, language_id):
    gain_attn, bias_attn, qkv_char, out_char, gain_mlp, bias_mlp, up_char, down_char, query_pool, proj_char, table_language, word_gain_attn, word_bias_attn, qkv_word, out_word, word_gain_mlp, word_bias_mlp, up_word, down_word = jax.tree.map(low, params)
    states = chars_seq.reshape(LEN * CHARS, C)
    normed = low(normalize(states, gain_attn, bias_attn))
    packed = low_back(low(matmul(normed, qkv_char))).reshape(LEN, CHARS, 3 * C)
    attn_mixed = attention(packed, allowed[:, None, None, :], CHAR_HEADS)
    after_attn = states + low_back(matmul(attn_mixed, out_char))
    normed = low(normalize(after_attn, gain_mlp, bias_mlp))
    hidden = low(jax.nn.gelu(low_back(matmul(normed, up_char)), approximate=False))
    after_mlp = after_attn + low_back(matmul(hidden, down_char))
    char_grid = after_mlp.reshape(LEN, CHARS, CHAR_HEADS, HEAD)
    pool_scores = high_sum('wlhd,hd->whl', char_grid, query_pool.reshape(CHAR_HEADS, HEAD)) * HEAD ** (-0.5)
    pool_probs = masked_softmax(pool_scores, allowed[:, None, :])
    pooled = high_sum('whl,wlhd->whd', pool_probs, char_grid).reshape(LEN, C)
    projected = low_back(matmul(low(pooled), proj_char))
    residual = words_seq + projected + table_language[language_id]
    normed = low(normalize(residual, word_gain_attn, word_bias_attn))
    packed = low_back(low(high_sum('rd,tdc->rtc', normed, qkv_word))).reshape(1, LEN, 3 * D)
    positions = jnp.arange(LEN)
    causal = positions[None, :] <= positions[:, None]
    attn_mixed = attention(packed, causal[None, None], HEADS)
    middle = residual + low_back(matmul(attn_mixed, out_word))
    normed = low(normalize(middle, word_gain_mlp, word_bias_mlp))
    hidden = low(jax.nn.gelu(low_back(matmul(normed, up_word)), approximate=False))
    return middle + low_back(matmul(hidden, down_word))

def reference(char_states, word_states, char_counts, language_group, output_grad, char_norm_gain, char_norm_bias, char_qkv, char_out, char_mlp_gain, char_mlp_bias, char_up, char_down, pool_query, char_proj, language_table, word_norm_gain, word_norm_bias, word_qkv, word_out, word_mlp_gain, word_mlp_bias, word_up, word_down):
    params = (char_norm_gain, char_norm_bias, char_qkv, char_out, char_mlp_gain, char_mlp_bias, char_up, char_down, pool_query, char_proj, language_table, word_norm_gain, word_norm_bias, word_qkv, word_out, word_mlp_gain, word_mlp_bias, word_up, word_down)
    chars_seqs = char_states.reshape(SEQS, LEN, CHARS, C)
    words_seqs = word_states.reshape(SEQS, LEN, D)
    counts_seqs = char_counts.reshape(SEQS, LEN)
    cotangents = output_grad.reshape(SEQS, LEN, D)

    def sequence_step(grad_total, step_inputs):
        chars_seq, words_seq, counts_seq, language_id, cotangent = step_inputs
        allowed = jnp.arange(CHARS)[None, :] < counts_seq[:, None]

        def forward(weights, chars_value, words_value):
            return one_sequence(weights, chars_value, words_value, allowed, language_id)
        result, pullback = jax.vjp(forward, params, chars_seq.astype(jnp.float32), words_seq.astype(jnp.float32))
        weight_grads, chars_grad, words_grad = pullback(cotangent.astype(jnp.float32))
        grad_total = jax.tree.map(lambda first_arg, second_arg: first_arg + second_arg, grad_total, weight_grads)
        return (grad_total, (result.astype(jnp.bfloat16), chars_grad.astype(jnp.bfloat16), words_grad.astype(jnp.bfloat16)))
    zero_grads = jax.tree.map(jnp.zeros_like, params)
    grad_total, (outputs, chars_grads, words_grads) = lax.scan(sequence_step, zero_grads, (chars_seqs, words_seqs, counts_seqs, language_group, cotangents))
    g_cng, g_cnb, g_cqkv, g_cout, g_cmg, g_cmb, g_cup, g_cdown, g_query, g_proj, g_table, g_wng, g_wnb, g_wqkv, g_wout, g_wmg, g_wmb, g_wup, g_wdown = grad_total
    return (outputs.reshape(WORDS, D), chars_grads.reshape(WORDS, CHARS, C), words_grads.reshape(WORDS, D), g_cng, g_cnb, g_cqkv, g_cout, g_cmg, g_cmb, g_cup, g_cdown, g_query, g_proj, g_table, g_wng, g_wnb, g_wqkv, g_wout, g_wmg, g_wmb, g_wup, g_wdown)
```

```python
import functools

import jax
import jax.numpy as jnp
from jax import lax
from jax.experimental import pallas as pl
from jax.experimental.pallas import tpu as pltpu
from jax.sharding import PartitionSpec as P

HEAD = 64
CHAR_HEADS = 4
LEN = 1024
GROUP = 128


NORM_EPS = 1e-05
NEG_FILL = -1000000000.0
BOTH = ("dp", "mp")

MILLS = (
    1.253311622689609,
    -0.9998335569639131,
    0.6248507927954006,
    -0.32579329131060497,
    0.14074676904952854,
    -0.047188345811725166,
    0.011029079583978085,
    -0.0015426209716767891,
    9.501547722234882e-05,
)

NN = (((1,), (0,)), ((), ()))
NT = (((1,), (1,)), ((), ()))
TN = (((0,), (0,)), ((), ()))


def mm(first_arg, second_arg, dims=NN):
    return lax.dot_general(first_arg, second_arg, dims, preferred_element_type=jnp.float32)


def matmul(first_arg, second_arg):
    return jnp.dot(first_arg, second_arg, preferred_element_type=jnp.float32)


def low_sum(pattern, first_arg, second_arg):
    return jnp.einsum(pattern, first_arg, second_arg, preferred_element_type=jnp.float32)


def standardize(values):
    centred = values - jnp.mean(values, axis=-1, keepdims=True)
    inverse = lax.rsqrt(jnp.mean(centred * centred, axis=-1, keepdims=True) + NORM_EPS)
    return (centred * inverse, inverse)


def apply_norm(values, gain_value, bias_value):
    unit_rows, inverse = standardize(values)
    normed = (unit_rows * gain_value + bias_value).astype(jnp.bfloat16)
    return (unit_rows, inverse, normed)


def norm_back(grad_out, unit_rows, inverse, gain_value):
    grad_unit = grad_out * gain_value
    inner_sum = jnp.mean(grad_unit * unit_rows, axis=-1, keepdims=True)
    return inverse * (
        grad_unit - jnp.mean(grad_unit, axis=-1, keepdims=True) - unit_rows * inner_sum
    )


def gelu_pair(values):
    size = jnp.abs(values)
    density = jnp.exp2(values * values * -0.7213475204444817 - 1.3257480647361593)
    ratio = size * MILLS[8] + MILLS[7]
    for term in MILLS[6::-1]:
        ratio = ratio * size + term
    tail = density * ratio
    value = jnp.maximum(values, 0.0) - size * tail
    low_slope = tail - size * density
    slope = jnp.where(values >= 0.0, 1.0 - low_slope, low_slope)
    return (value, slope)


def split_two(values):
    high = values.astype(jnp.bfloat16)
    return (high, (values - high.astype(jnp.float32)).astype(jnp.bfloat16))


def fold_rows(values):
    return jnp.sum(values.reshape(values.shape[0] // 8, 8, values.shape[1]), axis=0)


def head_rows(rows, masks):
    return jnp.concatenate([rows * masks[h : h + 1] for h in range(CHAR_HEADS)], axis=0)


def gather_diagonal(square, lane_word, chars):
    words = square.shape[1] // chars
    blocks = square.reshape(CHAR_HEADS, words, chars, square.shape[1])
    kept = blocks[:, 0]
    for word in range(1, words):
        kept = jnp.where(lane_word == word, blocks[:, word], kept)
    return kept


def spread_diagonal(kept, word_masks, chars):
    words = kept.shape[2] // chars
    parts = [kept * word_masks[word : word + 1] for word in range(words)]
    return jnp.stack(parts, axis=1)


def char_forward_kernel(
    chars,
    chars_ref,
    lane_count_ref,
    row_count_ref,
    qkv_ref,
    out_ref,
    up_ref,
    down_ref,
    pool_ref,
    vecs_ref,
    head_mask_ref,
    word_mask_ref,
    cp_ref,
    probs_ref,
    co_ref,
    y1_ref,
    hidden_ref,
    slope_ref,
    y2_ref,
    pi_ref,
    pooled_ref,
):
    rows, width = chars_ref.shape
    states = chars_ref[...].astype(jnp.float32)
    _, _, normed = apply_norm(states, vecs_ref[0:1, :], vecs_ref[1:2, :])
    for part in range(3):
        cols = slice(part * width, (part + 1) * width)
        cp_ref[:, cols] = mm(normed, qkv_ref[:, cols]).astype(jnp.bfloat16)
    lane_word = lax.broadcasted_iota(jnp.int32, (1, 1, GROUP), 2) // chars
    key_slot = lax.broadcasted_iota(jnp.int32, (1, chars, GROUP), 1)
    masks = head_mask_ref[...]
    word_masks = word_mask_ref[...]
    for group in range(rows // GROUP):
        span = slice(group * GROUP, (group + 1) * GROUP)
        queries = cp_ref[span, 0:width]
        keys = head_rows(cp_ref[span, width : 2 * width], masks)
        values = head_rows(cp_ref[span, 2 * width : 3 * width], masks)
        scores = gather_diagonal(mm(keys, queries, NT), lane_word, chars) * HEAD ** (-0.5)
        scores = jnp.where(key_slot < lane_count_ref[group], scores, NEG_FILL)
        powers = jnp.exp(scores - jnp.max(scores, axis=1, keepdims=True))
        probs = (powers / jnp.sum(powers, axis=1, keepdims=True)).astype(jnp.bfloat16)
        probs_ref[group] = probs.reshape(CHAR_HEADS * chars, GROUP)
        spread = spread_diagonal(probs, word_masks, chars).reshape(CHAR_HEADS * GROUP, GROUP)
        co_ref[span, :] = mm(spread, values, TN).astype(jnp.bfloat16)
    after_attn = states + mm(co_ref[...], out_ref[...])
    y1_ref[...] = after_attn
    _, _, normed = apply_norm(after_attn, vecs_ref[2:3, :], vecs_ref[3:4, :])
    after_mlp = after_attn
    for part in range(up_ref.shape[1] // width):
        cols = slice(part * width, (part + 1) * width)
        hidden, slope = gelu_pair(mm(normed, up_ref[:, cols]))
        hidden = hidden.astype(jnp.bfloat16)
        hidden_ref[:, cols] = hidden
        slope_ref[:, cols] = slope.astype(jnp.bfloat16)
        after_mlp = after_mlp + mm(hidden, down_ref[cols, :])
    y2_ref[...] = after_mlp
    high, low = split_two(after_mlp)
    scores = mm(high, pool_ref[...]) + mm(low, pool_ref[...])
    scores = scores.reshape(rows // chars, chars, width)
    grid = after_mlp.reshape(rows // chars, chars, width)
    slot = lax.broadcasted_iota(jnp.int32, (1, chars, width), 1)
    scores = jnp.where(slot < row_count_ref[...], scores, NEG_FILL)
    powers = jnp.exp(scores - jnp.max(scores, axis=1, keepdims=True))
    pi = powers / jnp.sum(powers, axis=1, keepdims=True)
    pi_ref[...] = pi.reshape(rows, width).astype(jnp.bfloat16)
    pooled_ref[...] = jnp.sum(pi * grid, axis=1).astype(jnp.bfloat16)


def char_mlp_back_kernel(
    chars,
    y1_ref,
    y2_ref,
    pi_ref,
    grad_pooled_ref,
    hidden_ref,
    slope_ref,
    up_t_ref,
    down_t_ref,
    vecs_ref,
    ones_ref,
    grad_y1_ref,
    grad_up_ref,
    grad_down_t_ref,
    grad_vecs_ref,
):
    rows, width = y1_ref.shape
    words = rows // chars

    @pl.when(pl.program_id(0) == 0)
    def _():
        grad_up_ref[...] = jnp.zeros_like(grad_up_ref)
        grad_down_t_ref[...] = jnp.zeros_like(grad_down_t_ref)
        grad_vecs_ref[...] = jnp.zeros_like(grad_vecs_ref)

    grid = y2_ref[...].reshape(words, chars, width)
    pi = pi_ref[...].astype(jnp.float32).reshape(words, chars, width)
    grad_pooled = grad_pooled_ref[...]
    high, low = split_two((grid * grad_pooled).reshape(rows, width))
    grad_pi = (mm(high, ones_ref[...]) + mm(low, ones_ref[...])).reshape(words, chars, width)
    inner = jnp.sum(pi * grad_pi, axis=1, keepdims=True)
    grad_scores = pi * (grad_pi - inner) * HEAD ** (-0.5)
    grad_vecs_ref[0] += fold_rows((grad_scores * grid).reshape(rows, width))
    grad_y2 = (pi * grad_pooled + grad_scores * vecs_ref[4:5, :]).reshape(rows, width)
    branch = grad_y2.astype(jnp.bfloat16)
    branch_t = branch.T
    unit, inverse, normed = apply_norm(y1_ref[...], vecs_ref[2:3, :], vecs_ref[3:4, :])
    normed_t = normed.T
    grad_normed = None
    for part in range(hidden_ref.shape[1] // width):
        cols = slice(part * width, (part + 1) * width)
        grad_down_t_ref[:, cols] += mm(branch_t, hidden_ref[:, cols])
        grad_pre = mm(branch, down_t_ref[:, cols]) * slope_ref[:, cols].astype(jnp.float32)
        grad_pre = grad_pre.astype(jnp.bfloat16)
        grad_up_ref[:, cols] += mm(normed_t, grad_pre)
        term = mm(grad_pre, up_t_ref[cols, :])
        grad_normed = term if grad_normed is None else grad_normed + term
    grad_vecs_ref[1] += fold_rows(grad_normed * unit)
    grad_vecs_ref[2] += fold_rows(grad_normed)
    grad_y1_ref[...] = grad_y2 + norm_back(grad_normed, unit, inverse, vecs_ref[2:3, :])


def char_attn_back_kernel(
    chars,
    chars_ref,
    cp_ref,
    probs_ref,
    co_ref,
    grad_y1_ref,
    qkv_t_ref,
    out_t_ref,
    vecs_ref,
    head_mask_ref,
    word_mask_ref,
    grad_chars_ref,
    grad_qkv_ref,
    grad_out_ref,
    grad_vecs_ref,
    grad_cp_ref,
    grad_co_ref,
):
    rows, width = chars_ref.shape

    @pl.when(pl.program_id(0) == 0)
    def _():
        grad_qkv_ref[...] = jnp.zeros_like(grad_qkv_ref)
        grad_out_ref[...] = jnp.zeros_like(grad_out_ref)
        grad_vecs_ref[...] = jnp.zeros_like(grad_vecs_ref)

    grad_y1 = grad_y1_ref[...]
    branch = grad_y1.astype(jnp.bfloat16)
    grad_out_ref[...] += mm(co_ref[...].T, branch)
    grad_co_ref[...] = mm(branch, out_t_ref[...]).astype(jnp.bfloat16)
    lane_word = lax.broadcasted_iota(jnp.int32, (1, 1, GROUP), 2) // chars
    masks = head_mask_ref[...]
    word_masks = word_mask_ref[...]
    scale = HEAD ** (-0.5)
    for group in range(rows // GROUP):
        span = slice(group * GROUP, (group + 1) * GROUP)
        queries = head_rows(cp_ref[span, 0:width], masks)
        keys = head_rows(cp_ref[span, width : 2 * width], masks)
        values = head_rows(cp_ref[span, 2 * width : 3 * width], masks)
        grad_co = grad_co_ref[span, :]
        probs = probs_ref[group].reshape(CHAR_HEADS, chars, GROUP)
        probs_wide = probs.astype(jnp.float32)
        grad_probs = gather_diagonal(mm(values, grad_co, NT), lane_word, chars)
        inner = jnp.sum(grad_probs * probs_wide, axis=1, keepdims=True)
        grad_scores = (probs_wide * (grad_probs - inner)).astype(jnp.bfloat16)
        spread = spread_diagonal(probs, word_masks, chars).reshape(CHAR_HEADS, GROUP, GROUP)
        side = jnp.concatenate([spread[h] for h in range(CHAR_HEADS)], axis=1)
        grad_values = mm(side, head_rows(grad_co, masks))
        spread = spread_diagonal(grad_scores, word_masks, chars).reshape(CHAR_HEADS, GROUP, GROUP)
        side = jnp.concatenate([spread[h] for h in range(CHAR_HEADS)], axis=1)
        grad_keys = mm(side, queries) * scale
        grad_queries = mm(spread.reshape(CHAR_HEADS * GROUP, GROUP), keys, TN) * scale
        grad_cp_ref[span, 0:width] = grad_queries.astype(jnp.bfloat16)
        grad_cp_ref[span, width : 2 * width] = grad_keys.astype(jnp.bfloat16)
        grad_cp_ref[span, 2 * width : 3 * width] = grad_values.astype(jnp.bfloat16)
    states = chars_ref[...].astype(jnp.float32)
    unit, inverse, normed = apply_norm(states, vecs_ref[0:1, :], vecs_ref[1:2, :])
    normed_t = normed.T
    grad_normed = None
    for part in range(3):
        cols = slice(part * width, (part + 1) * width)
        grad_part = grad_cp_ref[:, cols]
        grad_qkv_ref[:, cols] += mm(normed_t, grad_part)
        term = mm(grad_part, qkv_t_ref[cols, :])
        grad_normed = term if grad_normed is None else grad_normed + term
    grad_vecs_ref[0] += fold_rows(grad_normed * unit)
    grad_vecs_ref[1] += fold_rows(grad_normed)
    grad_states = grad_y1 + norm_back(grad_normed, unit, inverse, vecs_ref[0:1, :])
    grad_chars_ref[...] = grad_states.astype(jnp.bfloat16)


def whole(shape):
    return pl.BlockSpec(shape, lambda step: (0,) * len(shape))


def blocked(shape):
    return pl.BlockSpec(shape, lambda step: (step,) + (0,) * (len(shape) - 1))


def params(megabytes):
    return pltpu.CompilerParams(
        dimension_semantics=("arbitrary",), vmem_limit_bytes=megabytes * 1024 * 1024
    )


def block_rows(rows, wanted):
    while rows % wanted:
        wanted //= 2
    return wanted


def char_forward(states, lane_counts, row_counts, weights, chars):
    rows, width = states.shape
    qkv, out, up, down, pool, vecs, head_masks, word_masks = weights
    block = block_rows(rows, 512)
    words, groups = block // chars, block // GROUP
    low, wide = jnp.bfloat16, jnp.float32
    shapes = (
        ((rows, 3 * width), low),
        ((rows // GROUP, CHAR_HEADS * chars, GROUP), low),
        ((rows, width), low),
        ((rows, width), wide),
        ((rows, up.shape[1]), low),
        ((rows, up.shape[1]), low),
        ((rows, width), wide),
        ((rows, width), low),
        ((rows // chars, width), low),
    )
    blocks = (
        (block, 3 * width),
        (groups, CHAR_HEADS * chars, GROUP),
        (block, width),
        (block, width),
        (block, up.shape[1]),
        (block, up.shape[1]),
        (block, width),
        (block, width),
        (words, width),
    )
    flops = 2 * rows * width * (4 * width + 2 * up.shape[1] + 8 * width)
    return pl.pallas_call(
        functools.partial(char_forward_kernel, chars),
        grid=(rows // block,),
        in_specs=[
            blocked((block, width)),
            blocked((groups, 1, GROUP)),
            blocked((words, 1, width)),
            whole(qkv.shape),
            whole(out.shape),
            whole(up.shape),
            whole(down.shape),
            whole(pool.shape),
            whole(vecs.shape),
            whole(head_masks.shape),
            whole(word_masks.shape),
        ],
        out_specs=[blocked(shape) for shape in blocks],
        out_shape=[jax.ShapeDtypeStruct(shape, kind) for shape, kind in shapes],
        compiler_params=params(56),
        cost_estimate=pl.CostEstimate(
            flops=flops, bytes_accessed=rows * width * 36, transcendentals=rows * width * 5
        ),
        name="char_forward",
    )(states, lane_counts, row_counts, qkv, out, up, down, pool, vecs, head_masks, word_masks)


def char_mlp_back(y1, y2, pi, grad_pooled, hidden, slope, weights, chars):
    rows, width = y1.shape
    up_t, down_t, vecs, ones = weights
    block = block_rows(rows, 512)
    hidden_width = hidden.shape[1]
    wide = jnp.float32
    flops = 2 * rows * width * (4 * hidden_width + 2 * width)
    return pl.pallas_call(
        functools.partial(char_mlp_back_kernel, chars),
        grid=(rows // block,),
        in_specs=[
            blocked((block, width)),
            blocked((block, width)),
            blocked((block, width)),
            blocked((block // chars, 1, width)),
            blocked((block, hidden_width)),
            blocked((block, hidden_width)),
            whole(up_t.shape),
            whole(down_t.shape),
            whole(vecs.shape),
            whole(ones.shape),
        ],
        out_specs=[
            blocked((block, width)),
            whole((width, hidden_width)),
            whole((width, hidden_width)),
            whole((3, 8, width)),
        ],
        out_shape=[
            jax.ShapeDtypeStruct((rows, width), wide),
            jax.ShapeDtypeStruct((width, hidden_width), wide),
            jax.ShapeDtypeStruct((width, hidden_width), wide),
            jax.ShapeDtypeStruct((3, 8, width), wide),
        ],
        compiler_params=params(56),
        cost_estimate=pl.CostEstimate(
            flops=flops, bytes_accessed=rows * width * 30, transcendentals=0
        ),
        name="char_mlp_back",
    )(y1, y2, pi, grad_pooled, hidden, slope, up_t, down_t, vecs, ones)


def char_attn_back(states, cp, probs, co, grad_y1, weights, chars):
    rows, width = states.shape
    qkv_t, out_t, vecs, head_masks, word_masks = weights
    block = block_rows(rows, 512)
    low, wide = jnp.bfloat16, jnp.float32
    flops = 2 * rows * width * 18 * width
    return pl.pallas_call(
        functools.partial(char_attn_back_kernel, chars),
        grid=(rows // block,),
        in_specs=[
            blocked((block, width)),
            blocked((block, 3 * width)),
            blocked((block // GROUP, CHAR_HEADS * chars, GROUP)),
            blocked((block, width)),
            blocked((block, width)),
            whole(qkv_t.shape),
            whole(out_t.shape),
            whole(vecs.shape),
            whole(head_masks.shape),
            whole(word_masks.shape),
        ],
        out_specs=[
            blocked((block, width)),
            whole((width, 3 * width)),
            whole((width, width)),
            whole((2, 8, width)),
        ],
        out_shape=[
            jax.ShapeDtypeStruct((rows, width), low),
            jax.ShapeDtypeStruct((width, 3 * width), wide),
            jax.ShapeDtypeStruct((width, width), wide),
            jax.ShapeDtypeStruct((2, 8, width), wide),
        ],
        scratch_shapes=[
            pltpu.VMEM((block, 3 * width), low),
            pltpu.VMEM((block, width), low),
        ],
        compiler_params=params(56),
        cost_estimate=pl.CostEstimate(
            flops=flops, bytes_accessed=rows * width * 18, transcendentals=0
        ),
        name="char_attn_back",
    )(states, cp, probs, co, grad_y1, qkv_t, out_t, vecs, head_masks, word_masks)


def attend_forward(queries, key_block, values, allowed):
    scores = low_sum("bqhd,bkhd->bhqk", queries, key_block) * HEAD ** (-0.5)
    scores = jnp.where(allowed, scores, NEG_FILL)
    row_max = jnp.max(scores, axis=-1, keepdims=True)
    powers = jnp.exp(scores - row_max)
    row_total = jnp.sum(powers, axis=-1, keepdims=True)
    attn_probs = (powers / row_total).astype(jnp.bfloat16)
    attn_mixed = low_sum("bhqk,bkhd->bqhd", attn_probs, values).astype(jnp.bfloat16)
    return (attn_mixed, row_max + jnp.log(row_total))


def attend_backward(queries, key_block, values, allowed, log_total, grad_mixed):
    scale = HEAD ** (-0.5)
    scores = low_sum("bqhd,bkhd->bhqk", queries, key_block) * scale
    attn_probs = jnp.where(allowed, jnp.exp(scores - log_total), 0.0)
    grad_probs = low_sum("bqhd,bkhd->bhqk", grad_mixed, values)
    grad_values = low_sum("bhqk,bqhd->bkhd", attn_probs.astype(jnp.bfloat16), grad_mixed)
    inner_sum = jnp.sum(grad_probs * attn_probs, axis=-1, keepdims=True)
    grad_scores = (attn_probs * (grad_probs - inner_sum)).astype(jnp.bfloat16)
    grad_queries = low_sum("bhqk,bkhd->bqhd", grad_scores, key_block) * scale
    grad_keys = low_sum("bhqk,bqhd->bkhd", grad_scores, queries) * scale
    return (grad_queries, grad_keys, grad_values)


def word_layer(residual, grad_rows, weights, norms, mp_size, mp_index):
    qkv, out_t, up, down_t = weights
    gain_one, bias_one, gain_two, bias_two = norms
    rows, width = residual.shape
    low = jnp.bfloat16
    sequences, length = max(1, rows // LEN), min(rows, LEN)
    share = LEN // length
    groups = [[a * share + b for b in range(share)] for a in range(mp_size // share)]
    unit_one, inverse_one, normed_one = apply_norm(residual, gain_one, bias_one)
    packed = low_sum("rd,tdc->trc", normed_one, qkv).astype(low)
    packed = packed.reshape(3, sequences, length, width // HEAD, HEAD)
    keys = packed[1:]
    start = 0
    if share > 1:
        keys = lax.all_gather(keys, "mp", axis=2, tiled=True, axis_index_groups=groups)
        start = lax.rem(mp_index, share) * length
    allowed = (
        lax.broadcasted_iota(jnp.int32, (length, LEN), 1)
        <= lax.broadcasted_iota(jnp.int32, (length, LEN), 0) + start
    )[None, None]
    mixed, log_total = attend_forward(packed[0], keys[0], keys[1], allowed)
    mixed_rows = mixed.reshape(rows, width)
    middle = residual + mm(mixed_rows, out_t, NT)
    unit_two, inverse_two, normed_two = apply_norm(middle, gain_two, bias_two)
    hidden, slope = gelu_pair(matmul(normed_two, up))
    hidden = hidden.astype(low)
    layer_output = (middle + mm(hidden, down_t, NT)).astype(low)
    grad_wide = grad_rows.astype(jnp.float32)
    grad_down_t = mm(grad_rows, hidden, TN)
    grad_pre = (matmul(grad_rows, down_t) * slope).astype(low)
    grad_up = mm(normed_two, grad_pre, TN)
    grad_normed = mm(grad_pre, up, NT)
    grad_gain_two = jnp.sum(grad_normed * unit_two, axis=0)
    grad_bias_two = jnp.sum(grad_normed, axis=0)
    grad_middle = grad_wide + norm_back(grad_normed, unit_two, inverse_two, gain_two)
    branch = grad_middle.astype(low)
    grad_out_t = mm(branch, mixed_rows, TN)
    grad_mixed = matmul(branch, out_t).astype(low).reshape(sequences, length, -1, HEAD)
    grad_queries, grad_keys, grad_values = attend_backward(
        packed[0], keys[0], keys[1], allowed, log_total, grad_mixed
    )
    grad_keys = jnp.stack((grad_keys, grad_values), axis=0)
    if share > 1:
        grad_keys = lax.psum_scatter(
            grad_keys, "mp", scatter_dimension=2, tiled=True, axis_index_groups=groups
        )
    grad_packed = jnp.concatenate((grad_queries[None], grad_keys), axis=0)
    grad_packed = grad_packed.reshape(3, rows, width).astype(low)
    grad_qkv = low_sum("rd,trc->tdc", normed_one, grad_packed)
    grad_normed = low_sum("trc,tdc->rd", grad_packed, qkv)
    grad_gain_one = jnp.sum(grad_normed * unit_one, axis=0)
    grad_bias_one = jnp.sum(grad_normed, axis=0)
    grad_residual = grad_middle + norm_back(grad_normed, unit_one, inverse_one, gain_one)
    return (
        layer_output,
        grad_residual,
        (grad_qkv, grad_out_t, grad_up, grad_down_t),
        (grad_gain_one, grad_bias_one, grad_gain_two, grad_bias_two),
    )


def blocks_of(array, count):
    return array.reshape(count, -1)


def shards(
    char_states,
    word_states,
    char_counts,
    language_group,
    output_grad,
    char_norm_gain,
    char_norm_bias,
    char_qkv,
    char_out,
    char_mlp_gain,
    char_mlp_bias,
    char_up,
    char_down,
    pool_query,
    char_proj,
    language_table,
    word_norm_gain,
    word_norm_bias,
    word_qkv,
    word_out,
    word_mlp_gain,
    word_mlp_bias,
    word_up,
    word_down,
):
    low, wide = jnp.bfloat16, jnp.float32
    dp_size, mp_size = lax.axis_size("dp"), lax.axis_size("mp")
    mp_index = lax.axis_index("mp")
    devices = dp_size * mp_size
    word_count, chars, width = char_states.shape
    model = word_states.shape[1]
    langs = language_table.shape[0]

    char_parts = (
        char_qkv,
        char_out,
        char_up,
        char_down,
        char_proj,
        char_norm_gain,
        char_norm_bias,
        char_mlp_gain,
        char_mlp_bias,
        pool_query,
        word_norm_gain,
        word_norm_bias,
        word_mlp_gain,
        word_mlp_bias,
        language_table.T,
    )
    flat = jnp.concatenate([part.astype(low).reshape(-1) for part in char_parts])
    flat_size = flat.shape[0]
    flat = jnp.pad(flat, (0, -flat_size % 2048))
    full = lax.all_gather(flat, BOTH, axis=0, tiled=False)
    unpacked, start = [], 0
    for part in char_parts:
        stop = start + part.size
        piece = full[:, start:stop].reshape((devices * part.shape[0],) + part.shape[1:])
        unpacked.append(piece)
        start = stop
    (
        qkv_char,
        out_char,
        up_char,
        down_char,
        proj_char,
        gain_attn,
        bias_attn,
        gain_mlp,
        bias_mlp,
        query_pool,
        gain_one,
        bias_one,
        gain_two,
        bias_two,
        table_t,
    ) = unpacked

    word_parts = (word_qkv, word_out.T, word_up, word_down.T)
    word_flat = jnp.concatenate([part.astype(low).reshape(-1, 128) for part in word_parts])
    word_full = lax.all_gather(word_flat, BOTH, axis=0, tiled=False)
    word_full = word_full.reshape(dp_size, mp_size, word_flat.shape[0], 128)
    word_weights, start = [], 0
    for part in word_parts:
        stop = start + part.size // 128
        piece = word_full[:, :, start:stop].reshape((dp_size, mp_size) + part.shape)
        if part.ndim == 3:
            piece = piece.transpose(2, 0, 3, 1, 4).reshape(3, model, model)
        else:
            piece = piece.transpose(0, 2, 1, 3)
            piece = piece.reshape(dp_size * part.shape[0], mp_size * part.shape[1])
        word_weights.append(piece)
        start = stop

    rows = word_count * chars
    states = char_states.reshape(rows, width)
    lane_counts = jnp.repeat(char_counts, chars).reshape(rows // GROUP, 1, GROUP)
    row_counts = jnp.broadcast_to(char_counts[:, None, None], (word_count, 1, width))
    feature_head = jnp.arange(width) // HEAD
    head_masks = (feature_head[None] == jnp.arange(8)[:, None]).astype(low)
    word_masks = (
        (jnp.arange(GROUP) // chars)[None] == jnp.arange(GROUP // chars)[:, None]
    ).astype(low)
    ones = (feature_head[:, None] == feature_head[None]).astype(low)
    pool = ones * (query_pool * HEAD ** (-0.5))[:, None]
    zero = jnp.zeros_like(gain_attn)
    vecs = jnp.stack(
        (gain_attn, bias_attn, gain_mlp, bias_mlp, query_pool, zero, zero, zero)
    ).astype(wide)
    cp, probs, co, y1, hidden, slope, y2, pi, pooled = char_forward(
        states,
        lane_counts,
        row_counts,
        (qkv_char, out_char, up_char, down_char, pool, vecs, head_masks, word_masks),
        chars,
    )

    sequences = max(1, word_count // LEN)
    first = (mp_index * word_count) // LEN
    language = lax.dynamic_slice_in_dim(language_group, first, sequences)
    language_hot = (language[:, None] == jnp.arange(langs)[None]).astype(wide)
    language_rows = jnp.sum(language_hot[:, :, None] * table_t.T.astype(wide)[None], axis=1)
    residual = word_states.astype(wide) + matmul(pooled, proj_char)
    residual = (
        residual.reshape(sequences, -1, model) + language_rows[:, None, :]
    ).reshape(word_count, model)
    norms = tuple(value.astype(wide) for value in (gain_one, bias_one, gain_two, bias_two))
    layer_output, grad_residual, word_grads, word_norm_grads = word_layer(
        residual, output_grad, word_weights, norms, mp_size, mp_index
    )
    grad_words = grad_residual.astype(low)
    sequence_grads = jnp.sum(grad_residual.reshape(sequences, -1, model), axis=1)
    grad_table = jnp.sum(language_hot[:, :, None] * sequence_grads[:, None, :], axis=0)

    pieces = []
    for part, grad in zip(word_parts, word_grads):
        if part.ndim == 3:
            grad = grad.reshape(3, dp_size, part.shape[1], mp_size, part.shape[2])
            grad = grad.transpose(3, 1, 0, 2, 4)
        else:
            grad = grad.reshape(dp_size, part.shape[0], mp_size, part.shape[1])
            grad = grad.transpose(2, 0, 1, 3)
        pieces.append(grad.astype(low).reshape(mp_size, dp_size, -1, 128))
    word_terms = jnp.concatenate(pieces, axis=2)
    word_terms = lax.psum_scatter(word_terms, "mp", scatter_dimension=0, tiled=True)
    word_terms = lax.psum_scatter(word_terms[0], "dp", scatter_dimension=0, tiled=True)[0]
    word_shares, start = [], 0
    for part in word_parts:
        stop = start + part.size // 128
        word_shares.append(word_terms[start:stop].reshape(part.shape).astype(wide))
        start = stop

    grad_proj = mm(pooled, grad_words, TN)
    grad_pooled = mm(grad_words, proj_char, NT).reshape(word_count, 1, width)
    grad_y1, grad_up, grad_down_t, mlp_vecs = char_mlp_back(
        y1, y2, pi, grad_pooled, hidden, slope, (up_char.T, down_char.T, vecs, ones), chars
    )
    mlp_vecs = jnp.sum(mlp_vecs, axis=1)
    early = (
        grad_up,
        grad_down_t.T,
        grad_proj,
        mlp_vecs[0],
        mlp_vecs[1],
        mlp_vecs[2],
        word_norm_grads[0],
        word_norm_grads[1],
        word_norm_grads[2],
        word_norm_grads[3],
        grad_table.T,
    )
    early_terms = jnp.concatenate([blocks_of(part, devices) for part in early], axis=1)
    early_size = early_terms.shape[1]
    early_terms = jnp.pad(early_terms, ((0, 0), (0, -early_size % 1024)))
    early_terms = lax.psum_scatter(early_terms, BOTH, scatter_dimension=0, tiled=True)[0]
    grad_chars, grad_qkv, grad_out, attn_vecs = char_attn_back(
        states, cp, probs, co, grad_y1, (qkv_char.T, out_char.T, vecs, head_masks, word_masks), chars
    )
    attn_vecs = jnp.sum(attn_vecs, axis=1)
    late = (grad_qkv, grad_out, attn_vecs[0], attn_vecs[1])
    late_terms = jnp.concatenate([blocks_of(part, devices) for part in late], axis=1)
    late_terms = jnp.pad(late_terms, ((0, 0), (0, -late_terms.shape[1] % 1024)))
    late_terms = lax.psum_scatter(late_terms, BOTH, scatter_dimension=0, tiled=True)[0]

    def take(terms, parts):
        shares, start = [], 0
        for part in parts:
            stop = start + part.size // devices
            shape = (part.shape[0] // devices,) + part.shape[1:]
            shares.append(terms[start:stop].reshape(shape))
            start = stop
        return shares

    (
        g_up,
        g_down,
        g_proj,
        g_query,
        g_gain_mlp,
        g_bias_mlp,
        g_gain_one,
        g_bias_one,
        g_gain_two,
        g_bias_two,
        g_table_t,
    ) = take(early_terms, early)
    g_qkv, g_out, g_gain_attn, g_bias_attn = take(late_terms, late)
    return (
        layer_output,
        grad_chars.reshape(char_states.shape),
        grad_words,
        g_gain_attn,
        g_bias_attn,
        g_qkv,
        g_out,
        g_gain_mlp,
        g_bias_mlp,
        g_up,
        g_down,
        g_query,
        g_proj,
        g_table_t.T,
        g_gain_one,
        g_bias_one,
        word_shares[0],
        word_shares[1].T,
        g_gain_two,
        g_bias_two,
        word_shares[2],
        word_shares[3].T,
    )


def solution(mesh):
    vector, rows = P(BOTH), P(BOTH, None)
    cube = P(BOTH, None, None)
    table = P(None, BOTH)
    words = (P(None, "dp", "mp"), P("mp", "dp"), P("dp", "mp"), P("mp", "dp"))
    char_weights = (
        vector, vector, rows, rows, vector, vector, rows, rows, vector, rows, table,
    )
    weights = char_weights + (
        vector, vector, words[0], words[1], vector, vector, words[2], words[3],
    )
    return jax.shard_map(
        shards,
        mesh=mesh,
        in_specs=(cube, rows, vector, P("dp"), rows) + weights,
        out_specs=(rows, cube, rows) + weights,
        check_vma=False,
    )
```

```python
import functools

import jax
import jax.numpy as jnp
from jax import lax
from jax.experimental import pallas as pl
from jax.experimental.pallas import tpu as pltpu
from jax.sharding import PartitionSpec as P

HEAD = 64
CHAR_HEADS = 4
LEN = 1024
GROUP = 128


NORM_EPS = 1e-05
NEG_FILL = -1000000000.0
BOTH = ("dp", "mp")
MESH = pl.DeviceIdType.MESH

MILLS = (
    1.253311622689609,
    -0.9998335569639131,
    0.6248507927954006,
    -0.32579329131060497,
    0.14074676904952854,
    -0.047188345811725166,
    0.011029079583978085,
    -0.0015426209716767891,
    9.501547722234882e-05,
)

NN = (((1,), (0,)), ((), ()))
NT = (((1,), (1,)), ((), ()))
TN = (((0,), (0,)), ((), ()))


def mm(first_arg, second_arg, dims=NN):
    return lax.dot_general(first_arg, second_arg, dims, preferred_element_type=jnp.float32)


def matmul(first_arg, second_arg):
    return jnp.dot(first_arg, second_arg, preferred_element_type=jnp.float32)


def low_sum(pattern, first_arg, second_arg):
    return jnp.einsum(pattern, first_arg, second_arg, preferred_element_type=jnp.float32)


def standardize(values):
    centred = values - jnp.mean(values, axis=-1, keepdims=True)
    inverse = lax.rsqrt(jnp.mean(centred * centred, axis=-1, keepdims=True) + NORM_EPS)
    return (centred * inverse, inverse)


def apply_norm(values, gain_value, bias_value):
    unit_rows, inverse = standardize(values)
    normed = (unit_rows * gain_value + bias_value).astype(jnp.bfloat16)
    return (unit_rows, inverse, normed)


def norm_back(grad_out, unit_rows, inverse, gain_value):
    grad_unit = grad_out * gain_value
    inner_sum = jnp.mean(grad_unit * unit_rows, axis=-1, keepdims=True)
    return inverse * (
        grad_unit - jnp.mean(grad_unit, axis=-1, keepdims=True) - unit_rows * inner_sum
    )


def gelu_pair(values):
    size = jnp.abs(values)
    density = jnp.exp2(values * values * -0.7213475204444817 - 1.3257480647361593)
    ratio = size * MILLS[8] + MILLS[7]
    for term in MILLS[6::-1]:
        ratio = ratio * size + term
    tail = density * ratio
    value = jnp.maximum(values, 0.0) - size * tail
    low_slope = tail - size * density
    slope = jnp.where(values >= 0.0, 1.0 - low_slope, low_slope)
    return (value, slope)


def split_two(values):
    high = values.astype(jnp.bfloat16)
    return (high, (values - high.astype(jnp.float32)).astype(jnp.bfloat16))


def fold_rows(values):
    return jnp.sum(values.reshape(values.shape[0] // 8, 8, values.shape[1]), axis=0)


class Place:
    def __init__(self, dp, mp):
        self.dp, self.mp, self.wide = dp, mp, mp // 2
        self.i, self.j = lax.axis_index("dp"), lax.axis_index("mp")
        self.x, self.core = self.j // 2, lax.rem(self.j, 2)

    def partner(self):
        return (self.i, 2 * self.x + 1 - self.core)

    def across(self, step):
        return (self.i, 2 * lax.rem(self.x + step, self.wide) + self.core)

    def along(self, step):
        return (lax.rem(self.i + step, self.dp), self.j)

    def greet(self):
        barrier = pltpu.get_barrier_semaphore()
        others = [self.partner()]
        others += [self.across(step) for step in range(1, self.wide)]
        others += [self.along(step) for step in range(1, self.dp)]
        for other in others:
            pl.semaphore_signal(barrier, inc=1, device_id=other, device_id_type=MESH)
        pl.semaphore_wait(barrier, len(others))


def remote(source, target, sems, index, device):
    return pltpu.make_async_remote_copy(
        src_ref=source,
        dst_ref=target,
        send_sem=sems[0].at[index],
        recv_sem=sems[1].at[index],
        device_id=device,
        device_id_type=MESH,
    )


class ScatterSum:
    def __init__(self, place, blocks, local, one, two, three, sems):
        self.place, self.blocks, self.local = place, blocks, local
        self.one, self.two, self.three, self.sems = one, two, three, sems

    def first(self):
        place = self.place
        return [
            remote(
                self.blocks.at[2 * e + 1 - place.core],
                self.one.at[e],
                self.sems,
                e,
                place.partner(),
            )
            for e in range(place.wide)
        ]

    def second(self):
        place = self.place
        return [
            remote(
                self.one.at[lax.rem(place.x + step, place.wide)],
                self.two.at[step - 1],
                self.sems,
                place.wide + step - 1,
                place.across(step),
            )
            for step in range(1, place.wide)
        ]

    def third(self):
        place = self.place
        return [
            remote(
                self.one.at[place.x, lax.rem(place.i + step, place.dp)],
                self.three.at[step - 1],
                self.sems,
                2 * place.wide - 1 + step - 1,
                place.along(step),
            )
            for step in range(1, place.dp)
        ]

    def start(self):
        for copy in self.first():
            copy.start()

    def go_across(self):
        place = self.place
        for copy in self.first():
            copy.wait()

        @pl.loop(0, place.dp)
        def _(row):
            for e in range(place.wide):
                own = self.local(e, row).astype(jnp.float32)
                total = self.one[e, row].astype(jnp.float32) + own
                self.one[e, row] = total.astype(jnp.bfloat16)

        for copy in self.second():
            copy.start()

    def go_along(self):
        place = self.place
        for copy in self.second():
            copy.wait()

        @pl.loop(0, place.dp)
        def _(row):
            total = self.one[place.x, row].astype(jnp.float32)
            for step in range(1, place.wide):
                total = total + self.two[step - 1, row].astype(jnp.float32)
            self.one[place.x, row] = total.astype(jnp.bfloat16)

        for copy in self.third():
            copy.start()

    def finish(self):
        place = self.place
        for copy in self.third():
            copy.wait()

        def own(rows):
            total = self.one[place.x, place.i, rows].astype(jnp.float32)
            for step in range(1, place.dp):
                total = total + self.three[step - 1, rows].astype(jnp.float32)
            return total

        return own


def scatter_scratch(dp, mp, n):
    wide = mp // 2
    copies = 2 * wide - 1 + dp - 1
    return [
        pltpu.VMEM((wide, dp, n, 128), jnp.bfloat16),
        pltpu.VMEM((max(1, wide - 1), dp, n, 128), jnp.bfloat16),
        pltpu.VMEM((dp - 1, n, 128), jnp.bfloat16),
        pltpu.SemaphoreType.DMA((copies,)),
        pltpu.SemaphoreType.DMA((copies,)),
    ]


def put_pairs(target, first_row, columns):
    mp, dp = target.shape[0], target.shape[1]
    rows = columns.shape[0] // (mp * dp)
    for pair in range(columns.shape[1] // 256):
        both = [
            columns[:, 256 * pair + 128 * c : 256 * pair + 128 * c + 128].reshape(
                dp, mp, rows, 128
            )
            for c in range(2)
        ]
        both = jnp.concatenate(both, axis=2).astype(jnp.bfloat16)
        spot = slice(first_row + 2 * rows * pair, first_row + 2 * rows * (pair + 1))
        for j in range(mp):
            target[j, :, spot, :] = both[:, j]


def gather_kernel(
    dp,
    mp,
    qkv_ref,
    out_ref,
    up_ref,
    down_ref,
    proj_ref,
    small_ref,
    word_qkv_ref,
    word_out_ref,
    word_up_ref,
    word_down_ref,
    qkv_all,
    qkv_t_all,
    out_all,
    out_t_all,
    up_all,
    up_t_all,
    down_all,
    down_t_all,
    proj_all,
    small_all,
    word_share,
    held,
    sends,
    arrivals,
):
    place = Place(dp, mp)
    low = jnp.bfloat16
    i, j = place.i, place.j
    row = 0
    for part in (qkv_ref, out_ref, up_ref, proj_ref):
        for pair in range(part.shape[1] // 256):
            both = [part[:, 256 * pair + 128 * c : 256 * pair + 128 * c + 128] for c in range(2)]
            held[i, j, row : row + 16, :] = jnp.concatenate(both, axis=0).astype(low)
            row += 16
    down_rows = down_ref.shape[0]
    for c in range(2):
        held[i, j, row : row + down_rows, :] = down_ref[:, 128 * c : 128 * c + 128].astype(low)
        row += down_rows
    held[i, j, row : row + 16, :] = small_ref[...].astype(low)
    place.greet()
    sems = (sends, arrivals)
    wide = place.wide

    def share(step, e):
        return held.at[
            lax.rem(i + dp - step, dp), 2 * lax.rem(place.x + wide - e, wide) + place.core
        ]

    def other_core(step, e):
        return held.at[
            lax.rem(i + dp - step, dp), 2 * lax.rem(place.x + wide - e, wide) + 1 - place.core
        ]

    def along(step):
        return remote(held.at[i, j], held.at[i, j], sems, step - 1, place.along(step))

    def across(step, e):
        index = dp - 1 + step * (wide - 1) + e - 1
        return remote(share(step, 0), share(step, 0), sems, index, place.across(e))

    def over(step, e):
        index = dp - 1 + dp * (wide - 1) + step * wide + e
        return remote(share(step, e), share(step, e), sems, index, place.partner())

    for step in range(1, dp):
        along(step).start()
    for e in range(1, wide):
        across(0, e).start()
    over(0, 0).start()

    rows = word_up_ref.shape[0]
    for t in range(3):
        word_share[rows * t : rows * (t + 1), :] = word_qkv_ref[t].astype(low)
    word_share[3 * rows : 4 * rows, :] = word_out_ref[...].T.astype(low)
    blocks = word_up_ref.shape[1] // 128
    for c in range(blocks):
        spot = slice((4 + c) * rows, (5 + c) * rows)
        word_share[spot, :] = word_up_ref[:, 128 * c : 128 * c + 128].astype(low)
        spot = slice((4 + blocks + c) * rows, (5 + blocks + c) * rows)
        word_share[spot, :] = word_down_ref[128 * c : 128 * c + 128, :].T.astype(low)

    for step in range(1, dp):
        along(step).wait_recv()
        for e in range(1, wide):
            across(step, e).start()
        over(step, 0).start()
    for step in range(dp):
        for e in range(1, wide):
            across(step, e).wait_recv()
            over(step, e).start()
    for step in range(dp):
        for e in range(wide):
            over(step, e).wait_recv()
    for step in range(1, dp):
        along(step).wait_send()
    for step in range(dp):
        for e in range(1, wide):
            across(step, e).wait_send()
        for e in range(wide):
            over(step, e).wait_send()

    count = dp * mp
    row = 0
    for target, target_t in (
        (qkv_all, qkv_t_all),
        (out_all, out_t_all),
        (up_all, up_t_all),
        (proj_all, None),
    ):
        for pair in range(target.shape[1] // 256):
            both = held[:, :, row : row + 16, :].reshape(count, 16, 128).astype(jnp.float32)
            row += 16
            for c in range(2):
                piece = both[:, 8 * c : 8 * c + 8].reshape(8 * count, 128).astype(low)
                spot = slice(256 * pair + 128 * c, 256 * pair + 128 * c + 128)
                target[:, spot] = piece
                if target_t is not None:
                    target_t[spot, :] = piece.T
    for c in range(2):
        piece = held[:, :, row : row + down_rows, :].reshape(count * down_rows, 128)
        row += down_rows
        down_all[:, 128 * c : 128 * c + 128] = piece
        down_t_all[128 * c : 128 * c + 128, :] = piece.T
    small_all[...] = held[:, :, row : row + 16, :].reshape(count, 16, 128)


def gather_weights(dp, mp, parts, small, word_parts):
    low = jnp.bfloat16
    qkv, out, up, down, proj = parts
    count = dp * mp
    width = qkv.shape[0] * count
    hidden = up.shape[1]
    model = proj.shape[1]
    rows = (qkv.shape[1] + out.shape[1] + up.shape[1] + proj.shape[1]) // 128 * 8
    rows += 2 * down.shape[0] + 16
    word_rows = sum(part.size for part in word_parts) // 128
    copies = dp - 1 + dp * (mp // 2 - 1) + dp * (mp // 2)
    shapes = (
        (width, 3 * width),
        (3 * width, width),
        (width, width),
        (width, width),
        (width, hidden),
        (hidden, width),
        (hidden, width),
        (width, hidden),
        (width, model),
        (count, 16, 128),
        (word_rows, 128),
    )
    vmem = pl.BlockSpec(memory_space=pltpu.VMEM)
    return pl.pallas_call(
        functools.partial(gather_kernel, dp, mp),
        in_specs=[vmem] * 10,
        out_specs=[vmem] * len(shapes),
        out_shape=[jax.ShapeDtypeStruct(shape, low) for shape in shapes],
        scratch_shapes=[
            pltpu.VMEM((dp, mp, rows, 128), low),
            pltpu.SemaphoreType.DMA((copies,)),
            pltpu.SemaphoreType.DMA((copies,)),
        ],
        compiler_params=pltpu.CompilerParams(
            collective_id=0, has_side_effects=True, vmem_limit_bytes=40 * 1024 * 1024
        ),
        name="gather_weights",
    )(qkv, out, up, down, proj, small, *word_parts)


def head_rows(rows, masks):
    return jnp.concatenate([rows * masks[h : h + 1] for h in range(CHAR_HEADS)], axis=0)


def gather_diagonal(square, lane_word, chars):
    words = square.shape[1] // chars
    blocks = square.reshape(CHAR_HEADS, words, chars, square.shape[1])
    kept = blocks[:, 0]
    for word in range(1, words):
        kept = jnp.where(lane_word == word, blocks[:, word], kept)
    return kept


def spread_diagonal(kept, word_masks, chars):
    words = kept.shape[2] // chars
    parts = [kept * word_masks[word : word + 1] for word in range(words)]
    return jnp.stack(parts, axis=1)


def char_forward_kernel(
    chars,
    chars_ref,
    lane_count_ref,
    row_count_ref,
    qkv_ref,
    out_ref,
    up_ref,
    down_ref,
    pool_ref,
    vecs_ref,
    head_mask_ref,
    word_mask_ref,
    cp_ref,
    probs_ref,
    co_ref,
    y1_ref,
    hidden_ref,
    slope_ref,
    y2_ref,
    pi_ref,
    pooled_ref,
):
    rows, width = chars_ref.shape
    states = chars_ref[...].astype(jnp.float32)
    _, _, normed = apply_norm(states, vecs_ref[0:1, :], vecs_ref[1:2, :])
    for part in range(3):
        cols = slice(part * width, (part + 1) * width)
        cp_ref[:, cols] = mm(normed, qkv_ref[:, cols]).astype(jnp.bfloat16)
    lane_word = lax.broadcasted_iota(jnp.int32, (1, 1, GROUP), 2) // chars
    key_slot = lax.broadcasted_iota(jnp.int32, (1, chars, GROUP), 1)
    masks = head_mask_ref[...]
    word_masks = word_mask_ref[...]
    for group in range(rows // GROUP):
        span = slice(group * GROUP, (group + 1) * GROUP)
        queries = cp_ref[span, 0:width]
        keys = head_rows(cp_ref[span, width : 2 * width], masks)
        values = head_rows(cp_ref[span, 2 * width : 3 * width], masks)
        scores = gather_diagonal(mm(keys, queries, NT), lane_word, chars) * HEAD ** (-0.5)
        scores = jnp.where(key_slot < lane_count_ref[group], scores, NEG_FILL)
        powers = jnp.exp(scores - jnp.max(scores, axis=1, keepdims=True))
        probs = (powers / jnp.sum(powers, axis=1, keepdims=True)).astype(jnp.bfloat16)
        probs_ref[group] = probs.reshape(CHAR_HEADS * chars, GROUP)
        spread = spread_diagonal(probs, word_masks, chars).reshape(CHAR_HEADS * GROUP, GROUP)
        co_ref[span, :] = mm(spread, values, TN).astype(jnp.bfloat16)
    after_attn = states + mm(co_ref[...], out_ref[...])
    y1_ref[...] = after_attn
    _, _, normed = apply_norm(after_attn, vecs_ref[2:3, :], vecs_ref[3:4, :])
    after_mlp = after_attn
    for part in range(up_ref.shape[1] // width):
        cols = slice(part * width, (part + 1) * width)
        hidden, slope = gelu_pair(mm(normed, up_ref[:, cols]))
        hidden = hidden.astype(jnp.bfloat16)
        hidden_ref[:, cols] = hidden
        slope_ref[:, cols] = slope.astype(jnp.bfloat16)
        after_mlp = after_mlp + mm(hidden, down_ref[cols, :])
    y2_ref[...] = after_mlp
    high, low = split_two(after_mlp)
    scores = mm(high, pool_ref[...]) + mm(low, pool_ref[...])
    scores = scores.reshape(rows // chars, chars, width)
    grid = after_mlp.reshape(rows // chars, chars, width)
    slot = lax.broadcasted_iota(jnp.int32, (1, chars, width), 1)
    scores = jnp.where(slot < row_count_ref[...], scores, NEG_FILL)
    powers = jnp.exp(scores - jnp.max(scores, axis=1, keepdims=True))
    pi = powers / jnp.sum(powers, axis=1, keepdims=True)
    pi_ref[...] = pi.reshape(rows, width).astype(jnp.bfloat16)
    pooled_ref[...] = jnp.sum(pi * grid, axis=1).astype(jnp.bfloat16)


def char_mlp_back_kernel(
    chars,
    exchange,
    y1_ref,
    y2_ref,
    pi_ref,
    grad_pooled_ref,
    hidden_ref,
    slope_ref,
    up_t_ref,
    down_t_ref,
    vecs_ref,
    ones_ref,
    *others,
):
    rows, width = y1_ref.shape
    words = rows // chars
    if exchange is None:
        grad_y1_ref, grad_up_ref, grad_down_t_ref, grad_vecs_ref = others
    else:
        (
            grad_proj_ref,
            word_small_ref,
            word_terms_ref,
            grad_y1_ref,
            char_terms_ref,
            word_qkv_ref,
            word_out_ref,
            word_up_ref,
            word_down_ref,
            grad_up_ref,
            grad_down_t_ref,
            grad_vecs_ref,
            local_ref,
            local_sem,
            one_ref,
            two_ref,
            three_ref,
            sends,
            arrivals,
        ) = others
        place = Place(*exchange)
        total = ScatterSum(
            place,
            word_terms_ref,
            lambda e, row: local_ref[e, row],
            one_ref,
            two_ref,
            three_ref,
            (sends, arrivals),
        )
        own = [
            pltpu.make_async_copy(
                word_terms_ref.at[2 * e + place.core], local_ref.at[e], local_sem.at[e]
            )
            for e in range(place.wide)
        ]
        step, last = pl.program_id(0), pl.num_programs(0) - 1

        @pl.when(step == 0)
        def _():
            place.greet()
            total.start()
            for copy in own:
                copy.start()

        @pl.when(step == last // 8)
        def _():
            for copy in own:
                copy.wait()
            total.go_across()

        @pl.when(step == last // 2 + 1)
        def _():
            total.go_along()

    @pl.when(pl.program_id(0) == 0)
    def _():
        grad_up_ref[...] = jnp.zeros_like(grad_up_ref)
        grad_down_t_ref[...] = jnp.zeros_like(grad_down_t_ref)
        grad_vecs_ref[...] = jnp.zeros_like(grad_vecs_ref)

    grid = y2_ref[...].reshape(words, chars, width)
    pi = pi_ref[...].astype(jnp.float32).reshape(words, chars, width)
    grad_pooled = grad_pooled_ref[...]
    high, low = split_two((grid * grad_pooled).reshape(rows, width))
    grad_pi = (mm(high, ones_ref[...]) + mm(low, ones_ref[...])).reshape(words, chars, width)
    inner = jnp.sum(pi * grad_pi, axis=1, keepdims=True)
    grad_scores = pi * (grad_pi - inner) * HEAD ** (-0.5)
    grad_vecs_ref[0] += fold_rows((grad_scores * grid).reshape(rows, width))
    grad_y2 = (pi * grad_pooled + grad_scores * vecs_ref[4:5, :]).reshape(rows, width)
    branch = grad_y2.astype(jnp.bfloat16)
    branch_t = branch.T
    unit, inverse, normed = apply_norm(y1_ref[...], vecs_ref[2:3, :], vecs_ref[3:4, :])
    normed_t = normed.T
    grad_normed = None
    for part in range(hidden_ref.shape[1] // width):
        cols = slice(part * width, (part + 1) * width)
        grad_down_t_ref[:, cols] += mm(branch_t, hidden_ref[:, cols])
        grad_pre = mm(branch, down_t_ref[:, cols]) * slope_ref[:, cols].astype(jnp.float32)
        grad_pre = grad_pre.astype(jnp.bfloat16)
        grad_up_ref[:, cols] += mm(normed_t, grad_pre)
        term = mm(grad_pre, up_t_ref[cols, :])
        grad_normed = term if grad_normed is None else grad_normed + term
    grad_vecs_ref[1] += fold_rows(grad_normed * unit)
    grad_vecs_ref[2] += fold_rows(grad_normed)
    grad_y1_ref[...] = grad_y2 + norm_back(grad_normed, unit, inverse, vecs_ref[2:3, :])
    if exchange is None:
        return

    @pl.when(step == last)
    def _():
        low = jnp.bfloat16
        share = hidden_ref.shape[1] // (place.dp * place.mp)
        put_pairs(char_terms_ref, 0, grad_up_ref[...])
        row = hidden_ref.shape[1] // 16
        for c in range(2):
            piece = grad_down_t_ref[128 * c : 128 * c + 128, :].T
            piece = piece.reshape(place.dp, place.mp, share, 128).astype(low)
            for j in range(place.mp):
                char_terms_ref[j, :, row : row + share, :] = piece[:, j]
            row += share
        put_pairs(char_terms_ref, row, grad_proj_ref[...])
        row += grad_proj_ref.shape[1] // 16
        sums = [jnp.sum(grad_vecs_ref[k], axis=0, keepdims=True) for k in range(3)]
        small_row = lax.broadcasted_iota(jnp.int32, (16, 128), 0)
        for b in range(word_small_ref.shape[0]):
            piece = word_small_ref[b]
            if b < 2:
                for k in range(3):
                    piece = jnp.where(
                        small_row == 12 + k, sums[k][:, 128 * b : 128 * b + 128], piece
                    )
            piece = jnp.broadcast_to(piece.astype(low), (place.dp, 16, 128))
            for j in range(place.mp):
                char_terms_ref[j, :, row : row + 16, :] = piece
            row += 16
        result = total.finish()
        block = word_up_ref.shape[0]
        for t in range(3):
            word_qkv_ref[t] = result(slice(block * t, block * (t + 1)))
        word_out_ref[...] = result(slice(3 * block, 4 * block)).T
        count = word_up_ref.shape[1] // 128
        for c in range(count):
            cols = slice(128 * c, 128 * c + 128)
            word_up_ref[:, cols] = result(slice((4 + c) * block, (5 + c) * block))
            spot = slice((4 + count + c) * block, (5 + count + c) * block)
            word_down_ref[cols, :] = result(spot).T


def char_attn_back_kernel(
    chars,
    exchange,
    chars_ref,
    cp_ref,
    probs_ref,
    co_ref,
    grad_y1_ref,
    qkv_t_ref,
    out_t_ref,
    vecs_ref,
    head_mask_ref,
    word_mask_ref,
    *others,
):
    rows, width = chars_ref.shape
    if exchange is None:
        (
            grad_chars_ref,
            grad_qkv_ref,
            grad_out_ref,
            grad_vecs_ref,
            grad_cp_ref,
            grad_co_ref,
        ) = others
    else:
        (
            early_terms_ref,
            grad_chars_ref,
            share_qkv_ref,
            share_out_ref,
            share_up_ref,
            share_down_ref,
            share_proj_ref,
            share_small_ref,
            share_vecs_ref,
            grad_cp_ref,
            grad_co_ref,
            grad_qkv_ref,
            grad_out_ref,
            grad_vecs_ref,
            local_ref,
            local_sem,
            late_terms_ref,
        ) = others[:17]
        early_refs, late_refs = others[17:22], others[22:27]
        place = Place(*exchange)
        early = ScatterSum(
            place,
            early_terms_ref,
            lambda e, row: local_ref[e, row],
            *early_refs[:3],
            early_refs[3:],
        )
        late = ScatterSum(
            place,
            late_terms_ref,
            lambda e, row: late_terms_ref[2 * e + place.core, row],
            *late_refs[:3],
            late_refs[3:],
        )
        own = [
            pltpu.make_async_copy(
                early_terms_ref.at[2 * e + place.core], local_ref.at[e], local_sem.at[e]
            )
            for e in range(place.wide)
        ]
        step, last = pl.program_id(0), pl.num_programs(0) - 1

        @pl.when(step == 0)
        def _():
            place.greet()
            early.start()
            for copy in own:
                copy.start()

        @pl.when(step == last // 8)
        def _():
            for copy in own:
                copy.wait()
            early.go_across()

        @pl.when(step == last // 2 + 1)
        def _():
            early.go_along()

    @pl.when(pl.program_id(0) == 0)
    def _():
        grad_qkv_ref[...] = jnp.zeros_like(grad_qkv_ref)
        grad_out_ref[...] = jnp.zeros_like(grad_out_ref)
        grad_vecs_ref[...] = jnp.zeros_like(grad_vecs_ref)

    grad_y1 = grad_y1_ref[...]
    branch = grad_y1.astype(jnp.bfloat16)
    grad_out_ref[...] += mm(co_ref[...].T, branch)
    grad_co_ref[...] = mm(branch, out_t_ref[...]).astype(jnp.bfloat16)
    lane_word = lax.broadcasted_iota(jnp.int32, (1, 1, GROUP), 2) // chars
    masks = head_mask_ref[...]
    word_masks = word_mask_ref[...]
    scale = HEAD ** (-0.5)
    for group in range(rows // GROUP):
        span = slice(group * GROUP, (group + 1) * GROUP)
        queries = head_rows(cp_ref[span, 0:width], masks)
        keys = head_rows(cp_ref[span, width : 2 * width], masks)
        values = head_rows(cp_ref[span, 2 * width : 3 * width], masks)
        grad_co = grad_co_ref[span, :]
        probs = probs_ref[group].reshape(CHAR_HEADS, chars, GROUP)
        probs_wide = probs.astype(jnp.float32)
        grad_probs = gather_diagonal(mm(values, grad_co, NT), lane_word, chars)
        inner = jnp.sum(grad_probs * probs_wide, axis=1, keepdims=True)
        grad_scores = (probs_wide * (grad_probs - inner)).astype(jnp.bfloat16)
        spread = spread_diagonal(probs, word_masks, chars).reshape(CHAR_HEADS, GROUP, GROUP)
        side = jnp.concatenate([spread[h] for h in range(CHAR_HEADS)], axis=1)
        grad_values = mm(side, head_rows(grad_co, masks))
        spread = spread_diagonal(grad_scores, word_masks, chars).reshape(CHAR_HEADS, GROUP, GROUP)
        side = jnp.concatenate([spread[h] for h in range(CHAR_HEADS)], axis=1)
        grad_keys = mm(side, queries) * scale
        grad_queries = mm(spread.reshape(CHAR_HEADS * GROUP, GROUP), keys, TN) * scale
        grad_cp_ref[span, 0:width] = grad_queries.astype(jnp.bfloat16)
        grad_cp_ref[span, width : 2 * width] = grad_keys.astype(jnp.bfloat16)
        grad_cp_ref[span, 2 * width : 3 * width] = grad_values.astype(jnp.bfloat16)
    states = chars_ref[...].astype(jnp.float32)
    unit, inverse, normed = apply_norm(states, vecs_ref[0:1, :], vecs_ref[1:2, :])
    normed_t = normed.T
    grad_normed = None
    for part in range(3):
        cols = slice(part * width, (part + 1) * width)
        grad_part = grad_cp_ref[:, cols]
        grad_qkv_ref[:, cols] += mm(normed_t, grad_part)
        term = mm(grad_part, qkv_t_ref[cols, :])
        grad_normed = term if grad_normed is None else grad_normed + term
    grad_vecs_ref[0] += fold_rows(grad_normed * unit)
    grad_vecs_ref[1] += fold_rows(grad_normed)
    grad_states = grad_y1 + norm_back(grad_normed, unit, inverse, vecs_ref[0:1, :])
    grad_chars_ref[...] = grad_states.astype(jnp.bfloat16)
    if exchange is None:
        return

    @pl.when(step == last)
    def _():
        low = jnp.bfloat16
        put_pairs(late_terms_ref, 0, grad_qkv_ref[...])
        row = 3 * width // 16
        put_pairs(late_terms_ref, row, grad_out_ref[...])
        row += width // 16
        sums = [jnp.sum(grad_vecs_ref[k], axis=0, keepdims=True) for k in range(2)]
        small_row = lax.broadcasted_iota(jnp.int32, (16, 128), 0)
        piece = jnp.zeros((16, 128), jnp.float32)
        for k in range(2):
            for b in range(2):
                piece = jnp.where(
                    small_row == 2 * k + b, sums[k][:, 128 * b : 128 * b + 128], piece
                )
        piece = jnp.broadcast_to(piece.astype(low), (place.dp, 16, 128))
        for j in range(place.mp):
            late_terms_ref[j, :, row : row + 16, :] = piece
        late.start()
        result = early.finish()
        row = 0
        for target, share in (
            (share_up_ref, 8),
            (share_down_ref, share_down_ref.shape[0]),
            (share_proj_ref, 8),
            (share_small_ref, 16),
        ):
            for c in range(target.shape[1] // 128):
                target[:, 128 * c : 128 * c + 128] = result(slice(row, row + share))
                row += share
        late.go_across()
        late.go_along()
        result = late.finish()
        row = 0
        for target in (share_qkv_ref, share_out_ref):
            for c in range(target.shape[1] // 128):
                target[:, 128 * c : 128 * c + 128] = result(slice(row, row + 8))
                row += 8
        share_vecs_ref[...] = result(slice(row, row + 16))


def whole(shape):
    return pl.BlockSpec(shape, lambda step: (0,) * len(shape))


def blocked(shape):
    return pl.BlockSpec(shape, lambda step: (step,) + (0,) * (len(shape) - 1))


def params(megabytes):
    return pltpu.CompilerParams(
        dimension_semantics=("arbitrary",), vmem_limit_bytes=megabytes * 1024 * 1024
    )


def block_rows(rows, wanted):
    while rows % wanted:
        wanted //= 2
    return wanted


def char_forward(states, lane_counts, row_counts, weights, chars):
    rows, width = states.shape
    qkv, out, up, down, pool, vecs, head_masks, word_masks = weights
    block = block_rows(rows, 512)
    words, groups = block // chars, block // GROUP
    low, wide = jnp.bfloat16, jnp.float32
    shapes = (
        ((rows, 3 * width), low),
        ((rows // GROUP, CHAR_HEADS * chars, GROUP), low),
        ((rows, width), low),
        ((rows, width), wide),
        ((rows, up.shape[1]), low),
        ((rows, up.shape[1]), low),
        ((rows, width), wide),
        ((rows, width), low),
        ((rows // chars, width), low),
    )
    blocks = (
        (block, 3 * width),
        (groups, CHAR_HEADS * chars, GROUP),
        (block, width),
        (block, width),
        (block, up.shape[1]),
        (block, up.shape[1]),
        (block, width),
        (block, width),
        (words, width),
    )
    flops = 2 * rows * width * (4 * width + 2 * up.shape[1] + 8 * width)
    return pl.pallas_call(
        functools.partial(char_forward_kernel, chars),
        grid=(rows // block,),
        in_specs=[
            blocked((block, width)),
            blocked((groups, 1, GROUP)),
            blocked((words, 1, width)),
            whole(qkv.shape),
            whole(out.shape),
            whole(up.shape),
            whole(down.shape),
            whole(pool.shape),
            whole(vecs.shape),
            whole(head_masks.shape),
            whole(word_masks.shape),
        ],
        out_specs=[blocked(shape) for shape in blocks],
        out_shape=[jax.ShapeDtypeStruct(shape, kind) for shape, kind in shapes],
        compiler_params=params(56),
        cost_estimate=pl.CostEstimate(
            flops=flops, bytes_accessed=rows * width * 36, transcendentals=rows * width * 5
        ),
        name="char_forward",
    )(states, lane_counts, row_counts, qkv, out, up, down, pool, vecs, head_masks, word_masks)


def char_mlp_back(y1, y2, pi, grad_pooled, hidden, slope, weights, chars):
    rows, width = y1.shape
    up_t, down_t, vecs, ones = weights
    block = block_rows(rows, 512)
    hidden_width = hidden.shape[1]
    wide = jnp.float32
    flops = 2 * rows * width * (4 * hidden_width + 2 * width)
    return pl.pallas_call(
        functools.partial(char_mlp_back_kernel, chars, None),
        grid=(rows // block,),
        in_specs=[
            blocked((block, width)),
            blocked((block, width)),
            blocked((block, width)),
            blocked((block // chars, 1, width)),
            blocked((block, hidden_width)),
            blocked((block, hidden_width)),
            whole(up_t.shape),
            whole(down_t.shape),
            whole(vecs.shape),
            whole(ones.shape),
        ],
        out_specs=[
            blocked((block, width)),
            whole((width, hidden_width)),
            whole((width, hidden_width)),
            whole((3, 8, width)),
        ],
        out_shape=[
            jax.ShapeDtypeStruct((rows, width), wide),
            jax.ShapeDtypeStruct((width, hidden_width), wide),
            jax.ShapeDtypeStruct((width, hidden_width), wide),
            jax.ShapeDtypeStruct((3, 8, width), wide),
        ],
        compiler_params=params(56),
        cost_estimate=pl.CostEstimate(
            flops=flops, bytes_accessed=rows * width * 30, transcendentals=0
        ),
        name="char_mlp_back",
    )(y1, y2, pi, grad_pooled, hidden, slope, up_t, down_t, vecs, ones)


def char_attn_back(states, cp, probs, co, grad_y1, weights, chars):
    rows, width = states.shape
    qkv_t, out_t, vecs, head_masks, word_masks = weights
    block = block_rows(rows, 512)
    low, wide = jnp.bfloat16, jnp.float32
    flops = 2 * rows * width * 18 * width
    return pl.pallas_call(
        functools.partial(char_attn_back_kernel, chars, None),
        grid=(rows // block,),
        in_specs=[
            blocked((block, width)),
            blocked((block, 3 * width)),
            blocked((block // GROUP, CHAR_HEADS * chars, GROUP)),
            blocked((block, width)),
            blocked((block, width)),
            whole(qkv_t.shape),
            whole(out_t.shape),
            whole(vecs.shape),
            whole(head_masks.shape),
            whole(word_masks.shape),
        ],
        out_specs=[
            blocked((block, width)),
            whole((width, 3 * width)),
            whole((width, width)),
            whole((2, 8, width)),
        ],
        out_shape=[
            jax.ShapeDtypeStruct((rows, width), low),
            jax.ShapeDtypeStruct((width, 3 * width), wide),
            jax.ShapeDtypeStruct((width, width), wide),
            jax.ShapeDtypeStruct((2, 8, width), wide),
        ],
        scratch_shapes=[
            pltpu.VMEM((block, 3 * width), low),
            pltpu.VMEM((block, width), low),
        ],
        compiler_params=params(56),
        cost_estimate=pl.CostEstimate(
            flops=flops, bytes_accessed=rows * width * 18, transcendentals=0
        ),
        name="char_attn_back",
    )(states, cp, probs, co, grad_y1, qkv_t, out_t, vecs, head_masks, word_masks)


def char_mlp_back_exchange(
    y1, y2, pi, grad_pooled, hidden, slope, weights, chars, mesh_size, grad_proj, word_small, word_terms
):
    rows, width = y1.shape
    up_t, down_t, vecs, ones = weights
    dp, mp = mesh_size
    block = block_rows(rows, 512)
    hidden_width = hidden.shape[1]
    low, wide = jnp.bfloat16, jnp.float32
    model = grad_proj.shape[1]
    flops = 2 * rows * width * (4 * hidden_width + 2 * width)
    char_rows = 2 * hidden_width // 16 + model // 16 + 16 * word_small.shape[0]
    n = word_terms.shape[2]
    share = model // dp
    outs = (
        ((rows, width), wide, blocked((block, width))),
        ((mp, dp, char_rows, 128), low, None),
        ((3, share, 128), wide, None),
        ((128, share), wide, None),
        ((share, model), wide, None),
        ((model, share), wide, None),
    )
    return pl.pallas_call(
        functools.partial(char_mlp_back_kernel, chars, mesh_size),
        grid=(rows // block,),
        in_specs=[
            blocked((block, width)),
            blocked((block, width)),
            blocked((block, width)),
            blocked((block // chars, 1, width)),
            blocked((block, hidden_width)),
            blocked((block, hidden_width)),
            whole(up_t.shape),
            whole(down_t.shape),
            whole(vecs.shape),
            whole(ones.shape),
            whole(grad_proj.shape),
            whole(word_small.shape),
            pl.BlockSpec(memory_space=pl.ANY),
        ],
        out_specs=[spec or whole(shape) for shape, _, spec in outs],
        out_shape=[jax.ShapeDtypeStruct(shape, kind) for shape, kind, _ in outs],
        scratch_shapes=[
            pltpu.VMEM((width, hidden_width), wide),
            pltpu.VMEM((width, hidden_width), wide),
            pltpu.VMEM((3, 8, width), wide),
            pltpu.VMEM((mp // 2, dp, n, 128), low),
            pltpu.SemaphoreType.DMA((mp // 2,)),
        ]
        + scatter_scratch(dp, mp, n),
        compiler_params=pltpu.CompilerParams(
            dimension_semantics=("arbitrary",),
            vmem_limit_bytes=60 * 1024 * 1024,
            collective_id=1,
            has_side_effects=True,
        ),
        cost_estimate=pl.CostEstimate(
            flops=flops, bytes_accessed=rows * width * 30, transcendentals=0
        ),
        name="char_mlp_back",
    )(
        y1, y2, pi, grad_pooled, hidden, slope, up_t, down_t, vecs, ones,
        grad_proj, word_small, word_terms,
    )


def char_attn_back_exchange(
    states, cp, probs, co, grad_y1, weights, chars, mesh_size, early_terms, hidden_width, model
):
    rows, width = states.shape
    qkv_t, out_t, vecs, head_masks, word_masks = weights
    dp, mp = mesh_size
    count = dp * mp
    block = block_rows(rows, 512)
    low, wide = jnp.bfloat16, jnp.float32
    flops = 2 * rows * width * 18 * width
    n = early_terms.shape[2]
    late = 4 * width // 16 + 16
    outs = (
        ((rows, width), low, blocked((block, width))),
        ((width // count, 3 * width), wide, None),
        ((width // count, width), wide, None),
        ((width // count, hidden_width), wide, None),
        ((hidden_width // count, width), wide, None),
        ((width // count, model), wide, None),
        ((16, model), wide, None),
        ((16, 128), wide, None),
    )
    return pl.pallas_call(
        functools.partial(char_attn_back_kernel, chars, mesh_size),
        grid=(rows // block,),
        in_specs=[
            blocked((block, width)),
            blocked((block, 3 * width)),
            blocked((block // GROUP, CHAR_HEADS * chars, GROUP)),
            blocked((block, width)),
            blocked((block, width)),
            whole(qkv_t.shape),
            whole(out_t.shape),
            whole(vecs.shape),
            whole(head_masks.shape),
            whole(word_masks.shape),
            pl.BlockSpec(memory_space=pl.ANY),
        ],
        out_specs=[spec or whole(shape) for shape, _, spec in outs],
        out_shape=[jax.ShapeDtypeStruct(shape, kind) for shape, kind, _ in outs],
        scratch_shapes=[
            pltpu.VMEM((block, 3 * width), low),
            pltpu.VMEM((block, width), low),
            pltpu.VMEM((width, 3 * width), wide),
            pltpu.VMEM((width, width), wide),
            pltpu.VMEM((2, 8, width), wide),
            pltpu.VMEM((mp // 2, dp, n, 128), low),
            pltpu.SemaphoreType.DMA((mp // 2,)),
            pltpu.VMEM((mp, dp, late, 128), low),
        ]
        + scatter_scratch(dp, mp, n)
        + scatter_scratch(dp, mp, late),
        compiler_params=pltpu.CompilerParams(
            dimension_semantics=("arbitrary",),
            vmem_limit_bytes=56 * 1024 * 1024,
            collective_id=2,
            has_side_effects=True,
        ),
        cost_estimate=pl.CostEstimate(
            flops=flops, bytes_accessed=rows * width * 18, transcendentals=0
        ),
        name="char_attn_back",
    )(states, cp, probs, co, grad_y1, qkv_t, out_t, vecs, head_masks, word_masks, early_terms)


def word_kernel(
    pooled_ref,
    words_ref,
    cotangent_ref,
    language_ref,
    language_hot_ref,
    proj_ref,
    weights_ref,
    norms_ref,
    head_mask_ref,
    layer_ref,
    grad_words_ref,
    terms_ref,
    grad_proj_ref,
    grad_pooled_ref,
    small_ref,
    residual_ref,
    normed_one_ref,
    packed_ref,
    probs_ref,
    mixed_ref,
    middle_ref,
    normed_two_ref,
    hidden_ref,
    slope_ref,
    grad_middle_ref,
    branch_ref,
    grad_mixed_ref,
    grad_keys_ref,
    grad_values_ref,
    sums_ref,
):
    low, wide = jnp.bfloat16, jnp.float32
    length, model = words_ref.shape
    dp, mp = weights_ref.shape[:2]
    share = model // dp
    row_block = 256
    blocks = length // row_block
    hidden_width = hidden_ref.shape[1]
    up_blocks = hidden_width // mp // 128
    scale = HEAD ** (-0.5)
    up_base, down_base = 4 * share, (4 + up_blocks) * share

    def weight(base, first, last):
        pieces = [
            weights_ref[:, j, base + c * share : base + (c + 1) * share, :].reshape(model, 128)
            for j, c in (column(base, block) for block in range(first, last))
        ]
        return jnp.concatenate(pieces, axis=1)

    def column(base, block):
        return (block, 0) if base < up_base else (block // up_blocks, block % up_blocks)

    def put(base, first, grad):
        for k in range(grad.shape[1] // 128):
            j, c = column(base, first + k)
            piece = grad[:, 128 * k : 128 * k + 128].reshape(dp, share, 128).astype(low)
            terms_ref[j, :, base + c * share : base + (c + 1) * share, :] = piece

    def norm(k):
        return norms_ref[k : k + 1, :]

    sums_ref[...] = jnp.zeros_like(sums_ref)

    @pl.loop(0, blocks)
    def _(block):
        span = pl.ds(pl.multiple_of(block * row_block, row_block), row_block)
        residual = words_ref[span, :].astype(wide) + mm(pooled_ref[span, :], proj_ref[...])
        residual = residual + language_ref[...]
        residual_ref[span, :] = residual
        _, _, normed = apply_norm(residual, norm(0), norm(1))
        normed_one_ref[span, :] = normed
        for t in range(3):
            for c in range(0, model // 128, 2):
                cols = slice(128 * c, 128 * c + 256)
                packed_ref[t, span, cols] = mm(normed, weight(t * share, c, c + 2)).astype(low)

    causal = lax.broadcasted_iota(jnp.int32, (row_block, row_block), 0) <= (
        lax.broadcasted_iota(jnp.int32, (row_block, row_block), 1)
    )

    @pl.loop(0, model // 128)
    def _(pair):
        lanes = pl.ds(pl.multiple_of(pair * 128, 128), 128)
        values_t = packed_ref[2, :, lanes].T
        for block in range(blocks):
            stop = (block + 1) * row_block
            span = slice(block * row_block, stop)
            first = block * (block + 1) // 2 * row_block
            queries = packed_ref[0, span, lanes]
            mixed = []
            for h in range(2):
                keys = packed_ref[1, 0:stop, lanes] * head_mask_ref[h : h + 1, 0:128]
                scores = mm(keys, queries, NT) * scale
                near = jnp.where(causal, scores[stop - row_block :], NEG_FILL)
                scores = jnp.concatenate([scores[: stop - row_block], near]) if block else near
                powers = jnp.exp(scores - jnp.max(scores, axis=0, keepdims=True))
                probs = powers * (1.0 / jnp.sum(powers, axis=0, keepdims=True))
                probs = probs.astype(low)
                probs_ref[2 * pair + h, first : first + stop, :] = probs
                mixed.append(mm(values_t[HEAD * h : HEAD * (h + 1), 0:stop], probs))
            mixed_ref[span, lanes] = jnp.concatenate(mixed, axis=0).T.astype(low)

    @pl.loop(0, blocks)
    def _(block):
        span = pl.ds(pl.multiple_of(block * row_block, row_block), row_block)
        out_t = weight(3 * share, 0, model // 128)
        middle = residual_ref[span, :] + mm(mixed_ref[span, :], out_t, NT)
        middle_ref[span, :] = middle
        _, _, normed = apply_norm(middle, norm(2), norm(3))
        normed_two_ref[span, :] = normed
        total = middle
        for c in range(0, hidden_width // 128, 4):
            cols = slice(128 * c, 128 * c + 512)
            hidden, slope = gelu_pair(mm(normed, weight(up_base, c, c + 4)))
            hidden = hidden.astype(low)
            hidden_ref[span, cols] = hidden
            slope_ref[span, cols] = slope.astype(low)
            total = total + mm(hidden, weight(down_base, c, c + 4), NT)
        layer_ref[span, :] = total.astype(low)

    cotangent_t = cotangent_ref[...].T
    for c in range(0, hidden_width // 128, 2):
        put(down_base, c, mm(cotangent_t, hidden_ref[:, 128 * c : 128 * c + 256]))

    @pl.loop(0, blocks)
    def _(block):
        span = pl.ds(pl.multiple_of(block * row_block, row_block), row_block)
        cotangent = cotangent_ref[span, :]
        grad_normed = None
        for c in range(0, hidden_width // 128, 4):
            cols = slice(128 * c, 128 * c + 512)
            grad_pre = mm(cotangent, weight(down_base, c, c + 4))
            grad_pre = (grad_pre * slope_ref[span, cols].astype(wide)).astype(low)
            slope_ref[span, cols] = grad_pre
            term = mm(grad_pre, weight(up_base, c, c + 4), NT)
            grad_normed = term if grad_normed is None else grad_normed + term
        unit, inverse = standardize(middle_ref[span, :])
        sums_ref[2] += fold_rows(grad_normed * unit)
        sums_ref[3] += fold_rows(grad_normed)
        grad_middle = cotangent.astype(wide) + norm_back(grad_normed, unit, inverse, norm(2))
        grad_middle_ref[span, :] = grad_middle
        branch = grad_middle.astype(low)
        branch_ref[span, :] = branch
        out_t = weight(3 * share, 0, model // 128)
        grad_mixed_ref[span, :] = mm(branch, out_t).astype(low)

    normed_t = normed_two_ref[...].T
    for c in range(0, hidden_width // 128, 2):
        put(up_base, c, mm(normed_t, slope_ref[:, 128 * c : 128 * c + 256]))
    branch_t = branch_ref[...].T
    for c in range(0, model // 128, 2):
        put(3 * share, c, mm(branch_t, mixed_ref[:, 128 * c : 128 * c + 256]))

    @pl.loop(0, model // 128)
    def _(pair):
        lanes = pl.ds(pl.multiple_of(pair * 128, 128), 128)
        grad_keys_ref[...] = jnp.zeros_like(grad_keys_ref)
        grad_values_ref[...] = jnp.zeros_like(grad_values_ref)
        keys_t = packed_ref[1, :, lanes].T
        for block in range(blocks):
            stop = (block + 1) * row_block
            span = slice(block * row_block, stop)
            first = block * (block + 1) // 2 * row_block
            queries = packed_ref[0, span, lanes]
            grad_mixed = grad_mixed_ref[span, lanes]
            grad_queries = []
            for h in range(2):
                mask = head_mask_ref[h : h + 1, 0:128]
                values = packed_ref[2, 0:stop, lanes] * mask
                grad_probs = mm(values, grad_mixed, NT)
                probs = probs_ref[2 * pair + h, first : first + stop, :]
                probs_wide = probs.astype(wide)
                inner = jnp.sum(grad_probs * probs_wide, axis=0, keepdims=True)
                grad_scores = (probs_wide * (grad_probs - inner)).astype(low)
                grad_values_ref[0:stop, :] += mm(probs, grad_mixed * mask)
                grad_keys_ref[0:stop, :] += mm(grad_scores, queries * mask)
                grad_queries.append(mm(keys_t[HEAD * h : HEAD * (h + 1), 0:stop], grad_scores))
            grad_queries = jnp.concatenate(grad_queries, axis=0) * scale
            packed_ref[0, span, lanes] = grad_queries.T.astype(low)
        packed_ref[1, :, lanes] = (grad_keys_ref[...] * scale).astype(low)
        packed_ref[2, :, lanes] = grad_values_ref[...].astype(low)

    normed_t = normed_one_ref[...].T
    for t in range(3):
        for c in range(0, model // 128, 2):
            put(t * share, c, mm(normed_t, packed_ref[t, :, 128 * c : 128 * c + 256]))

    @pl.loop(0, blocks)
    def _(block):
        span = pl.ds(pl.multiple_of(block * row_block, row_block), row_block)
        grad_normed = None
        for t in range(3):
            term = mm(packed_ref[t, span, :], weight(t * share, 0, model // 128), NT)
            grad_normed = term if grad_normed is None else grad_normed + term
        unit, inverse = standardize(residual_ref[span, :])
        sums_ref[0] += fold_rows(grad_normed * unit)
        sums_ref[1] += fold_rows(grad_normed)
        grad = grad_middle_ref[span, :] + norm_back(grad_normed, unit, inverse, norm(0))
        sums_ref[4] += fold_rows(grad)
        grad = grad.astype(low)
        grad_words_ref[span, :] = grad
        grad_pooled_ref[span] = mm(grad, proj_ref[...], NT)[:, None, :]

    grad_proj_ref[...] = mm(pooled_ref[...].T, grad_words_ref[...])

    sums = [jnp.sum(sums_ref[k], axis=0, keepdims=True) for k in range(5)]
    small_row = lax.broadcasted_iota(jnp.int32, (8, 128), 0)
    for b in range(model // 128):
        cols = slice(128 * b, 128 * b + 128)
        small_ref[b, 0:8, :] = language_hot_ref[...] * sums[4][:, cols]
        piece = jnp.zeros((8, 128), wide)
        for k in range(4):
            piece = jnp.where(small_row == k, sums[k][:, cols], piece)
        small_ref[b, 8:16, :] = piece


def word_layer_kernel(pooled, words, cotangent, language_row, language_hot, proj, weights, norms, head_masks):
    low, wide = jnp.bfloat16, jnp.float32
    length, model = words.shape
    width = pooled.shape[1]
    dp, mp, n = weights.shape[:3]
    hidden_width = (n * dp // model - 4) // 2 * 128 * mp
    blocks = length // 256
    heads = model // HEAD
    vmem = pl.BlockSpec(memory_space=pltpu.VMEM)
    outs = (
        ((length, model), low),
        ((length, model), low),
        ((mp, dp, n, 128), low),
        ((width, model), wide),
        ((length, 1, width), wide),
        ((model // 128, 16, 128), wide),
    )
    return pl.pallas_call(
        word_kernel,
        in_specs=[vmem] * 9,
        out_specs=[vmem] * len(outs),
        out_shape=[jax.ShapeDtypeStruct(shape, kind) for shape, kind in outs],
        scratch_shapes=[
            pltpu.VMEM((length, model), wide),
            pltpu.VMEM((length, model), low),
            pltpu.VMEM((3, length, model), low),
            pltpu.VMEM((heads, blocks * (blocks + 1) // 2 * 256, 256), low),
            pltpu.VMEM((length, model), low),
            pltpu.VMEM((length, model), wide),
            pltpu.VMEM((length, model), low),
            pltpu.VMEM((length, hidden_width), low),
            pltpu.VMEM((length, hidden_width), low),
            pltpu.VMEM((length, model), wide),
            pltpu.VMEM((length, model), low),
            pltpu.VMEM((length, model), low),
            pltpu.VMEM((length, 128), wide),
            pltpu.VMEM((length, 128), wide),
            pltpu.VMEM((5, 8, model), wide),
        ],
        compiler_params=pltpu.CompilerParams(vmem_limit_bytes=62 * 1024 * 1024),
        cost_estimate=pl.CostEstimate(
            flops=40 * 10**9, bytes_accessed=20 * 2**20, transcendentals=10**7
        ),
        name="word_layer",
    )(pooled, words, cotangent, language_row, language_hot, proj, weights, norms, head_masks)


def attend_forward(queries, key_block, values, allowed):
    scores = low_sum("bqhd,bkhd->bhqk", queries, key_block) * HEAD ** (-0.5)
    scores = jnp.where(allowed, scores, NEG_FILL)
    row_max = jnp.max(scores, axis=-1, keepdims=True)
    powers = jnp.exp(scores - row_max)
    row_total = jnp.sum(powers, axis=-1, keepdims=True)
    attn_probs = (powers / row_total).astype(jnp.bfloat16)
    attn_mixed = low_sum("bhqk,bkhd->bqhd", attn_probs, values).astype(jnp.bfloat16)
    return (attn_mixed, row_max + jnp.log(row_total))


def attend_backward(queries, key_block, values, allowed, log_total, grad_mixed):
    scale = HEAD ** (-0.5)
    scores = low_sum("bqhd,bkhd->bhqk", queries, key_block) * scale
    attn_probs = jnp.where(allowed, jnp.exp(scores - log_total), 0.0)
    grad_probs = low_sum("bqhd,bkhd->bhqk", grad_mixed, values)
    grad_values = low_sum("bhqk,bqhd->bkhd", attn_probs.astype(jnp.bfloat16), grad_mixed)
    inner_sum = jnp.sum(grad_probs * attn_probs, axis=-1, keepdims=True)
    grad_scores = (attn_probs * (grad_probs - inner_sum)).astype(jnp.bfloat16)
    grad_queries = low_sum("bhqk,bkhd->bqhd", grad_scores, key_block) * scale
    grad_keys = low_sum("bhqk,bqhd->bkhd", grad_scores, queries) * scale
    return (grad_queries, grad_keys, grad_values)


def word_layer(residual, grad_rows, weights, norms, mp_size, mp_index):
    qkv, out_t, up, down_t = weights
    gain_one, bias_one, gain_two, bias_two = norms
    rows, width = residual.shape
    low = jnp.bfloat16
    sequences, length = max(1, rows // LEN), min(rows, LEN)
    share = LEN // length
    groups = [[a * share + b for b in range(share)] for a in range(mp_size // share)]
    unit_one, inverse_one, normed_one = apply_norm(residual, gain_one, bias_one)
    packed = low_sum("rd,tdc->trc", normed_one, qkv).astype(low)
    packed = packed.reshape(3, sequences, length, width // HEAD, HEAD)
    keys = packed[1:]
    start = 0
    if share > 1:
        keys = lax.all_gather(keys, "mp", axis=2, tiled=True, axis_index_groups=groups)
        start = lax.rem(mp_index, share) * length
    allowed = (
        lax.broadcasted_iota(jnp.int32, (length, LEN), 1)
        <= lax.broadcasted_iota(jnp.int32, (length, LEN), 0) + start
    )[None, None]
    mixed, log_total = attend_forward(packed[0], keys[0], keys[1], allowed)
    mixed_rows = mixed.reshape(rows, width)
    middle = residual + mm(mixed_rows, out_t, NT)
    unit_two, inverse_two, normed_two = apply_norm(middle, gain_two, bias_two)
    hidden, slope = gelu_pair(matmul(normed_two, up))
    hidden = hidden.astype(low)
    layer_output = (middle + mm(hidden, down_t, NT)).astype(low)
    grad_wide = grad_rows.astype(jnp.float32)
    grad_down_t = mm(grad_rows, hidden, TN)
    grad_pre = (matmul(grad_rows, down_t) * slope).astype(low)
    grad_up = mm(normed_two, grad_pre, TN)
    grad_normed = mm(grad_pre, up, NT)
    grad_gain_two = jnp.sum(grad_normed * unit_two, axis=0)
    grad_bias_two = jnp.sum(grad_normed, axis=0)
    grad_middle = grad_wide + norm_back(grad_normed, unit_two, inverse_two, gain_two)
    branch = grad_middle.astype(low)
    grad_out_t = mm(branch, mixed_rows, TN)
    grad_mixed = matmul(branch, out_t).astype(low).reshape(sequences, length, -1, HEAD)
    grad_queries, grad_keys, grad_values = attend_backward(
        packed[0], keys[0], keys[1], allowed, log_total, grad_mixed
    )
    grad_keys = jnp.stack((grad_keys, grad_values), axis=0)
    if share > 1:
        grad_keys = lax.psum_scatter(
            grad_keys, "mp", scatter_dimension=2, tiled=True, axis_index_groups=groups
        )
    grad_packed = jnp.concatenate((grad_queries[None], grad_keys), axis=0)
    grad_packed = grad_packed.reshape(3, rows, width).astype(low)
    grad_qkv = low_sum("rd,trc->tdc", normed_one, grad_packed)
    grad_normed = low_sum("trc,tdc->rd", grad_packed, qkv)
    grad_gain_one = jnp.sum(grad_normed * unit_one, axis=0)
    grad_bias_one = jnp.sum(grad_normed, axis=0)
    grad_residual = grad_middle + norm_back(grad_normed, unit_one, inverse_one, gain_one)
    return (
        layer_output,
        grad_residual,
        (grad_qkv, grad_out_t, grad_up, grad_down_t),
        (grad_gain_one, grad_bias_one, grad_gain_two, grad_bias_two),
    )


def blocks_of(array, count):
    return array.reshape(count, -1)


def shards_general(
    char_states,
    word_states,
    char_counts,
    language_group,
    output_grad,
    char_norm_gain,
    char_norm_bias,
    char_qkv,
    char_out,
    char_mlp_gain,
    char_mlp_bias,
    char_up,
    char_down,
    pool_query,
    char_proj,
    language_table,
    word_norm_gain,
    word_norm_bias,
    word_qkv,
    word_out,
    word_mlp_gain,
    word_mlp_bias,
    word_up,
    word_down,
):
    low, wide = jnp.bfloat16, jnp.float32
    dp_size, mp_size = lax.axis_size("dp"), lax.axis_size("mp")
    mp_index = lax.axis_index("mp")
    devices = dp_size * mp_size
    word_count, chars, width = char_states.shape
    model = word_states.shape[1]
    langs = language_table.shape[0]

    char_parts = (
        char_qkv,
        char_out,
        char_up,
        char_down,
        char_proj,
        char_norm_gain,
        char_norm_bias,
        char_mlp_gain,
        char_mlp_bias,
        pool_query,
        word_norm_gain,
        word_norm_bias,
        word_mlp_gain,
        word_mlp_bias,
        language_table.T,
    )
    flat = jnp.concatenate([part.astype(low).reshape(-1) for part in char_parts])
    flat_size = flat.shape[0]
    flat = jnp.pad(flat, (0, -flat_size % 2048))
    full = lax.all_gather(flat, BOTH, axis=0, tiled=False)
    unpacked, start = [], 0
    for part in char_parts:
        stop = start + part.size
        piece = full[:, start:stop].reshape((devices * part.shape[0],) + part.shape[1:])
        unpacked.append(piece)
        start = stop
    (
        qkv_char,
        out_char,
        up_char,
        down_char,
        proj_char,
        gain_attn,
        bias_attn,
        gain_mlp,
        bias_mlp,
        query_pool,
        gain_one,
        bias_one,
        gain_two,
        bias_two,
        table_t,
    ) = unpacked

    word_parts = (word_qkv, word_out.T, word_up, word_down.T)
    word_flat = jnp.concatenate([part.astype(low).reshape(-1, 128) for part in word_parts])
    word_full = lax.all_gather(word_flat, BOTH, axis=0, tiled=False)
    word_full = word_full.reshape(dp_size, mp_size, word_flat.shape[0], 128)
    word_weights, start = [], 0
    for part in word_parts:
        stop = start + part.size // 128
        piece = word_full[:, :, start:stop].reshape((dp_size, mp_size) + part.shape)
        if part.ndim == 3:
            piece = piece.transpose(2, 0, 3, 1, 4).reshape(3, model, model)
        else:
            piece = piece.transpose(0, 2, 1, 3)
            piece = piece.reshape(dp_size * part.shape[0], mp_size * part.shape[1])
        word_weights.append(piece)
        start = stop

    rows = word_count * chars
    states = char_states.reshape(rows, width)
    lane_counts = jnp.repeat(char_counts, chars).reshape(rows // GROUP, 1, GROUP)
    row_counts = jnp.broadcast_to(char_counts[:, None, None], (word_count, 1, width))
    feature_head = jnp.arange(width) // HEAD
    head_masks = (feature_head[None] == jnp.arange(8)[:, None]).astype(low)
    word_masks = (
        (jnp.arange(GROUP) // chars)[None] == jnp.arange(GROUP // chars)[:, None]
    ).astype(low)
    ones = (feature_head[:, None] == feature_head[None]).astype(low)
    pool = ones * (query_pool * HEAD ** (-0.5))[:, None]
    zero = jnp.zeros_like(gain_attn)
    vecs = jnp.stack(
        (gain_attn, bias_attn, gain_mlp, bias_mlp, query_pool, zero, zero, zero)
    ).astype(wide)
    cp, probs, co, y1, hidden, slope, y2, pi, pooled = char_forward(
        states,
        lane_counts,
        row_counts,
        (qkv_char, out_char, up_char, down_char, pool, vecs, head_masks, word_masks),
        chars,
    )

    sequences = max(1, word_count // LEN)
    first = (mp_index * word_count) // LEN
    language = lax.dynamic_slice_in_dim(language_group, first, sequences)
    language_hot = (language[:, None] == jnp.arange(langs)[None]).astype(wide)
    language_rows = jnp.sum(language_hot[:, :, None] * table_t.T.astype(wide)[None], axis=1)
    residual = word_states.astype(wide) + matmul(pooled, proj_char)
    residual = (
        residual.reshape(sequences, -1, model) + language_rows[:, None, :]
    ).reshape(word_count, model)
    norms = tuple(value.astype(wide) for value in (gain_one, bias_one, gain_two, bias_two))
    layer_output, grad_residual, word_grads, word_norm_grads = word_layer(
        residual, output_grad, word_weights, norms, mp_size, mp_index
    )
    grad_words = grad_residual.astype(low)
    sequence_grads = jnp.sum(grad_residual.reshape(sequences, -1, model), axis=1)
    grad_table = jnp.sum(language_hot[:, :, None] * sequence_grads[:, None, :], axis=0)

    pieces = []
    for part, grad in zip(word_parts, word_grads):
        if part.ndim == 3:
            grad = grad.reshape(3, dp_size, part.shape[1], mp_size, part.shape[2])
            grad = grad.transpose(3, 1, 0, 2, 4)
        else:
            grad = grad.reshape(dp_size, part.shape[0], mp_size, part.shape[1])
            grad = grad.transpose(2, 0, 1, 3)
        pieces.append(grad.astype(low).reshape(mp_size, dp_size, -1, 128))
    word_terms = jnp.concatenate(pieces, axis=2)
    word_terms = lax.psum_scatter(word_terms, "mp", scatter_dimension=0, tiled=True)
    word_terms = lax.psum_scatter(word_terms[0], "dp", scatter_dimension=0, tiled=True)[0]
    word_shares, start = [], 0
    for part in word_parts:
        stop = start + part.size // 128
        word_shares.append(word_terms[start:stop].reshape(part.shape).astype(wide))
        start = stop

    grad_proj = mm(pooled, grad_words, TN)
    grad_pooled = mm(grad_words, proj_char, NT).reshape(word_count, 1, width)
    grad_y1, grad_up, grad_down_t, mlp_vecs = char_mlp_back(
        y1, y2, pi, grad_pooled, hidden, slope, (up_char.T, down_char.T, vecs, ones), chars
    )
    mlp_vecs = jnp.sum(mlp_vecs, axis=1)
    early = (
        grad_up,
        grad_down_t.T,
        grad_proj,
        mlp_vecs[0],
        mlp_vecs[1],
        mlp_vecs[2],
        word_norm_grads[0],
        word_norm_grads[1],
        word_norm_grads[2],
        word_norm_grads[3],
        grad_table.T,
    )
    early_terms = jnp.concatenate([blocks_of(part, devices) for part in early], axis=1)
    early_size = early_terms.shape[1]
    early_terms = jnp.pad(early_terms, ((0, 0), (0, -early_size % 1024)))
    early_terms = lax.psum_scatter(early_terms, BOTH, scatter_dimension=0, tiled=True)[0]
    grad_chars, grad_qkv, grad_out, attn_vecs = char_attn_back(
        states, cp, probs, co, grad_y1, (qkv_char.T, out_char.T, vecs, head_masks, word_masks), chars
    )
    attn_vecs = jnp.sum(attn_vecs, axis=1)
    late = (grad_qkv, grad_out, attn_vecs[0], attn_vecs[1])
    late_terms = jnp.concatenate([blocks_of(part, devices) for part in late], axis=1)
    late_terms = jnp.pad(late_terms, ((0, 0), (0, -late_terms.shape[1] % 1024)))
    late_terms = lax.psum_scatter(late_terms, BOTH, scatter_dimension=0, tiled=True)[0]

    def take(terms, parts):
        shares, start = [], 0
        for part in parts:
            stop = start + part.size // devices
            shape = (part.shape[0] // devices,) + part.shape[1:]
            shares.append(terms[start:stop].reshape(shape))
            start = stop
        return shares

    (
        g_up,
        g_down,
        g_proj,
        g_query,
        g_gain_mlp,
        g_bias_mlp,
        g_gain_one,
        g_bias_one,
        g_gain_two,
        g_bias_two,
        g_table_t,
    ) = take(early_terms, early)
    g_qkv, g_out, g_gain_attn, g_bias_attn = take(late_terms, late)
    return (
        layer_output,
        grad_chars.reshape(char_states.shape),
        grad_words,
        g_gain_attn,
        g_bias_attn,
        g_qkv,
        g_out,
        g_gain_mlp,
        g_bias_mlp,
        g_up,
        g_down,
        g_query,
        g_proj,
        g_table_t.T,
        g_gain_one,
        g_bias_one,
        word_shares[0],
        word_shares[1].T,
        g_gain_two,
        g_bias_two,
        word_shares[2],
        word_shares[3].T,
    )


def fits(dp, mp, words, model, width, chars, hidden_width, langs):
    count = dp * mp
    return (
        words == LEN
        and mp % 2 == 0
        and model == 128 * mp
        and model // dp % 16 == 0
        and width == 256
        and width == 8 * count
        and hidden_width % (16 * count) == 0
        and GROUP % chars == 0
        and langs == 8
    )


def shards(*arrays):
    char_states, word_states = arrays[:2]
    dp, mp = lax.axis_size("dp"), lax.axis_size("mp")
    words, chars, width = char_states.shape
    model, hidden_width = word_states.shape[1], arrays[11].shape[1]
    if not fits(dp, mp, words, model, width, chars, hidden_width, arrays[15].shape[0]):
        return shards_general(*arrays)
    return shards_whole(*arrays)


def shards_whole(
    char_states,
    word_states,
    char_counts,
    language_group,
    output_grad,
    char_norm_gain,
    char_norm_bias,
    char_qkv,
    char_out,
    char_mlp_gain,
    char_mlp_bias,
    char_up,
    char_down,
    pool_query,
    char_proj,
    language_table,
    word_norm_gain,
    word_norm_bias,
    word_qkv,
    word_out,
    word_mlp_gain,
    word_mlp_bias,
    word_up,
    word_down,
):
    low, wide = jnp.bfloat16, jnp.float32
    dp, mp = lax.axis_size("dp"), lax.axis_size("mp")
    count = dp * mp
    index = lax.axis_index("dp") * mp + lax.axis_index("mp")
    words, chars, width = char_states.shape
    model = word_states.shape[1]
    langs = language_table.shape[0]
    hidden_width = char_up.shape[1]
    char_small = (char_norm_gain, char_norm_bias, char_mlp_gain, char_mlp_bias, pool_query)
    word_small = (word_norm_gain, word_norm_bias, word_mlp_gain, word_mlp_bias)
    small = jnp.concatenate(char_small + word_small + (language_table.reshape(-1),))
    small = jnp.pad(small, (0, 16 * 128 - small.shape[0])).reshape(16, 128)
    (
        qkv,
        qkv_t,
        out,
        out_t,
        up,
        up_t,
        down,
        down_t,
        proj,
        small_all,
        word_share,
    ) = gather_weights(
        dp,
        mp,
        (char_qkv, char_out, char_up, char_down, char_proj),
        small,
        (word_qkv, word_out, word_up, word_down),
    )
    word_weights = lax.all_gather(word_share, BOTH, axis=0, tiled=False)
    word_weights = word_weights.reshape(dp, mp, word_share.shape[0], 128)
    char_share, word_part = width // count, model // count
    first, second = 5 * char_share, 5 * char_share + 4 * word_part
    flat = small_all.reshape(count, -1).astype(wide)
    vecs = flat[:, :first].reshape(count, 5, char_share).transpose(1, 0, 2).reshape(5, width)
    norms = flat[:, first:second].reshape(count, 4, word_part).transpose(1, 0, 2)
    norms = norms.reshape(4, model)
    table = flat[:, second : second + langs * word_part].reshape(count, langs, word_part)
    table = table.transpose(1, 0, 2).reshape(langs, model)
    query = vecs[4]
    vecs = jnp.pad(vecs, ((0, 3), (0, 0)))

    rows = words * chars
    states = char_states.reshape(rows, width)
    lane_counts = jnp.repeat(char_counts, chars).reshape(rows // GROUP, 1, GROUP)
    row_counts = jnp.broadcast_to(char_counts[:, None, None], (words, 1, width))
    feature_head = jnp.arange(width) // HEAD
    head_masks = (feature_head[None] == jnp.arange(8)[:, None]).astype(low)
    word_masks = (
        (jnp.arange(GROUP) // chars)[None] == jnp.arange(GROUP // chars)[:, None]
    ).astype(low)
    ones = (feature_head[:, None] == feature_head[None]).astype(low)
    pool = (ones * (query * HEAD ** (-0.5))[:, None]).astype(low)
    cp, probs, co, y1, hidden, slope, y2, pi, pooled = char_forward(
        states,
        lane_counts,
        row_counts,
        (qkv, out, up, down, pool, vecs, head_masks, word_masks),
        chars,
    )

    language = lax.dynamic_slice_in_dim(language_group, lax.axis_index("mp"), 1)
    hot = (language == jnp.arange(langs)).astype(wide)[:, None]
    language_row = jnp.sum(hot * table, axis=0, keepdims=True)
    layer_output, grad_words, word_terms, grad_proj, grad_pooled, small_terms = word_layer_kernel(
        pooled,
        word_states,
        output_grad,
        language_row,
        jnp.broadcast_to(hot, (langs, 128)),
        proj,
        word_weights,
        norms,
        head_masks,
    )

    grad_y1, char_terms, g_word_qkv, g_word_out, g_word_up, g_word_down = char_mlp_back_exchange(
        y1, y2, pi, grad_pooled, hidden, slope, (up_t, down_t, vecs, ones), chars, (dp, mp),
        grad_proj, small_terms, word_terms,
    )
    grad_chars, g_qkv, g_out, g_up, g_down, g_proj, g_small, g_vecs = char_attn_back_exchange(
        states, cp, probs, co, grad_y1, (qkv_t, out_t, vecs, head_masks, word_masks), chars,
        (dp, mp), char_terms, hidden_width, model,
    )
    word_small = lax.dynamic_slice_in_dim(g_small[:12], index * word_part, word_part, 1)
    char_small = lax.dynamic_slice_in_dim(g_small[12:15, :width], index * char_share, char_share, 1)
    late_small = lax.dynamic_slice_in_dim(
        g_vecs[:4].reshape(2, width), index * char_share, char_share, 1
    )
    return (
        layer_output,
        grad_chars.reshape(char_states.shape),
        grad_words,
        late_small[0],
        late_small[1],
        g_qkv,
        g_out,
        char_small[1],
        char_small[2],
        g_up,
        g_down,
        char_small[0],
        g_proj,
        word_small[:langs],
        word_small[8],
        word_small[9],
        g_word_qkv,
        g_word_out,
        word_small[10],
        word_small[11],
        g_word_up,
        g_word_down,
    )


def solution(mesh):
    vector, rows = P(BOTH), P(BOTH, None)
    cube = P(BOTH, None, None)
    table = P(None, BOTH)
    words = (P(None, "dp", "mp"), P("mp", "dp"), P("dp", "mp"), P("mp", "dp"))
    char_weights = (
        vector, vector, rows, rows, vector, vector, rows, rows, vector, rows, table,
    )
    weights = char_weights + (
        vector, vector, words[0], words[1], vector, vector, words[2], words[3],
    )
    return jax.shard_map(
        shards,
        mesh=mesh,
        in_specs=(cube, rows, vector, P("dp"), rows) + weights,
        out_specs=(rows, cube, rows) + weights,
        check_vma=False,
    )
```

```python
import functools

import jax
import jax.numpy as jnp
import ml_dtypes
import numpy as np
from jax import lax
from jax.experimental import pallas as pl
from jax.experimental.pallas import tpu as pltpu
from jax.sharding import PartitionSpec as P

HEAD = 64
CHAR_HEADS = 4
LEN = 1024
GROUP = 128
SUB = 256


NORM_EPS = 1e-05
NEG_FILL = -1000000000.0
BOTH = ("dp", "mp")
MESH = pl.DeviceIdType.MESH

LOGIT = (
    0.7978697123195114,
    0.036392286136226214,
    -8.782649734580825e-05,
    -3.669345726473906e-05,
    1.4250064727244771e-06,
)

NN = (((1,), (0,)), ((), ()))
NT = (((1,), (1,)), ((), ()))
TN = (((0,), (0,)), ((), ()))


def mm(first_arg, second_arg, dims=NN):
    return lax.dot_general(first_arg, second_arg, dims, preferred_element_type=jnp.float32)


def matmul(first_arg, second_arg):
    return jnp.dot(first_arg, second_arg, preferred_element_type=jnp.float32)


def low_sum(pattern, first_arg, second_arg):
    return jnp.einsum(pattern, first_arg, second_arg, preferred_element_type=jnp.float32)


def standardize(values):
    centred = values - jnp.mean(values, axis=-1, keepdims=True)
    inverse = lax.rsqrt(jnp.mean(centred * centred, axis=-1, keepdims=True) + NORM_EPS)
    return (centred * inverse, inverse)


def apply_norm(values, gain_value, bias_value):
    unit_rows, inverse = standardize(values)
    normed = (unit_rows * gain_value + bias_value).astype(jnp.bfloat16)
    return (unit_rows, inverse, normed)


def norm_back(grad_out, unit_rows, inverse, gain_value):
    grad_unit = grad_out * gain_value
    inner_sum = jnp.mean(grad_unit * unit_rows, axis=-1, keepdims=True)
    return inverse * (
        grad_unit - jnp.mean(grad_unit, axis=-1, keepdims=True) - unit_rows * inner_sum
    )


def gelu_pair(values):
    square = values * values
    logit = square * LOGIT[4] + LOGIT[3]
    for term in LOGIT[2::-1]:
        logit = logit * square + term
    normal = jnp.tanh(logit * values) * 0.5 + 0.5
    density = jnp.exp2(square * -0.7213475204444817 - 1.3257480647361593)
    return (values * normal, values * density + normal)


def strips(function, size, *arrays):
    parts = [
        function(*(array[row : row + size] for array in arrays))
        for row in range(0, arrays[0].shape[0], size)
    ]
    return tuple(jnp.concatenate(part, axis=0) for part in zip(*parts))


def gelu_low(values):
    return strips(
        lambda strip: tuple(part.astype(jnp.bfloat16) for part in gelu_pair(strip)),
        32 * 256 // values.shape[1],
        values,
    )


def split_two(values):
    high = values.astype(jnp.bfloat16)
    return (high, (values - high.astype(jnp.float32)).astype(jnp.bfloat16))


def fold_rows(values):
    return jnp.sum(values.reshape(values.shape[0] // 8, 8, values.shape[1]), axis=0)


class Place:
    def __init__(self, dp, mp):
        self.dp, self.mp, self.wide = dp, mp, mp // 2
        self.i, self.j = lax.axis_index("dp"), lax.axis_index("mp")
        self.x, self.core = self.j // 2, lax.rem(self.j, 2)

    def partner(self):
        return (self.i, 2 * self.x + 1 - self.core)

    def across(self, step):
        return (self.i, 2 * lax.rem(self.x + step, self.wide) + self.core)

    def along(self, step):
        return (lax.rem(self.i + step, self.dp), self.j)

    def greet(self):
        barrier = pltpu.get_barrier_semaphore()
        others = [self.partner()]
        others += [self.across(step) for step in range(1, self.wide)]
        others += [self.along(step) for step in range(1, self.dp)]
        for other in others:
            pl.semaphore_signal(barrier, inc=1, device_id=other, device_id_type=MESH)
        pl.semaphore_wait(barrier, len(others))


def remote(source, target, sems, index, device):
    return pltpu.make_async_remote_copy(
        src_ref=source,
        dst_ref=target,
        send_sem=sems[0].at[index],
        recv_sem=sems[1].at[index],
        device_id=device,
        device_id_type=MESH,
    )


class ScatterSum:
    def __init__(self, place, blocks, local, one, two, three, sems):
        self.place, self.blocks, self.local = place, blocks, local
        self.one, self.two, self.three, self.sems = one, two, three, sems

    def first(self):
        place = self.place
        return [
            remote(
                self.blocks.at[2 * e + 1 - place.core],
                self.one.at[e],
                self.sems,
                e,
                place.partner(),
            )
            for e in range(place.wide)
        ]

    def second(self):
        place = self.place
        return [
            remote(
                self.one.at[lax.rem(place.x + step, place.wide)],
                self.two.at[step - 1],
                self.sems,
                place.wide + step - 1,
                place.across(step),
            )
            for step in range(1, place.wide)
        ]

    def third(self):
        place = self.place
        return [
            remote(
                self.one.at[place.x, lax.rem(place.i + step, place.dp)],
                self.three.at[step - 1],
                self.sems,
                2 * place.wide - 1 + step - 1,
                place.along(step),
            )
            for step in range(1, place.dp)
        ]

    def start(self):
        for copy in self.first():
            copy.start()

    def go_across(self):
        place = self.place
        for copy in self.first():
            copy.wait()

        @pl.loop(0, place.dp)
        def _(row):
            for e in range(place.wide):
                own = self.local(e, row).astype(jnp.float32)
                total = self.one[e, row].astype(jnp.float32) + own
                self.one[e, row] = total.astype(jnp.bfloat16)

        for copy in self.second():
            copy.start()

    def go_along(self):
        place = self.place
        for copy in self.second():
            copy.wait()

        @pl.loop(0, place.dp)
        def _(row):
            total = self.one[place.x, row].astype(jnp.float32)
            for step in range(1, place.wide):
                total = total + self.two[step - 1, row].astype(jnp.float32)
            self.one[place.x, row] = total.astype(jnp.bfloat16)

        for copy in self.third():
            copy.start()

    def finish(self):
        place = self.place
        for copy in self.third():
            copy.wait()

        def own(rows):
            total = self.one[place.x, place.i, rows].astype(jnp.float32)
            for step in range(1, place.dp):
                total = total + self.three[step - 1, rows].astype(jnp.float32)
            return total

        return own


def scatter_scratch(dp, mp, n):
    wide = mp // 2
    copies = 2 * wide - 1 + dp - 1
    return [
        pltpu.VMEM((wide, dp, n, 128), jnp.bfloat16),
        pltpu.VMEM((max(1, wide - 1), dp, n, 128), jnp.bfloat16),
        pltpu.VMEM((dp - 1, n, 128), jnp.bfloat16),
        pltpu.SemaphoreType.DMA((copies,)),
        pltpu.SemaphoreType.DMA((copies,)),
    ]


def put_pairs(target, first_row, columns):
    mp, dp = target.shape[0], target.shape[1]
    rows = columns.shape[0] // (mp * dp)
    for pair in range(columns.shape[1] // 256):
        both = [
            columns[:, 256 * pair + 128 * c : 256 * pair + 128 * c + 128].reshape(
                dp, mp, rows, 128
            )
            for c in range(2)
        ]
        both = jnp.concatenate(both, axis=2).astype(jnp.bfloat16)
        spot = slice(first_row + 2 * rows * pair, first_row + 2 * rows * (pair + 1))
        for j in range(mp):
            target[j, :, spot, :] = both[:, j]


def gather_kernel(
    dp,
    mp,
    qkv_ref,
    out_ref,
    up_ref,
    down_ref,
    proj_ref,
    small_ref,
    word_qkv_ref,
    word_out_ref,
    word_up_ref,
    word_down_ref,
    qkv_all,
    qkv_t_all,
    out_all,
    out_t_all,
    up_all,
    up_t_all,
    down_all,
    down_t_all,
    proj_all,
    small_all,
    word_share,
    held,
    sends,
    arrivals,
):
    place = Place(dp, mp)
    low = jnp.bfloat16
    i, j = place.i, place.j
    row = 0
    for part in (qkv_ref, out_ref, up_ref, proj_ref):
        for pair in range(part.shape[1] // 256):
            both = [part[:, 256 * pair + 128 * c : 256 * pair + 128 * c + 128] for c in range(2)]
            held[i, j, row : row + 16, :] = jnp.concatenate(both, axis=0).astype(low)
            row += 16
    down_rows = down_ref.shape[0]
    for c in range(2):
        held[i, j, row : row + down_rows, :] = down_ref[:, 128 * c : 128 * c + 128].astype(low)
        row += down_rows
    held[i, j, row : row + 16, :] = small_ref[...].astype(low)
    place.greet()
    sems = (sends, arrivals)
    wide = place.wide

    def share(step, e):
        return held.at[
            lax.rem(i + dp - step, dp), 2 * lax.rem(place.x + wide - e, wide) + place.core
        ]

    def other_core(step, e):
        return held.at[
            lax.rem(i + dp - step, dp), 2 * lax.rem(place.x + wide - e, wide) + 1 - place.core
        ]

    def along(step):
        return remote(held.at[i, j], held.at[i, j], sems, step - 1, place.along(step))

    def across(step, e):
        index = dp - 1 + step * (wide - 1) + e - 1
        return remote(share(step, 0), share(step, 0), sems, index, place.across(e))

    def over(step, e):
        index = dp - 1 + dp * (wide - 1) + step * wide + e
        return remote(share(step, e), share(step, e), sems, index, place.partner())

    for step in range(1, dp):
        along(step).start()
    for e in range(1, wide):
        across(0, e).start()
    over(0, 0).start()

    rows = word_up_ref.shape[0]
    for t in range(3):
        word_share[rows * t : rows * (t + 1), :] = word_qkv_ref[t].astype(low)
    word_share[3 * rows : 4 * rows, :] = word_out_ref[...].astype(low)
    blocks = word_up_ref.shape[1] // 128
    for c in range(blocks):
        spot = slice((4 + c) * rows, (5 + c) * rows)
        word_share[spot, :] = word_up_ref[:, 128 * c : 128 * c + 128].astype(low)
        spot = slice((4 + blocks + c) * rows, (5 + blocks + c) * rows)
        word_share[spot, :] = word_down_ref[:, 128 * c : 128 * c + 128].astype(low)

    for step in range(1, dp):
        along(step).wait_recv()
        for e in range(1, wide):
            across(step, e).start()
        over(step, 0).start()
    for step in range(dp):
        for e in range(1, wide):
            across(step, e).wait_recv()
            over(step, e).start()
    for step in range(dp):
        for e in range(wide):
            over(step, e).wait_recv()
    for step in range(1, dp):
        along(step).wait_send()
    for step in range(dp):
        for e in range(1, wide):
            across(step, e).wait_send()
        for e in range(wide):
            over(step, e).wait_send()

    count = dp * mp
    row = 0
    for target, target_t in (
        (qkv_all, qkv_t_all),
        (out_all, out_t_all),
        (up_all, up_t_all),
        (proj_all, None),
    ):
        for pair in range(target.shape[1] // 256):
            both = held[:, :, row : row + 16, :].reshape(count, 16, 128).astype(jnp.float32)
            row += 16
            for c in range(2):
                piece = both[:, 8 * c : 8 * c + 8].reshape(8 * count, 128).astype(low)
                spot = slice(256 * pair + 128 * c, 256 * pair + 128 * c + 128)
                target[:, spot] = piece
                if target_t is not None:
                    target_t[spot, :] = piece.T
    for c in range(2):
        piece = held[:, :, row : row + down_rows, :].reshape(count * down_rows, 128)
        row += down_rows
        down_all[:, 128 * c : 128 * c + 128] = piece
        down_t_all[128 * c : 128 * c + 128, :] = piece.T
    small_all[...] = held[:, :, row : row + 16, :].reshape(count, 16, 128)


def gather_weights(dp, mp, parts, small, word_parts):
    low = jnp.bfloat16
    qkv, out, up, down, proj = parts
    count = dp * mp
    width = qkv.shape[0] * count
    hidden = up.shape[1]
    model = proj.shape[1]
    rows = (qkv.shape[1] + out.shape[1] + up.shape[1] + proj.shape[1]) // 128 * 8
    rows += 2 * down.shape[0] + 16
    word_rows = sum(part.size for part in word_parts) // 128
    copies = dp - 1 + dp * (mp // 2 - 1) + dp * (mp // 2)
    shapes = (
        (width, 3 * width),
        (3 * width, width),
        (width, width),
        (width, width),
        (width, hidden),
        (hidden, width),
        (hidden, width),
        (width, hidden),
        (width, model),
        (count, 16, 128),
        (word_rows, 128),
    )
    arrays = (qkv, out, up, down, proj, small, *word_parts)
    return pl.pallas_call(
        functools.partial(gather_kernel, dp, mp),
        grid=(1,),
        in_specs=[once(array.shape) for array in arrays],
        out_specs=[once(shape) for shape in shapes],
        out_shape=[jax.ShapeDtypeStruct(shape, low) for shape in shapes],
        scratch_shapes=[
            pltpu.VMEM((dp, mp, rows, 128), low),
            pltpu.SemaphoreType.DMA((copies,)),
            pltpu.SemaphoreType.DMA((copies,)),
        ],
        compiler_params=pltpu.CompilerParams(
            collective_id=0, has_side_effects=True, vmem_limit_bytes=60 * 1024 * 1024
        ),
        name="gather_weights",
    )(*arrays)


def head_rows(rows, masks):
    return jnp.concatenate([rows * masks[h : h + 1] for h in range(CHAR_HEADS)], axis=0)


def gather_diagonal(square, lane_word, chars):
    words = square.shape[1] // chars
    blocks = square.reshape(CHAR_HEADS, words, chars, square.shape[1])
    kept = blocks[:, 0]
    for word in range(1, words):
        kept = jnp.where(lane_word == word, blocks[:, word], kept)
    return kept


def spread_diagonal(kept, word_masks, chars):
    words = kept.shape[2] // chars
    parts = [kept * word_masks[word : word + 1] for word in range(words)]
    return jnp.stack(parts, axis=1)


def norm_strips(values, gain_value, bias_value):
    return strips(lambda strip: apply_norm(strip, gain_value, bias_value), 64, values)


def char_forward_kernel(
    chars,
    chars_ref,
    lane_count_ref,
    qkv_ref,
    out_ref,
    up_ref,
    down_ref,
    ones_ref,
    vecs_ref,
    head_mask_ref,
    word_mask_ref,
    cp_ref,
    probs_ref,
    co_ref,
    y1_ref,
    hidden_ref,
    slope_ref,
    y2_ref,
    pi_ref,
    pooled_ref,
):
    rows, width = chars_ref.shape
    low, wide = jnp.bfloat16, jnp.float32
    lane_word = lax.broadcasted_iota(jnp.int32, (1, 1, GROUP), 2) // chars
    key_slot = lax.broadcasted_iota(jnp.int32, (1, chars, GROUP), 1)
    row_slot = lax.rem(lax.broadcasted_iota(jnp.int32, (GROUP, GROUP), 0), chars)
    masks = head_mask_ref[...]
    word_masks = word_mask_ref[...]
    block = SUB
    parts = up_ref.shape[1] // width

    def project(s):
        span = slice(s * block, (s + 1) * block)
        states = chars_ref[span, :].astype(wide)
        _, _, normed = norm_strips(states, vecs_ref[0:1, :], vecs_ref[1:2, :])
        for part in range(3):
            cols = slice(part * width, (part + 1) * width)
            cp_ref[span, cols] = mm(normed, qkv_ref[:, cols]).astype(low)

    def attend(s):
        spans = [
            slice(row, row + GROUP) for row in range(s * block, (s + 1) * block, GROUP)
        ]
        scores = []
        for span in spans:
            keys = head_rows(cp_ref[span, width : 2 * width], masks)
            square = mm(keys, cp_ref[span, 0:width], NT)
            scores.append(gather_diagonal(square, lane_word, chars))
        probs = []
        for span, score in zip(spans, scores):
            group = span.start // GROUP
            score = score * HEAD ** (-0.5)
            score = jnp.where(key_slot < lane_count_ref[group], score, NEG_FILL)
            powers = jnp.exp(score - jnp.max(score, axis=1, keepdims=True))
            share = 1.0 / jnp.sum(powers, axis=1, keepdims=True)
            probs.append((powers * share).astype(low))
            probs_ref[group] = probs[-1].reshape(CHAR_HEADS * chars, GROUP)
        for span, prob in zip(spans, probs):
            values = head_rows(cp_ref[span, 2 * width : 3 * width], masks)
            spread = spread_diagonal(prob, word_masks, chars)
            spread = spread.reshape(CHAR_HEADS * GROUP, GROUP)
            co_ref[span, :] = mm(spread, values, TN).astype(low)

    def middle(s):
        span = slice(s * block, (s + 1) * block)
        after_attn = chars_ref[span, :].astype(wide) + mm(co_ref[span, :], out_ref[...])
        y1_ref[span, :] = after_attn
        return norm_strips(after_attn, vecs_ref[2:3, :], vecs_ref[3:4, :])[2]

    def pool(s, total):
        query = vecs_ref[4:5, :] * HEAD ** (-0.5)
        high, low_part = strips(lambda strip: split_two(strip * query), 64, total)
        scores = mm(high, ones_ref[...]) + mm(low_part, ones_ref[...])
        pooled = []
        for k in range(block // GROUP):
            group = s * block // GROUP + k
            spot = slice(k * GROUP, (k + 1) * GROUP)
            span = slice(s * block + k * GROUP, s * block + (k + 1) * GROUP)
            counts = jnp.broadcast_to(lane_count_ref[group], (GROUP, GROUP)).T
            valid = row_slot < counts
            halves = []
            for half in range(width // GROUP):
                cols = slice(half * GROUP, (half + 1) * GROUP)
                score = jnp.where(valid, scores[spot, cols], NEG_FILL)
                score = score.reshape(GROUP // chars, chars, GROUP)
                powers = jnp.exp(score - jnp.max(score, axis=1, keepdims=True))
                pi = powers * (1.0 / jnp.sum(powers, axis=1, keepdims=True))
                pi_ref[span, cols] = pi.reshape(GROUP, GROUP).astype(low)
                grid = total[spot, cols].reshape(GROUP // chars, chars, GROUP)
                halves.append(jnp.sum(pi * grid, axis=1))
            pooled.append(jnp.concatenate(halves, axis=1))
        words = block // chars
        pooled_ref[s * words : (s + 1) * words, :] = jnp.concatenate(pooled, axis=0).astype(low)

    count = rows // block
    for s in range(count):
        project(s)
    for s in range(count):
        attend(s)
    normed, totals = {}, {}

    def up(s, part):
        if part == 0:
            normed[s] = middle(s)
        return mm(normed[s], up_ref[:, part * width : (part + 1) * width])

    order = [(s, part) for first in range(0, count, 2) for part in range(parts)
             for s in range(first, min(first + 2, count))]
    ahead = up(*order[0])
    for place, (s, part) in enumerate(order):
        current = ahead
        if place + 1 < len(order):
            ahead = up(*order[place + 1])
        span, cols = slice(s * block, (s + 1) * block), slice(part * width, (part + 1) * width)
        hidden, slope = gelu_low(current)
        hidden_ref[span, cols] = hidden
        slope_ref[span, cols] = slope
        term = mm(hidden, down_ref[cols, :])
        totals[s] = term if part == 0 else totals[s] + term
        if part == parts - 1:
            totals[s] = totals[s] + y1_ref[span, :]
            y2_ref[span, :] = totals[s]
            pool(s, totals[s])


def char_mlp_back_kernel(
    chars,
    exchange,
    y1_ref,
    y2_ref,
    pi_ref,
    grad_pooled_ref,
    hidden_ref,
    slope_ref,
    up_t_ref,
    down_t_ref,
    vecs_ref,
    ones_ref,
    *others,
):
    rows, width = y1_ref.shape
    words = rows // chars
    if exchange is None:
        grad_y1_ref, grad_up_ref, grad_down_t_ref, grad_vecs_ref = others
    else:
        (
            grad_proj_ref,
            word_small_ref,
            word_terms_ref,
            grad_y1_ref,
            char_terms_ref,
            word_qkv_ref,
            word_out_ref,
            word_up_ref,
            word_down_ref,
            grad_up_ref,
            grad_down_t_ref,
            grad_vecs_ref,
            local_ref,
            local_sem,
            one_ref,
            two_ref,
            three_ref,
            sends,
            arrivals,
        ) = others
        place = Place(*exchange)
        total = ScatterSum(
            place,
            word_terms_ref,
            lambda e, row: local_ref[e, row],
            one_ref,
            two_ref,
            three_ref,
            (sends, arrivals),
        )
        own = [
            pltpu.make_async_copy(
                word_terms_ref.at[2 * e + place.core], local_ref.at[e], local_sem.at[e]
            )
            for e in range(place.wide)
        ]
        step, last = pl.program_id(0), pl.num_programs(0) - 1

        @pl.when(step == 0)
        def _():
            place.greet()
            total.start()
            for copy in own:
                copy.start()

        @pl.when(step == last // 8)
        def _():
            for copy in own:
                copy.wait()
            total.go_across()

        @pl.when(step == last // 2 + 1)
        def _():
            total.go_along()

    @pl.when(pl.program_id(0) == 0)
    def _():
        grad_up_ref[...] = jnp.zeros_like(grad_up_ref)
        grad_down_t_ref[...] = jnp.zeros_like(grad_down_t_ref)
        grad_vecs_ref[...] = jnp.zeros_like(grad_vecs_ref)

    low, wide = jnp.bfloat16, jnp.float32
    block = SUB
    count, parts = rows // block, hidden_ref.shape[1] // width
    query = vecs_ref[4:5, :]
    per = 64 // chars

    def pool_back(s):
        spots = [
            (slice(row, row + 64), slice(row // chars, row // chars + per))
            for row in range(s * block, (s + 1) * block, 64)
        ]
        split = [
            split_two(
                (y2_ref[span, :].reshape(per, chars, width) * grad_pooled_ref[span_words]).reshape(
                    64, width
                )
            )
            for span, span_words in spots
        ]
        high, rest = (jnp.concatenate(side, axis=0) for side in zip(*split))
        grad_pi = mm(high, ones_ref[...]) + mm(rest, ones_ref[...])
        wide_parts, low_parts, query_sum = [], [], None
        for k, (span, span_words) in enumerate(spots):
            pi = pi_ref[span, :].astype(wide).reshape(per, chars, width)
            part = grad_pi[64 * k : 64 * (k + 1)].reshape(per, chars, width)
            inner = jnp.sum(pi * part, axis=1, keepdims=True)
            grad_scores = pi * (part - inner) * HEAD ** (-0.5)
            grid = y2_ref[span, :].reshape(per, chars, width)
            term = fold_rows((grad_scores * grid).reshape(64, width))
            query_sum = term if query_sum is None else query_sum + term
            grad = (pi * grad_pooled_ref[span_words] + grad_scores * query).reshape(64, width)
            wide_parts.append(grad)
            low_parts.append(grad.astype(low))
        grad_vecs_ref[0] += query_sum
        return jnp.concatenate(wide_parts, axis=0), jnp.concatenate(low_parts, axis=0)

    def norm_again(s):
        span = slice(s * block, (s + 1) * block)
        return norm_strips(y1_ref[span, :], vecs_ref[2:3, :], vecs_ref[3:4, :])

    def feed_back(s, branch):
        span = slice(s * block, (s + 1) * block)
        grads, total = [], None
        ahead = mm(branch, down_t_ref[:, 0:width])
        for part in range(parts):
            cols = slice(part * width, (part + 1) * width)
            current = ahead
            if part + 1 < parts:
                ahead = mm(branch, down_t_ref[:, (part + 1) * width : (part + 2) * width])
            (grad_pre,) = strips(
                lambda strip, slope: ((strip * slope.astype(wide)).astype(low),),
                32,
                current,
                slope_ref[span, cols],
            )
            grads.append(grad_pre)
            term = mm(grad_pre, up_t_ref[cols, :])
            total = term if total is None else total + term
        return grads, total

    def norm_finish(s, grad_normed, unit, inverse, grad_y2):
        span = slice(s * block, (s + 1) * block)
        gain = vecs_ref[2:3, :]
        gain_sum, bias_sum = None, None
        for row in range(0, block, 64):
            spot = slice(row, row + 64)
            part, part_unit = grad_normed[spot], unit[spot]
            one, two = fold_rows(part * part_unit), fold_rows(part)
            gain_sum = one if gain_sum is None else gain_sum + one
            bias_sum = two if bias_sum is None else bias_sum + two
            grad_y1_ref[s * block + row : s * block + row + 64, :] = grad_y2[spot] + norm_back(
                part, part_unit, inverse[spot], gain
            )
        grad_vecs_ref[1] += gain_sum
        grad_vecs_ref[2] += bias_sum

    pooled, norms, grads, totals = {}, {}, {}, {}
    pooled[0] = pool_back(0)
    norms[0] = norm_again(0)
    for s in range(count):
        grads[s], totals[s] = feed_back(s, pooled[s][1])
        if s + 1 < count:
            pooled[s + 1] = pool_back(s + 1)
            norms[s + 1] = norm_again(s + 1)
    branch_t = jnp.concatenate([pooled[s][1] for s in range(count)], axis=0).T
    normed_t = jnp.concatenate([norms[s][2] for s in range(count)], axis=0).T
    for part in range(parts):
        cols = slice(part * width, (part + 1) * width)
        grad_down_t_ref[:, cols] += mm(branch_t, hidden_ref[:, cols])
        grad_pre = jnp.concatenate([grads[s][part] for s in range(count)], axis=0)
        grad_up_ref[:, cols] += mm(normed_t, grad_pre)
        if part < count:
            norm_finish(part, totals[part], norms[part][0], norms[part][1], pooled[part][0])
    if exchange is None:
        return

    @pl.when(step == last)
    def _():
        low = jnp.bfloat16
        share = hidden_ref.shape[1] // (place.dp * place.mp)
        put_pairs(char_terms_ref, 0, grad_up_ref[...])
        row = hidden_ref.shape[1] // 16
        for c in range(2):
            piece = grad_down_t_ref[128 * c : 128 * c + 128, :].T
            piece = piece.reshape(place.dp, place.mp, share, 128).astype(low)
            for j in range(place.mp):
                char_terms_ref[j, :, row : row + share, :] = piece[:, j]
            row += share
        put_pairs(char_terms_ref, row, grad_proj_ref[...])
        row += grad_proj_ref.shape[1] // 16
        sums = [jnp.sum(grad_vecs_ref[k], axis=0, keepdims=True) for k in range(3)]
        small_row = lax.broadcasted_iota(jnp.int32, (16, 128), 0)
        for b in range(word_small_ref.shape[0]):
            piece = word_small_ref[b]
            if b < 2:
                for k in range(3):
                    piece = jnp.where(
                        small_row == 12 + k, sums[k][:, 128 * b : 128 * b + 128], piece
                    )
            piece = jnp.broadcast_to(piece.astype(low), (place.dp, 16, 128))
            for j in range(place.mp):
                char_terms_ref[j, :, row : row + 16, :] = piece
            row += 16
        result = total.finish()
        block = word_up_ref.shape[0]
        for t in range(3):
            word_qkv_ref[t] = result(slice(block * t, block * (t + 1)))
        word_out_ref[...] = result(slice(3 * block, 4 * block))
        count = word_up_ref.shape[1] // 128
        for c in range(count):
            cols = slice(128 * c, 128 * c + 128)
            word_up_ref[:, cols] = result(slice((4 + c) * block, (5 + c) * block))
            spot = slice((4 + count + c) * block, (5 + count + c) * block)
            word_down_ref[:, cols] = result(spot)


def char_attn_back_kernel(
    chars,
    exchange,
    chars_ref,
    cp_ref,
    probs_ref,
    co_ref,
    grad_y1_ref,
    qkv_t_ref,
    out_t_ref,
    vecs_ref,
    head_mask_ref,
    word_mask_ref,
    *others,
):
    rows, width = chars_ref.shape
    if exchange is None:
        (
            grad_chars_ref,
            grad_qkv_ref,
            grad_out_ref,
            grad_vecs_ref,
            grad_cp_ref,
            grad_co_ref,
        ) = others
    else:
        (
            early_terms_ref,
            grad_chars_ref,
            share_qkv_ref,
            share_out_ref,
            share_up_ref,
            share_down_ref,
            share_proj_ref,
            share_small_ref,
            share_vecs_ref,
            grad_cp_ref,
            grad_co_ref,
            grad_qkv_ref,
            grad_out_ref,
            grad_vecs_ref,
            local_ref,
            local_sem,
            late_terms_ref,
        ) = others[:17]
        early_refs, late_refs = others[17:22], others[22:27]
        place = Place(*exchange)
        early = ScatterSum(
            place,
            early_terms_ref,
            lambda e, row: local_ref[e, row],
            *early_refs[:3],
            early_refs[3:],
        )
        late = ScatterSum(
            place,
            late_terms_ref,
            lambda e, row: late_terms_ref[2 * e + place.core, row],
            *late_refs[:3],
            late_refs[3:],
        )
        own = [
            pltpu.make_async_copy(
                early_terms_ref.at[2 * e + place.core], local_ref.at[e], local_sem.at[e]
            )
            for e in range(place.wide)
        ]
        step, last = pl.program_id(0), pl.num_programs(0) - 1

        @pl.when(step == 0)
        def _():
            place.greet()
            early.start()
            for copy in own:
                copy.start()

        @pl.when(step == last // 8)
        def _():
            for copy in own:
                copy.wait()
            early.go_across()

        @pl.when(step == last // 2 + 1)
        def _():
            early.go_along()

    @pl.when(pl.program_id(0) == 0)
    def _():
        grad_qkv_ref[...] = jnp.zeros_like(grad_qkv_ref)
        grad_out_ref[...] = jnp.zeros_like(grad_out_ref)
        grad_vecs_ref[...] = jnp.zeros_like(grad_vecs_ref)

    low, wide = jnp.bfloat16, jnp.float32
    lane_word = lax.broadcasted_iota(jnp.int32, (1, 1, GROUP), 2) // chars
    masks = head_mask_ref[...]
    word_masks = word_mask_ref[...]
    scale = HEAD ** (-0.5)
    block = SUB
    count = rows // block

    def out_back(s):
        span = slice(s * block, (s + 1) * block)
        branch = grad_y1_ref[span, :].astype(low)
        grad_co_ref[span, :] = mm(branch, out_t_ref[...]).astype(low)
        return branch

    def norm_again(s):
        span = slice(s * block, (s + 1) * block)
        return norm_strips(
            chars_ref[span, :].astype(wide), vecs_ref[0:1, :], vecs_ref[1:2, :]
        )

    def side_by_side(spread):
        return jnp.concatenate([spread[h] for h in range(CHAR_HEADS)], axis=1)

    def attend_back(s):
        spans = [
            slice(row, row + GROUP) for row in range(s * block, (s + 1) * block, GROUP)
        ]
        grad_probs = []
        for span in spans:
            values = head_rows(cp_ref[span, 2 * width : 3 * width], masks)
            square = mm(values, grad_co_ref[span, :], NT)
            grad_probs.append(gather_diagonal(square, lane_word, chars))
        grad_scores = []
        for span, part in zip(spans, grad_probs):
            probs = probs_ref[span.start // GROUP].reshape(CHAR_HEADS, chars, GROUP)
            spread = spread_diagonal(probs, word_masks, chars)
            spread = spread.reshape(CHAR_HEADS, GROUP, GROUP)
            grad_values = mm(side_by_side(spread), head_rows(grad_co_ref[span, :], masks))
            grad_cp_ref[span, 2 * width : 3 * width] = grad_values.astype(low)
            probs = probs.astype(wide)
            inner = jnp.sum(part * probs, axis=1, keepdims=True)
            grad_scores.append((probs * (part - inner)).astype(low))
        for span, part in zip(spans, grad_scores):
            spread = spread_diagonal(part, word_masks, chars)
            spread = spread.reshape(CHAR_HEADS, GROUP, GROUP)
            queries = head_rows(cp_ref[span, 0:width], masks)
            grad_keys = mm(side_by_side(spread), queries) * scale
            grad_cp_ref[span, width : 2 * width] = grad_keys.astype(low)
            keys = head_rows(cp_ref[span, width : 2 * width], masks)
            grad_queries = mm(spread.reshape(CHAR_HEADS * GROUP, GROUP), keys, TN) * scale
            grad_cp_ref[span, 0:width] = grad_queries.astype(low)

    def project_back(s):
        span = slice(s * block, (s + 1) * block)
        total = None
        for part in range(3):
            cols = slice(part * width, (part + 1) * width)
            term = mm(grad_cp_ref[span, cols], qkv_t_ref[cols, :])
            total = term if total is None else total + term
        return total

    def norm_finish(s, grad_normed, unit, inverse):
        gain = vecs_ref[0:1, :]
        gain_sum, bias_sum = None, None
        for row in range(0, block, 64):
            spot, span = slice(row, row + 64), slice(s * block + row, s * block + row + 64)
            part, part_unit = grad_normed[spot], unit[spot]
            one, two = fold_rows(part * part_unit), fold_rows(part)
            gain_sum = one if gain_sum is None else gain_sum + one
            bias_sum = two if bias_sum is None else bias_sum + two
            grad = grad_y1_ref[span, :] + norm_back(part, part_unit, inverse[spot], gain)
            grad_chars_ref[span, :] = grad.astype(low)
        grad_vecs_ref[0] += gain_sum
        grad_vecs_ref[1] += bias_sum

    branches = [out_back(s) for s in range(count)]
    norms, totals = {}, {}
    for s in range(count):
        attend_back(s)
        norms[s] = norm_again(s)
        totals[s] = project_back(s)
    grad_out_ref[...] += mm(co_ref[...].T, jnp.concatenate(branches, axis=0))
    normed_t = jnp.concatenate([norms[s][2] for s in range(count)], axis=0).T
    for part in range(3):
        cols = slice(part * width, (part + 1) * width)
        grad_qkv_ref[:, cols] += mm(normed_t, grad_cp_ref[:, cols])
        if part < count:
            norm_finish(part, totals[part], norms[part][0], norms[part][1])
    for s in range(3, count):
        norm_finish(s, totals[s], norms[s][0], norms[s][1])
    if exchange is None:
        return

    @pl.when(step == last)
    def _():
        low = jnp.bfloat16
        put_pairs(late_terms_ref, 0, grad_qkv_ref[...])
        row = 3 * width // 16
        put_pairs(late_terms_ref, row, grad_out_ref[...])
        row += width // 16
        sums = [jnp.sum(grad_vecs_ref[k], axis=0, keepdims=True) for k in range(2)]
        small_row = lax.broadcasted_iota(jnp.int32, (16, 128), 0)
        piece = jnp.zeros((16, 128), jnp.float32)
        for k in range(2):
            for b in range(2):
                piece = jnp.where(
                    small_row == 2 * k + b, sums[k][:, 128 * b : 128 * b + 128], piece
                )
        piece = jnp.broadcast_to(piece.astype(low), (place.dp, 16, 128))
        for j in range(place.mp):
            late_terms_ref[j, :, row : row + 16, :] = piece
        late.start()
        result = early.finish()
        row = 0
        for target, share in (
            (share_up_ref, 8),
            (share_down_ref, share_down_ref.shape[0]),
            (share_proj_ref, 8),
            (share_small_ref, 16),
        ):
            for c in range(target.shape[1] // 128):
                target[:, 128 * c : 128 * c + 128] = result(slice(row, row + share))
                row += share
        late.go_across()
        late.go_along()
        result = late.finish()
        row = 0
        for target in (share_qkv_ref, share_out_ref):
            for c in range(target.shape[1] // 128):
                target[:, 128 * c : 128 * c + 128] = result(slice(row, row + 8))
                row += 8
        share_vecs_ref[...] = result(slice(row, row + 16))


def whole(shape):
    return pl.BlockSpec(shape, lambda step: (0,) * len(shape))


def once(shape):
    return pl.BlockSpec(shape, lambda step: (0,) * len(shape), pipeline_mode=pl.Buffered(1))


def blocked(shape):
    return pl.BlockSpec(shape, lambda step: (step,) + (0,) * (len(shape) - 1))


def params(megabytes):
    return pltpu.CompilerParams(
        dimension_semantics=("arbitrary",), vmem_limit_bytes=megabytes * 1024 * 1024
    )


def block_rows(rows, wanted):
    while rows % wanted:
        wanted //= 2
    return wanted


def char_forward(states, lane_counts, weights, chars):
    rows, width = states.shape
    qkv, out, up, down, ones, vecs, head_masks, word_masks = weights
    block = block_rows(rows, 512)
    words, groups = block // chars, block // GROUP
    low, wide = jnp.bfloat16, jnp.float32
    shapes = (
        ((rows, 3 * width), low),
        ((rows // GROUP, CHAR_HEADS * chars, GROUP), low),
        ((rows, width), low),
        ((rows, width), wide),
        ((rows, up.shape[1]), low),
        ((rows, up.shape[1]), low),
        ((rows, width), wide),
        ((rows, width), low),
        ((rows // chars, width), low),
    )
    blocks = (
        (block, 3 * width),
        (groups, CHAR_HEADS * chars, GROUP),
        (block, width),
        (block, width),
        (block, up.shape[1]),
        (block, up.shape[1]),
        (block, width),
        (block, width),
        (words, width),
    )
    flops = 2 * rows * width * (4 * width + 2 * up.shape[1] + 8 * width)
    return pl.pallas_call(
        functools.partial(char_forward_kernel, chars),
        grid=(rows // block,),
        in_specs=[
            blocked((block, width)),
            blocked((groups, 1, GROUP)),
            whole(qkv.shape),
            whole(out.shape),
            whole(up.shape),
            whole(down.shape),
            whole(ones.shape),
            whole(vecs.shape),
            whole(head_masks.shape),
            whole(word_masks.shape),
        ],
        out_specs=[blocked(shape) for shape in blocks],
        out_shape=[jax.ShapeDtypeStruct(shape, kind) for shape, kind in shapes],
        compiler_params=params(56),
        cost_estimate=pl.CostEstimate(
            flops=flops, bytes_accessed=rows * width * 36, transcendentals=rows * width * 5
        ),
        name="char_forward",
    )(states, lane_counts, qkv, out, up, down, ones, vecs, head_masks, word_masks)


def char_mlp_back(y1, y2, pi, grad_pooled, hidden, slope, weights, chars):
    rows, width = y1.shape
    up_t, down_t, vecs, ones = weights
    block = block_rows(rows, 512)
    hidden_width = hidden.shape[1]
    wide = jnp.float32
    flops = 2 * rows * width * (4 * hidden_width + 2 * width)
    return pl.pallas_call(
        functools.partial(char_mlp_back_kernel, chars, None),
        grid=(rows // block,),
        in_specs=[
            blocked((block, width)),
            blocked((block, width)),
            blocked((block, width)),
            blocked((block // chars, 1, width)),
            blocked((block, hidden_width)),
            blocked((block, hidden_width)),
            whole(up_t.shape),
            whole(down_t.shape),
            whole(vecs.shape),
            whole(ones.shape),
        ],
        out_specs=[
            blocked((block, width)),
            whole((width, hidden_width)),
            whole((width, hidden_width)),
            whole((3, 8, width)),
        ],
        out_shape=[
            jax.ShapeDtypeStruct((rows, width), wide),
            jax.ShapeDtypeStruct((width, hidden_width), wide),
            jax.ShapeDtypeStruct((width, hidden_width), wide),
            jax.ShapeDtypeStruct((3, 8, width), wide),
        ],
        compiler_params=params(56),
        cost_estimate=pl.CostEstimate(
            flops=flops, bytes_accessed=rows * width * 30, transcendentals=0
        ),
        name="char_mlp_back",
    )(y1, y2, pi, grad_pooled, hidden, slope, up_t, down_t, vecs, ones)


def char_attn_back(states, cp, probs, co, grad_y1, weights, chars):
    rows, width = states.shape
    qkv_t, out_t, vecs, head_masks, word_masks = weights
    block = block_rows(rows, 512)
    low, wide = jnp.bfloat16, jnp.float32
    flops = 2 * rows * width * 18 * width
    return pl.pallas_call(
        functools.partial(char_attn_back_kernel, chars, None),
        grid=(rows // block,),
        in_specs=[
            blocked((block, width)),
            blocked((block, 3 * width)),
            blocked((block // GROUP, CHAR_HEADS * chars, GROUP)),
            blocked((block, width)),
            blocked((block, width)),
            whole(qkv_t.shape),
            whole(out_t.shape),
            whole(vecs.shape),
            whole(head_masks.shape),
            whole(word_masks.shape),
        ],
        out_specs=[
            blocked((block, width)),
            whole((width, 3 * width)),
            whole((width, width)),
            whole((2, 8, width)),
        ],
        out_shape=[
            jax.ShapeDtypeStruct((rows, width), low),
            jax.ShapeDtypeStruct((width, 3 * width), wide),
            jax.ShapeDtypeStruct((width, width), wide),
            jax.ShapeDtypeStruct((2, 8, width), wide),
        ],
        scratch_shapes=[
            pltpu.VMEM((block, 3 * width), low),
            pltpu.VMEM((block, width), low),
        ],
        compiler_params=params(56),
        cost_estimate=pl.CostEstimate(
            flops=flops, bytes_accessed=rows * width * 18, transcendentals=0
        ),
        name="char_attn_back",
    )(states, cp, probs, co, grad_y1, qkv_t, out_t, vecs, head_masks, word_masks)


def char_mlp_back_exchange(
    y1, y2, pi, grad_pooled, hidden, slope, weights, chars, mesh_size, grad_proj, word_small, word_terms
):
    rows, width = y1.shape
    up_t, down_t, vecs, ones = weights
    dp, mp = mesh_size
    block = block_rows(rows, 512)
    hidden_width = hidden.shape[1]
    low, wide = jnp.bfloat16, jnp.float32
    model = grad_proj.shape[1]
    flops = 2 * rows * width * (4 * hidden_width + 2 * width)
    char_rows = 2 * hidden_width // 16 + model // 16 + 16 * word_small.shape[0]
    n = word_terms.shape[2]
    share = model // dp
    outs = (
        ((rows, width), wide, blocked((block, width))),
        ((mp, dp, char_rows, 128), low, None),
        ((3, share, 128), wide, None),
        ((share, 128), wide, None),
        ((share, model), wide, None),
        ((share, model), wide, None),
    )
    return pl.pallas_call(
        functools.partial(char_mlp_back_kernel, chars, mesh_size),
        grid=(rows // block,),
        in_specs=[
            blocked((block, width)),
            blocked((block, width)),
            blocked((block, width)),
            blocked((block // chars, 1, width)),
            blocked((block, hidden_width)),
            blocked((block, hidden_width)),
            whole(up_t.shape),
            whole(down_t.shape),
            whole(vecs.shape),
            whole(ones.shape),
            whole(grad_proj.shape),
            whole(word_small.shape),
            pl.BlockSpec(memory_space=pl.ANY),
        ],
        out_specs=[spec or whole(shape) for shape, _, spec in outs],
        out_shape=[jax.ShapeDtypeStruct(shape, kind) for shape, kind, _ in outs],
        scratch_shapes=[
            pltpu.VMEM((width, hidden_width), wide),
            pltpu.VMEM((width, hidden_width), wide),
            pltpu.VMEM((3, 8, width), wide),
            pltpu.VMEM((mp // 2, dp, n, 128), low),
            pltpu.SemaphoreType.DMA((mp // 2,)),
        ]
        + scatter_scratch(dp, mp, n),
        compiler_params=pltpu.CompilerParams(
            dimension_semantics=("arbitrary",),
            vmem_limit_bytes=60 * 1024 * 1024,
            collective_id=1,
            has_side_effects=True,
        ),
        cost_estimate=pl.CostEstimate(
            flops=flops, bytes_accessed=rows * width * 30, transcendentals=0
        ),
        name="char_mlp_back",
    )(
        y1, y2, pi, grad_pooled, hidden, slope, up_t, down_t, vecs, ones,
        grad_proj, word_small, word_terms,
    )


def char_attn_back_exchange(
    states, cp, probs, co, grad_y1, weights, chars, mesh_size, early_terms, hidden_width, model
):
    rows, width = states.shape
    qkv_t, out_t, vecs, head_masks, word_masks = weights
    dp, mp = mesh_size
    count = dp * mp
    block = block_rows(rows, 512)
    low, wide = jnp.bfloat16, jnp.float32
    flops = 2 * rows * width * 18 * width
    n = early_terms.shape[2]
    late = 4 * width // 16 + 16
    outs = (
        ((rows, width), low, blocked((block, width))),
        ((width // count, 3 * width), wide, None),
        ((width // count, width), wide, None),
        ((width // count, hidden_width), wide, None),
        ((hidden_width // count, width), wide, None),
        ((width // count, model), wide, None),
        ((16, model), wide, None),
        ((16, 128), wide, None),
    )
    return pl.pallas_call(
        functools.partial(char_attn_back_kernel, chars, mesh_size),
        grid=(rows // block,),
        in_specs=[
            blocked((block, width)),
            blocked((block, 3 * width)),
            blocked((block // GROUP, CHAR_HEADS * chars, GROUP)),
            blocked((block, width)),
            blocked((block, width)),
            whole(qkv_t.shape),
            whole(out_t.shape),
            whole(vecs.shape),
            whole(head_masks.shape),
            whole(word_masks.shape),
            pl.BlockSpec(memory_space=pl.ANY),
        ],
        out_specs=[spec or whole(shape) for shape, _, spec in outs],
        out_shape=[jax.ShapeDtypeStruct(shape, kind) for shape, kind, _ in outs],
        scratch_shapes=[
            pltpu.VMEM((block, 3 * width), low),
            pltpu.VMEM((block, width), low),
            pltpu.VMEM((width, 3 * width), wide),
            pltpu.VMEM((width, width), wide),
            pltpu.VMEM((2, 8, width), wide),
            pltpu.VMEM((mp // 2, dp, n, 128), low),
            pltpu.SemaphoreType.DMA((mp // 2,)),
            pltpu.VMEM((mp, dp, late, 128), low),
        ]
        + scatter_scratch(dp, mp, n)
        + scatter_scratch(dp, mp, late),
        compiler_params=pltpu.CompilerParams(
            dimension_semantics=("arbitrary",),
            vmem_limit_bytes=56 * 1024 * 1024,
            collective_id=2,
            has_side_effects=True,
        ),
        cost_estimate=pl.CostEstimate(
            flops=flops, bytes_accessed=rows * width * 18, transcendentals=0
        ),
        name="char_attn_back",
    )(states, cp, probs, co, grad_y1, qkv_t, out_t, vecs, head_masks, word_masks, early_terms)


def word_kernel(
    pooled_ref,
    words_ref,
    cotangent_ref,
    language_ref,
    language_hot_ref,
    proj_ref,
    weights_ref,
    norms_ref,
    head_mask_ref,
    layer_ref,
    grad_words_ref,
    terms_ref,
    grad_proj_ref,
    grad_pooled_ref,
    small_ref,
    residual_ref,
    normed_one_ref,
    packed_ref,
    probs_ref,
    mixed_ref,
    middle_ref,
    normed_two_ref,
    hidden_ref,
    slope_ref,
    grad_middle_ref,
    branch_ref,
    grad_mixed_ref,
    grad_keys_ref,
    grad_values_ref,
    sums_ref,
):
    low, wide = jnp.bfloat16, jnp.float32
    length, model = words_ref.shape
    dp, mp = weights_ref.shape[:2]
    share = model // dp
    row_block = 256
    blocks = length // row_block
    hidden_width = hidden_ref.shape[1]
    up_blocks = hidden_width // mp // 128
    scale = HEAD ** (-0.5)
    up_base, down_base = 4 * share, (4 + up_blocks) * share

    def weight(base, first, last):
        pieces = [
            weights_ref[:, j, base + c * share : base + (c + 1) * share, :].reshape(model, 128)
            for j, c in (column(base, block) for block in range(first, last))
        ]
        return jnp.concatenate(pieces, axis=1)

    def column(base, block):
        return (block, 0) if base < up_base else (block // up_blocks, block % up_blocks)

    def put(base, first, grad):
        for k in range(grad.shape[1] // 128):
            j, c = column(base, first + k)
            piece = grad[:, 128 * k : 128 * k + 128].reshape(dp, share, 128).astype(low)
            terms_ref[j, :, base + c * share : base + (c + 1) * share, :] = piece

    def norm(k):
        return norms_ref[k : k + 1, :]

    sums_ref[...] = jnp.zeros_like(sums_ref)

    @pl.loop(0, blocks)
    def _(block):
        span = pl.ds(pl.multiple_of(block * row_block, row_block), row_block)
        residual = words_ref[span, :].astype(wide) + mm(pooled_ref[span, :], proj_ref[...])
        residual = residual + language_ref[...]
        residual_ref[span, :] = residual
        _, _, normed = apply_norm(residual, norm(0), norm(1))
        normed_one_ref[span, :] = normed
        for t in range(3):
            for c in range(0, model // 128, 2):
                cols = slice(128 * c, 128 * c + 256)
                packed_ref[t, span, cols] = mm(normed, weight(t * share, c, c + 2)).astype(low)

    causal = lax.broadcasted_iota(jnp.int32, (row_block, row_block), 0) <= (
        lax.broadcasted_iota(jnp.int32, (row_block, row_block), 1)
    )

    @pl.loop(0, model // 128)
    def _(pair):
        lanes = pl.ds(pl.multiple_of(pair * 128, 128), 128)
        values_t = packed_ref[2, :, lanes].T
        for block in range(blocks):
            stop = (block + 1) * row_block
            span = slice(block * row_block, stop)
            first = block * (block + 1) // 2 * row_block
            queries = packed_ref[0, span, lanes]
            mixed = []
            for h in range(2):
                keys = packed_ref[1, 0:stop, lanes] * head_mask_ref[h : h + 1, 0:128]
                scores = mm(keys, queries, NT) * scale
                near = jnp.where(causal, scores[stop - row_block :], NEG_FILL)
                scores = jnp.concatenate([scores[: stop - row_block], near]) if block else near
                powers = jnp.exp(scores - jnp.max(scores, axis=0, keepdims=True))
                probs = powers * (1.0 / jnp.sum(powers, axis=0, keepdims=True))
                probs = probs.astype(low)
                probs_ref[2 * pair + h, first : first + stop, :] = probs
                mixed.append(mm(values_t[HEAD * h : HEAD * (h + 1), 0:stop], probs))
            mixed_ref[span, lanes] = jnp.concatenate(mixed, axis=0).T.astype(low)

    @pl.loop(0, blocks)
    def _(block):
        span = pl.ds(pl.multiple_of(block * row_block, row_block), row_block)
        out_t = weight(3 * share, 0, model // 128)
        middle = residual_ref[span, :] + mm(mixed_ref[span, :], out_t, NT)
        middle_ref[span, :] = middle
        _, _, normed = apply_norm(middle, norm(2), norm(3))
        normed_two_ref[span, :] = normed
        total = middle
        for c in range(0, hidden_width // 128, 4):
            cols = slice(128 * c, 128 * c + 512)
            hidden, slope = gelu_low(mm(normed, weight(up_base, c, c + 4)))
            hidden_ref[span, cols] = hidden
            slope_ref[span, cols] = slope
            total = total + mm(hidden, weight(down_base, c, c + 4), NT)
        layer_ref[span, :] = total.astype(low)

    cotangent_t = cotangent_ref[...].T
    for c in range(0, hidden_width // 128, 2):
        put(down_base, c, mm(cotangent_t, hidden_ref[:, 128 * c : 128 * c + 256]))

    @pl.loop(0, blocks)
    def _(block):
        span = pl.ds(pl.multiple_of(block * row_block, row_block), row_block)
        cotangent = cotangent_ref[span, :]
        grad_normed = None
        for c in range(0, hidden_width // 128, 4):
            cols = slice(128 * c, 128 * c + 512)
            grad_pre = mm(cotangent, weight(down_base, c, c + 4))
            grad_pre = (grad_pre * slope_ref[span, cols].astype(wide)).astype(low)
            slope_ref[span, cols] = grad_pre
            term = mm(grad_pre, weight(up_base, c, c + 4), NT)
            grad_normed = term if grad_normed is None else grad_normed + term
        unit, inverse = standardize(middle_ref[span, :])
        sums_ref[2] += fold_rows(grad_normed * unit)
        sums_ref[3] += fold_rows(grad_normed)
        grad_middle = cotangent.astype(wide) + norm_back(grad_normed, unit, inverse, norm(2))
        grad_middle_ref[span, :] = grad_middle
        branch = grad_middle.astype(low)
        branch_ref[span, :] = branch
        out_t = weight(3 * share, 0, model // 128)
        grad_mixed_ref[span, :] = mm(branch, out_t).astype(low)

    normed_t = normed_two_ref[...].T
    for c in range(0, hidden_width // 128, 2):
        put(up_base, c, mm(normed_t, slope_ref[:, 128 * c : 128 * c + 256]))
    branch_t = branch_ref[...].T
    for c in range(0, model // 128, 2):
        put(3 * share, c, mm(branch_t, mixed_ref[:, 128 * c : 128 * c + 256]))

    @pl.loop(0, model // 128)
    def _(pair):
        lanes = pl.ds(pl.multiple_of(pair * 128, 128), 128)
        grad_keys_ref[...] = jnp.zeros_like(grad_keys_ref)
        grad_values_ref[...] = jnp.zeros_like(grad_values_ref)
        keys_t = packed_ref[1, :, lanes].T
        for block in range(blocks):
            stop = (block + 1) * row_block
            span = slice(block * row_block, stop)
            first = block * (block + 1) // 2 * row_block
            queries = packed_ref[0, span, lanes]
            grad_mixed = grad_mixed_ref[span, lanes]
            grad_queries = []
            for h in range(2):
                mask = head_mask_ref[h : h + 1, 0:128]
                values = packed_ref[2, 0:stop, lanes] * mask
                grad_probs = mm(values, grad_mixed, NT)
                probs = probs_ref[2 * pair + h, first : first + stop, :]
                probs_wide = probs.astype(wide)
                inner = jnp.sum(grad_probs * probs_wide, axis=0, keepdims=True)
                grad_scores = (probs_wide * (grad_probs - inner)).astype(low)
                grad_values_ref[0:stop, :] += mm(probs, grad_mixed * mask)
                grad_keys_ref[0:stop, :] += mm(grad_scores, queries * mask)
                grad_queries.append(mm(keys_t[HEAD * h : HEAD * (h + 1), 0:stop], grad_scores))
            grad_queries = jnp.concatenate(grad_queries, axis=0) * scale
            packed_ref[0, span, lanes] = grad_queries.T.astype(low)
        packed_ref[1, :, lanes] = (grad_keys_ref[...] * scale).astype(low)
        packed_ref[2, :, lanes] = grad_values_ref[...].astype(low)

    normed_t = normed_one_ref[...].T
    for t in range(3):
        for c in range(0, model // 128, 2):
            put(t * share, c, mm(normed_t, packed_ref[t, :, 128 * c : 128 * c + 256]))

    @pl.loop(0, blocks)
    def _(block):
        span = pl.ds(pl.multiple_of(block * row_block, row_block), row_block)
        grad_normed = None
        for t in range(3):
            term = mm(packed_ref[t, span, :], weight(t * share, 0, model // 128), NT)
            grad_normed = term if grad_normed is None else grad_normed + term
        unit, inverse = standardize(residual_ref[span, :])
        sums_ref[0] += fold_rows(grad_normed * unit)
        sums_ref[1] += fold_rows(grad_normed)
        grad = grad_middle_ref[span, :] + norm_back(grad_normed, unit, inverse, norm(0))
        sums_ref[4] += fold_rows(grad)
        grad = grad.astype(low)
        grad_words_ref[span, :] = grad
        grad_pooled_ref[span] = mm(grad, proj_ref[...], NT)[:, None, :]

    grad_proj_ref[...] = mm(pooled_ref[...].T, grad_words_ref[...])

    sums = [jnp.sum(sums_ref[k], axis=0, keepdims=True) for k in range(5)]
    small_row = lax.broadcasted_iota(jnp.int32, (8, 128), 0)
    for b in range(model // 128):
        cols = slice(128 * b, 128 * b + 128)
        small_ref[b, 0:8, :] = language_hot_ref[...] * sums[4][:, cols]
        piece = jnp.zeros((8, 128), wide)
        for k in range(4):
            piece = jnp.where(small_row == k, sums[k][:, cols], piece)
        small_ref[b, 8:16, :] = piece


def word_layer_kernel(pooled, words, cotangent, language_row, language_hot, proj, weights, norms, head_masks):
    low, wide = jnp.bfloat16, jnp.float32
    length, model = words.shape
    width = pooled.shape[1]
    dp, mp, n = weights.shape[:3]
    hidden_width = (n * dp // model - 4) // 2 * 128 * mp
    blocks = length // 256
    heads = model // HEAD
    arrays = (pooled, words, cotangent, language_row, language_hot, proj, weights, norms, head_masks)
    outs = (
        ((length, model), low),
        ((length, model), low),
        ((mp, dp, n, 128), low),
        ((width, model), wide),
        ((length, 1, width), wide),
        ((model // 128, 16, 128), wide),
    )
    return pl.pallas_call(
        word_kernel,
        grid=(1,),
        in_specs=[once(array.shape) for array in arrays],
        out_specs=[once(shape) for shape, _ in outs],
        out_shape=[jax.ShapeDtypeStruct(shape, kind) for shape, kind in outs],
        scratch_shapes=[
            pltpu.VMEM((length, model), wide),
            pltpu.VMEM((length, model), low),
            pltpu.VMEM((3, length, model), low),
            pltpu.VMEM((heads, blocks * (blocks + 1) // 2 * 256, 256), low),
            pltpu.VMEM((length, model), low),
            pltpu.VMEM((length, model), wide),
            pltpu.VMEM((length, model), low),
            pltpu.VMEM((length, hidden_width), low),
            pltpu.VMEM((length, hidden_width), low),
            pltpu.VMEM((length, model), wide),
            pltpu.VMEM((length, model), low),
            pltpu.VMEM((length, model), low),
            pltpu.VMEM((length, 128), wide),
            pltpu.VMEM((length, 128), wide),
            pltpu.VMEM((5, 8, model), wide),
        ],
        compiler_params=pltpu.CompilerParams(vmem_limit_bytes=62 * 1024 * 1024),
        cost_estimate=pl.CostEstimate(
            flops=40 * 10**9, bytes_accessed=20 * 2**20, transcendentals=10**7
        ),
        name="word_layer",
    )(*arrays)


def attend_forward(queries, key_block, values, allowed):
    scores = low_sum("bqhd,bkhd->bhqk", queries, key_block) * HEAD ** (-0.5)
    scores = jnp.where(allowed, scores, NEG_FILL)
    row_max = jnp.max(scores, axis=-1, keepdims=True)
    powers = jnp.exp(scores - row_max)
    row_total = jnp.sum(powers, axis=-1, keepdims=True)
    attn_probs = (powers / row_total).astype(jnp.bfloat16)
    attn_mixed = low_sum("bhqk,bkhd->bqhd", attn_probs, values).astype(jnp.bfloat16)
    return (attn_mixed, row_max + jnp.log(row_total))


def attend_backward(queries, key_block, values, allowed, log_total, grad_mixed):
    scale = HEAD ** (-0.5)
    scores = low_sum("bqhd,bkhd->bhqk", queries, key_block) * scale
    attn_probs = jnp.where(allowed, jnp.exp(scores - log_total), 0.0)
    grad_probs = low_sum("bqhd,bkhd->bhqk", grad_mixed, values)
    grad_values = low_sum("bhqk,bqhd->bkhd", attn_probs.astype(jnp.bfloat16), grad_mixed)
    inner_sum = jnp.sum(grad_probs * attn_probs, axis=-1, keepdims=True)
    grad_scores = (attn_probs * (grad_probs - inner_sum)).astype(jnp.bfloat16)
    grad_queries = low_sum("bhqk,bkhd->bqhd", grad_scores, key_block) * scale
    grad_keys = low_sum("bhqk,bqhd->bkhd", grad_scores, queries) * scale
    return (grad_queries, grad_keys, grad_values)


def word_layer(residual, grad_rows, weights, norms, mp_size, mp_index):
    qkv, out_t, up, down_t = weights
    gain_one, bias_one, gain_two, bias_two = norms
    rows, width = residual.shape
    low = jnp.bfloat16
    sequences, length = max(1, rows // LEN), min(rows, LEN)
    share = LEN // length
    groups = [[a * share + b for b in range(share)] for a in range(mp_size // share)]
    unit_one, inverse_one, normed_one = apply_norm(residual, gain_one, bias_one)
    packed = low_sum("rd,tdc->trc", normed_one, qkv).astype(low)
    packed = packed.reshape(3, sequences, length, width // HEAD, HEAD)
    keys = packed[1:]
    start = 0
    if share > 1:
        keys = lax.all_gather(keys, "mp", axis=2, tiled=True, axis_index_groups=groups)
        start = lax.rem(mp_index, share) * length
    allowed = (
        lax.broadcasted_iota(jnp.int32, (length, LEN), 1)
        <= lax.broadcasted_iota(jnp.int32, (length, LEN), 0) + start
    )[None, None]
    mixed, log_total = attend_forward(packed[0], keys[0], keys[1], allowed)
    mixed_rows = mixed.reshape(rows, width)
    middle = residual + mm(mixed_rows, out_t, NT)
    unit_two, inverse_two, normed_two = apply_norm(middle, gain_two, bias_two)
    hidden, slope = gelu_pair(matmul(normed_two, up))
    hidden = hidden.astype(low)
    layer_output = (middle + mm(hidden, down_t, NT)).astype(low)
    grad_wide = grad_rows.astype(jnp.float32)
    grad_down_t = mm(grad_rows, hidden, TN)
    grad_pre = (matmul(grad_rows, down_t) * slope).astype(low)
    grad_up = mm(normed_two, grad_pre, TN)
    grad_normed = mm(grad_pre, up, NT)
    grad_gain_two = jnp.sum(grad_normed * unit_two, axis=0)
    grad_bias_two = jnp.sum(grad_normed, axis=0)
    grad_middle = grad_wide + norm_back(grad_normed, unit_two, inverse_two, gain_two)
    branch = grad_middle.astype(low)
    grad_out_t = mm(branch, mixed_rows, TN)
    grad_mixed = matmul(branch, out_t).astype(low).reshape(sequences, length, -1, HEAD)
    grad_queries, grad_keys, grad_values = attend_backward(
        packed[0], keys[0], keys[1], allowed, log_total, grad_mixed
    )
    grad_keys = jnp.stack((grad_keys, grad_values), axis=0)
    if share > 1:
        grad_keys = lax.psum_scatter(
            grad_keys, "mp", scatter_dimension=2, tiled=True, axis_index_groups=groups
        )
    grad_packed = jnp.concatenate((grad_queries[None], grad_keys), axis=0)
    grad_packed = grad_packed.reshape(3, rows, width).astype(low)
    grad_qkv = low_sum("rd,trc->tdc", normed_one, grad_packed)
    grad_normed = low_sum("trc,tdc->rd", grad_packed, qkv)
    grad_gain_one = jnp.sum(grad_normed * unit_one, axis=0)
    grad_bias_one = jnp.sum(grad_normed, axis=0)
    grad_residual = grad_middle + norm_back(grad_normed, unit_one, inverse_one, gain_one)
    return (
        layer_output,
        grad_residual,
        (grad_qkv, grad_out_t, grad_up, grad_down_t),
        (grad_gain_one, grad_bias_one, grad_gain_two, grad_bias_two),
    )


def mask_constants(width, chars):
    head, word = np.arange(width) // HEAD, np.arange(GROUP) // chars
    head_masks = head[None] == np.arange(8)[:, None]
    word_masks = word[None] == np.arange(GROUP // chars)[:, None]
    ones = head[:, None] == head[None]
    return tuple(jnp.asarray(mask.astype(ml_dtypes.bfloat16)) for mask in (head_masks, word_masks, ones))


def blocks_of(array, count):
    return array.reshape(count, -1)


def shards_general(
    char_states,
    word_states,
    char_counts,
    language_group,
    output_grad,
    char_norm_gain,
    char_norm_bias,
    char_qkv,
    char_out,
    char_mlp_gain,
    char_mlp_bias,
    char_up,
    char_down,
    pool_query,
    char_proj,
    language_table,
    word_norm_gain,
    word_norm_bias,
    word_qkv,
    word_out,
    word_mlp_gain,
    word_mlp_bias,
    word_up,
    word_down,
):
    low, wide = jnp.bfloat16, jnp.float32
    dp_size, mp_size = lax.axis_size("dp"), lax.axis_size("mp")
    mp_index = lax.axis_index("mp")
    devices = dp_size * mp_size
    word_count, chars, width = char_states.shape
    model = word_states.shape[1]
    langs = language_table.shape[0]

    char_parts = (
        char_qkv,
        char_out,
        char_up,
        char_down,
        char_proj,
        char_norm_gain,
        char_norm_bias,
        char_mlp_gain,
        char_mlp_bias,
        pool_query,
        word_norm_gain,
        word_norm_bias,
        word_mlp_gain,
        word_mlp_bias,
        language_table.T,
    )
    flat = jnp.concatenate([part.astype(low).reshape(-1) for part in char_parts])
    flat_size = flat.shape[0]
    flat = jnp.pad(flat, (0, -flat_size % 2048))
    full = lax.all_gather(flat, BOTH, axis=0, tiled=False)
    unpacked, start = [], 0
    for part in char_parts:
        stop = start + part.size
        piece = full[:, start:stop].reshape((devices * part.shape[0],) + part.shape[1:])
        unpacked.append(piece)
        start = stop
    (
        qkv_char,
        out_char,
        up_char,
        down_char,
        proj_char,
        gain_attn,
        bias_attn,
        gain_mlp,
        bias_mlp,
        query_pool,
        gain_one,
        bias_one,
        gain_two,
        bias_two,
        table_t,
    ) = unpacked

    word_parts = (word_qkv, word_out.T, word_up, word_down.T)
    word_flat = jnp.concatenate([part.astype(low).reshape(-1, 128) for part in word_parts])
    word_full = lax.all_gather(word_flat, BOTH, axis=0, tiled=False)
    word_full = word_full.reshape(dp_size, mp_size, word_flat.shape[0], 128)
    word_weights, start = [], 0
    for part in word_parts:
        stop = start + part.size // 128
        piece = word_full[:, :, start:stop].reshape((dp_size, mp_size) + part.shape)
        if part.ndim == 3:
            piece = piece.transpose(2, 0, 3, 1, 4).reshape(3, model, model)
        else:
            piece = piece.transpose(0, 2, 1, 3)
            piece = piece.reshape(dp_size * part.shape[0], mp_size * part.shape[1])
        word_weights.append(piece)
        start = stop

    rows = word_count * chars
    states = char_states.reshape(rows, width)
    lane_counts = jnp.repeat(char_counts, chars).reshape(rows // GROUP, 1, GROUP)
    head_masks, word_masks, ones = mask_constants(width, chars)
    zero = jnp.zeros_like(gain_attn)
    vecs = jnp.stack(
        (gain_attn, bias_attn, gain_mlp, bias_mlp, query_pool, zero, zero, zero)
    ).astype(wide)
    cp, probs, co, y1, hidden, slope, y2, pi, pooled = char_forward(
        states,
        lane_counts,
        (qkv_char, out_char, up_char, down_char, ones, vecs, head_masks, word_masks),
        chars,
    )

    sequences = max(1, word_count // LEN)
    first = (mp_index * word_count) // LEN
    language = lax.dynamic_slice_in_dim(language_group, first, sequences)
    language_hot = (language[:, None] == jnp.arange(langs)[None]).astype(wide)
    language_rows = jnp.sum(language_hot[:, :, None] * table_t.T.astype(wide)[None], axis=1)
    residual = word_states.astype(wide) + matmul(pooled, proj_char)
    residual = (
        residual.reshape(sequences, -1, model) + language_rows[:, None, :]
    ).reshape(word_count, model)
    norms = tuple(value.astype(wide) for value in (gain_one, bias_one, gain_two, bias_two))
    layer_output, grad_residual, word_grads, word_norm_grads = word_layer(
        residual, output_grad, word_weights, norms, mp_size, mp_index
    )
    grad_words = grad_residual.astype(low)
    sequence_grads = jnp.sum(grad_residual.reshape(sequences, -1, model), axis=1)
    grad_table = jnp.sum(language_hot[:, :, None] * sequence_grads[:, None, :], axis=0)

    pieces = []
    for part, grad in zip(word_parts, word_grads):
        if part.ndim == 3:
            grad = grad.reshape(3, dp_size, part.shape[1], mp_size, part.shape[2])
            grad = grad.transpose(3, 1, 0, 2, 4)
        else:
            grad = grad.reshape(dp_size, part.shape[0], mp_size, part.shape[1])
            grad = grad.transpose(2, 0, 1, 3)
        pieces.append(grad.astype(low).reshape(mp_size, dp_size, -1, 128))
    word_terms = jnp.concatenate(pieces, axis=2)
    word_terms = lax.psum_scatter(word_terms, "mp", scatter_dimension=0, tiled=True)
    word_terms = lax.psum_scatter(word_terms[0], "dp", scatter_dimension=0, tiled=True)[0]
    word_shares, start = [], 0
    for part in word_parts:
        stop = start + part.size // 128
        word_shares.append(word_terms[start:stop].reshape(part.shape).astype(wide))
        start = stop

    grad_proj = mm(pooled, grad_words, TN)
    grad_pooled = mm(grad_words, proj_char, NT).reshape(word_count, 1, width)
    grad_y1, grad_up, grad_down_t, mlp_vecs = char_mlp_back(
        y1, y2, pi, grad_pooled, hidden, slope, (up_char.T, down_char.T, vecs, ones), chars
    )
    mlp_vecs = jnp.sum(mlp_vecs, axis=1)
    early = (
        grad_up,
        grad_down_t.T,
        grad_proj,
        mlp_vecs[0],
        mlp_vecs[1],
        mlp_vecs[2],
        word_norm_grads[0],
        word_norm_grads[1],
        word_norm_grads[2],
        word_norm_grads[3],
        grad_table.T,
    )
    early_terms = jnp.concatenate([blocks_of(part, devices) for part in early], axis=1)
    early_size = early_terms.shape[1]
    early_terms = jnp.pad(early_terms, ((0, 0), (0, -early_size % 1024)))
    early_terms = lax.psum_scatter(early_terms, BOTH, scatter_dimension=0, tiled=True)[0]
    grad_chars, grad_qkv, grad_out, attn_vecs = char_attn_back(
        states, cp, probs, co, grad_y1, (qkv_char.T, out_char.T, vecs, head_masks, word_masks), chars
    )
    attn_vecs = jnp.sum(attn_vecs, axis=1)
    late = (grad_qkv, grad_out, attn_vecs[0], attn_vecs[1])
    late_terms = jnp.concatenate([blocks_of(part, devices) for part in late], axis=1)
    late_terms = jnp.pad(late_terms, ((0, 0), (0, -late_terms.shape[1] % 1024)))
    late_terms = lax.psum_scatter(late_terms, BOTH, scatter_dimension=0, tiled=True)[0]

    def take(terms, parts):
        shares, start = [], 0
        for part in parts:
            stop = start + part.size // devices
            shape = (part.shape[0] // devices,) + part.shape[1:]
            shares.append(terms[start:stop].reshape(shape))
            start = stop
        return shares

    (
        g_up,
        g_down,
        g_proj,
        g_query,
        g_gain_mlp,
        g_bias_mlp,
        g_gain_one,
        g_bias_one,
        g_gain_two,
        g_bias_two,
        g_table_t,
    ) = take(early_terms, early)
    g_qkv, g_out, g_gain_attn, g_bias_attn = take(late_terms, late)
    return (
        layer_output,
        grad_chars.reshape(char_states.shape),
        grad_words,
        g_gain_attn,
        g_bias_attn,
        g_qkv,
        g_out,
        g_gain_mlp,
        g_bias_mlp,
        g_up,
        g_down,
        g_query,
        g_proj,
        g_table_t.T,
        g_gain_one,
        g_bias_one,
        word_shares[0],
        word_shares[1].T,
        g_gain_two,
        g_bias_two,
        word_shares[2],
        word_shares[3].T,
    )


def fits(dp, mp, words, model, width, chars, hidden_width, langs):
    count = dp * mp
    return (
        words == LEN
        and mp % 2 == 0
        and model == 128 * mp
        and model // dp % 16 == 0
        and width == 256
        and width == 8 * count
        and hidden_width % (16 * count) == 0
        and GROUP % chars == 0
        and langs == 8
    )


def shards(*arrays):
    char_states, word_states = arrays[:2]
    dp, mp = lax.axis_size("dp"), lax.axis_size("mp")
    words, chars, width = char_states.shape
    model, hidden_width = word_states.shape[1], arrays[11].shape[1]
    if not fits(dp, mp, words, model, width, chars, hidden_width, arrays[15].shape[0]):
        return shards_general(*arrays)
    return shards_whole(*arrays)


def shards_whole(
    char_states,
    word_states,
    char_counts,
    language_group,
    output_grad,
    char_norm_gain,
    char_norm_bias,
    char_qkv,
    char_out,
    char_mlp_gain,
    char_mlp_bias,
    char_up,
    char_down,
    pool_query,
    char_proj,
    language_table,
    word_norm_gain,
    word_norm_bias,
    word_qkv,
    word_out,
    word_mlp_gain,
    word_mlp_bias,
    word_up,
    word_down,
):
    low, wide = jnp.bfloat16, jnp.float32
    dp, mp = lax.axis_size("dp"), lax.axis_size("mp")
    count = dp * mp
    index = lax.axis_index("dp") * mp + lax.axis_index("mp")
    words, chars, width = char_states.shape
    model = word_states.shape[1]
    langs = language_table.shape[0]
    hidden_width = char_up.shape[1]
    char_small = (char_norm_gain, char_norm_bias, char_mlp_gain, char_mlp_bias, pool_query)
    word_small = (word_norm_gain, word_norm_bias, word_mlp_gain, word_mlp_bias)
    small = jnp.concatenate(char_small + word_small + (language_table.reshape(-1),))
    small = jnp.pad(small, (0, 16 * 128 - small.shape[0])).reshape(16, 128)
    (
        qkv,
        qkv_t,
        out,
        out_t,
        up,
        up_t,
        down,
        down_t,
        proj,
        small_all,
        word_share,
    ) = gather_weights(
        dp,
        mp,
        (char_qkv, char_out, char_up, char_down, char_proj),
        small,
        (word_qkv, word_out.T, word_up, word_down.T),
    )
    word_weights = lax.all_gather(word_share, BOTH, axis=0, tiled=False)
    word_weights = word_weights.reshape(dp, mp, word_share.shape[0], 128)
    char_share, word_part = width // count, model // count
    first, second = 5 * char_share, 5 * char_share + 4 * word_part
    flat = small_all.reshape(count, -1).astype(wide)
    vecs = flat[:, :first].reshape(count, 5, char_share).transpose(1, 0, 2).reshape(5, width)
    norms = flat[:, first:second].reshape(count, 4, word_part).transpose(1, 0, 2)
    norms = norms.reshape(4, model)
    table = flat[:, second : second + langs * word_part].reshape(count, langs, word_part)
    table = table.transpose(1, 0, 2).reshape(langs, model)
    vecs = jnp.pad(vecs, ((0, 3), (0, 0)))

    rows = words * chars
    states = char_states.reshape(rows, width)
    lane_counts = jnp.repeat(char_counts, chars).reshape(rows // GROUP, 1, GROUP)
    head_masks, word_masks, ones = mask_constants(width, chars)
    cp, probs, co, y1, hidden, slope, y2, pi, pooled = char_forward(
        states,
        lane_counts,
        (qkv, out, up, down, ones, vecs, head_masks, word_masks),
        chars,
    )

    language = lax.dynamic_slice_in_dim(language_group, lax.axis_index("mp"), 1)
    hot = (language == jnp.arange(langs)).astype(wide)[:, None]
    language_row = jnp.sum(hot * table, axis=0, keepdims=True)
    layer_output, grad_words, word_terms, grad_proj, grad_pooled, small_terms = word_layer_kernel(
        pooled,
        word_states,
        output_grad,
        language_row,
        jnp.broadcast_to(hot, (langs, 128)),
        proj,
        word_weights,
        norms,
        head_masks,
    )

    grad_y1, char_terms, g_word_qkv, g_word_out, g_word_up, g_word_down = char_mlp_back_exchange(
        y1, y2, pi, grad_pooled, hidden, slope, (up_t, down_t, vecs, ones), chars, (dp, mp),
        grad_proj, small_terms, word_terms,
    )
    grad_chars, g_qkv, g_out, g_up, g_down, g_proj, g_small, g_vecs = char_attn_back_exchange(
        states, cp, probs, co, grad_y1, (qkv_t, out_t, vecs, head_masks, word_masks), chars,
        (dp, mp), char_terms, hidden_width, model,
    )
    word_small = lax.dynamic_slice_in_dim(g_small[:12], index * word_part, word_part, 1)
    char_small = lax.dynamic_slice_in_dim(g_small[12:15, :width], index * char_share, char_share, 1)
    late_small = lax.dynamic_slice_in_dim(
        g_vecs[:4].reshape(2, width), index * char_share, char_share, 1
    )
    return (
        layer_output,
        grad_chars.reshape(char_states.shape),
        grad_words,
        late_small[0],
        late_small[1],
        g_qkv,
        g_out,
        char_small[1],
        char_small[2],
        g_up,
        g_down,
        char_small[0],
        g_proj,
        word_small[:langs],
        word_small[8],
        word_small[9],
        g_word_qkv,
        g_word_out.T,
        word_small[10],
        word_small[11],
        g_word_up,
        g_word_down.T,
    )


def solution(mesh):
    vector, rows = P(BOTH), P(BOTH, None)
    cube = P(BOTH, None, None)
    table = P(None, BOTH)
    words = (P(None, "dp", "mp"), P("mp", "dp"), P("dp", "mp"), P("mp", "dp"))
    char_weights = (
        vector, vector, rows, rows, vector, vector, rows, rows, vector, rows, table,
    )
    weights = char_weights + (
        vector, vector, words[0], words[1], vector, vector, words[2], words[3],
    )
    return jax.shard_map(
        shards,
        mesh=mesh,
        in_specs=(cube, rows, vector, P("dp"), rows) + weights,
        out_specs=(rows, cube, rows) + weights,
        check_vma=False,
    )
```

```python
import functools

import jax
import jax.numpy as jnp
import ml_dtypes
import numpy as np
from jax import lax
from jax.experimental import pallas as pl
from jax.experimental.pallas import tpu as pltpu
from jax.sharding import PartitionSpec as P

HEAD = 64
CHAR_HEADS = 4
LEN = 1024
GROUP = 128
SUB = 512
CHUNK = 512


NORM_EPS = 1e-05
NEG_FILL = -1000000000.0
BOTH = ("dp", "mp")
MESH = pl.DeviceIdType.MESH

LOGIT = (
    0.7978697123195114,
    0.036392286136226214,
    -8.782649734580825e-05,
    -3.669345726473906e-05,
    1.4250064727244771e-06,
)

NN = (((1,), (0,)), ((), ()))
NT = (((1,), (1,)), ((), ()))
TN = (((0,), (0,)), ((), ()))


def mm(first_arg, second_arg, dims=NN):
    return lax.dot_general(first_arg, second_arg, dims, preferred_element_type=jnp.float32)


def matmul(first_arg, second_arg):
    return jnp.dot(first_arg, second_arg, preferred_element_type=jnp.float32)


def low_sum(pattern, first_arg, second_arg):
    return jnp.einsum(pattern, first_arg, second_arg, preferred_element_type=jnp.float32)


def standardize(values):
    centred = values - jnp.mean(values, axis=-1, keepdims=True)
    inverse = lax.rsqrt(jnp.mean(centred * centred, axis=-1, keepdims=True) + NORM_EPS)
    return (centred * inverse, inverse)


def apply_norm(values, gain_value, bias_value):
    unit_rows, inverse = standardize(values)
    normed = (unit_rows * gain_value + bias_value).astype(jnp.bfloat16)
    return (unit_rows, inverse, normed)


def norm_back(grad_out, unit_rows, inverse, gain_value):
    grad_unit = grad_out * gain_value
    inner_sum = jnp.mean(grad_unit * unit_rows, axis=-1, keepdims=True)
    return inverse * (
        grad_unit - jnp.mean(grad_unit, axis=-1, keepdims=True) - unit_rows * inner_sum
    )


def gelu_pair(values):
    square = values * values
    logit = square * LOGIT[4] + LOGIT[3]
    for term in LOGIT[2::-1]:
        logit = logit * square + term
    normal = jnp.tanh(logit * values) * 0.5 + 0.5
    density = jnp.exp2(square * -0.7213475204444817 - 1.3257480647361593)
    return (values * normal, values * density + normal)


def strips(function, size, *arrays):
    parts = [
        function(*(array[row : row + size] for array in arrays))
        for row in range(0, arrays[0].shape[0], size)
    ]
    return tuple(jnp.concatenate(part, axis=0) for part in zip(*parts))


def gelu_low(values):
    return strips(
        lambda strip: tuple(part.astype(jnp.bfloat16) for part in gelu_pair(strip)),
        32 * 256 // values.shape[1],
        values,
    )


def split_two(values):
    high = values.astype(jnp.bfloat16)
    return (high, (values - high.astype(jnp.float32)).astype(jnp.bfloat16))


def fold_rows(values):
    return jnp.sum(values.reshape(values.shape[0] // 8, 8, values.shape[1]), axis=0)


class Place:
    def __init__(self, dp, mp):
        self.dp, self.mp, self.wide = dp, mp, mp // 2
        self.i, self.j = lax.axis_index("dp"), lax.axis_index("mp")
        self.x, self.core = self.j // 2, lax.rem(self.j, 2)

    def partner(self):
        return (self.i, 2 * self.x + 1 - self.core)

    def across(self, step):
        return (self.i, 2 * lax.rem(self.x + step, self.wide) + self.core)

    def along(self, step):
        return (lax.rem(self.i + step, self.dp), self.j)

    def greet(self):
        barrier = pltpu.get_barrier_semaphore()
        others = [self.partner()]
        others += [self.across(step) for step in range(1, self.wide)]
        others += [self.along(step) for step in range(1, self.dp)]
        for other in others:
            pl.semaphore_signal(barrier, inc=1, device_id=other, device_id_type=MESH)
        pl.semaphore_wait(barrier, len(others))


def remote(source, target, sems, index, device):
    return pltpu.make_async_remote_copy(
        src_ref=source,
        dst_ref=target,
        send_sem=sems[0].at[index],
        recv_sem=sems[1].at[index],
        device_id=device,
        device_id_type=MESH,
    )


class ScatterSum:
    def __init__(self, place, blocks, local, one, two, three, sems):
        self.place, self.blocks, self.local = place, blocks, local
        self.one, self.two, self.three, self.sems = one, two, three, sems

    def first(self):
        place = self.place
        return [
            remote(
                self.blocks.at[2 * e + 1 - place.core],
                self.one.at[e],
                self.sems,
                e,
                place.partner(),
            )
            for e in range(place.wide)
        ]

    def second(self):
        place = self.place
        return [
            remote(
                self.one.at[lax.rem(place.x + step, place.wide)],
                self.two.at[step - 1],
                self.sems,
                place.wide + step - 1,
                place.across(step),
            )
            for step in range(1, place.wide)
        ]

    def third(self):
        place = self.place
        return [
            remote(
                self.one.at[place.x, lax.rem(place.i + step, place.dp)],
                self.three.at[step - 1],
                self.sems,
                2 * place.wide - 1 + step - 1,
                place.along(step),
            )
            for step in range(1, place.dp)
        ]

    def start(self):
        for copy in self.first():
            copy.start()

    def go_across(self):
        place = self.place
        for copy in self.first():
            copy.wait()

        @pl.loop(0, place.dp)
        def _(row):
            for e in range(place.wide):
                own = self.local(e, row).astype(jnp.float32)
                total = self.one[e, row].astype(jnp.float32) + own
                self.one[e, row] = total.astype(jnp.bfloat16)

        for copy in self.second():
            copy.start()

    def go_along(self):
        place = self.place
        for copy in self.second():
            copy.wait()

        @pl.loop(0, place.dp)
        def _(row):
            total = self.one[place.x, row].astype(jnp.float32)
            for step in range(1, place.wide):
                total = total + self.two[step - 1, row].astype(jnp.float32)
            self.one[place.x, row] = total.astype(jnp.bfloat16)

        for copy in self.third():
            copy.start()

    def finish(self):
        place = self.place
        for copy in self.third():
            copy.wait()

        def own(rows):
            total = self.one[place.x, place.i, rows].astype(jnp.float32)
            for step in range(1, place.dp):
                total = total + self.three[step - 1, rows].astype(jnp.float32)
            return total

        return own


def scatter_scratch(dp, mp, n):
    wide = mp // 2
    copies = 2 * wide - 1 + dp - 1
    return [
        pltpu.VMEM((wide, dp, n, 128), jnp.bfloat16),
        pltpu.VMEM((max(1, wide - 1), dp, n, 128), jnp.bfloat16),
        pltpu.VMEM((dp - 1, n, 128), jnp.bfloat16),
        pltpu.SemaphoreType.DMA((copies,)),
        pltpu.SemaphoreType.DMA((copies,)),
    ]


def put_pairs(target, first_row, columns):
    mp, dp = target.shape[0], target.shape[1]
    rows = columns.shape[0] // (mp * dp)
    for pair in range(columns.shape[1] // 256):
        both = [
            columns[:, 256 * pair + 128 * c : 256 * pair + 128 * c + 128].reshape(
                dp, mp, rows, 128
            )
            for c in range(2)
        ]
        both = jnp.concatenate(both, axis=2).astype(jnp.bfloat16)
        spot = slice(first_row + 2 * rows * pair, first_row + 2 * rows * (pair + 1))
        for j in range(mp):
            target[j, :, spot, :] = both[:, j]


def gather_kernel(
    dp,
    mp,
    qkv_ref,
    out_ref,
    up_ref,
    down_ref,
    proj_ref,
    small_ref,
    word_qkv_ref,
    word_out_ref,
    word_up_ref,
    word_down_ref,
    qkv_all,
    qkv_t_all,
    out_all,
    out_t_all,
    up_all,
    up_t_all,
    down_all,
    down_t_all,
    proj_all,
    small_all,
    word_share,
    held,
    sends,
    arrivals,
):
    place = Place(dp, mp)
    low = jnp.bfloat16
    i, j = place.i, place.j
    row = 0
    for part in (qkv_ref, out_ref, up_ref, proj_ref):
        for pair in range(part.shape[1] // 256):
            both = [part[:, 256 * pair + 128 * c : 256 * pair + 128 * c + 128] for c in range(2)]
            held[i, j, row : row + 16, :] = jnp.concatenate(both, axis=0).astype(low)
            row += 16
    down_rows = down_ref.shape[0]
    for c in range(2):
        held[i, j, row : row + down_rows, :] = down_ref[:, 128 * c : 128 * c + 128].astype(low)
        row += down_rows
    held[i, j, row : row + 16, :] = small_ref[...].astype(low)
    place.greet()
    sems = (sends, arrivals)
    wide = place.wide

    def share(step, e):
        return held.at[
            lax.rem(i + dp - step, dp), 2 * lax.rem(place.x + wide - e, wide) + place.core
        ]

    def other_core(step, e):
        return held.at[
            lax.rem(i + dp - step, dp), 2 * lax.rem(place.x + wide - e, wide) + 1 - place.core
        ]

    def along(step):
        return remote(held.at[i, j], held.at[i, j], sems, step - 1, place.along(step))

    def across(step, e):
        index = dp - 1 + step * (wide - 1) + e - 1
        return remote(share(step, 0), share(step, 0), sems, index, place.across(e))

    def over(step, e):
        index = dp - 1 + dp * (wide - 1) + step * wide + e
        return remote(share(step, e), share(step, e), sems, index, place.partner())

    for step in range(1, dp):
        along(step).start()
    for e in range(1, wide):
        across(0, e).start()
    over(0, 0).start()

    rows = word_up_ref.shape[0]
    for t in range(3):
        word_share[rows * t : rows * (t + 1), :] = word_qkv_ref[t].astype(low)
    word_share[3 * rows : 4 * rows, :] = word_out_ref[...].astype(low)
    blocks = word_up_ref.shape[1] // 128
    for c in range(blocks):
        spot = slice((4 + c) * rows, (5 + c) * rows)
        word_share[spot, :] = word_up_ref[:, 128 * c : 128 * c + 128].astype(low)
        spot = slice((4 + blocks + c) * rows, (5 + blocks + c) * rows)
        word_share[spot, :] = word_down_ref[:, 128 * c : 128 * c + 128].astype(low)

    for step in range(1, dp):
        along(step).wait_recv()
        for e in range(1, wide):
            across(step, e).start()
        over(step, 0).start()
    for step in range(dp):
        for e in range(1, wide):
            across(step, e).wait_recv()
            over(step, e).start()
    for step in range(dp):
        for e in range(wide):
            over(step, e).wait_recv()
    for step in range(1, dp):
        along(step).wait_send()
    for step in range(dp):
        for e in range(1, wide):
            across(step, e).wait_send()
        for e in range(wide):
            over(step, e).wait_send()

    count = dp * mp
    row = 0
    for target, target_t in (
        (qkv_all, qkv_t_all),
        (out_all, out_t_all),
        (up_all, up_t_all),
        (proj_all, None),
    ):
        for pair in range(target.shape[1] // 256):
            both = held[:, :, row : row + 16, :].reshape(count, 16, 128).astype(jnp.float32)
            row += 16
            for c in range(2):
                piece = both[:, 8 * c : 8 * c + 8].reshape(8 * count, 128).astype(low)
                spot = slice(256 * pair + 128 * c, 256 * pair + 128 * c + 128)
                target[:, spot] = piece
                if target_t is not None:
                    target_t[spot, :] = piece.T
    for c in range(2):
        piece = held[:, :, row : row + down_rows, :].reshape(count * down_rows, 128)
        row += down_rows
        down_all[:, 128 * c : 128 * c + 128] = piece
        down_t_all[128 * c : 128 * c + 128, :] = piece.T
    small_all[...] = held[:, :, row : row + 16, :].reshape(count, 16, 128)


def gather_weights(dp, mp, parts, small, word_parts):
    low = jnp.bfloat16
    qkv, out, up, down, proj = parts
    count = dp * mp
    width = qkv.shape[0] * count
    hidden = up.shape[1]
    model = proj.shape[1]
    rows = (qkv.shape[1] + out.shape[1] + up.shape[1] + proj.shape[1]) // 128 * 8
    rows += 2 * down.shape[0] + 16
    word_rows = sum(part.size for part in word_parts) // 128
    copies = dp - 1 + dp * (mp // 2 - 1) + dp * (mp // 2)
    shapes = (
        (width, 3 * width),
        (3 * width, width),
        (width, width),
        (width, width),
        (width, hidden),
        (hidden, width),
        (hidden, width),
        (width, hidden),
        (width, model),
        (count, 16, 128),
        (word_rows, 128),
    )
    arrays = (qkv, out, up, down, proj, small, *word_parts)
    return pl.pallas_call(
        functools.partial(gather_kernel, dp, mp),
        grid=(1,),
        in_specs=[once(array.shape) for array in arrays],
        out_specs=[once(shape) for shape in shapes],
        out_shape=[jax.ShapeDtypeStruct(shape, low) for shape in shapes],
        scratch_shapes=[
            pltpu.VMEM((dp, mp, rows, 128), low),
            pltpu.SemaphoreType.DMA((copies,)),
            pltpu.SemaphoreType.DMA((copies,)),
        ],
        compiler_params=pltpu.CompilerParams(
            collective_id=0, has_side_effects=True, vmem_limit_bytes=60 * 1024 * 1024
        ),
        name="gather_weights",
    )(*arrays)


def head_rows(rows, masks):
    return jnp.concatenate([rows * masks[h : h + 1] for h in range(CHAR_HEADS)], axis=0)


def gather_diagonal(square, lane_word, chars):
    words = square.shape[1] // chars
    blocks = square.reshape(CHAR_HEADS, words, chars, square.shape[1])
    kept = blocks[:, 0]
    for word in range(1, words):
        kept = jnp.where(lane_word == word, blocks[:, word], kept)
    return kept


def spread_diagonal(kept, word_masks, chars):
    words = kept.shape[2] // chars
    parts = [kept * word_masks[word : word + 1] for word in range(words)]
    return jnp.stack(parts, axis=1)


def norm_strips(values, gain_value, bias_value):
    return strips(lambda strip: apply_norm(strip, gain_value, bias_value), 64, values)


def char_forward_kernel(
    chars,
    chars_ref,
    lane_count_ref,
    qkv_ref,
    out_ref,
    up_ref,
    down_ref,
    ones_ref,
    vecs_ref,
    head_mask_ref,
    word_mask_ref,
    cp_ref,
    probs_ref,
    co_ref,
    y1_ref,
    hidden_ref,
    slope_ref,
    y2_ref,
    pi_ref,
    pooled_ref,
):
    rows, width = chars_ref.shape
    low, wide = jnp.bfloat16, jnp.float32
    lane_word = lax.broadcasted_iota(jnp.int32, (1, 1, GROUP), 2) // chars
    key_slot = lax.broadcasted_iota(jnp.int32, (1, chars, GROUP), 1)
    row_slot = lax.rem(lax.broadcasted_iota(jnp.int32, (GROUP, GROUP), 0), chars)
    masks = head_mask_ref[...]
    word_masks = word_mask_ref[...]
    block = SUB
    parts = up_ref.shape[1] // CHUNK

    def project(s):
        span = slice(s * block, (s + 1) * block)
        states = chars_ref[span, :].astype(wide)
        _, _, normed = norm_strips(states, vecs_ref[0:1, :], vecs_ref[1:2, :])
        cp_ref[span, :] = mm(normed, qkv_ref[...]).astype(low)

    def attend(s):
        spans = [
            slice(row, row + GROUP) for row in range(s * block, (s + 1) * block, GROUP)
        ]
        scores = []
        for span in spans:
            keys = head_rows(cp_ref[span, width : 2 * width], masks)
            square = mm(keys, cp_ref[span, 0:width], NT)
            scores.append(gather_diagonal(square, lane_word, chars))
        probs = []
        for span, score in zip(spans, scores):
            group = span.start // GROUP
            score = score * HEAD ** (-0.5)
            score = jnp.where(key_slot < lane_count_ref[group], score, NEG_FILL)
            powers = jnp.exp(score - jnp.max(score, axis=1, keepdims=True))
            share = 1.0 / jnp.sum(powers, axis=1, keepdims=True)
            probs.append((powers * share).astype(low))
            probs_ref[group] = probs[-1].reshape(CHAR_HEADS * chars, GROUP)
        for span, prob in zip(spans, probs):
            values = head_rows(cp_ref[span, 2 * width : 3 * width], masks)
            spread = spread_diagonal(prob, word_masks, chars)
            spread = spread.reshape(CHAR_HEADS * GROUP, GROUP)
            co_ref[span, :] = mm(spread, values, TN).astype(low)

    def middle(s):
        span = slice(s * block, (s + 1) * block)
        after_attn = chars_ref[span, :].astype(wide) + mm(co_ref[span, :], out_ref[...])
        y1_ref[span, :] = after_attn
        return norm_strips(after_attn, vecs_ref[2:3, :], vecs_ref[3:4, :])[2]

    def pool(s, total):
        query = vecs_ref[4:5, :] * HEAD ** (-0.5)
        high, low_part = strips(lambda strip: split_two(strip * query), 64, total)
        scores = mm(high, ones_ref[...]) + mm(low_part, ones_ref[...])
        pooled = []
        for k in range(block // GROUP):
            group = s * block // GROUP + k
            spot = slice(k * GROUP, (k + 1) * GROUP)
            span = slice(s * block + k * GROUP, s * block + (k + 1) * GROUP)
            counts = jnp.broadcast_to(lane_count_ref[group], (GROUP, GROUP)).T
            valid = row_slot < counts
            halves = []
            for half in range(width // GROUP):
                cols = slice(half * GROUP, (half + 1) * GROUP)
                score = jnp.where(valid, scores[spot, cols], NEG_FILL)
                score = score.reshape(GROUP // chars, chars, GROUP)
                powers = jnp.exp(score - jnp.max(score, axis=1, keepdims=True))
                pi = powers * (1.0 / jnp.sum(powers, axis=1, keepdims=True))
                pi_ref[span, cols] = pi.reshape(GROUP, GROUP).astype(low)
                grid = total[spot, cols].reshape(GROUP // chars, chars, GROUP)
                halves.append(jnp.sum(pi * grid, axis=1))
            pooled.append(jnp.concatenate(halves, axis=1))
        words = block // chars
        pooled_ref[s * words : (s + 1) * words, :] = jnp.concatenate(pooled, axis=0).astype(low)

    count = rows // block
    for s in range(count):
        project(s)
    for s in range(count):
        attend(s)
    normed, totals = {}, {}

    def up(s, part):
        if part == 0:
            normed[s] = middle(s)
        return mm(normed[s], up_ref[:, part * CHUNK : (part + 1) * CHUNK])

    order = [(s, part) for first in range(0, count, 2) for part in range(parts)
             for s in range(first, min(first + 2, count))]
    ahead = up(*order[0])
    for place, (s, part) in enumerate(order):
        current = ahead
        if place + 1 < len(order):
            ahead = up(*order[place + 1])
        span, cols = slice(s * block, (s + 1) * block), slice(part * CHUNK, (part + 1) * CHUNK)
        hidden, slope = gelu_low(current)
        hidden_ref[span, cols] = hidden
        slope_ref[span, cols] = slope
        term = mm(hidden, down_ref[cols, :])
        totals[s] = term if part == 0 else totals[s] + term
        if part == parts - 1:
            totals[s] = totals[s] + y1_ref[span, :]
            y2_ref[span, :] = totals[s]
            pool(s, totals[s])


def char_mlp_back_kernel(
    chars,
    exchange,
    y1_ref,
    y2_ref,
    pi_ref,
    grad_pooled_ref,
    hidden_ref,
    slope_ref,
    up_t_ref,
    down_t_ref,
    vecs_ref,
    ones_ref,
    *others,
):
    rows, width = y1_ref.shape
    words = rows // chars
    if exchange is None:
        grad_y1_ref, grad_up_ref, grad_down_t_ref, grad_vecs_ref = others
    else:
        (
            grad_proj_ref,
            word_small_ref,
            word_terms_ref,
            grad_y1_ref,
            char_terms_ref,
            word_qkv_ref,
            word_out_ref,
            word_up_ref,
            word_down_ref,
            grad_up_ref,
            grad_down_t_ref,
            grad_vecs_ref,
            local_ref,
            local_sem,
            one_ref,
            two_ref,
            three_ref,
            sends,
            arrivals,
        ) = others
        place = Place(*exchange)
        total = ScatterSum(
            place,
            word_terms_ref,
            lambda e, row: local_ref[e, row],
            one_ref,
            two_ref,
            three_ref,
            (sends, arrivals),
        )
        own = [
            pltpu.make_async_copy(
                word_terms_ref.at[2 * e + place.core], local_ref.at[e], local_sem.at[e]
            )
            for e in range(place.wide)
        ]
        step, last = pl.program_id(0), pl.num_programs(0) - 1

        @pl.when(step == 0)
        def _():
            place.greet()
            total.start()
            for copy in own:
                copy.start()

        @pl.when(step == last // 8)
        def _():
            for copy in own:
                copy.wait()
            total.go_across()

        @pl.when(step == last // 2 + 1)
        def _():
            total.go_along()

    @pl.when(pl.program_id(0) == 0)
    def _():
        grad_up_ref[...] = jnp.zeros_like(grad_up_ref)
        grad_down_t_ref[...] = jnp.zeros_like(grad_down_t_ref)
        grad_vecs_ref[...] = jnp.zeros_like(grad_vecs_ref)

    low, wide = jnp.bfloat16, jnp.float32
    block = SUB
    count, parts = rows // block, hidden_ref.shape[1] // CHUNK
    query = vecs_ref[4:5, :]
    per = 64 // chars

    def pool_back(s):
        spots = [
            (slice(row, row + 64), slice(row // chars, row // chars + per))
            for row in range(s * block, (s + 1) * block, 64)
        ]
        split = [
            split_two(
                (y2_ref[span, :].reshape(per, chars, width) * grad_pooled_ref[span_words]).reshape(
                    64, width
                )
            )
            for span, span_words in spots
        ]
        high, rest = (jnp.concatenate(side, axis=0) for side in zip(*split))
        grad_pi = mm(high, ones_ref[...]) + mm(rest, ones_ref[...])
        wide_parts, low_parts, query_sum = [], [], None
        for k, (span, span_words) in enumerate(spots):
            pi = pi_ref[span, :].astype(wide).reshape(per, chars, width)
            part = grad_pi[64 * k : 64 * (k + 1)].reshape(per, chars, width)
            inner = jnp.sum(pi * part, axis=1, keepdims=True)
            grad_scores = pi * (part - inner) * HEAD ** (-0.5)
            grid = y2_ref[span, :].reshape(per, chars, width)
            term = fold_rows((grad_scores * grid).reshape(64, width))
            query_sum = term if query_sum is None else query_sum + term
            grad = (pi * grad_pooled_ref[span_words] + grad_scores * query).reshape(64, width)
            wide_parts.append(grad)
            low_parts.append(grad.astype(low))
        grad_vecs_ref[0] += query_sum
        return jnp.concatenate(wide_parts, axis=0), jnp.concatenate(low_parts, axis=0)

    def norm_again(s):
        span = slice(s * block, (s + 1) * block)
        return norm_strips(y1_ref[span, :], vecs_ref[2:3, :], vecs_ref[3:4, :])

    def feed_back(s, branch):
        span = slice(s * block, (s + 1) * block)
        grads, total = [], None
        ahead = mm(branch, down_t_ref[:, 0:CHUNK])
        for part in range(parts):
            cols = slice(part * CHUNK, (part + 1) * CHUNK)
            current = ahead
            if part + 1 < parts:
                ahead = mm(branch, down_t_ref[:, (part + 1) * CHUNK : (part + 2) * CHUNK])
            (grad_pre,) = strips(
                lambda strip, slope: ((strip * slope.astype(wide)).astype(low),),
                16,
                current,
                slope_ref[span, cols],
            )
            grads.append(grad_pre)
            term = mm(grad_pre, up_t_ref[cols, :])
            total = term if total is None else total + term
        return grads, total

    def norm_finish(s, grad_normed, unit, inverse, grad_y2):
        span = slice(s * block, (s + 1) * block)
        gain = vecs_ref[2:3, :]
        gain_sum, bias_sum = None, None
        for row in range(0, block, 64):
            spot = slice(row, row + 64)
            part, part_unit = grad_normed[spot], unit[spot]
            one, two = fold_rows(part * part_unit), fold_rows(part)
            gain_sum = one if gain_sum is None else gain_sum + one
            bias_sum = two if bias_sum is None else bias_sum + two
            grad_y1_ref[s * block + row : s * block + row + 64, :] = grad_y2[spot] + norm_back(
                part, part_unit, inverse[spot], gain
            )
        grad_vecs_ref[1] += gain_sum
        grad_vecs_ref[2] += bias_sum

    pooled, norms, grads, totals = {}, {}, {}, {}
    pooled[0] = pool_back(0)
    norms[0] = norm_again(0)
    for s in range(count):
        grads[s], totals[s] = feed_back(s, pooled[s][1])
        if s + 1 < count:
            pooled[s + 1] = pool_back(s + 1)
            norms[s + 1] = norm_again(s + 1)
    branch_t = jnp.concatenate([pooled[s][1] for s in range(count)], axis=0).T
    normed_t = jnp.concatenate([norms[s][2] for s in range(count)], axis=0).T
    for part in range(parts):
        cols = slice(part * CHUNK, (part + 1) * CHUNK)
        grad_down_t_ref[:, cols] += mm(branch_t, hidden_ref[:, cols])
        grad_pre = jnp.concatenate([grads[s][part] for s in range(count)], axis=0)
        grad_up_ref[:, cols] += mm(normed_t, grad_pre)
    for s in range(count):
        norm_finish(s, totals[s], norms[s][0], norms[s][1], pooled[s][0])
    if exchange is None:
        return

    @pl.when(step == last)
    def _():
        low = jnp.bfloat16
        share = hidden_ref.shape[1] // (place.dp * place.mp)
        put_pairs(char_terms_ref, 0, grad_up_ref[...])
        row = hidden_ref.shape[1] // 16
        for c in range(2):
            piece = grad_down_t_ref[128 * c : 128 * c + 128, :].T
            piece = piece.reshape(place.dp, place.mp, share, 128).astype(low)
            for j in range(place.mp):
                char_terms_ref[j, :, row : row + share, :] = piece[:, j]
            row += share
        put_pairs(char_terms_ref, row, grad_proj_ref[...])
        row += grad_proj_ref.shape[1] // 16
        sums = [jnp.sum(grad_vecs_ref[k], axis=0, keepdims=True) for k in range(3)]
        small_row = lax.broadcasted_iota(jnp.int32, (16, 128), 0)
        for b in range(word_small_ref.shape[0]):
            piece = word_small_ref[b]
            if b < 2:
                for k in range(3):
                    piece = jnp.where(
                        small_row == 12 + k, sums[k][:, 128 * b : 128 * b + 128], piece
                    )
            piece = jnp.broadcast_to(piece.astype(low), (place.dp, 16, 128))
            for j in range(place.mp):
                char_terms_ref[j, :, row : row + 16, :] = piece
            row += 16
        result = total.finish()
        block = word_up_ref.shape[0]
        for t in range(3):
            word_qkv_ref[t] = result(slice(block * t, block * (t + 1)))
        word_out_ref[...] = result(slice(3 * block, 4 * block))
        count = word_up_ref.shape[1] // 128
        for c in range(count):
            cols = slice(128 * c, 128 * c + 128)
            word_up_ref[:, cols] = result(slice((4 + c) * block, (5 + c) * block))
            spot = slice((4 + count + c) * block, (5 + count + c) * block)
            word_down_ref[:, cols] = result(spot)


def char_attn_back_kernel(
    chars,
    exchange,
    chars_ref,
    cp_ref,
    probs_ref,
    co_ref,
    grad_y1_ref,
    qkv_t_ref,
    out_t_ref,
    vecs_ref,
    head_mask_ref,
    word_mask_ref,
    *others,
):
    rows, width = chars_ref.shape
    if exchange is None:
        (
            grad_chars_ref,
            grad_qkv_ref,
            grad_out_ref,
            grad_vecs_ref,
            grad_cp_ref,
            grad_co_ref,
        ) = others
    else:
        (
            early_terms_ref,
            grad_chars_ref,
            share_qkv_ref,
            share_out_ref,
            share_up_ref,
            share_down_ref,
            share_proj_ref,
            share_small_ref,
            share_vecs_ref,
            grad_cp_ref,
            grad_co_ref,
            grad_qkv_ref,
            grad_out_ref,
            grad_vecs_ref,
            local_ref,
            local_sem,
            late_terms_ref,
        ) = others[:17]
        early_refs, late_refs = others[17:22], others[22:27]
        place = Place(*exchange)
        early = ScatterSum(
            place,
            early_terms_ref,
            lambda e, row: local_ref[e, row],
            *early_refs[:3],
            early_refs[3:],
        )
        late = ScatterSum(
            place,
            late_terms_ref,
            lambda e, row: late_terms_ref[2 * e + place.core, row],
            *late_refs[:3],
            late_refs[3:],
        )
        own = [
            pltpu.make_async_copy(
                early_terms_ref.at[2 * e + place.core], local_ref.at[e], local_sem.at[e]
            )
            for e in range(place.wide)
        ]
        step, last = pl.program_id(0), pl.num_programs(0) - 1

        @pl.when(step == 0)
        def _():
            place.greet()
            early.start()
            for copy in own:
                copy.start()

        @pl.when(step == last // 8)
        def _():
            for copy in own:
                copy.wait()
            early.go_across()

        @pl.when(step == last // 2 + 1)
        def _():
            early.go_along()

    @pl.when(pl.program_id(0) == 0)
    def _():
        grad_qkv_ref[...] = jnp.zeros_like(grad_qkv_ref)
        grad_out_ref[...] = jnp.zeros_like(grad_out_ref)
        grad_vecs_ref[...] = jnp.zeros_like(grad_vecs_ref)

    low, wide = jnp.bfloat16, jnp.float32
    lane_word = lax.broadcasted_iota(jnp.int32, (1, 1, GROUP), 2) // chars
    masks = head_mask_ref[...]
    word_masks = word_mask_ref[...]
    scale = HEAD ** (-0.5)
    block = SUB
    count = rows // block

    def out_back(s):
        span = slice(s * block, (s + 1) * block)
        branch = grad_y1_ref[span, :].astype(low)
        grad_co_ref[span, :] = mm(branch, out_t_ref[...]).astype(low)
        return branch

    def norm_again(s):
        span = slice(s * block, (s + 1) * block)
        return norm_strips(
            chars_ref[span, :].astype(wide), vecs_ref[0:1, :], vecs_ref[1:2, :]
        )

    def side_by_side(spread):
        return jnp.concatenate([spread[h] for h in range(CHAR_HEADS)], axis=1)

    def attend_back(s):
        spans = [
            slice(row, row + GROUP) for row in range(s * block, (s + 1) * block, GROUP)
        ]
        grad_probs = []
        for span in spans:
            values = head_rows(cp_ref[span, 2 * width : 3 * width], masks)
            square = mm(values, grad_co_ref[span, :], NT)
            grad_probs.append(gather_diagonal(square, lane_word, chars))
        grad_scores = []
        for span, part in zip(spans, grad_probs):
            probs = probs_ref[span.start // GROUP].reshape(CHAR_HEADS, chars, GROUP)
            spread = spread_diagonal(probs, word_masks, chars)
            spread = spread.reshape(CHAR_HEADS, GROUP, GROUP)
            grad_values = mm(side_by_side(spread), head_rows(grad_co_ref[span, :], masks))
            grad_cp_ref[span, 2 * width : 3 * width] = grad_values.astype(low)
            probs = probs.astype(wide)
            inner = jnp.sum(part * probs, axis=1, keepdims=True)
            grad_scores.append((probs * (part - inner)).astype(low))
        for span, part in zip(spans, grad_scores):
            spread = spread_diagonal(part, word_masks, chars)
            spread = spread.reshape(CHAR_HEADS, GROUP, GROUP)
            queries = head_rows(cp_ref[span, 0:width], masks)
            grad_keys = mm(side_by_side(spread), queries) * scale
            grad_cp_ref[span, width : 2 * width] = grad_keys.astype(low)
            keys = head_rows(cp_ref[span, width : 2 * width], masks)
            grad_queries = mm(spread.reshape(CHAR_HEADS * GROUP, GROUP), keys, TN) * scale
            grad_cp_ref[span, 0:width] = grad_queries.astype(low)

    def project_back(s):
        span = slice(s * block, (s + 1) * block)
        return mm(grad_cp_ref[span, :], qkv_t_ref[...])

    def norm_finish(s, grad_normed, unit, inverse):
        gain = vecs_ref[0:1, :]
        gain_sum, bias_sum = None, None
        for row in range(0, block, 64):
            spot, span = slice(row, row + 64), slice(s * block + row, s * block + row + 64)
            part, part_unit = grad_normed[spot], unit[spot]
            one, two = fold_rows(part * part_unit), fold_rows(part)
            gain_sum = one if gain_sum is None else gain_sum + one
            bias_sum = two if bias_sum is None else bias_sum + two
            grad = grad_y1_ref[span, :] + norm_back(part, part_unit, inverse[spot], gain)
            grad_chars_ref[span, :] = grad.astype(low)
        grad_vecs_ref[0] += gain_sum
        grad_vecs_ref[1] += bias_sum

    branches = [out_back(s) for s in range(count)]
    norms, totals = {}, {}
    for s in range(count):
        attend_back(s)
        norms[s] = norm_again(s)
        totals[s] = project_back(s)
    grad_out_ref[...] += mm(co_ref[...].T, jnp.concatenate(branches, axis=0))
    normed_t = jnp.concatenate([norms[s][2] for s in range(count)], axis=0).T
    grad_qkv_ref[...] += mm(normed_t, grad_cp_ref[...])
    for s in range(count):
        norm_finish(s, totals[s], norms[s][0], norms[s][1])
    if exchange is None:
        return

    @pl.when(step == last)
    def _():
        low = jnp.bfloat16
        put_pairs(late_terms_ref, 0, grad_qkv_ref[...])
        row = 3 * width // 16
        put_pairs(late_terms_ref, row, grad_out_ref[...])
        row += width // 16
        sums = [jnp.sum(grad_vecs_ref[k], axis=0, keepdims=True) for k in range(2)]
        small_row = lax.broadcasted_iota(jnp.int32, (16, 128), 0)
        piece = jnp.zeros((16, 128), jnp.float32)
        for k in range(2):
            for b in range(2):
                piece = jnp.where(
                    small_row == 2 * k + b, sums[k][:, 128 * b : 128 * b + 128], piece
                )
        piece = jnp.broadcast_to(piece.astype(low), (place.dp, 16, 128))
        for j in range(place.mp):
            late_terms_ref[j, :, row : row + 16, :] = piece
        late.start()
        result = early.finish()
        row = 0
        for target, share in (
            (share_up_ref, 8),
            (share_down_ref, share_down_ref.shape[0]),
            (share_proj_ref, 8),
            (share_small_ref, 16),
        ):
            for c in range(target.shape[1] // 128):
                target[:, 128 * c : 128 * c + 128] = result(slice(row, row + share))
                row += share
        late.go_across()
        late.go_along()
        result = late.finish()
        row = 0
        for target in (share_qkv_ref, share_out_ref):
            for c in range(target.shape[1] // 128):
                target[:, 128 * c : 128 * c + 128] = result(slice(row, row + 8))
                row += 8
        share_vecs_ref[...] = result(slice(row, row + 16))


def whole(shape):
    return pl.BlockSpec(shape, lambda step: (0,) * len(shape))


def once(shape):
    return pl.BlockSpec(shape, lambda step: (0,) * len(shape), pipeline_mode=pl.Buffered(1))


def blocked(shape):
    return pl.BlockSpec(shape, lambda step: (step,) + (0,) * (len(shape) - 1))


def params(megabytes):
    return pltpu.CompilerParams(
        dimension_semantics=("arbitrary",), vmem_limit_bytes=megabytes * 1024 * 1024
    )


def block_rows(rows, wanted):
    while rows % wanted:
        wanted //= 2
    return wanted


def char_forward(states, lane_counts, weights, chars):
    rows, width = states.shape
    qkv, out, up, down, ones, vecs, head_masks, word_masks = weights
    block = block_rows(rows, 1024)
    words, groups = block // chars, block // GROUP
    low, wide = jnp.bfloat16, jnp.float32
    shapes = (
        ((rows, 3 * width), low),
        ((rows // GROUP, CHAR_HEADS * chars, GROUP), low),
        ((rows, width), low),
        ((rows, width), wide),
        ((rows, up.shape[1]), low),
        ((rows, up.shape[1]), low),
        ((rows, width), wide),
        ((rows, width), low),
        ((rows // chars, width), low),
    )
    blocks = (
        (block, 3 * width),
        (groups, CHAR_HEADS * chars, GROUP),
        (block, width),
        (block, width),
        (block, up.shape[1]),
        (block, up.shape[1]),
        (block, width),
        (block, width),
        (words, width),
    )
    flops = 2 * rows * width * (4 * width + 2 * up.shape[1] + 8 * width)
    return pl.pallas_call(
        functools.partial(char_forward_kernel, chars),
        grid=(rows // block,),
        in_specs=[
            blocked((block, width)),
            blocked((groups, 1, GROUP)),
            whole(qkv.shape),
            whole(out.shape),
            whole(up.shape),
            whole(down.shape),
            whole(ones.shape),
            whole(vecs.shape),
            whole(head_masks.shape),
            whole(word_masks.shape),
        ],
        out_specs=[blocked(shape) for shape in blocks],
        out_shape=[jax.ShapeDtypeStruct(shape, kind) for shape, kind in shapes],
        compiler_params=params(56),
        cost_estimate=pl.CostEstimate(
            flops=flops, bytes_accessed=rows * width * 36, transcendentals=rows * width * 5
        ),
        name="char_forward",
    )(states, lane_counts, qkv, out, up, down, ones, vecs, head_masks, word_masks)


def char_mlp_back(y1, y2, pi, grad_pooled, hidden, slope, weights, chars):
    rows, width = y1.shape
    up_t, down_t, vecs, ones = weights
    block = block_rows(rows, 1024)
    hidden_width = hidden.shape[1]
    wide = jnp.float32
    flops = 2 * rows * width * (4 * hidden_width + 2 * width)
    return pl.pallas_call(
        functools.partial(char_mlp_back_kernel, chars, None),
        grid=(rows // block,),
        in_specs=[
            blocked((block, width)),
            blocked((block, width)),
            blocked((block, width)),
            blocked((block // chars, 1, width)),
            blocked((block, hidden_width)),
            blocked((block, hidden_width)),
            whole(up_t.shape),
            whole(down_t.shape),
            whole(vecs.shape),
            whole(ones.shape),
        ],
        out_specs=[
            blocked((block, width)),
            whole((width, hidden_width)),
            whole((width, hidden_width)),
            whole((3, 8, width)),
        ],
        out_shape=[
            jax.ShapeDtypeStruct((rows, width), wide),
            jax.ShapeDtypeStruct((width, hidden_width), wide),
            jax.ShapeDtypeStruct((width, hidden_width), wide),
            jax.ShapeDtypeStruct((3, 8, width), wide),
        ],
        compiler_params=params(56),
        cost_estimate=pl.CostEstimate(
            flops=flops, bytes_accessed=rows * width * 30, transcendentals=0
        ),
        name="char_mlp_back",
    )(y1, y2, pi, grad_pooled, hidden, slope, up_t, down_t, vecs, ones)


def char_attn_back(states, cp, probs, co, grad_y1, weights, chars):
    rows, width = states.shape
    qkv_t, out_t, vecs, head_masks, word_masks = weights
    block = block_rows(rows, 1024)
    low, wide = jnp.bfloat16, jnp.float32
    flops = 2 * rows * width * 18 * width
    return pl.pallas_call(
        functools.partial(char_attn_back_kernel, chars, None),
        grid=(rows // block,),
        in_specs=[
            blocked((block, width)),
            blocked((block, 3 * width)),
            blocked((block // GROUP, CHAR_HEADS * chars, GROUP)),
            blocked((block, width)),
            blocked((block, width)),
            whole(qkv_t.shape),
            whole(out_t.shape),
            whole(vecs.shape),
            whole(head_masks.shape),
            whole(word_masks.shape),
        ],
        out_specs=[
            blocked((block, width)),
            whole((width, 3 * width)),
            whole((width, width)),
            whole((2, 8, width)),
        ],
        out_shape=[
            jax.ShapeDtypeStruct((rows, width), low),
            jax.ShapeDtypeStruct((width, 3 * width), wide),
            jax.ShapeDtypeStruct((width, width), wide),
            jax.ShapeDtypeStruct((2, 8, width), wide),
        ],
        scratch_shapes=[
            pltpu.VMEM((block, 3 * width), low),
            pltpu.VMEM((block, width), low),
        ],
        compiler_params=params(56),
        cost_estimate=pl.CostEstimate(
            flops=flops, bytes_accessed=rows * width * 18, transcendentals=0
        ),
        name="char_attn_back",
    )(states, cp, probs, co, grad_y1, qkv_t, out_t, vecs, head_masks, word_masks)


def char_mlp_back_exchange(
    y1, y2, pi, grad_pooled, hidden, slope, weights, chars, mesh_size, grad_proj, word_small, word_terms
):
    rows, width = y1.shape
    up_t, down_t, vecs, ones = weights
    dp, mp = mesh_size
    block = block_rows(rows, 1024)
    hidden_width = hidden.shape[1]
    low, wide = jnp.bfloat16, jnp.float32
    model = grad_proj.shape[1]
    flops = 2 * rows * width * (4 * hidden_width + 2 * width)
    char_rows = 2 * hidden_width // 16 + model // 16 + 16 * word_small.shape[0]
    n = word_terms.shape[2]
    share = model // dp
    outs = (
        ((rows, width), wide, blocked((block, width))),
        ((mp, dp, char_rows, 128), low, None),
        ((3, share, 128), wide, None),
        ((share, 128), wide, None),
        ((share, model), wide, None),
        ((share, model), wide, None),
    )
    return pl.pallas_call(
        functools.partial(char_mlp_back_kernel, chars, mesh_size),
        grid=(rows // block,),
        in_specs=[
            blocked((block, width)),
            blocked((block, width)),
            blocked((block, width)),
            blocked((block // chars, 1, width)),
            blocked((block, hidden_width)),
            blocked((block, hidden_width)),
            whole(up_t.shape),
            whole(down_t.shape),
            whole(vecs.shape),
            whole(ones.shape),
            whole(grad_proj.shape),
            whole(word_small.shape),
            pl.BlockSpec(memory_space=pl.ANY),
        ],
        out_specs=[spec or whole(shape) for shape, _, spec in outs],
        out_shape=[jax.ShapeDtypeStruct(shape, kind) for shape, kind, _ in outs],
        scratch_shapes=[
            pltpu.VMEM((width, hidden_width), wide),
            pltpu.VMEM((width, hidden_width), wide),
            pltpu.VMEM((3, 8, width), wide),
            pltpu.VMEM((mp // 2, dp, n, 128), low),
            pltpu.SemaphoreType.DMA((mp // 2,)),
        ]
        + scatter_scratch(dp, mp, n),
        compiler_params=pltpu.CompilerParams(
            dimension_semantics=("arbitrary",),
            vmem_limit_bytes=60 * 1024 * 1024,
            collective_id=1,
            has_side_effects=True,
        ),
        cost_estimate=pl.CostEstimate(
            flops=flops, bytes_accessed=rows * width * 30, transcendentals=0
        ),
        name="char_mlp_back",
    )(
        y1, y2, pi, grad_pooled, hidden, slope, up_t, down_t, vecs, ones,
        grad_proj, word_small, word_terms,
    )


def char_attn_back_exchange(
    states, cp, probs, co, grad_y1, weights, chars, mesh_size, early_terms, hidden_width, model
):
    rows, width = states.shape
    qkv_t, out_t, vecs, head_masks, word_masks = weights
    dp, mp = mesh_size
    count = dp * mp
    block = block_rows(rows, 1024)
    low, wide = jnp.bfloat16, jnp.float32
    flops = 2 * rows * width * 18 * width
    n = early_terms.shape[2]
    late = 4 * width // 16 + 16
    outs = (
        ((rows, width), low, blocked((block, width))),
        ((width // count, 3 * width), wide, None),
        ((width // count, width), wide, None),
        ((width // count, hidden_width), wide, None),
        ((hidden_width // count, width), wide, None),
        ((width // count, model), wide, None),
        ((16, model), wide, None),
        ((16, 128), wide, None),
    )
    return pl.pallas_call(
        functools.partial(char_attn_back_kernel, chars, mesh_size),
        grid=(rows // block,),
        in_specs=[
            blocked((block, width)),
            blocked((block, 3 * width)),
            blocked((block // GROUP, CHAR_HEADS * chars, GROUP)),
            blocked((block, width)),
            blocked((block, width)),
            whole(qkv_t.shape),
            whole(out_t.shape),
            whole(vecs.shape),
            whole(head_masks.shape),
            whole(word_masks.shape),
            pl.BlockSpec(memory_space=pl.ANY),
        ],
        out_specs=[spec or whole(shape) for shape, _, spec in outs],
        out_shape=[jax.ShapeDtypeStruct(shape, kind) for shape, kind, _ in outs],
        scratch_shapes=[
            pltpu.VMEM((block, 3 * width), low),
            pltpu.VMEM((block, width), low),
            pltpu.VMEM((width, 3 * width), wide),
            pltpu.VMEM((width, width), wide),
            pltpu.VMEM((2, 8, width), wide),
            pltpu.VMEM((mp // 2, dp, n, 128), low),
            pltpu.SemaphoreType.DMA((mp // 2,)),
            pltpu.VMEM((mp, dp, late, 128), low),
        ]
        + scatter_scratch(dp, mp, n)
        + scatter_scratch(dp, mp, late),
        compiler_params=pltpu.CompilerParams(
            dimension_semantics=("arbitrary",),
            vmem_limit_bytes=56 * 1024 * 1024,
            collective_id=2,
            has_side_effects=True,
        ),
        cost_estimate=pl.CostEstimate(
            flops=flops, bytes_accessed=rows * width * 18, transcendentals=0
        ),
        name="char_attn_back",
    )(states, cp, probs, co, grad_y1, qkv_t, out_t, vecs, head_masks, word_masks, early_terms)


def word_kernel(
    pooled_ref,
    words_ref,
    cotangent_ref,
    language_ref,
    language_hot_ref,
    proj_ref,
    weights_ref,
    norms_ref,
    head_mask_ref,
    layer_ref,
    grad_words_ref,
    terms_ref,
    grad_proj_ref,
    grad_pooled_ref,
    small_ref,
    residual_ref,
    normed_one_ref,
    packed_ref,
    probs_ref,
    mixed_ref,
    middle_ref,
    normed_two_ref,
    hidden_ref,
    slope_ref,
    grad_middle_ref,
    branch_ref,
    grad_mixed_ref,
    grad_keys_ref,
    grad_values_ref,
    sums_ref,
):
    low, wide = jnp.bfloat16, jnp.float32
    length, model = words_ref.shape
    dp, mp = weights_ref.shape[:2]
    share = model // dp
    row_block = 256
    blocks = length // row_block
    hidden_width = hidden_ref.shape[1]
    up_blocks = hidden_width // mp // 128
    scale = HEAD ** (-0.5)
    up_base, down_base = 4 * share, (4 + up_blocks) * share

    def weight(base, first, last):
        pieces = [
            weights_ref[:, j, base + c * share : base + (c + 1) * share, :].reshape(model, 128)
            for j, c in (column(base, block) for block in range(first, last))
        ]
        return jnp.concatenate(pieces, axis=1)

    def column(base, block):
        return (block, 0) if base < up_base else (block // up_blocks, block % up_blocks)

    def put(base, first, grad):
        for k in range(grad.shape[1] // 128):
            j, c = column(base, first + k)
            piece = grad[:, 128 * k : 128 * k + 128].reshape(dp, share, 128).astype(low)
            terms_ref[j, :, base + c * share : base + (c + 1) * share, :] = piece

    def norm(k):
        return norms_ref[k : k + 1, :]

    sums_ref[...] = jnp.zeros_like(sums_ref)

    @pl.loop(0, blocks)
    def _(block):
        span = pl.ds(pl.multiple_of(block * row_block, row_block), row_block)
        residual = words_ref[span, :].astype(wide) + mm(pooled_ref[span, :], proj_ref[...])
        residual = residual + language_ref[...]
        residual_ref[span, :] = residual
        _, _, normed = apply_norm(residual, norm(0), norm(1))
        normed_one_ref[span, :] = normed
        for t in range(3):
            for c in range(0, model // 128, 2):
                cols = slice(128 * c, 128 * c + 256)
                packed_ref[t, span, cols] = mm(normed, weight(t * share, c, c + 2)).astype(low)

    causal = lax.broadcasted_iota(jnp.int32, (row_block, row_block), 0) <= (
        lax.broadcasted_iota(jnp.int32, (row_block, row_block), 1)
    )

    @pl.loop(0, model // 128)
    def _(pair):
        lanes = pl.ds(pl.multiple_of(pair * 128, 128), 128)
        values_t = packed_ref[2, :, lanes].T
        for block in range(blocks):
            stop = (block + 1) * row_block
            span = slice(block * row_block, stop)
            first = block * (block + 1) // 2 * row_block
            queries = packed_ref[0, span, lanes]
            mixed = []
            for h in range(2):
                keys = packed_ref[1, 0:stop, lanes] * head_mask_ref[h : h + 1, 0:128]
                scores = mm(keys, queries, NT) * scale
                near = jnp.where(causal, scores[stop - row_block :], NEG_FILL)
                scores = jnp.concatenate([scores[: stop - row_block], near]) if block else near
                powers = jnp.exp(scores - jnp.max(scores, axis=0, keepdims=True))
                probs = powers * (1.0 / jnp.sum(powers, axis=0, keepdims=True))
                probs = probs.astype(low)
                probs_ref[2 * pair + h, first : first + stop, :] = probs
                mixed.append(mm(values_t[HEAD * h : HEAD * (h + 1), 0:stop], probs))
            mixed_ref[span, lanes] = jnp.concatenate(mixed, axis=0).T.astype(low)

    @pl.loop(0, blocks)
    def _(block):
        span = pl.ds(pl.multiple_of(block * row_block, row_block), row_block)
        out_t = weight(3 * share, 0, model // 128)
        middle = residual_ref[span, :] + mm(mixed_ref[span, :], out_t, NT)
        middle_ref[span, :] = middle
        _, _, normed = apply_norm(middle, norm(2), norm(3))
        normed_two_ref[span, :] = normed
        total = middle
        for c in range(0, hidden_width // 128, 4):
            cols = slice(128 * c, 128 * c + 512)
            hidden, slope = gelu_low(mm(normed, weight(up_base, c, c + 4)))
            hidden_ref[span, cols] = hidden
            slope_ref[span, cols] = slope
            total = total + mm(hidden, weight(down_base, c, c + 4), NT)
        layer_ref[span, :] = total.astype(low)

    cotangent_t = cotangent_ref[...].T
    for c in range(0, hidden_width // 128, 2):
        put(down_base, c, mm(cotangent_t, hidden_ref[:, 128 * c : 128 * c + 256]))

    @pl.loop(0, blocks)
    def _(block):
        span = pl.ds(pl.multiple_of(block * row_block, row_block), row_block)
        cotangent = cotangent_ref[span, :]
        grad_normed = None
        for c in range(0, hidden_width // 128, 4):
            cols = slice(128 * c, 128 * c + 512)
            grad_pre = mm(cotangent, weight(down_base, c, c + 4))
            grad_pre = (grad_pre * slope_ref[span, cols].astype(wide)).astype(low)
            slope_ref[span, cols] = grad_pre
            term = mm(grad_pre, weight(up_base, c, c + 4), NT)
            grad_normed = term if grad_normed is None else grad_normed + term
        unit, inverse = standardize(middle_ref[span, :])
        sums_ref[2] += fold_rows(grad_normed * unit)
        sums_ref[3] += fold_rows(grad_normed)
        grad_middle = cotangent.astype(wide) + norm_back(grad_normed, unit, inverse, norm(2))
        grad_middle_ref[span, :] = grad_middle
        branch = grad_middle.astype(low)
        branch_ref[span, :] = branch
        out_t = weight(3 * share, 0, model // 128)
        grad_mixed_ref[span, :] = mm(branch, out_t).astype(low)

    normed_t = normed_two_ref[...].T
    for c in range(0, hidden_width // 128, 2):
        put(up_base, c, mm(normed_t, slope_ref[:, 128 * c : 128 * c + 256]))
    branch_t = branch_ref[...].T
    for c in range(0, model // 128, 2):
        put(3 * share, c, mm(branch_t, mixed_ref[:, 128 * c : 128 * c + 256]))

    @pl.loop(0, model // 128)
    def _(pair):
        lanes = pl.ds(pl.multiple_of(pair * 128, 128), 128)
        grad_keys_ref[...] = jnp.zeros_like(grad_keys_ref)
        grad_values_ref[...] = jnp.zeros_like(grad_values_ref)
        keys_t = packed_ref[1, :, lanes].T
        for block in range(blocks):
            stop = (block + 1) * row_block
            span = slice(block * row_block, stop)
            first = block * (block + 1) // 2 * row_block
            queries = packed_ref[0, span, lanes]
            grad_mixed = grad_mixed_ref[span, lanes]
            grad_queries = []
            for h in range(2):
                mask = head_mask_ref[h : h + 1, 0:128]
                values = packed_ref[2, 0:stop, lanes] * mask
                grad_probs = mm(values, grad_mixed, NT)
                probs = probs_ref[2 * pair + h, first : first + stop, :]
                probs_wide = probs.astype(wide)
                inner = jnp.sum(grad_probs * probs_wide, axis=0, keepdims=True)
                grad_scores = (probs_wide * (grad_probs - inner)).astype(low)
                grad_values_ref[0:stop, :] += mm(probs, grad_mixed * mask)
                grad_keys_ref[0:stop, :] += mm(grad_scores, queries * mask)
                grad_queries.append(mm(keys_t[HEAD * h : HEAD * (h + 1), 0:stop], grad_scores))
            grad_queries = jnp.concatenate(grad_queries, axis=0) * scale
            packed_ref[0, span, lanes] = grad_queries.T.astype(low)
        packed_ref[1, :, lanes] = (grad_keys_ref[...] * scale).astype(low)
        packed_ref[2, :, lanes] = grad_values_ref[...].astype(low)

    normed_t = normed_one_ref[...].T
    for t in range(3):
        for c in range(0, model // 128, 2):
            put(t * share, c, mm(normed_t, packed_ref[t, :, 128 * c : 128 * c + 256]))

    @pl.loop(0, blocks)
    def _(block):
        span = pl.ds(pl.multiple_of(block * row_block, row_block), row_block)
        grad_normed = None
        for t in range(3):
            term = mm(packed_ref[t, span, :], weight(t * share, 0, model // 128), NT)
            grad_normed = term if grad_normed is None else grad_normed + term
        unit, inverse = standardize(residual_ref[span, :])
        sums_ref[0] += fold_rows(grad_normed * unit)
        sums_ref[1] += fold_rows(grad_normed)
        grad = grad_middle_ref[span, :] + norm_back(grad_normed, unit, inverse, norm(0))
        sums_ref[4] += fold_rows(grad)
        grad = grad.astype(low)
        grad_words_ref[span, :] = grad
        grad_pooled_ref[span] = mm(grad, proj_ref[...], NT)[:, None, :]

    grad_proj_ref[...] = mm(pooled_ref[...].T, grad_words_ref[...])

    sums = [jnp.sum(sums_ref[k], axis=0, keepdims=True) for k in range(5)]
    small_row = lax.broadcasted_iota(jnp.int32, (8, 128), 0)
    for b in range(model // 128):
        cols = slice(128 * b, 128 * b + 128)
        small_ref[b, 0:8, :] = language_hot_ref[...] * sums[4][:, cols]
        piece = jnp.zeros((8, 128), wide)
        for k in range(4):
            piece = jnp.where(small_row == k, sums[k][:, cols], piece)
        small_ref[b, 8:16, :] = piece


def word_layer_kernel(pooled, words, cotangent, language_row, language_hot, proj, weights, norms, head_masks):
    low, wide = jnp.bfloat16, jnp.float32
    length, model = words.shape
    width = pooled.shape[1]
    dp, mp, n = weights.shape[:3]
    hidden_width = (n * dp // model - 4) // 2 * 128 * mp
    blocks = length // 256
    heads = model // HEAD
    arrays = (pooled, words, cotangent, language_row, language_hot, proj, weights, norms, head_masks)
    outs = (
        ((length, model), low),
        ((length, model), low),
        ((mp, dp, n, 128), low),
        ((width, model), wide),
        ((length, 1, width), wide),
        ((model // 128, 16, 128), wide),
    )
    return pl.pallas_call(
        word_kernel,
        grid=(1,),
        in_specs=[once(array.shape) for array in arrays],
        out_specs=[once(shape) for shape, _ in outs],
        out_shape=[jax.ShapeDtypeStruct(shape, kind) for shape, kind in outs],
        scratch_shapes=[
            pltpu.VMEM((length, model), wide),
            pltpu.VMEM((length, model), low),
            pltpu.VMEM((3, length, model), low),
            pltpu.VMEM((heads, blocks * (blocks + 1) // 2 * 256, 256), low),
            pltpu.VMEM((length, model), low),
            pltpu.VMEM((length, model), wide),
            pltpu.VMEM((length, model), low),
            pltpu.VMEM((length, hidden_width), low),
            pltpu.VMEM((length, hidden_width), low),
            pltpu.VMEM((length, model), wide),
            pltpu.VMEM((length, model), low),
            pltpu.VMEM((length, model), low),
            pltpu.VMEM((length, 128), wide),
            pltpu.VMEM((length, 128), wide),
            pltpu.VMEM((5, 8, model), wide),
        ],
        compiler_params=pltpu.CompilerParams(vmem_limit_bytes=62 * 1024 * 1024),
        cost_estimate=pl.CostEstimate(
            flops=40 * 10**9, bytes_accessed=20 * 2**20, transcendentals=10**7
        ),
        name="word_layer",
    )(*arrays)


def attend_forward(queries, key_block, values, allowed):
    scores = low_sum("bqhd,bkhd->bhqk", queries, key_block) * HEAD ** (-0.5)
    scores = jnp.where(allowed, scores, NEG_FILL)
    row_max = jnp.max(scores, axis=-1, keepdims=True)
    powers = jnp.exp(scores - row_max)
    row_total = jnp.sum(powers, axis=-1, keepdims=True)
    attn_probs = (powers / row_total).astype(jnp.bfloat16)
    attn_mixed = low_sum("bhqk,bkhd->bqhd", attn_probs, values).astype(jnp.bfloat16)
    return (attn_mixed, row_max + jnp.log(row_total))


def attend_backward(queries, key_block, values, allowed, log_total, grad_mixed):
    scale = HEAD ** (-0.5)
    scores = low_sum("bqhd,bkhd->bhqk", queries, key_block) * scale
    attn_probs = jnp.where(allowed, jnp.exp(scores - log_total), 0.0)
    grad_probs = low_sum("bqhd,bkhd->bhqk", grad_mixed, values)
    grad_values = low_sum("bhqk,bqhd->bkhd", attn_probs.astype(jnp.bfloat16), grad_mixed)
    inner_sum = jnp.sum(grad_probs * attn_probs, axis=-1, keepdims=True)
    grad_scores = (attn_probs * (grad_probs - inner_sum)).astype(jnp.bfloat16)
    grad_queries = low_sum("bhqk,bkhd->bqhd", grad_scores, key_block) * scale
    grad_keys = low_sum("bhqk,bqhd->bkhd", grad_scores, queries) * scale
    return (grad_queries, grad_keys, grad_values)


def word_layer(residual, grad_rows, weights, norms, mp_size, mp_index):
    qkv, out_t, up, down_t = weights
    gain_one, bias_one, gain_two, bias_two = norms
    rows, width = residual.shape
    low = jnp.bfloat16
    sequences, length = max(1, rows // LEN), min(rows, LEN)
    share = LEN // length
    groups = [[a * share + b for b in range(share)] for a in range(mp_size // share)]
    unit_one, inverse_one, normed_one = apply_norm(residual, gain_one, bias_one)
    packed = low_sum("rd,tdc->trc", normed_one, qkv).astype(low)
    packed = packed.reshape(3, sequences, length, width // HEAD, HEAD)
    keys = packed[1:]
    start = 0
    if share > 1:
        keys = lax.all_gather(keys, "mp", axis=2, tiled=True, axis_index_groups=groups)
        start = lax.rem(mp_index, share) * length
    allowed = (
        lax.broadcasted_iota(jnp.int32, (length, LEN), 1)
        <= lax.broadcasted_iota(jnp.int32, (length, LEN), 0) + start
    )[None, None]
    mixed, log_total = attend_forward(packed[0], keys[0], keys[1], allowed)
    mixed_rows = mixed.reshape(rows, width)
    middle = residual + mm(mixed_rows, out_t, NT)
    unit_two, inverse_two, normed_two = apply_norm(middle, gain_two, bias_two)
    hidden, slope = gelu_pair(matmul(normed_two, up))
    hidden = hidden.astype(low)
    layer_output = (middle + mm(hidden, down_t, NT)).astype(low)
    grad_wide = grad_rows.astype(jnp.float32)
    grad_down_t = mm(grad_rows, hidden, TN)
    grad_pre = (matmul(grad_rows, down_t) * slope).astype(low)
    grad_up = mm(normed_two, grad_pre, TN)
    grad_normed = mm(grad_pre, up, NT)
    grad_gain_two = jnp.sum(grad_normed * unit_two, axis=0)
    grad_bias_two = jnp.sum(grad_normed, axis=0)
    grad_middle = grad_wide + norm_back(grad_normed, unit_two, inverse_two, gain_two)
    branch = grad_middle.astype(low)
    grad_out_t = mm(branch, mixed_rows, TN)
    grad_mixed = matmul(branch, out_t).astype(low).reshape(sequences, length, -1, HEAD)
    grad_queries, grad_keys, grad_values = attend_backward(
        packed[0], keys[0], keys[1], allowed, log_total, grad_mixed
    )
    grad_keys = jnp.stack((grad_keys, grad_values), axis=0)
    if share > 1:
        grad_keys = lax.psum_scatter(
            grad_keys, "mp", scatter_dimension=2, tiled=True, axis_index_groups=groups
        )
    grad_packed = jnp.concatenate((grad_queries[None], grad_keys), axis=0)
    grad_packed = grad_packed.reshape(3, rows, width).astype(low)
    grad_qkv = low_sum("rd,trc->tdc", normed_one, grad_packed)
    grad_normed = low_sum("trc,tdc->rd", grad_packed, qkv)
    grad_gain_one = jnp.sum(grad_normed * unit_one, axis=0)
    grad_bias_one = jnp.sum(grad_normed, axis=0)
    grad_residual = grad_middle + norm_back(grad_normed, unit_one, inverse_one, gain_one)
    return (
        layer_output,
        grad_residual,
        (grad_qkv, grad_out_t, grad_up, grad_down_t),
        (grad_gain_one, grad_bias_one, grad_gain_two, grad_bias_two),
    )


def mask_constants(width, chars):
    head, word = np.arange(width) // HEAD, np.arange(GROUP) // chars
    head_masks = head[None] == np.arange(8)[:, None]
    word_masks = word[None] == np.arange(GROUP // chars)[:, None]
    ones = head[:, None] == head[None]
    return tuple(jnp.asarray(mask.astype(ml_dtypes.bfloat16)) for mask in (head_masks, word_masks, ones))


def blocks_of(array, count):
    return array.reshape(count, -1)


def shards_general(
    char_states,
    word_states,
    char_counts,
    language_group,
    output_grad,
    char_norm_gain,
    char_norm_bias,
    char_qkv,
    char_out,
    char_mlp_gain,
    char_mlp_bias,
    char_up,
    char_down,
    pool_query,
    char_proj,
    language_table,
    word_norm_gain,
    word_norm_bias,
    word_qkv,
    word_out,
    word_mlp_gain,
    word_mlp_bias,
    word_up,
    word_down,
):
    low, wide = jnp.bfloat16, jnp.float32
    dp_size, mp_size = lax.axis_size("dp"), lax.axis_size("mp")
    mp_index = lax.axis_index("mp")
    devices = dp_size * mp_size
    word_count, chars, width = char_states.shape
    model = word_states.shape[1]
    langs = language_table.shape[0]

    char_parts = (
        char_qkv,
        char_out,
        char_up,
        char_down,
        char_proj,
        char_norm_gain,
        char_norm_bias,
        char_mlp_gain,
        char_mlp_bias,
        pool_query,
        word_norm_gain,
        word_norm_bias,
        word_mlp_gain,
        word_mlp_bias,
        language_table.T,
    )
    flat = jnp.concatenate([part.astype(low).reshape(-1) for part in char_parts])
    flat_size = flat.shape[0]
    flat = jnp.pad(flat, (0, -flat_size % 2048))
    full = lax.all_gather(flat, BOTH, axis=0, tiled=False)
    unpacked, start = [], 0
    for part in char_parts:
        stop = start + part.size
        piece = full[:, start:stop].reshape((devices * part.shape[0],) + part.shape[1:])
        unpacked.append(piece)
        start = stop
    (
        qkv_char,
        out_char,
        up_char,
        down_char,
        proj_char,
        gain_attn,
        bias_attn,
        gain_mlp,
        bias_mlp,
        query_pool,
        gain_one,
        bias_one,
        gain_two,
        bias_two,
        table_t,
    ) = unpacked

    word_parts = (word_qkv, word_out.T, word_up, word_down.T)
    word_flat = jnp.concatenate([part.astype(low).reshape(-1, 128) for part in word_parts])
    word_full = lax.all_gather(word_flat, BOTH, axis=0, tiled=False)
    word_full = word_full.reshape(dp_size, mp_size, word_flat.shape[0], 128)
    word_weights, start = [], 0
    for part in word_parts:
        stop = start + part.size // 128
        piece = word_full[:, :, start:stop].reshape((dp_size, mp_size) + part.shape)
        if part.ndim == 3:
            piece = piece.transpose(2, 0, 3, 1, 4).reshape(3, model, model)
        else:
            piece = piece.transpose(0, 2, 1, 3)
            piece = piece.reshape(dp_size * part.shape[0], mp_size * part.shape[1])
        word_weights.append(piece)
        start = stop

    rows = word_count * chars
    states = char_states.reshape(rows, width)
    lane_counts = jnp.repeat(char_counts, chars).reshape(rows // GROUP, 1, GROUP)
    head_masks, word_masks, ones = mask_constants(width, chars)
    zero = jnp.zeros_like(gain_attn)
    vecs = jnp.stack(
        (gain_attn, bias_attn, gain_mlp, bias_mlp, query_pool, zero, zero, zero)
    ).astype(wide)
    cp, probs, co, y1, hidden, slope, y2, pi, pooled = char_forward(
        states,
        lane_counts,
        (qkv_char, out_char, up_char, down_char, ones, vecs, head_masks, word_masks),
        chars,
    )

    sequences = max(1, word_count // LEN)
    first = (mp_index * word_count) // LEN
    language = lax.dynamic_slice_in_dim(language_group, first, sequences)
    language_hot = (language[:, None] == jnp.arange(langs)[None]).astype(wide)
    language_rows = jnp.sum(language_hot[:, :, None] * table_t.T.astype(wide)[None], axis=1)
    residual = word_states.astype(wide) + matmul(pooled, proj_char)
    residual = (
        residual.reshape(sequences, -1, model) + language_rows[:, None, :]
    ).reshape(word_count, model)
    norms = tuple(value.astype(wide) for value in (gain_one, bias_one, gain_two, bias_two))
    layer_output, grad_residual, word_grads, word_norm_grads = word_layer(
        residual, output_grad, word_weights, norms, mp_size, mp_index
    )
    grad_words = grad_residual.astype(low)
    sequence_grads = jnp.sum(grad_residual.reshape(sequences, -1, model), axis=1)
    grad_table = jnp.sum(language_hot[:, :, None] * sequence_grads[:, None, :], axis=0)

    pieces = []
    for part, grad in zip(word_parts, word_grads):
        if part.ndim == 3:
            grad = grad.reshape(3, dp_size, part.shape[1], mp_size, part.shape[2])
            grad = grad.transpose(3, 1, 0, 2, 4)
        else:
            grad = grad.reshape(dp_size, part.shape[0], mp_size, part.shape[1])
            grad = grad.transpose(2, 0, 1, 3)
        pieces.append(grad.astype(low).reshape(mp_size, dp_size, -1, 128))
    word_terms = jnp.concatenate(pieces, axis=2)
    word_terms = lax.psum_scatter(word_terms, "mp", scatter_dimension=0, tiled=True)
    word_terms = lax.psum_scatter(word_terms[0], "dp", scatter_dimension=0, tiled=True)[0]
    word_shares, start = [], 0
    for part in word_parts:
        stop = start + part.size // 128
        word_shares.append(word_terms[start:stop].reshape(part.shape).astype(wide))
        start = stop

    grad_proj = mm(pooled, grad_words, TN)
    grad_pooled = mm(grad_words, proj_char, NT).reshape(word_count, 1, width)
    grad_y1, grad_up, grad_down_t, mlp_vecs = char_mlp_back(
        y1, y2, pi, grad_pooled, hidden, slope, (up_char.T, down_char.T, vecs, ones), chars
    )
    mlp_vecs = jnp.sum(mlp_vecs, axis=1)
    early = (
        grad_up,
        grad_down_t.T,
        grad_proj,
        mlp_vecs[0],
        mlp_vecs[1],
        mlp_vecs[2],
        word_norm_grads[0],
        word_norm_grads[1],
        word_norm_grads[2],
        word_norm_grads[3],
        grad_table.T,
    )
    early_terms = jnp.concatenate([blocks_of(part, devices) for part in early], axis=1)
    early_size = early_terms.shape[1]
    early_terms = jnp.pad(early_terms, ((0, 0), (0, -early_size % 1024)))
    early_terms = lax.psum_scatter(early_terms, BOTH, scatter_dimension=0, tiled=True)[0]
    grad_chars, grad_qkv, grad_out, attn_vecs = char_attn_back(
        states, cp, probs, co, grad_y1, (qkv_char.T, out_char.T, vecs, head_masks, word_masks), chars
    )
    attn_vecs = jnp.sum(attn_vecs, axis=1)
    late = (grad_qkv, grad_out, attn_vecs[0], attn_vecs[1])
    late_terms = jnp.concatenate([blocks_of(part, devices) for part in late], axis=1)
    late_terms = jnp.pad(late_terms, ((0, 0), (0, -late_terms.shape[1] % 1024)))
    late_terms = lax.psum_scatter(late_terms, BOTH, scatter_dimension=0, tiled=True)[0]

    def take(terms, parts):
        shares, start = [], 0
        for part in parts:
            stop = start + part.size // devices
            shape = (part.shape[0] // devices,) + part.shape[1:]
            shares.append(terms[start:stop].reshape(shape))
            start = stop
        return shares

    (
        g_up,
        g_down,
        g_proj,
        g_query,
        g_gain_mlp,
        g_bias_mlp,
        g_gain_one,
        g_bias_one,
        g_gain_two,
        g_bias_two,
        g_table_t,
    ) = take(early_terms, early)
    g_qkv, g_out, g_gain_attn, g_bias_attn = take(late_terms, late)
    return (
        layer_output,
        grad_chars.reshape(char_states.shape),
        grad_words,
        g_gain_attn,
        g_bias_attn,
        g_qkv,
        g_out,
        g_gain_mlp,
        g_bias_mlp,
        g_up,
        g_down,
        g_query,
        g_proj,
        g_table_t.T,
        g_gain_one,
        g_bias_one,
        word_shares[0],
        word_shares[1].T,
        g_gain_two,
        g_bias_two,
        word_shares[2],
        word_shares[3].T,
    )


def fits(dp, mp, words, model, width, chars, hidden_width, langs):
    count = dp * mp
    return (
        words == LEN
        and mp % 2 == 0
        and model == 128 * mp
        and model // dp % 16 == 0
        and width == 256
        and width == 8 * count
        and hidden_width % (16 * count) == 0
        and GROUP % chars == 0
        and langs == 8
    )


def shards(*arrays):
    char_states, word_states = arrays[:2]
    dp, mp = lax.axis_size("dp"), lax.axis_size("mp")
    words, chars, width = char_states.shape
    model, hidden_width = word_states.shape[1], arrays[11].shape[1]
    if not fits(dp, mp, words, model, width, chars, hidden_width, arrays[15].shape[0]):
        return shards_general(*arrays)
    return shards_whole(*arrays)


def shards_whole(
    char_states,
    word_states,
    char_counts,
    language_group,
    output_grad,
    char_norm_gain,
    char_norm_bias,
    char_qkv,
    char_out,
    char_mlp_gain,
    char_mlp_bias,
    char_up,
    char_down,
    pool_query,
    char_proj,
    language_table,
    word_norm_gain,
    word_norm_bias,
    word_qkv,
    word_out,
    word_mlp_gain,
    word_mlp_bias,
    word_up,
    word_down,
):
    low, wide = jnp.bfloat16, jnp.float32
    dp, mp = lax.axis_size("dp"), lax.axis_size("mp")
    count = dp * mp
    index = lax.axis_index("dp") * mp + lax.axis_index("mp")
    words, chars, width = char_states.shape
    model = word_states.shape[1]
    langs = language_table.shape[0]
    hidden_width = char_up.shape[1]
    char_small = (char_norm_gain, char_norm_bias, char_mlp_gain, char_mlp_bias, pool_query)
    word_small = (word_norm_gain, word_norm_bias, word_mlp_gain, word_mlp_bias)
    small = jnp.concatenate(char_small + word_small + (language_table.reshape(-1),))
    small = jnp.pad(small, (0, 16 * 128 - small.shape[0])).reshape(16, 128)
    (
        qkv,
        qkv_t,
        out,
        out_t,
        up,
        up_t,
        down,
        down_t,
        proj,
        small_all,
        word_share,
    ) = gather_weights(
        dp,
        mp,
        (char_qkv, char_out, char_up, char_down, char_proj),
        small,
        (word_qkv, word_out.T, word_up, word_down.T),
    )
    word_weights = lax.all_gather(word_share, BOTH, axis=0, tiled=False)
    word_weights = word_weights.reshape(dp, mp, word_share.shape[0], 128)
    char_share, word_part = width // count, model // count
    first, second = 5 * char_share, 5 * char_share + 4 * word_part
    flat = small_all.reshape(count, -1).astype(wide)
    vecs = flat[:, :first].reshape(count, 5, char_share).transpose(1, 0, 2).reshape(5, width)
    norms = flat[:, first:second].reshape(count, 4, word_part).transpose(1, 0, 2)
    norms = norms.reshape(4, model)
    table = flat[:, second : second + langs * word_part].reshape(count, langs, word_part)
    table = table.transpose(1, 0, 2).reshape(langs, model)
    vecs = jnp.pad(vecs, ((0, 3), (0, 0)))

    rows = words * chars
    states = char_states.reshape(rows, width)
    lane_counts = jnp.repeat(char_counts, chars).reshape(rows // GROUP, 1, GROUP)
    head_masks, word_masks, ones = mask_constants(width, chars)
    cp, probs, co, y1, hidden, slope, y2, pi, pooled = char_forward(
        states,
        lane_counts,
        (qkv, out, up, down, ones, vecs, head_masks, word_masks),
        chars,
    )

    language = lax.dynamic_slice_in_dim(language_group, lax.axis_index("mp"), 1)
    hot = (language == jnp.arange(langs)).astype(wide)[:, None]
    language_row = jnp.sum(hot * table, axis=0, keepdims=True)
    layer_output, grad_words, word_terms, grad_proj, grad_pooled, small_terms = word_layer_kernel(
        pooled,
        word_states,
        output_grad,
        language_row,
        jnp.broadcast_to(hot, (langs, 128)),
        proj,
        word_weights,
        norms,
        head_masks,
    )

    grad_y1, char_terms, g_word_qkv, g_word_out, g_word_up, g_word_down = char_mlp_back_exchange(
        y1, y2, pi, grad_pooled, hidden, slope, (up_t, down_t, vecs, ones), chars, (dp, mp),
        grad_proj, small_terms, word_terms,
    )
    grad_chars, g_qkv, g_out, g_up, g_down, g_proj, g_small, g_vecs = char_attn_back_exchange(
        states, cp, probs, co, grad_y1, (qkv_t, out_t, vecs, head_masks, word_masks), chars,
        (dp, mp), char_terms, hidden_width, model,
    )
    word_small = lax.dynamic_slice_in_dim(g_small[:12], index * word_part, word_part, 1)
    char_small = lax.dynamic_slice_in_dim(g_small[12:15, :width], index * char_share, char_share, 1)
    late_small = lax.dynamic_slice_in_dim(
        g_vecs[:4].reshape(2, width), index * char_share, char_share, 1
    )
    return (
        layer_output,
        grad_chars.reshape(char_states.shape),
        grad_words,
        late_small[0],
        late_small[1],
        g_qkv,
        g_out,
        char_small[1],
        char_small[2],
        g_up,
        g_down,
        char_small[0],
        g_proj,
        word_small[:langs],
        word_small[8],
        word_small[9],
        g_word_qkv,
        g_word_out.T,
        word_small[10],
        word_small[11],
        g_word_up,
        g_word_down.T,
    )


def solution(mesh):
    vector, rows = P(BOTH), P(BOTH, None)
    cube = P(BOTH, None, None)
    table = P(None, BOTH)
    words = (P(None, "dp", "mp"), P("mp", "dp"), P("dp", "mp"), P("mp", "dp"))
    char_weights = (
        vector, vector, rows, rows, vector, vector, rows, rows, vector, rows, table,
    )
    weights = char_weights + (
        vector, vector, words[0], words[1], vector, vector, words[2], words[3],
    )
    return jax.shard_map(
        shards,
        mesh=mesh,
        in_specs=(cube, rows, vector, P("dp"), rows) + weights,
        out_specs=(rows, cube, rows) + weights,
        check_vma=False,
    )
```

```python
import functools

import jax
import jax.numpy as jnp
import ml_dtypes
import numpy as np
from jax import lax
from jax.experimental import pallas as pl
from jax.experimental.pallas import tpu as pltpu
from jax.sharding import PartitionSpec as P

HEAD = 64
CHAR_HEADS = 4
LEN = 1024
GROUP = 128
SUB = 512
CHUNK = 512
WORD_PARTS = 4


NORM_EPS = 1e-05
NEG_FILL = -1000000000.0
BOTH = ("dp", "mp")
MESH = pl.DeviceIdType.MESH

LOGIT = (
    0.7978697123195114,
    0.036392286136226214,
    -8.782649734580825e-05,
    -3.669345726473906e-05,
    1.4250064727244771e-06,
)

EXP2_SCALE = HEAD ** (-0.5) * 1.4426950408889634
NN = (((1,), (0,)), ((), ()))
NT = (((1,), (1,)), ((), ()))
TN = (((0,), (0,)), ((), ()))


def mm(first_arg, second_arg, dims=NN):
    return lax.dot_general(first_arg, second_arg, dims, preferred_element_type=jnp.float32)


def matmul(first_arg, second_arg):
    return jnp.dot(first_arg, second_arg, preferred_element_type=jnp.float32)


def low_sum(pattern, first_arg, second_arg):
    return jnp.einsum(pattern, first_arg, second_arg, preferred_element_type=jnp.float32)


def standardize(values):
    centred = values - jnp.mean(values, axis=-1, keepdims=True)
    inverse = lax.rsqrt(jnp.mean(centred * centred, axis=-1, keepdims=True) + NORM_EPS)
    return (centred * inverse, inverse)


def apply_norm(values, gain_value, bias_value):
    unit_rows, inverse = standardize(values)
    normed = (unit_rows * gain_value + bias_value).astype(jnp.bfloat16)
    return (unit_rows, inverse, normed)


def norm_back(grad_out, unit_rows, inverse, gain_value):
    grad_unit = grad_out * gain_value
    inner_sum = jnp.mean(grad_unit * unit_rows, axis=-1, keepdims=True)
    return inverse * (
        grad_unit - jnp.mean(grad_unit, axis=-1, keepdims=True) - unit_rows * inner_sum
    )


def gelu_pair(values):
    square = values * values
    logit = square * LOGIT[4] + LOGIT[3]
    for term in LOGIT[2::-1]:
        logit = logit * square + term
    normal = jnp.tanh(logit * values) * 0.5 + 0.5
    density = jnp.exp2(square * -0.7213475204444817 - 1.3257480647361593)
    return (values * normal, values * density + normal)


def strips(function, size, *arrays):
    parts = [
        function(*(array[row : row + size] for array in arrays))
        for row in range(0, arrays[0].shape[0], size)
    ]
    return tuple(jnp.concatenate(part, axis=0) for part in zip(*parts))


def gelu_low(values):
    return strips(
        lambda strip: tuple(part.astype(jnp.bfloat16) for part in gelu_pair(strip)),
        32 * 256 // values.shape[1],
        values,
    )


def split_two(values):
    high = values.astype(jnp.bfloat16)
    return (high, (values - high.astype(jnp.float32)).astype(jnp.bfloat16))


def fold_rows(values):
    return jnp.sum(values.reshape(values.shape[0] // 8, 8, values.shape[1]), axis=0)


class Place:
    def __init__(self, dp, mp):
        self.dp, self.mp, self.wide = dp, mp, mp // 2
        self.i, self.j = lax.axis_index("dp"), lax.axis_index("mp")
        self.x, self.core = self.j // 2, lax.rem(self.j, 2)

    def partner(self):
        return (self.i, 2 * self.x + 1 - self.core)

    def across(self, step):
        return (self.i, 2 * lax.rem(self.x + step, self.wide) + self.core)

    def along(self, step):
        return (lax.rem(self.i + step, self.dp), self.j)

    def greet(self):
        barrier = pltpu.get_barrier_semaphore()
        others = [self.partner()]
        others += [self.across(step) for step in range(1, self.wide)]
        others += [self.along(step) for step in range(1, self.dp)]
        for other in others:
            pl.semaphore_signal(barrier, inc=1, device_id=other, device_id_type=MESH)
        pl.semaphore_wait(barrier, len(others))


def remote(source, target, sems, index, device):
    return pltpu.make_async_remote_copy(
        src_ref=source,
        dst_ref=target,
        send_sem=sems[0].at[index],
        recv_sem=sems[1].at[index],
        device_id=device,
        device_id_type=MESH,
    )


class ScatterSum:
    def __init__(self, place, blocks, local, one, two, three, sems, part=0, parts=1):
        self.place, self.blocks, self.local = place, blocks, local
        self.one, self.two, self.three, self.sems = one, two, three, sems
        size = blocks.shape[2] // parts
        self.span = slice(part * size, (part + 1) * size)
        self.sem = part * copies_of(place.dp, place.mp)

    def first(self):
        place = self.place
        return [
            remote(
                self.blocks.at[2 * e + 1 - place.core, :, self.span],
                self.one.at[e, :, self.span],
                self.sems,
                self.sem + e,
                place.partner(),
            )
            for e in range(place.wide)
        ]

    def second(self):
        place = self.place
        return [
            remote(
                self.one.at[lax.rem(place.x + step, place.wide), :, self.span],
                self.two.at[step - 1, :, self.span],
                self.sems,
                self.sem + place.wide + step - 1,
                place.across(step),
            )
            for step in range(1, place.wide)
        ]

    def third(self):
        place = self.place
        return [
            remote(
                self.one.at[place.x, lax.rem(place.i + step, place.dp), self.span],
                self.three.at[step - 1, self.span],
                self.sems,
                self.sem + 2 * place.wide - 1 + step - 1,
                place.along(step),
            )
            for step in range(1, place.dp)
        ]

    def start(self):
        for copy in self.first():
            copy.start()

    def go_across(self):
        place, span = self.place, self.span
        for copy in self.first():
            copy.wait()

        @pl.loop(0, place.dp)
        def _(row):
            for e in range(place.wide):
                own = self.local(e, row, span).astype(jnp.float32)
                total = self.one[e, row, span].astype(jnp.float32) + own
                self.one[e, row, span] = total.astype(jnp.bfloat16)

        for copy in self.second():
            copy.start()

    def go_along(self):
        place, span = self.place, self.span
        for copy in self.second():
            copy.wait()

        @pl.loop(0, place.dp)
        def _(row):
            total = self.one[place.x, row, span].astype(jnp.float32)
            for step in range(1, place.wide):
                total = total + self.two[step - 1, row, span].astype(jnp.float32)
            self.one[place.x, row, span] = total.astype(jnp.bfloat16)

        for copy in self.third():
            copy.start()

    def finish(self):
        place = self.place
        for copy in self.third():
            copy.wait()

        def own(rows):
            total = self.one[place.x, place.i, rows].astype(jnp.float32)
            for step in range(1, place.dp):
                total = total + self.three[step - 1, rows].astype(jnp.float32)
            return total

        return own


def copies_of(dp, mp):
    return 2 * (mp // 2) - 1 + dp - 1


def scatter_scratch(dp, mp, n, parts=1):
    wide = mp // 2
    copies = copies_of(dp, mp) * parts
    return [
        pltpu.VMEM((wide, dp, n, 128), jnp.bfloat16),
        pltpu.VMEM((max(1, wide - 1), dp, n, 128), jnp.bfloat16),
        pltpu.VMEM((dp - 1, n, 128), jnp.bfloat16),
        pltpu.SemaphoreType.DMA((copies,)),
        pltpu.SemaphoreType.DMA((copies,)),
    ]


def put_pairs(target, first_row, columns):
    mp, dp = target.shape[0], target.shape[1]
    rows = columns.shape[0] // (mp * dp)
    for pair in range(columns.shape[1] // 256):
        both = [
            columns[:, 256 * pair + 128 * c : 256 * pair + 128 * c + 128].reshape(
                dp, mp, rows, 128
            )
            for c in range(2)
        ]
        both = jnp.concatenate(both, axis=2).astype(jnp.bfloat16)
        spot = slice(first_row + 2 * rows * pair, first_row + 2 * rows * (pair + 1))
        for j in range(mp):
            target[j, :, spot, :] = both[:, j]


def gather_kernel(
    dp,
    mp,
    qkv_ref,
    out_ref,
    up_ref,
    down_ref,
    proj_ref,
    small_ref,
    word_qkv_ref,
    word_out_ref,
    word_up_ref,
    word_down_ref,
    qkv_all,
    qkv_t_all,
    out_all,
    out_t_all,
    up_all,
    up_t_all,
    down_all,
    down_t_all,
    proj_all,
    small_all,
    word_share,
    held,
    sends,
    arrivals,
):
    place = Place(dp, mp)
    low = jnp.bfloat16
    i, j = place.i, place.j
    row = 0
    for part in (qkv_ref, out_ref, up_ref, proj_ref):
        for pair in range(part.shape[1] // 256):
            both = [part[:, 256 * pair + 128 * c : 256 * pair + 128 * c + 128] for c in range(2)]
            held[i, j, row : row + 16, :] = jnp.concatenate(both, axis=0).astype(low)
            row += 16
    down_rows = down_ref.shape[0]
    for c in range(2):
        held[i, j, row : row + down_rows, :] = down_ref[:, 128 * c : 128 * c + 128].astype(low)
        row += down_rows
    held[i, j, row : row + 16, :] = small_ref[...].astype(low)
    place.greet()
    sems = (sends, arrivals)
    wide = place.wide

    def share(step, e):
        return held.at[
            lax.rem(i + dp - step, dp), 2 * lax.rem(place.x + wide - e, wide) + place.core
        ]

    def other_core(step, e):
        return held.at[
            lax.rem(i + dp - step, dp), 2 * lax.rem(place.x + wide - e, wide) + 1 - place.core
        ]

    def along(step):
        return remote(held.at[i, j], held.at[i, j], sems, step - 1, place.along(step))

    def across(step, e):
        index = dp - 1 + step * (wide - 1) + e - 1
        return remote(share(step, 0), share(step, 0), sems, index, place.across(e))

    def over(step, e):
        index = dp - 1 + dp * (wide - 1) + step * wide + e
        return remote(share(step, e), share(step, e), sems, index, place.partner())

    for step in range(1, dp):
        along(step).start()
    for e in range(1, wide):
        across(0, e).start()
    over(0, 0).start()

    rows = word_up_ref.shape[0]
    for t in range(3):
        word_share[rows * t : rows * (t + 1), :] = word_qkv_ref[t].astype(low)
    word_share[3 * rows : 4 * rows, :] = word_out_ref[...].astype(low)
    blocks = word_up_ref.shape[1] // 128
    for c in range(blocks):
        spot = slice((4 + c) * rows, (5 + c) * rows)
        word_share[spot, :] = word_up_ref[:, 128 * c : 128 * c + 128].astype(low)
        spot = slice((4 + blocks + c) * rows, (5 + blocks + c) * rows)
        word_share[spot, :] = word_down_ref[:, 128 * c : 128 * c + 128].astype(low)

    for step in range(1, dp):
        along(step).wait_recv()
        for e in range(1, wide):
            across(step, e).start()
        over(step, 0).start()
    for step in range(dp):
        for e in range(1, wide):
            across(step, e).wait_recv()
            over(step, e).start()
    for step in range(dp):
        for e in range(wide):
            over(step, e).wait_recv()
    for step in range(1, dp):
        along(step).wait_send()
    for step in range(dp):
        for e in range(1, wide):
            across(step, e).wait_send()
        for e in range(wide):
            over(step, e).wait_send()

    count = dp * mp
    row = 0
    for target, target_t in (
        (qkv_all, qkv_t_all),
        (out_all, out_t_all),
        (up_all, up_t_all),
        (proj_all, None),
    ):
        for pair in range(target.shape[1] // 256):
            both = held[:, :, row : row + 16, :].reshape(count, 16, 128).astype(jnp.float32)
            row += 16
            for c in range(2):
                piece = both[:, 8 * c : 8 * c + 8].reshape(8 * count, 128).astype(low)
                spot = slice(256 * pair + 128 * c, 256 * pair + 128 * c + 128)
                target[:, spot] = piece
                if target_t is not None:
                    target_t[spot, :] = piece.T
    for c in range(2):
        piece = held[:, :, row : row + down_rows, :].reshape(count * down_rows, 128)
        row += down_rows
        down_all[:, 128 * c : 128 * c + 128] = piece
        down_t_all[128 * c : 128 * c + 128, :] = piece.T
    small_all[...] = held[:, :, row : row + 16, :].reshape(count, 16, 128)


def gather_weights(dp, mp, parts, small, word_parts):
    low = jnp.bfloat16
    qkv, out, up, down, proj = parts
    count = dp * mp
    width = qkv.shape[0] * count
    hidden = up.shape[1]
    model = proj.shape[1]
    rows = (qkv.shape[1] + out.shape[1] + up.shape[1] + proj.shape[1]) // 128 * 8
    rows += 2 * down.shape[0] + 16
    word_rows = sum(part.size for part in word_parts) // 128
    copies = dp - 1 + dp * (mp // 2 - 1) + dp * (mp // 2)
    shapes = (
        (width, 3 * width),
        (3 * width, width),
        (width, width),
        (width, width),
        (width, hidden),
        (hidden, width),
        (hidden, width),
        (width, hidden),
        (width, model),
        (count, 16, 128),
        (word_rows, 128),
    )
    arrays = (qkv, out, up, down, proj, small, *word_parts)
    return pl.pallas_call(
        functools.partial(gather_kernel, dp, mp),
        grid=(1,),
        in_specs=[once(array.shape) for array in arrays],
        out_specs=[once(shape) for shape in shapes],
        out_shape=[jax.ShapeDtypeStruct(shape, low) for shape in shapes],
        scratch_shapes=[
            pltpu.VMEM((dp, mp, rows, 128), low),
            pltpu.SemaphoreType.DMA((copies,)),
            pltpu.SemaphoreType.DMA((copies,)),
        ],
        compiler_params=pltpu.CompilerParams(
            collective_id=0, has_side_effects=True, vmem_limit_bytes=60 * 1024 * 1024
        ),
        name="gather_weights",
    )(*arrays)


def head_rows(rows, masks):
    return jnp.concatenate([rows * masks[h : h + 1] for h in range(CHAR_HEADS)], axis=0)


def gather_diagonal(square, lane_word, chars):
    words = square.shape[1] // chars
    blocks = square.reshape(CHAR_HEADS, words, chars, square.shape[1])
    kept = blocks[:, 0]
    for word in range(1, words):
        kept = jnp.where(lane_word == word, blocks[:, word], kept)
    return kept


def spread_diagonal(kept, word_masks, chars):
    words = kept.shape[2] // chars
    parts = [kept * word_masks[word : word + 1] for word in range(words)]
    return jnp.stack(parts, axis=1)


def norm_strips(values, gain_value, bias_value):
    return strips(lambda strip: apply_norm(strip, gain_value, bias_value), 64, values)


def char_forward_kernel(
    chars,
    chars_ref,
    count_ref,
    qkv_ref,
    out_ref,
    up_ref,
    down_ref,
    ones_ref,
    vecs_ref,
    head_mask_ref,
    word_mask_ref,
    cp_ref,
    probs_ref,
    co_ref,
    y1_ref,
    hidden_ref,
    slope_ref,
    y2_ref,
    pi_ref,
    pooled_ref,
):
    rows, width = chars_ref.shape
    low, wide = jnp.bfloat16, jnp.float32
    lane_word = lax.broadcasted_iota(jnp.int32, (1, 1, GROUP), 2) // chars
    key_slot = lax.broadcasted_iota(jnp.int32, (1, chars, GROUP), 1).astype(wide)
    lane_counts = mm(count_ref[...].astype(wide).astype(low), word_mask_ref[...])
    row_slot = lax.rem(lax.broadcasted_iota(jnp.int32, (GROUP, GROUP), 0), chars).astype(wide)
    masks = head_mask_ref[...]
    word_masks = word_mask_ref[...]
    block = SUB
    parts = up_ref.shape[1] // CHUNK

    def project(s):
        span = slice(s * block, (s + 1) * block)
        states = chars_ref[span, :].astype(wide)
        _, _, normed = norm_strips(states, vecs_ref[0:1, :], vecs_ref[1:2, :])
        cp_ref[span, :] = mm(normed, qkv_ref[...]).astype(low)

    def groups_of(s):
        return [slice(row, row + GROUP) for row in range(s * block, (s + 1) * block, GROUP)]

    scores, probs = {}, {}

    def attend_scores(s):
        scores[s] = []
        for span in groups_of(s):
            keys = head_rows(cp_ref[span, width : 2 * width], masks)
            square = mm(keys, cp_ref[span, 0:width], NT)
            scores[s].append(gather_diagonal(square, lane_word, chars))

    def attend_probs(s):
        probs[s] = []
        for span, score in zip(groups_of(s), scores[s]):
            group = span.start // GROUP
            score = jnp.where(
                key_slot < lane_counts[group : group + 1], score * EXP2_SCALE, NEG_FILL
            )
            powers = jnp.exp2(score - jnp.max(score, axis=1, keepdims=True))
            share = 1.0 / jnp.sum(powers, axis=1, keepdims=True)
            probs[s].append((powers * share).astype(low))
            probs_ref[group] = probs[s][-1].reshape(CHAR_HEADS * chars, GROUP)

    def attend_values(s):
        for span, prob in zip(groups_of(s), probs[s]):
            values = head_rows(cp_ref[span, 2 * width : 3 * width], masks)
            spread = spread_diagonal(prob, word_masks, chars)
            spread = spread.reshape(CHAR_HEADS * GROUP, GROUP)
            co_ref[span, :] = mm(spread, values, TN).astype(low)

    def middle(s):
        span = slice(s * block, (s + 1) * block)
        after_attn = chars_ref[span, :].astype(wide) + mm(co_ref[span, :], out_ref[...])
        y1_ref[span, :] = after_attn
        return norm_strips(after_attn, vecs_ref[2:3, :], vecs_ref[3:4, :])[2]

    def pool_scores(s):
        query = vecs_ref[4:5, :] * EXP2_SCALE
        high, low_part = strips(lambda strip: split_two(strip * query), 64, totals[s])
        return mm(high, ones_ref[...]) + mm(low_part, ones_ref[...])

    def pool(s, scores):
        total = totals[s]
        pooled = []
        for k in range(block // GROUP):
            group = s * block // GROUP + k
            spot = slice(k * GROUP, (k + 1) * GROUP)
            span = slice(s * block + k * GROUP, s * block + (k + 1) * GROUP)
            counts = jnp.broadcast_to(lane_counts[group : group + 1], (GROUP, GROUP)).T
            valid = row_slot < counts
            halves = []
            for half in range(width // GROUP):
                cols = slice(half * GROUP, (half + 1) * GROUP)
                score = jnp.where(valid, scores[spot, cols], NEG_FILL)
                score = score.reshape(GROUP // chars, chars, GROUP)
                powers = jnp.exp2(score - jnp.max(score, axis=1, keepdims=True))
                pi = powers * (1.0 / jnp.sum(powers, axis=1, keepdims=True))
                pi_ref[span, cols] = pi.reshape(GROUP, GROUP).astype(low)
                grid = total[spot, cols].reshape(GROUP // chars, chars, GROUP)
                halves.append(jnp.sum(pi * grid, axis=1))
            pooled.append(jnp.concatenate(halves, axis=1))
        words = block // chars
        pooled_ref[s * words : (s + 1) * words, :] = jnp.concatenate(pooled, axis=0).astype(low)

    count = rows // block
    normed, totals, hiddens = {}, {}, {}

    def up(s, part):
        if part == 0:
            normed[s] = middle(s)
        return mm(normed[s], up_ref[:, part * CHUNK : (part + 1) * CHUNK])

    def activate(s, part, current):
        span, cols = slice(s * block, (s + 1) * block), slice(part * CHUNK, (part + 1) * CHUNK)
        hidden, slope = gelu_low(current)
        hidden_ref[span, cols] = hidden
        slope_ref[span, cols] = slope
        hiddens[s] = hidden

    def down(s, part):
        span, cols = slice(s * block, (s + 1) * block), slice(part * CHUNK, (part + 1) * CHUNK)
        term = mm(hiddens[s], down_ref[cols, :])
        totals[s] = term if part == 0 else totals[s] + term
        if part == parts - 1:
            totals[s] = totals[s] + y1_ref[span, :]
            y2_ref[span, :] = totals[s]

    for first in range(0, count, 2):
        pair = range(first, min(first + 2, count))
        for s in pair:
            project(s)
            attend_scores(s)
        for s in pair:
            attend_probs(s)
            attend_values(s)
        order = [(s, part) for part in range(parts) for s in pair]
        ahead = [up(*order[0])]
        pools = []
        for place, (s, part) in enumerate(order):
            if place + 1 < len(order):
                ahead.append(up(*order[place + 1]))
            activate(s, part, ahead[place])
            down(s, part)
            if part == parts - 1:
                pools.append((s, pool_scores(s)))
                if len(pools) > 1:
                    pool(*pools[-2])
        pool(*pools[-1])


def char_mlp_back_kernel(
    chars,
    exchange,
    y1_ref,
    y2_ref,
    pi_ref,
    grad_pooled_ref,
    hidden_ref,
    slope_ref,
    up_t_ref,
    down_t_ref,
    vecs_ref,
    ones_ref,
    *others,
):
    rows, width = y1_ref.shape
    words = rows // chars
    if exchange is None:
        grad_y1_ref, grad_up_ref, grad_down_t_ref, grad_vecs_ref = others
    else:
        (
            grad_proj_ref,
            word_small_ref,
            word_terms_ref,
            grad_y1_ref,
            char_terms_ref,
            word_qkv_ref,
            word_out_ref,
            word_up_ref,
            word_down_ref,
            grad_up_ref,
            grad_down_t_ref,
            grad_vecs_ref,
            local_ref,
            local_sem,
            one_ref,
            two_ref,
            three_ref,
            sends,
            arrivals,
        ) = others
        place = Place(*exchange)
        totals_word = [
            ScatterSum(
                place,
                word_terms_ref,
                lambda e, row, span: local_ref[e, row, span],
                one_ref,
                two_ref,
                three_ref,
                (sends, arrivals),
                part,
                WORD_PARTS,
            )
            for part in range(WORD_PARTS)
        ]
        own = [
            pltpu.make_async_copy(
                word_terms_ref.at[2 * e + place.core], local_ref.at[e], local_sem.at[e]
            )
            for e in range(place.wide)
        ]
        step, last = pl.program_id(0), pl.num_programs(0) - 1

        @pl.when(step == 0)
        def _():
            place.greet()
            for total in totals_word:
                total.start()
            for copy in own:
                copy.start()

        for part, total in enumerate(totals_word):

            @pl.when(step == (1 + part) * last // 15)
            def _(part=part, total=total):
                if part == 0:
                    for copy in own:
                        copy.wait()
                total.go_across()

            @pl.when(step == (4 + 2 * part) * last // 15)
            def _(total=total):
                total.go_along()

    @pl.when(pl.program_id(0) == 0)
    def _():
        grad_up_ref[...] = jnp.zeros_like(grad_up_ref)
        grad_down_t_ref[...] = jnp.zeros_like(grad_down_t_ref)
        grad_vecs_ref[...] = jnp.zeros_like(grad_vecs_ref)

    low, wide = jnp.bfloat16, jnp.float32
    block = SUB
    count, parts = rows // block, hidden_ref.shape[1] // CHUNK
    query = vecs_ref[4:5, :]
    per = 64 // chars

    def pool_back(s):
        spots = [
            (slice(row, row + 64), slice(row // chars, row // chars + per))
            for row in range(s * block, (s + 1) * block, 64)
        ]
        split = [
            split_two(
                (y2_ref[span, :].reshape(per, chars, width) * grad_pooled_ref[span_words]).reshape(
                    64, width
                )
            )
            for span, span_words in spots
        ]
        high, rest = (jnp.concatenate(side, axis=0) for side in zip(*split))
        grad_pi = mm(high, ones_ref[...]) + mm(rest, ones_ref[...])
        wide_parts, low_parts, query_sum = [], [], None
        for k, (span, span_words) in enumerate(spots):
            pi = pi_ref[span, :].astype(wide).reshape(per, chars, width)
            part = grad_pi[64 * k : 64 * (k + 1)].reshape(per, chars, width)
            inner = jnp.sum(pi * part, axis=1, keepdims=True)
            grad_scores = pi * (part - inner) * HEAD ** (-0.5)
            grid = y2_ref[span, :].reshape(per, chars, width)
            term = fold_rows((grad_scores * grid).reshape(64, width))
            query_sum = term if query_sum is None else query_sum + term
            grad = (pi * grad_pooled_ref[span_words] + grad_scores * query).reshape(64, width)
            wide_parts.append(grad)
            low_parts.append(grad.astype(low))
        grad_vecs_ref[0] += query_sum
        return jnp.concatenate(wide_parts, axis=0), jnp.concatenate(low_parts, axis=0)

    def norm_again(s):
        span = slice(s * block, (s + 1) * block)
        return norm_strips(y1_ref[span, :], vecs_ref[2:3, :], vecs_ref[3:4, :])

    def feed_back(s, branch):
        span = slice(s * block, (s + 1) * block)
        grads, total = [], None
        ahead = mm(branch, down_t_ref[:, 0:CHUNK])
        for part in range(parts):
            cols = slice(part * CHUNK, (part + 1) * CHUNK)
            current = ahead
            if part + 1 < parts:
                ahead = mm(branch, down_t_ref[:, (part + 1) * CHUNK : (part + 2) * CHUNK])
            (grad_pre,) = strips(
                lambda strip, slope: ((strip * slope.astype(wide)).astype(low),),
                16,
                current,
                slope_ref[span, cols],
            )
            grads.append(grad_pre)
            term = mm(grad_pre, up_t_ref[cols, :])
            total = term if total is None else total + term
        return grads, total

    def norm_finish(s, grad_normed, unit, inverse, grad_y2):
        span = slice(s * block, (s + 1) * block)
        gain = vecs_ref[2:3, :]
        gain_sum, bias_sum = None, None
        for row in range(0, block, 64):
            spot = slice(row, row + 64)
            part, part_unit = grad_normed[spot], unit[spot]
            one, two = fold_rows(part * part_unit), fold_rows(part)
            gain_sum = one if gain_sum is None else gain_sum + one
            bias_sum = two if bias_sum is None else bias_sum + two
            grad_y1_ref[s * block + row : s * block + row + 64, :] = grad_y2[spot] + norm_back(
                part, part_unit, inverse[spot], gain
            )
        grad_vecs_ref[1] += gain_sum
        grad_vecs_ref[2] += bias_sum

    pooled, norms, grads, totals = {}, {}, {}, {}
    pooled[0] = pool_back(0)
    norms[0] = norm_again(0)
    for s in range(count):
        grads[s], totals[s] = feed_back(s, pooled[s][1])
        if s + 1 < count:
            pooled[s + 1] = pool_back(s + 1)
            norms[s + 1] = norm_again(s + 1)
    branch_t = jnp.concatenate([pooled[s][1] for s in range(count)], axis=0).T
    normed_t = jnp.concatenate([norms[s][2] for s in range(count)], axis=0).T
    for part in range(parts):
        cols = slice(part * CHUNK, (part + 1) * CHUNK)
        grad_down_t_ref[:, cols] += mm(branch_t, hidden_ref[:, cols])
        grad_pre = jnp.concatenate([grads[s][part] for s in range(count)], axis=0)
        grad_up_ref[:, cols] += mm(normed_t, grad_pre)
    for s in range(count):
        norm_finish(s, totals[s], norms[s][0], norms[s][1], pooled[s][0])
    if exchange is None:
        return

    @pl.when(step == last)
    def _():
        low = jnp.bfloat16
        share = hidden_ref.shape[1] // (place.dp * place.mp)
        put_pairs(char_terms_ref, 0, grad_up_ref[...])
        row = hidden_ref.shape[1] // 16
        for c in range(2):
            piece = grad_down_t_ref[128 * c : 128 * c + 128, :].T
            piece = piece.reshape(place.dp, place.mp, share, 128).astype(low)
            for j in range(place.mp):
                char_terms_ref[j, :, row : row + share, :] = piece[:, j]
            row += share
        put_pairs(char_terms_ref, row, grad_proj_ref[...])
        row += grad_proj_ref.shape[1] // 16
        sums = [jnp.sum(grad_vecs_ref[k], axis=0, keepdims=True) for k in range(3)]
        small_row = lax.broadcasted_iota(jnp.int32, (16, 128), 0)
        for b in range(word_small_ref.shape[0]):
            piece = word_small_ref[b]
            if b < 2:
                for k in range(3):
                    piece = jnp.where(
                        small_row == 12 + k, sums[k][:, 128 * b : 128 * b + 128], piece
                    )
            piece = jnp.broadcast_to(piece.astype(low), (place.dp, 16, 128))
            for j in range(place.mp):
                char_terms_ref[j, :, row : row + 16, :] = piece
            row += 16
        for total in totals_word:
            result = total.finish()
        block = word_up_ref.shape[0]
        for t in range(3):
            word_qkv_ref[t] = result(slice(block * t, block * (t + 1)))
        word_out_ref[...] = result(slice(3 * block, 4 * block))
        count = word_up_ref.shape[1] // 128
        for c in range(count):
            cols = slice(128 * c, 128 * c + 128)
            word_up_ref[:, cols] = result(slice((4 + c) * block, (5 + c) * block))
            spot = slice((4 + count + c) * block, (5 + count + c) * block)
            word_down_ref[:, cols] = result(spot)


def char_attn_back_kernel(
    chars,
    exchange,
    chars_ref,
    cp_ref,
    probs_ref,
    co_ref,
    grad_y1_ref,
    qkv_t_ref,
    out_t_ref,
    vecs_ref,
    head_mask_ref,
    word_mask_ref,
    *others,
):
    rows, width = chars_ref.shape
    if exchange is None:
        (
            grad_chars_ref,
            grad_qkv_ref,
            grad_out_ref,
            grad_vecs_ref,
            grad_cp_ref,
            grad_co_ref,
        ) = others
    else:
        (
            early_terms_ref,
            grad_chars_ref,
            share_qkv_ref,
            share_out_ref,
            share_up_ref,
            share_down_ref,
            share_proj_ref,
            share_small_ref,
            share_vecs_ref,
            grad_cp_ref,
            grad_co_ref,
            grad_qkv_ref,
            grad_out_ref,
            grad_vecs_ref,
            local_ref,
            local_sem,
            late_terms_ref,
        ) = others[:17]
        early_refs, late_refs = others[17:22], others[22:27]
        place = Place(*exchange)
        early = ScatterSum(
            place,
            early_terms_ref,
            lambda e, row, span: local_ref[e, row, span],
            *early_refs[:3],
            early_refs[3:],
        )
        late = ScatterSum(
            place,
            late_terms_ref,
            lambda e, row, span: late_terms_ref[2 * e + place.core, row, span],
            *late_refs[:3],
            late_refs[3:],
        )
        own = [
            pltpu.make_async_copy(
                early_terms_ref.at[2 * e + place.core], local_ref.at[e], local_sem.at[e]
            )
            for e in range(place.wide)
        ]
        step, last = pl.program_id(0), pl.num_programs(0) - 1

        @pl.when(step == 0)
        def _():
            place.greet()
            early.start()
            for copy in own:
                copy.start()

        @pl.when(step == last // 15)
        def _():
            for copy in own:
                copy.wait()
            early.go_across()

        @pl.when(step == last // 3)
        def _():
            early.go_along()

    @pl.when(pl.program_id(0) == 0)
    def _():
        grad_qkv_ref[...] = jnp.zeros_like(grad_qkv_ref)
        grad_out_ref[...] = jnp.zeros_like(grad_out_ref)
        grad_vecs_ref[...] = jnp.zeros_like(grad_vecs_ref)

    low, wide = jnp.bfloat16, jnp.float32
    lane_word = lax.broadcasted_iota(jnp.int32, (1, 1, GROUP), 2) // chars
    masks = head_mask_ref[...]
    word_masks = word_mask_ref[...]
    scale = HEAD ** (-0.5)
    block = SUB
    count = rows // block

    def out_back(s):
        span = slice(s * block, (s + 1) * block)
        branch = grad_y1_ref[span, :].astype(low)
        grad_co_ref[span, :] = mm(branch, out_t_ref[...]).astype(low)
        return branch

    def norm_again(s):
        span = slice(s * block, (s + 1) * block)
        return norm_strips(
            chars_ref[span, :].astype(wide), vecs_ref[0:1, :], vecs_ref[1:2, :]
        )

    def side_by_side(spread):
        return jnp.concatenate([spread[h] for h in range(CHAR_HEADS)], axis=1)

    def groups_of(s):
        return [slice(row, row + GROUP) for row in range(s * block, (s + 1) * block, GROUP)]

    grad_probs, grad_scores = {}, {}

    def back_probs(s):
        grad_probs[s] = []
        for span in groups_of(s):
            values = head_rows(cp_ref[span, 2 * width : 3 * width], masks)
            square = mm(values, grad_co_ref[span, :], NT)
            grad_probs[s].append(gather_diagonal(square, lane_word, chars))

    def back_scores(s):
        grad_scores[s] = []
        for span, part in zip(groups_of(s), grad_probs[s]):
            probs = probs_ref[span.start // GROUP].reshape(CHAR_HEADS, chars, GROUP)
            spread = spread_diagonal(probs, word_masks, chars)
            spread = spread.reshape(CHAR_HEADS, GROUP, GROUP)
            grad_values = mm(side_by_side(spread), head_rows(grad_co_ref[span, :], masks))
            grad_cp_ref[span, 2 * width : 3 * width] = grad_values.astype(low)
            probs = probs.astype(wide)
            inner = jnp.sum(part * probs, axis=1, keepdims=True)
            grad_scores[s].append((probs * (part - inner)).astype(low))

    def back_keys(s):
        for span, part in zip(groups_of(s), grad_scores[s]):
            spread = spread_diagonal(part, word_masks, chars)
            spread = spread.reshape(CHAR_HEADS, GROUP, GROUP)
            queries = head_rows(cp_ref[span, 0:width], masks)
            grad_keys = mm(side_by_side(spread), queries) * scale
            grad_cp_ref[span, width : 2 * width] = grad_keys.astype(low)
            keys = head_rows(cp_ref[span, width : 2 * width], masks)
            grad_queries = mm(spread.reshape(CHAR_HEADS * GROUP, GROUP), keys, TN) * scale
            grad_cp_ref[span, 0:width] = grad_queries.astype(low)

    def project_back(s):
        span = slice(s * block, (s + 1) * block)
        return mm(grad_cp_ref[span, :], qkv_t_ref[...])

    def norm_finish(s, grad_normed, unit, inverse):
        gain = vecs_ref[0:1, :]
        gain_sum, bias_sum = None, None
        for row in range(0, block, 64):
            spot, span = slice(row, row + 64), slice(s * block + row, s * block + row + 64)
            part, part_unit = grad_normed[spot], unit[spot]
            one, two = fold_rows(part * part_unit), fold_rows(part)
            gain_sum = one if gain_sum is None else gain_sum + one
            bias_sum = two if bias_sum is None else bias_sum + two
            grad = grad_y1_ref[span, :] + norm_back(part, part_unit, inverse[spot], gain)
            grad_chars_ref[span, :] = grad.astype(low)
        grad_vecs_ref[0] += gain_sum
        grad_vecs_ref[1] += bias_sum

    branches, norms, totals = [], {}, {}
    for s in range(count):
        branches.append(out_back(s))
        back_probs(s)
    norms[0] = norm_again(0)
    for s in range(count):
        back_scores(s)
        back_keys(s)
        if s + 1 < count:
            norms[s + 1] = norm_again(s + 1)
        totals[s] = project_back(s)
    grad_out_ref[...] += mm(co_ref[...].T, jnp.concatenate(branches, axis=0))
    normed_t = jnp.concatenate([norms[s][2] for s in range(count)], axis=0).T
    grad_qkv_ref[...] += mm(normed_t, grad_cp_ref[...])
    for s in range(count):
        norm_finish(s, totals[s], norms[s][0], norms[s][1])
    if exchange is None:
        return

    @pl.when(step == last)
    def _():
        low = jnp.bfloat16
        put_pairs(late_terms_ref, 0, grad_qkv_ref[...])
        row = 3 * width // 16
        put_pairs(late_terms_ref, row, grad_out_ref[...])
        row += width // 16
        sums = [jnp.sum(grad_vecs_ref[k], axis=0, keepdims=True) for k in range(2)]
        small_row = lax.broadcasted_iota(jnp.int32, (16, 128), 0)
        piece = jnp.zeros((16, 128), jnp.float32)
        for k in range(2):
            for b in range(2):
                piece = jnp.where(
                    small_row == 2 * k + b, sums[k][:, 128 * b : 128 * b + 128], piece
                )
        piece = jnp.broadcast_to(piece.astype(low), (place.dp, 16, 128))
        for j in range(place.mp):
            late_terms_ref[j, :, row : row + 16, :] = piece
        late.start()
        result = early.finish()
        row = 0
        for target, share in (
            (share_up_ref, 8),
            (share_down_ref, share_down_ref.shape[0]),
            (share_proj_ref, 8),
            (share_small_ref, 16),
        ):
            for c in range(target.shape[1] // 128):
                target[:, 128 * c : 128 * c + 128] = result(slice(row, row + share))
                row += share
        late.go_across()
        late.go_along()
        result = late.finish()
        row = 0
        for target in (share_qkv_ref, share_out_ref):
            for c in range(target.shape[1] // 128):
                target[:, 128 * c : 128 * c + 128] = result(slice(row, row + 8))
                row += 8
        share_vecs_ref[...] = result(slice(row, row + 16))


def whole(shape):
    return pl.BlockSpec(shape, lambda step: (0,) * len(shape))


def once(shape):
    return pl.BlockSpec(shape, lambda step: (0,) * len(shape), pipeline_mode=pl.Buffered(1))


def blocked(shape):
    return pl.BlockSpec(shape, lambda step: (step,) + (0,) * (len(shape) - 1))


def params(megabytes):
    return pltpu.CompilerParams(
        dimension_semantics=("arbitrary",), vmem_limit_bytes=megabytes * 1024 * 1024
    )


def block_rows(rows, wanted):
    while rows % wanted:
        wanted //= 2
    return wanted


def char_forward(states, counts, weights, chars):
    rows, width = states.shape
    qkv, out, up, down, ones, vecs, head_masks, word_masks = weights
    block = block_rows(rows, 1024)
    words, groups = block // chars, block // GROUP
    low, wide = jnp.bfloat16, jnp.float32
    shapes = (
        ((rows, 3 * width), low),
        ((rows // GROUP, CHAR_HEADS * chars, GROUP), low),
        ((rows, width), low),
        ((rows, width), wide),
        ((rows, up.shape[1]), low),
        ((rows, up.shape[1]), low),
        ((rows, width), wide),
        ((rows, width), low),
        ((rows // chars, width), low),
    )
    blocks = (
        (block, 3 * width),
        (groups, CHAR_HEADS * chars, GROUP),
        (block, width),
        (block, width),
        (block, up.shape[1]),
        (block, up.shape[1]),
        (block, width),
        (block, width),
        (words, width),
    )
    flops = 2 * rows * width * (4 * width + 2 * up.shape[1] + 8 * width)
    return pl.pallas_call(
        functools.partial(char_forward_kernel, chars),
        grid=(rows // block,),
        in_specs=[
            blocked((block, width)),
            blocked((groups, GROUP // chars)),
            whole(qkv.shape),
            whole(out.shape),
            whole(up.shape),
            whole(down.shape),
            whole(ones.shape),
            whole(vecs.shape),
            whole(head_masks.shape),
            whole(word_masks.shape),
        ],
        out_specs=[blocked(shape) for shape in blocks],
        out_shape=[jax.ShapeDtypeStruct(shape, kind) for shape, kind in shapes],
        compiler_params=params(56),
        cost_estimate=pl.CostEstimate(
            flops=flops, bytes_accessed=rows * width * 36, transcendentals=rows * width * 5
        ),
        name="char_forward",
    )(states, counts, qkv, out, up, down, ones, vecs, head_masks, word_masks)


def char_mlp_back(y1, y2, pi, grad_pooled, hidden, slope, weights, chars):
    rows, width = y1.shape
    up_t, down_t, vecs, ones = weights
    block = block_rows(rows, 1024)
    hidden_width = hidden.shape[1]
    wide = jnp.float32
    flops = 2 * rows * width * (4 * hidden_width + 2 * width)
    return pl.pallas_call(
        functools.partial(char_mlp_back_kernel, chars, None),
        grid=(rows // block,),
        in_specs=[
            blocked((block, width)),
            blocked((block, width)),
            blocked((block, width)),
            blocked((block // chars, 1, width)),
            blocked((block, hidden_width)),
            blocked((block, hidden_width)),
            whole(up_t.shape),
            whole(down_t.shape),
            whole(vecs.shape),
            whole(ones.shape),
        ],
        out_specs=[
            blocked((block, width)),
            whole((width, hidden_width)),
            whole((width, hidden_width)),
            whole((3, 8, width)),
        ],
        out_shape=[
            jax.ShapeDtypeStruct((rows, width), wide),
            jax.ShapeDtypeStruct((width, hidden_width), wide),
            jax.ShapeDtypeStruct((width, hidden_width), wide),
            jax.ShapeDtypeStruct((3, 8, width), wide),
        ],
        compiler_params=params(56),
        cost_estimate=pl.CostEstimate(
            flops=flops, bytes_accessed=rows * width * 30, transcendentals=0
        ),
        name="char_mlp_back",
    )(y1, y2, pi, grad_pooled, hidden, slope, up_t, down_t, vecs, ones)


def char_attn_back(states, cp, probs, co, grad_y1, weights, chars):
    rows, width = states.shape
    qkv_t, out_t, vecs, head_masks, word_masks = weights
    block = block_rows(rows, 1024)
    low, wide = jnp.bfloat16, jnp.float32
    flops = 2 * rows * width * 18 * width
    return pl.pallas_call(
        functools.partial(char_attn_back_kernel, chars, None),
        grid=(rows // block,),
        in_specs=[
            blocked((block, width)),
            blocked((block, 3 * width)),
            blocked((block // GROUP, CHAR_HEADS * chars, GROUP)),
            blocked((block, width)),
            blocked((block, width)),
            whole(qkv_t.shape),
            whole(out_t.shape),
            whole(vecs.shape),
            whole(head_masks.shape),
            whole(word_masks.shape),
        ],
        out_specs=[
            blocked((block, width)),
            whole((width, 3 * width)),
            whole((width, width)),
            whole((2, 8, width)),
        ],
        out_shape=[
            jax.ShapeDtypeStruct((rows, width), low),
            jax.ShapeDtypeStruct((width, 3 * width), wide),
            jax.ShapeDtypeStruct((width, width), wide),
            jax.ShapeDtypeStruct((2, 8, width), wide),
        ],
        scratch_shapes=[
            pltpu.VMEM((block, 3 * width), low),
            pltpu.VMEM((block, width), low),
        ],
        compiler_params=params(56),
        cost_estimate=pl.CostEstimate(
            flops=flops, bytes_accessed=rows * width * 18, transcendentals=0
        ),
        name="char_attn_back",
    )(states, cp, probs, co, grad_y1, qkv_t, out_t, vecs, head_masks, word_masks)


def char_mlp_back_exchange(
    y1, y2, pi, grad_pooled, hidden, slope, weights, chars, mesh_size, grad_proj, word_small, word_terms
):
    rows, width = y1.shape
    up_t, down_t, vecs, ones = weights
    dp, mp = mesh_size
    block = block_rows(rows, 1024)
    hidden_width = hidden.shape[1]
    low, wide = jnp.bfloat16, jnp.float32
    model = grad_proj.shape[1]
    flops = 2 * rows * width * (4 * hidden_width + 2 * width)
    char_rows = 2 * hidden_width // 16 + model // 16 + 16 * word_small.shape[0]
    n = word_terms.shape[2]
    share = model // dp
    outs = (
        ((rows, width), wide, blocked((block, width))),
        ((mp, dp, char_rows, 128), low, None),
        ((3, share, 128), wide, None),
        ((share, 128), wide, None),
        ((share, model), wide, None),
        ((share, model), wide, None),
    )
    return pl.pallas_call(
        functools.partial(char_mlp_back_kernel, chars, mesh_size),
        grid=(rows // block,),
        in_specs=[
            blocked((block, width)),
            blocked((block, width)),
            blocked((block, width)),
            blocked((block // chars, 1, width)),
            blocked((block, hidden_width)),
            blocked((block, hidden_width)),
            whole(up_t.shape),
            whole(down_t.shape),
            whole(vecs.shape),
            whole(ones.shape),
            whole(grad_proj.shape),
            whole(word_small.shape),
            pl.BlockSpec(memory_space=pl.ANY),
        ],
        out_specs=[spec or whole(shape) for shape, _, spec in outs],
        out_shape=[jax.ShapeDtypeStruct(shape, kind) for shape, kind, _ in outs],
        scratch_shapes=[
            pltpu.VMEM((width, hidden_width), wide),
            pltpu.VMEM((width, hidden_width), wide),
            pltpu.VMEM((3, 8, width), wide),
            pltpu.VMEM((mp // 2, dp, n, 128), low),
            pltpu.SemaphoreType.DMA((mp // 2,)),
        ]
        + scatter_scratch(dp, mp, n, WORD_PARTS),
        compiler_params=pltpu.CompilerParams(
            dimension_semantics=("arbitrary",),
            vmem_limit_bytes=60 * 1024 * 1024,
            collective_id=1,
            has_side_effects=True,
        ),
        cost_estimate=pl.CostEstimate(
            flops=flops, bytes_accessed=rows * width * 30, transcendentals=0
        ),
        name="char_mlp_back",
    )(
        y1, y2, pi, grad_pooled, hidden, slope, up_t, down_t, vecs, ones,
        grad_proj, word_small, word_terms,
    )


def char_attn_back_exchange(
    states, cp, probs, co, grad_y1, weights, chars, mesh_size, early_terms, hidden_width, model
):
    rows, width = states.shape
    qkv_t, out_t, vecs, head_masks, word_masks = weights
    dp, mp = mesh_size
    count = dp * mp
    block = block_rows(rows, 1024)
    low, wide = jnp.bfloat16, jnp.float32
    flops = 2 * rows * width * 18 * width
    n = early_terms.shape[2]
    late = 4 * width // 16 + 16
    outs = (
        ((rows, width), low, blocked((block, width))),
        ((width // count, 3 * width), wide, None),
        ((width // count, width), wide, None),
        ((width // count, hidden_width), wide, None),
        ((hidden_width // count, width), wide, None),
        ((width // count, model), wide, None),
        ((16, model), wide, None),
        ((16, 128), wide, None),
    )
    return pl.pallas_call(
        functools.partial(char_attn_back_kernel, chars, mesh_size),
        grid=(rows // block,),
        in_specs=[
            blocked((block, width)),
            blocked((block, 3 * width)),
            blocked((block // GROUP, CHAR_HEADS * chars, GROUP)),
            blocked((block, width)),
            blocked((block, width)),
            whole(qkv_t.shape),
            whole(out_t.shape),
            whole(vecs.shape),
            whole(head_masks.shape),
            whole(word_masks.shape),
            pl.BlockSpec(memory_space=pl.ANY),
        ],
        out_specs=[spec or whole(shape) for shape, _, spec in outs],
        out_shape=[jax.ShapeDtypeStruct(shape, kind) for shape, kind, _ in outs],
        scratch_shapes=[
            pltpu.VMEM((block, 3 * width), low),
            pltpu.VMEM((block, width), low),
            pltpu.VMEM((width, 3 * width), wide),
            pltpu.VMEM((width, width), wide),
            pltpu.VMEM((2, 8, width), wide),
            pltpu.VMEM((mp // 2, dp, n, 128), low),
            pltpu.SemaphoreType.DMA((mp // 2,)),
            pltpu.VMEM((mp, dp, late, 128), low),
        ]
        + scatter_scratch(dp, mp, n)
        + scatter_scratch(dp, mp, late),
        compiler_params=pltpu.CompilerParams(
            dimension_semantics=("arbitrary",),
            vmem_limit_bytes=56 * 1024 * 1024,
            collective_id=2,
            has_side_effects=True,
        ),
        cost_estimate=pl.CostEstimate(
            flops=flops, bytes_accessed=rows * width * 18, transcendentals=0
        ),
        name="char_attn_back",
    )(states, cp, probs, co, grad_y1, qkv_t, out_t, vecs, head_masks, word_masks, early_terms)


def word_kernel(
    pooled_ref,
    words_ref,
    cotangent_ref,
    language_ref,
    language_hot_ref,
    proj_ref,
    weights_ref,
    norms_ref,
    head_mask_ref,
    layer_ref,
    grad_words_ref,
    terms_ref,
    grad_proj_ref,
    grad_pooled_ref,
    small_ref,
    residual_ref,
    normed_one_ref,
    packed_ref,
    probs_ref,
    mixed_ref,
    middle_ref,
    normed_two_ref,
    hidden_ref,
    slope_ref,
    grad_keys_ref,
    grad_values_ref,
    sums_ref,
):
    low, wide = jnp.bfloat16, jnp.float32
    length, model = words_ref.shape
    dp, mp = weights_ref.shape[:2]
    share = model // dp
    row_block, large = 256, 512
    blocks = length // row_block
    hidden_width = hidden_ref.shape[1]
    up_blocks = hidden_width // mp // 128
    scale = HEAD ** (-0.5)
    up_base, down_base = 4 * share, (4 + up_blocks) * share

    def weight(base, first, last):
        pieces = [
            weights_ref[:, j, base + c * share : base + (c + 1) * share, :].reshape(model, 128)
            for j, c in (column(base, block) for block in range(first, last))
        ]
        return jnp.concatenate(pieces, axis=1)

    def column(base, block):
        return (block, 0) if base < up_base else (block // up_blocks, block % up_blocks)

    def put(base, first, grad):
        for k in range(grad.shape[1] // 128):
            j, c = column(base, first + k)
            piece = grad[:, 128 * k : 128 * k + 128].reshape(dp, share, 128).astype(low)
            terms_ref[j, :, base + c * share : base + (c + 1) * share, :] = piece

    def norm(k):
        return norms_ref[k : k + 1, :]

    sums_ref[...] = jnp.zeros_like(sums_ref)

    spans = [slice(row, row + large) for row in range(0, length, large)]
    normed = []
    for span in spans:
        residual = words_ref[span, :].astype(wide) + mm(pooled_ref[span, :], proj_ref[...])
        residual = residual + language_ref[...]
        residual_ref[span, :] = residual
        normed.append(norm_strips(residual, norm(0), norm(1))[2])
        normed_one_ref[span, :] = normed[-1]
    for t in range(3):
        whole_weight = weight(t * share, 0, model // 128)
        for span, rows in zip(spans, normed):
            packed_ref[t, span, :] = mm(rows, whole_weight).astype(low)

    causal = lax.broadcasted_iota(jnp.int32, (row_block, row_block), 0) <= (
        lax.broadcasted_iota(jnp.int32, (row_block, row_block), 1)
    )

    @pl.loop(0, model // 128)
    def _(pair):
        lanes = pl.ds(pl.multiple_of(pair * 128, 128), 128)
        values_t = packed_ref[2, :, lanes].T

        def scores_of(block, h):
            stop = (block + 1) * row_block
            queries = packed_ref[0, block * row_block : stop, lanes]
            keys = packed_ref[1, 0:stop, lanes] * head_mask_ref[h : h + 1, 0:128]
            return mm(keys, queries, NT)

        order = [(block, h) for block in range(blocks) for h in range(2)]
        ahead = scores_of(*order[0])
        mixed = []
        for place, (block, h) in enumerate(order):
            scores = ahead * EXP2_SCALE
            if place + 1 < len(order):
                ahead = scores_of(*order[place + 1])
            stop = (block + 1) * row_block
            first = block * (block + 1) // 2 * row_block
            near = jnp.where(causal, scores[stop - row_block :], NEG_FILL)
            scores = jnp.concatenate([scores[: stop - row_block], near]) if block else near
            powers = jnp.exp2(scores - jnp.max(scores, axis=0, keepdims=True))
            probs = powers * (1.0 / jnp.sum(powers, axis=0, keepdims=True))
            probs = probs.astype(low)
            probs_ref[2 * pair + h, first : first + stop, :] = probs
            mixed.append(mm(values_t[HEAD * h : HEAD * (h + 1), 0:stop], probs))
            if h == 1:
                both = jnp.concatenate(mixed, axis=0).T.astype(low)
                mixed_ref[block * row_block : stop, lanes] = both
                mixed = []

    out_t = weight(3 * share, 0, model // 128)
    normed, totals = [], []
    for span in spans:
        middle = residual_ref[span, :] + mm(mixed_ref[span, :], out_t, NT)
        middle_ref[span, :] = middle
        normed.append(norm_strips(middle, norm(2), norm(3))[2])
        normed_two_ref[span, :] = normed[-1]
        totals.append(middle)
    order = [(c, s) for c in range(0, hidden_width // 128, 4) for s in range(len(spans))]

    def up(c, s):
        return mm(normed[s], weight(up_base, c, c + 4))

    ahead = up(*order[0])
    for place, (c, s) in enumerate(order):
        current = ahead
        if place + 1 < len(order):
            ahead = up(*order[place + 1])
        cols = slice(128 * c, 128 * c + 512)
        hidden, slope = gelu_low(current)
        hidden_ref[spans[s], cols] = hidden
        slope_ref[spans[s], cols] = slope
        totals[s] = totals[s] + mm(hidden, weight(down_base, c, c + 4), NT)
    for span, total in zip(spans, totals):
        layer_ref[span, :] = total.astype(low)

    cotangent_t = cotangent_ref[...].T
    order = [(c, s) for c in range(0, hidden_width // 128, 4) for s in range(len(spans))]

    def down_back(c, s):
        return mm(cotangent_ref[spans[s], :], weight(down_base, c, c + 4))

    ahead = down_back(*order[0])
    totals = [None] * len(spans)
    for place, (c, s) in enumerate(order):
        current = ahead
        if place + 1 < len(order):
            ahead = down_back(*order[place + 1])
        cols = slice(128 * c, 128 * c + 512)
        (grad_pre,) = strips(
            lambda strip, slope: ((strip * slope.astype(wide)).astype(low),),
            16,
            current,
            slope_ref[spans[s], cols],
        )
        slope_ref[spans[s], cols] = grad_pre
        term = mm(grad_pre, weight(up_base, c, c + 4), NT)
        totals[s] = term if totals[s] is None else totals[s] + term
        if s == 0:
            put(down_base, c, mm(cotangent_t, hidden_ref[:, cols]))
    normed_t = normed_two_ref[...].T
    for c in range(0, hidden_width // 128, 4):
        put(up_base, c, mm(normed_t, slope_ref[:, 128 * c : 128 * c + 512]))
    for s, span in enumerate(spans):

        def finish(part, middle, cotangent):
            unit, inverse = standardize(middle)
            sums_ref[2] += fold_rows(part * unit)
            sums_ref[3] += fold_rows(part)
            grad = cotangent.astype(wide) + norm_back(part, unit, inverse, norm(2))
            return grad, grad.astype(low)

        grad_middle, branch = strips(
            finish, 64, totals[s], middle_ref[span, :], cotangent_ref[span, :]
        )
        middle_ref[span, :] = grad_middle
        normed_two_ref[span, :] = branch
    put(3 * share, 0, mm(normed_two_ref[...].T, mixed_ref[...]))
    for span in spans:
        mixed_ref[span, :] = mm(normed_two_ref[span, :], out_t).astype(low)


    @pl.loop(0, model // 128)
    def _(pair):
        lanes = pl.ds(pl.multiple_of(pair * 128, 128), 128)
        grad_keys_ref[...] = jnp.zeros_like(grad_keys_ref)
        grad_values_ref[...] = jnp.zeros_like(grad_values_ref)
        keys_t = packed_ref[1, :, lanes].T

        def grad_probs_of(block, h):
            stop = (block + 1) * row_block
            grad_mixed = mixed_ref[block * row_block : stop, lanes]
            values = packed_ref[2, 0:stop, lanes] * head_mask_ref[h : h + 1, 0:128]
            return mm(values, grad_mixed, NT)

        order = [(block, h) for block in range(blocks) for h in range(2)]
        ahead = grad_probs_of(*order[0])
        sides = []
        for place, (block, h) in enumerate(order):
            grad_probs = ahead
            if place + 1 < len(order):
                ahead = grad_probs_of(*order[place + 1])
            stop = (block + 1) * row_block
            span = slice(block * row_block, stop)
            first = block * (block + 1) // 2 * row_block
            probs = probs_ref[2 * pair + h, first : first + stop, :]
            probs_wide = probs.astype(wide)
            inner = jnp.sum(grad_probs * probs_wide, axis=0, keepdims=True)
            grad_scores = (probs_wide * (grad_probs - inner)).astype(low)
            grad_queries = mm(keys_t[HEAD * h : HEAD * (h + 1), 0:stop], grad_scores)
            sides.append((probs, grad_scores, grad_queries))
            if h == 1:
                probs, grad_scores, grad_queries = (list(side) for side in zip(*sides))
                sides = []
                masks = [head_mask_ref[k : k + 1, 0:128] for k in range(2)]
                grad_mixed, queries = mixed_ref[span, lanes], packed_ref[0, span, lanes]
                grad_values_ref[0:stop, :] += mm(
                    jnp.concatenate(probs, axis=1),
                    jnp.concatenate([grad_mixed * mask for mask in masks], axis=0),
                )
                grad_keys_ref[0:stop, :] += mm(
                    jnp.concatenate(grad_scores, axis=1),
                    jnp.concatenate([queries * mask for mask in masks], axis=0),
                )
                both = jnp.concatenate(grad_queries, axis=0) * scale
                packed_ref[0, span, lanes] = both.T.astype(low)
        packed_ref[1, :, lanes] = (grad_keys_ref[...] * scale).astype(low)
        packed_ref[2, :, lanes] = grad_values_ref[...].astype(low)

    normed_t = normed_one_ref[...].T
    totals = [None] * len(spans)
    for t in range(3):
        put(t * share, 0, mm(normed_t, packed_ref[t]))
        for s, span in enumerate(spans):
            term = mm(packed_ref[t, span, :], weight(t * share, 0, model // 128), NT)
            totals[s] = term if totals[s] is None else totals[s] + term
    for s, span in enumerate(spans):

        def finish(part, residual, grad_middle):
            unit, inverse = standardize(residual)
            sums_ref[0] += fold_rows(part * unit)
            sums_ref[1] += fold_rows(part)
            grad = grad_middle + norm_back(part, unit, inverse, norm(0))
            sums_ref[4] += fold_rows(grad)
            return (grad.astype(low),)

        (grad,) = strips(finish, 64, totals[s], residual_ref[span, :], middle_ref[span, :])
        grad_words_ref[span, :] = grad
        grad_pooled_ref[span] = mm(grad, proj_ref[...], NT)[:, None, :]

    grad_proj_ref[...] = mm(pooled_ref[...].T, grad_words_ref[...])

    sums = [jnp.sum(sums_ref[k], axis=0, keepdims=True) for k in range(5)]
    small_row = lax.broadcasted_iota(jnp.int32, (8, 128), 0)
    for b in range(model // 128):
        cols = slice(128 * b, 128 * b + 128)
        small_ref[b, 0:8, :] = language_hot_ref[...] * sums[4][:, cols]
        piece = jnp.zeros((8, 128), wide)
        for k in range(4):
            piece = jnp.where(small_row == k, sums[k][:, cols], piece)
        small_ref[b, 8:16, :] = piece


def word_layer_kernel(pooled, words, cotangent, language_row, language_hot, proj, weights, norms, head_masks):
    low, wide = jnp.bfloat16, jnp.float32
    length, model = words.shape
    width = pooled.shape[1]
    dp, mp, n = weights.shape[:3]
    hidden_width = (n * dp // model - 4) // 2 * 128 * mp
    blocks = length // 256
    heads = model // HEAD
    arrays = (pooled, words, cotangent, language_row, language_hot, proj, weights, norms, head_masks)
    outs = (
        ((length, model), low),
        ((length, model), low),
        ((mp, dp, n, 128), low),
        ((width, model), wide),
        ((length, 1, width), wide),
        ((model // 128, 16, 128), wide),
    )
    return pl.pallas_call(
        word_kernel,
        grid=(1,),
        in_specs=[once(array.shape) for array in arrays],
        out_specs=[once(shape) for shape, _ in outs],
        out_shape=[jax.ShapeDtypeStruct(shape, kind) for shape, kind in outs],
        scratch_shapes=[
            pltpu.VMEM((length, model), wide),
            pltpu.VMEM((length, model), low),
            pltpu.VMEM((3, length, model), low),
            pltpu.VMEM((heads, blocks * (blocks + 1) // 2 * 256, 256), low),
            pltpu.VMEM((length, model), low),
            pltpu.VMEM((length, model), wide),
            pltpu.VMEM((length, model), low),
            pltpu.VMEM((length, hidden_width), low),
            pltpu.VMEM((length, hidden_width), low),
            pltpu.VMEM((length, 128), wide),
            pltpu.VMEM((length, 128), wide),
            pltpu.VMEM((5, 8, model), wide),
        ],
        compiler_params=pltpu.CompilerParams(vmem_limit_bytes=62 * 1024 * 1024),
        cost_estimate=pl.CostEstimate(
            flops=40 * 10**9, bytes_accessed=20 * 2**20, transcendentals=10**7
        ),
        name="word_layer",
    )(*arrays)


def attend_forward(queries, key_block, values, allowed):
    scores = low_sum("bqhd,bkhd->bhqk", queries, key_block) * HEAD ** (-0.5)
    scores = jnp.where(allowed, scores, NEG_FILL)
    row_max = jnp.max(scores, axis=-1, keepdims=True)
    powers = jnp.exp(scores - row_max)
    row_total = jnp.sum(powers, axis=-1, keepdims=True)
    attn_probs = (powers / row_total).astype(jnp.bfloat16)
    attn_mixed = low_sum("bhqk,bkhd->bqhd", attn_probs, values).astype(jnp.bfloat16)
    return (attn_mixed, row_max + jnp.log(row_total))


def attend_backward(queries, key_block, values, allowed, log_total, grad_mixed):
    scale = HEAD ** (-0.5)
    scores = low_sum("bqhd,bkhd->bhqk", queries, key_block) * scale
    attn_probs = jnp.where(allowed, jnp.exp(scores - log_total), 0.0)
    grad_probs = low_sum("bqhd,bkhd->bhqk", grad_mixed, values)
    grad_values = low_sum("bhqk,bqhd->bkhd", attn_probs.astype(jnp.bfloat16), grad_mixed)
    inner_sum = jnp.sum(grad_probs * attn_probs, axis=-1, keepdims=True)
    grad_scores = (attn_probs * (grad_probs - inner_sum)).astype(jnp.bfloat16)
    grad_queries = low_sum("bhqk,bkhd->bqhd", grad_scores, key_block) * scale
    grad_keys = low_sum("bhqk,bqhd->bkhd", grad_scores, queries) * scale
    return (grad_queries, grad_keys, grad_values)


def word_layer(residual, grad_rows, weights, norms, mp_size, mp_index):
    qkv, out_t, up, down_t = weights
    gain_one, bias_one, gain_two, bias_two = norms
    rows, width = residual.shape
    low = jnp.bfloat16
    sequences, length = max(1, rows // LEN), min(rows, LEN)
    share = LEN // length
    groups = [[a * share + b for b in range(share)] for a in range(mp_size // share)]
    unit_one, inverse_one, normed_one = apply_norm(residual, gain_one, bias_one)
    packed = low_sum("rd,tdc->trc", normed_one, qkv).astype(low)
    packed = packed.reshape(3, sequences, length, width // HEAD, HEAD)
    keys = packed[1:]
    start = 0
    if share > 1:
        keys = lax.all_gather(keys, "mp", axis=2, tiled=True, axis_index_groups=groups)
        start = lax.rem(mp_index, share) * length
    allowed = (
        lax.broadcasted_iota(jnp.int32, (length, LEN), 1)
        <= lax.broadcasted_iota(jnp.int32, (length, LEN), 0) + start
    )[None, None]
    mixed, log_total = attend_forward(packed[0], keys[0], keys[1], allowed)
    mixed_rows = mixed.reshape(rows, width)
    middle = residual + mm(mixed_rows, out_t, NT)
    unit_two, inverse_two, normed_two = apply_norm(middle, gain_two, bias_two)
    hidden, slope = gelu_pair(matmul(normed_two, up))
    hidden = hidden.astype(low)
    layer_output = (middle + mm(hidden, down_t, NT)).astype(low)
    grad_wide = grad_rows.astype(jnp.float32)
    grad_down_t = mm(grad_rows, hidden, TN)
    grad_pre = (matmul(grad_rows, down_t) * slope).astype(low)
    grad_up = mm(normed_two, grad_pre, TN)
    grad_normed = mm(grad_pre, up, NT)
    grad_gain_two = jnp.sum(grad_normed * unit_two, axis=0)
    grad_bias_two = jnp.sum(grad_normed, axis=0)
    grad_middle = grad_wide + norm_back(grad_normed, unit_two, inverse_two, gain_two)
    branch = grad_middle.astype(low)
    grad_out_t = mm(branch, mixed_rows, TN)
    grad_mixed = matmul(branch, out_t).astype(low).reshape(sequences, length, -1, HEAD)
    grad_queries, grad_keys, grad_values = attend_backward(
        packed[0], keys[0], keys[1], allowed, log_total, grad_mixed
    )
    grad_keys = jnp.stack((grad_keys, grad_values), axis=0)
    if share > 1:
        grad_keys = lax.psum_scatter(
            grad_keys, "mp", scatter_dimension=2, tiled=True, axis_index_groups=groups
        )
    grad_packed = jnp.concatenate((grad_queries[None], grad_keys), axis=0)
    grad_packed = grad_packed.reshape(3, rows, width).astype(low)
    grad_qkv = low_sum("rd,trc->tdc", normed_one, grad_packed)
    grad_normed = low_sum("trc,tdc->rd", grad_packed, qkv)
    grad_gain_one = jnp.sum(grad_normed * unit_one, axis=0)
    grad_bias_one = jnp.sum(grad_normed, axis=0)
    grad_residual = grad_middle + norm_back(grad_normed, unit_one, inverse_one, gain_one)
    return (
        layer_output,
        grad_residual,
        (grad_qkv, grad_out_t, grad_up, grad_down_t),
        (grad_gain_one, grad_bias_one, grad_gain_two, grad_bias_two),
    )


def mask_constants(width, chars):
    head, word = np.arange(width) // HEAD, np.arange(GROUP) // chars
    head_masks = head[None] == np.arange(8)[:, None]
    word_masks = word[None] == np.arange(GROUP // chars)[:, None]
    ones = head[:, None] == head[None]
    return tuple(jnp.asarray(mask.astype(ml_dtypes.bfloat16)) for mask in (head_masks, word_masks, ones))


def blocks_of(array, count):
    return array.reshape(count, -1)


def shards_general(
    char_states,
    word_states,
    char_counts,
    language_group,
    output_grad,
    char_norm_gain,
    char_norm_bias,
    char_qkv,
    char_out,
    char_mlp_gain,
    char_mlp_bias,
    char_up,
    char_down,
    pool_query,
    char_proj,
    language_table,
    word_norm_gain,
    word_norm_bias,
    word_qkv,
    word_out,
    word_mlp_gain,
    word_mlp_bias,
    word_up,
    word_down,
):
    low, wide = jnp.bfloat16, jnp.float32
    dp_size, mp_size = lax.axis_size("dp"), lax.axis_size("mp")
    mp_index = lax.axis_index("mp")
    devices = dp_size * mp_size
    word_count, chars, width = char_states.shape
    model = word_states.shape[1]
    langs = language_table.shape[0]

    char_parts = (
        char_qkv,
        char_out,
        char_up,
        char_down,
        char_proj,
        char_norm_gain,
        char_norm_bias,
        char_mlp_gain,
        char_mlp_bias,
        pool_query,
        word_norm_gain,
        word_norm_bias,
        word_mlp_gain,
        word_mlp_bias,
        language_table.T,
    )
    flat = jnp.concatenate([part.astype(low).reshape(-1) for part in char_parts])
    flat_size = flat.shape[0]
    flat = jnp.pad(flat, (0, -flat_size % 2048))
    full = lax.all_gather(flat, BOTH, axis=0, tiled=False)
    unpacked, start = [], 0
    for part in char_parts:
        stop = start + part.size
        piece = full[:, start:stop].reshape((devices * part.shape[0],) + part.shape[1:])
        unpacked.append(piece)
        start = stop
    (
        qkv_char,
        out_char,
        up_char,
        down_char,
        proj_char,
        gain_attn,
        bias_attn,
        gain_mlp,
        bias_mlp,
        query_pool,
        gain_one,
        bias_one,
        gain_two,
        bias_two,
        table_t,
    ) = unpacked

    word_parts = (word_qkv, word_out.T, word_up, word_down.T)
    word_flat = jnp.concatenate([part.astype(low).reshape(-1, 128) for part in word_parts])
    word_full = lax.all_gather(word_flat, BOTH, axis=0, tiled=False)
    word_full = word_full.reshape(dp_size, mp_size, word_flat.shape[0], 128)
    word_weights, start = [], 0
    for part in word_parts:
        stop = start + part.size // 128
        piece = word_full[:, :, start:stop].reshape((dp_size, mp_size) + part.shape)
        if part.ndim == 3:
            piece = piece.transpose(2, 0, 3, 1, 4).reshape(3, model, model)
        else:
            piece = piece.transpose(0, 2, 1, 3)
            piece = piece.reshape(dp_size * part.shape[0], mp_size * part.shape[1])
        word_weights.append(piece)
        start = stop

    rows = word_count * chars
    states = char_states.reshape(rows, width)
    counts = char_counts.reshape(rows // GROUP, GROUP // chars)
    head_masks, word_masks, ones = mask_constants(width, chars)
    zero = jnp.zeros_like(gain_attn)
    vecs = jnp.stack(
        (gain_attn, bias_attn, gain_mlp, bias_mlp, query_pool, zero, zero, zero)
    ).astype(wide)
    cp, probs, co, y1, hidden, slope, y2, pi, pooled = char_forward(
        states,
        counts,
        (qkv_char, out_char, up_char, down_char, ones, vecs, head_masks, word_masks),
        chars,
    )

    sequences = max(1, word_count // LEN)
    first = (mp_index * word_count) // LEN
    language = lax.dynamic_slice_in_dim(language_group, first, sequences)
    language_hot = (language[:, None] == jnp.arange(langs)[None]).astype(wide)
    language_rows = jnp.sum(language_hot[:, :, None] * table_t.T.astype(wide)[None], axis=1)
    residual = word_states.astype(wide) + matmul(pooled, proj_char)
    residual = (
        residual.reshape(sequences, -1, model) + language_rows[:, None, :]
    ).reshape(word_count, model)
    norms = tuple(value.astype(wide) for value in (gain_one, bias_one, gain_two, bias_two))
    layer_output, grad_residual, word_grads, word_norm_grads = word_layer(
        residual, output_grad, word_weights, norms, mp_size, mp_index
    )
    grad_words = grad_residual.astype(low)
    sequence_grads = jnp.sum(grad_residual.reshape(sequences, -1, model), axis=1)
    grad_table = jnp.sum(language_hot[:, :, None] * sequence_grads[:, None, :], axis=0)

    pieces = []
    for part, grad in zip(word_parts, word_grads):
        if part.ndim == 3:
            grad = grad.reshape(3, dp_size, part.shape[1], mp_size, part.shape[2])
            grad = grad.transpose(3, 1, 0, 2, 4)
        else:
            grad = grad.reshape(dp_size, part.shape[0], mp_size, part.shape[1])
            grad = grad.transpose(2, 0, 1, 3)
        pieces.append(grad.astype(low).reshape(mp_size, dp_size, -1, 128))
    word_terms = jnp.concatenate(pieces, axis=2)
    word_terms = lax.psum_scatter(word_terms, "mp", scatter_dimension=0, tiled=True)
    word_terms = lax.psum_scatter(word_terms[0], "dp", scatter_dimension=0, tiled=True)[0]
    word_shares, start = [], 0
    for part in word_parts:
        stop = start + part.size // 128
        word_shares.append(word_terms[start:stop].reshape(part.shape).astype(wide))
        start = stop

    grad_proj = mm(pooled, grad_words, TN)
    grad_pooled = mm(grad_words, proj_char, NT).reshape(word_count, 1, width)
    grad_y1, grad_up, grad_down_t, mlp_vecs = char_mlp_back(
        y1, y2, pi, grad_pooled, hidden, slope, (up_char.T, down_char.T, vecs, ones), chars
    )
    mlp_vecs = jnp.sum(mlp_vecs, axis=1)
    early = (
        grad_up,
        grad_down_t.T,
        grad_proj,
        mlp_vecs[0],
        mlp_vecs[1],
        mlp_vecs[2],
        word_norm_grads[0],
        word_norm_grads[1],
        word_norm_grads[2],
        word_norm_grads[3],
        grad_table.T,
    )
    early_terms = jnp.concatenate([blocks_of(part, devices) for part in early], axis=1)
    early_size = early_terms.shape[1]
    early_terms = jnp.pad(early_terms, ((0, 0), (0, -early_size % 1024)))
    early_terms = lax.psum_scatter(early_terms, BOTH, scatter_dimension=0, tiled=True)[0]
    grad_chars, grad_qkv, grad_out, attn_vecs = char_attn_back(
        states, cp, probs, co, grad_y1, (qkv_char.T, out_char.T, vecs, head_masks, word_masks), chars
    )
    attn_vecs = jnp.sum(attn_vecs, axis=1)
    late = (grad_qkv, grad_out, attn_vecs[0], attn_vecs[1])
    late_terms = jnp.concatenate([blocks_of(part, devices) for part in late], axis=1)
    late_terms = jnp.pad(late_terms, ((0, 0), (0, -late_terms.shape[1] % 1024)))
    late_terms = lax.psum_scatter(late_terms, BOTH, scatter_dimension=0, tiled=True)[0]

    def take(terms, parts):
        shares, start = [], 0
        for part in parts:
            stop = start + part.size // devices
            shape = (part.shape[0] // devices,) + part.shape[1:]
            shares.append(terms[start:stop].reshape(shape))
            start = stop
        return shares

    (
        g_up,
        g_down,
        g_proj,
        g_query,
        g_gain_mlp,
        g_bias_mlp,
        g_gain_one,
        g_bias_one,
        g_gain_two,
        g_bias_two,
        g_table_t,
    ) = take(early_terms, early)
    g_qkv, g_out, g_gain_attn, g_bias_attn = take(late_terms, late)
    return (
        layer_output,
        grad_chars.reshape(char_states.shape),
        grad_words,
        g_gain_attn,
        g_bias_attn,
        g_qkv,
        g_out,
        g_gain_mlp,
        g_bias_mlp,
        g_up,
        g_down,
        g_query,
        g_proj,
        g_table_t.T,
        g_gain_one,
        g_bias_one,
        word_shares[0],
        word_shares[1].T,
        g_gain_two,
        g_bias_two,
        word_shares[2],
        word_shares[3].T,
    )


def fits(dp, mp, words, model, width, chars, hidden_width, langs):
    count = dp * mp
    return (
        words == LEN
        and mp % 2 == 0
        and model == 128 * mp
        and model // dp % 16 == 0
        and width == 256
        and width == 8 * count
        and hidden_width % (16 * count) == 0
        and GROUP % chars == 0
        and langs == 8
    )


def shards(*arrays):
    char_states, word_states = arrays[:2]
    dp, mp = lax.axis_size("dp"), lax.axis_size("mp")
    words, chars, width = char_states.shape
    model, hidden_width = word_states.shape[1], arrays[11].shape[1]
    if not fits(dp, mp, words, model, width, chars, hidden_width, arrays[15].shape[0]):
        return shards_general(*arrays)
    return shards_whole(*arrays)


def shards_whole(
    char_states,
    word_states,
    char_counts,
    language_group,
    output_grad,
    char_norm_gain,
    char_norm_bias,
    char_qkv,
    char_out,
    char_mlp_gain,
    char_mlp_bias,
    char_up,
    char_down,
    pool_query,
    char_proj,
    language_table,
    word_norm_gain,
    word_norm_bias,
    word_qkv,
    word_out,
    word_mlp_gain,
    word_mlp_bias,
    word_up,
    word_down,
):
    low, wide = jnp.bfloat16, jnp.float32
    dp, mp = lax.axis_size("dp"), lax.axis_size("mp")
    count = dp * mp
    index = lax.axis_index("dp") * mp + lax.axis_index("mp")
    words, chars, width = char_states.shape
    model = word_states.shape[1]
    langs = language_table.shape[0]
    hidden_width = char_up.shape[1]
    char_small = (char_norm_gain, char_norm_bias, char_mlp_gain, char_mlp_bias, pool_query)
    word_small = (word_norm_gain, word_norm_bias, word_mlp_gain, word_mlp_bias)
    small = jnp.concatenate(char_small + word_small + (language_table.reshape(-1),))
    small = jnp.pad(small, (0, 16 * 128 - small.shape[0])).reshape(16, 128)
    (
        qkv,
        qkv_t,
        out,
        out_t,
        up,
        up_t,
        down,
        down_t,
        proj,
        small_all,
        word_share,
    ) = gather_weights(
        dp,
        mp,
        (char_qkv, char_out, char_up, char_down, char_proj),
        small,
        (word_qkv, word_out.T, word_up, word_down.T),
    )
    word_weights = lax.all_gather(word_share, BOTH, axis=0, tiled=False)
    word_weights = word_weights.reshape(dp, mp, word_share.shape[0], 128)
    char_share, word_part = width // count, model // count
    first, second = 5 * char_share, 5 * char_share + 4 * word_part
    flat = small_all.reshape(count, -1).astype(wide)
    vecs = flat[:, :first].reshape(count, 5, char_share).transpose(1, 0, 2).reshape(5, width)
    norms = flat[:, first:second].reshape(count, 4, word_part).transpose(1, 0, 2)
    norms = norms.reshape(4, model)
    table = flat[:, second : second + langs * word_part].reshape(count, langs, word_part)
    table = table.transpose(1, 0, 2).reshape(langs, model)
    vecs = jnp.pad(vecs, ((0, 3), (0, 0)))

    rows = words * chars
    states = char_states.reshape(rows, width)
    counts = char_counts.reshape(rows // GROUP, GROUP // chars)
    head_masks, word_masks, ones = mask_constants(width, chars)
    cp, probs, co, y1, hidden, slope, y2, pi, pooled = char_forward(
        states,
        counts,
        (qkv, out, up, down, ones, vecs, head_masks, word_masks),
        chars,
    )

    language = lax.dynamic_slice_in_dim(language_group, lax.axis_index("mp"), 1)
    hot = (language == jnp.arange(langs)).astype(wide)[:, None]
    language_row = jnp.sum(hot * table, axis=0, keepdims=True)
    layer_output, grad_words, word_terms, grad_proj, grad_pooled, small_terms = word_layer_kernel(
        pooled,
        word_states,
        output_grad,
        language_row,
        jnp.broadcast_to(hot, (langs, 128)),
        proj,
        word_weights,
        norms,
        head_masks,
    )

    grad_y1, char_terms, g_word_qkv, g_word_out, g_word_up, g_word_down = char_mlp_back_exchange(
        y1, y2, pi, grad_pooled, hidden, slope, (up_t, down_t, vecs, ones), chars, (dp, mp),
        grad_proj, small_terms, word_terms,
    )
    grad_chars, g_qkv, g_out, g_up, g_down, g_proj, g_small, g_vecs = char_attn_back_exchange(
        states, cp, probs, co, grad_y1, (qkv_t, out_t, vecs, head_masks, word_masks), chars,
        (dp, mp), char_terms, hidden_width, model,
    )
    word_small = lax.dynamic_slice_in_dim(g_small[:12], index * word_part, word_part, 1)
    char_small = lax.dynamic_slice_in_dim(g_small[12:15, :width], index * char_share, char_share, 1)
    late_small = lax.dynamic_slice_in_dim(
        g_vecs[:4].reshape(2, width), index * char_share, char_share, 1
    )
    return (
        layer_output,
        grad_chars.reshape(char_states.shape),
        grad_words,
        late_small[0],
        late_small[1],
        g_qkv,
        g_out,
        char_small[1],
        char_small[2],
        g_up,
        g_down,
        char_small[0],
        g_proj,
        word_small[:langs],
        word_small[8],
        word_small[9],
        g_word_qkv,
        g_word_out.T,
        word_small[10],
        word_small[11],
        g_word_up,
        g_word_down.T,
    )


def solution(mesh):
    vector, rows = P(BOTH), P(BOTH, None)
    cube = P(BOTH, None, None)
    table = P(None, BOTH)
    words = (P(None, "dp", "mp"), P("mp", "dp"), P("dp", "mp"), P("mp", "dp"))
    char_weights = (
        vector, vector, rows, rows, vector, vector, rows, rows, vector, rows, table,
    )
    weights = char_weights + (
        vector, vector, words[0], words[1], vector, vector, words[2], words[3],
    )
    return jax.shard_map(
        shards,
        mesh=mesh,
        in_specs=(cube, rows, vector, P("dp"), rows) + weights,
        out_specs=(rows, cube, rows) + weights,
        check_vma=False,
    )
```

```python
import functools

import jax
import jax.numpy as jnp
import ml_dtypes
import numpy as np
from jax import lax
from jax.experimental import pallas as pl
from jax.experimental.pallas import tpu as pltpu
from jax.sharding import PartitionSpec as P

HEAD = 64
CHAR_HEADS = 4
LEN = 1024
GROUP = 128
SUB = 512
CHUNK = 512
SHARES = 9
WORD_PARTS = 4


NORM_EPS = 1e-05
NEG_FILL = -1000000000.0
BOTH = ("dp", "mp")
MESH = pl.DeviceIdType.MESH

LOGIT = (
    0.7978697123195114,
    0.036392286136226214,
    -8.782649734580825e-05,
    -3.669345726473906e-05,
    1.4250064727244771e-06,
)

EXP2_SCALE = HEAD ** (-0.5) * 1.4426950408889634
NN = (((1,), (0,)), ((), ()))
NT = (((1,), (1,)), ((), ()))
TN = (((0,), (0,)), ((), ()))


def mm(first_arg, second_arg, dims=NN):
    return lax.dot_general(first_arg, second_arg, dims, preferred_element_type=jnp.float32)


def matmul(first_arg, second_arg):
    return jnp.dot(first_arg, second_arg, preferred_element_type=jnp.float32)


def low_sum(pattern, first_arg, second_arg):
    return jnp.einsum(pattern, first_arg, second_arg, preferred_element_type=jnp.float32)


def standardize(values):
    centred = values - jnp.mean(values, axis=-1, keepdims=True)
    inverse = lax.rsqrt(jnp.mean(centred * centred, axis=-1, keepdims=True) + NORM_EPS)
    return (centred * inverse, inverse)


def apply_norm(values, gain_value, bias_value):
    unit_rows, inverse = standardize(values)
    normed = (unit_rows * gain_value + bias_value).astype(jnp.bfloat16)
    return (unit_rows, inverse, normed)


def norm_back(grad_out, unit_rows, inverse, gain_value):
    grad_unit = grad_out * gain_value
    inner_sum = jnp.mean(grad_unit * unit_rows, axis=-1, keepdims=True)
    return inverse * (
        grad_unit - jnp.mean(grad_unit, axis=-1, keepdims=True) - unit_rows * inner_sum
    )


def gelu_pair(values):
    square = values * values
    logit = square * LOGIT[4] + LOGIT[3]
    for term in LOGIT[2::-1]:
        logit = logit * square + term
    normal = jnp.tanh(logit * values) * 0.5 + 0.5
    density = jnp.exp2(square * -0.7213475204444817 - 1.3257480647361593)
    return (values * normal, values * density + normal)


def strips(function, size, *arrays):
    parts = [
        function(*(array[row : row + size] for array in arrays))
        for row in range(0, arrays[0].shape[0], size)
    ]
    return tuple(jnp.concatenate(part, axis=0) for part in zip(*parts))


def gelu_low(values):
    return strips(
        lambda strip: gelu_pair(strip.astype(jnp.bfloat16)), 64 * 256 // values.shape[1], values
    )


def split_two(values):
    high = values.astype(jnp.bfloat16)
    return (high, (values - high.astype(jnp.float32)).astype(jnp.bfloat16))


def fold_rows(values):
    return jnp.sum(values.reshape(values.shape[0] // 8, 8, values.shape[1]), axis=0)


class Place:
    def __init__(self, dp, mp):
        self.dp, self.mp, self.wide = dp, mp, mp // 2
        self.i, self.j = lax.axis_index("dp"), lax.axis_index("mp")
        self.x, self.core = self.j // 2, lax.rem(self.j, 2)

    def partner(self):
        return (self.i, 2 * self.x + 1 - self.core)

    def across(self, step):
        return (self.i, 2 * lax.rem(self.x + step, self.wide) + self.core)

    def along(self, step):
        return (lax.rem(self.i + step, self.dp), self.j)

    def greet(self):
        barrier = pltpu.get_barrier_semaphore()
        others = [self.partner()]
        others += [self.across(step) for step in range(1, self.wide)]
        others += [self.along(step) for step in range(1, self.dp)]
        for other in others:
            pl.semaphore_signal(barrier, inc=1, device_id=other, device_id_type=MESH)
        pl.semaphore_wait(barrier, len(others))


def remote(source, target, sems, index, device):
    return pltpu.make_async_remote_copy(
        src_ref=source,
        dst_ref=target,
        send_sem=sems[0].at[index],
        recv_sem=sems[1].at[index],
        device_id=device,
        device_id_type=MESH,
    )


class ScatterSum:
    def __init__(self, place, blocks, local, one, two, three, sems, part=0, parts=1):
        self.place, self.blocks, self.local = place, blocks, local
        self.one, self.two, self.three, self.sems = one, two, three, sems
        size = blocks.shape[2] // parts
        self.span = slice(part * size, (part + 1) * size)
        self.sem = part * copies_of(place.dp, place.mp)

    def first(self):
        place = self.place
        return [
            remote(
                self.blocks.at[2 * e + 1 - place.core, :, self.span],
                self.one.at[e, :, self.span],
                self.sems,
                self.sem + e,
                place.partner(),
            )
            for e in range(place.wide)
        ]

    def second(self):
        place = self.place
        return [
            remote(
                self.one.at[lax.rem(place.x + step, place.wide), :, self.span],
                self.two.at[step - 1, :, self.span],
                self.sems,
                self.sem + place.wide + step - 1,
                place.across(step),
            )
            for step in range(1, place.wide)
        ]

    def third(self):
        place = self.place
        return [
            remote(
                self.one.at[place.x, lax.rem(place.i + step, place.dp), self.span],
                self.three.at[step - 1, self.span],
                self.sems,
                self.sem + 2 * place.wide - 1 + step - 1,
                place.along(step),
            )
            for step in range(1, place.dp)
        ]

    def start(self):
        for copy in self.first():
            copy.start()

    def go_across(self):
        place, span = self.place, self.span
        for copy in self.first():
            copy.wait()

        @pl.loop(0, place.dp)
        def _(row):
            for e in range(place.wide):
                own = self.local(e, row, span).astype(jnp.float32)
                total = self.one[e, row, span].astype(jnp.float32) + own
                self.one[e, row, span] = total.astype(jnp.bfloat16)

        for copy in self.second():
            copy.start()

    def go_along(self):
        place, span = self.place, self.span
        for copy in self.second():
            copy.wait()

        @pl.loop(0, place.dp)
        def _(row):
            total = self.one[place.x, row, span].astype(jnp.float32)
            for step in range(1, place.wide):
                total = total + self.two[step - 1, row, span].astype(jnp.float32)
            self.one[place.x, row, span] = total.astype(jnp.bfloat16)

        for copy in self.third():
            copy.start()

    def finish(self):
        place = self.place
        for copy in self.third():
            copy.wait()

        def own(rows):
            total = self.one[place.x, place.i, rows].astype(jnp.float32)
            for step in range(1, place.dp):
                total = total + self.three[step - 1, rows].astype(jnp.float32)
            return total

        return own


def copies_of(dp, mp):
    return 2 * (mp // 2) - 1 + dp - 1


def scatter_scratch(dp, mp, n, parts=1):
    wide = mp // 2
    copies = copies_of(dp, mp) * parts
    return [
        pltpu.VMEM((wide, dp, n, 128), jnp.bfloat16),
        pltpu.VMEM((max(1, wide - 1), dp, n, 128), jnp.bfloat16),
        pltpu.VMEM((dp - 1, n, 128), jnp.bfloat16),
        pltpu.SemaphoreType.DMA((copies,)),
        pltpu.SemaphoreType.DMA((copies,)),
    ]


def put_pairs(target, first_row, columns):
    mp, dp = target.shape[0], target.shape[1]
    rows = columns.shape[0] // (mp * dp)
    for pair in range(columns.shape[1] // 256):
        both = [
            columns[:, 256 * pair + 128 * c : 256 * pair + 128 * c + 128].reshape(
                dp, mp, rows, 128
            )
            for c in range(2)
        ]
        both = jnp.concatenate(both, axis=2).astype(jnp.bfloat16)
        spot = slice(first_row + 2 * rows * pair, first_row + 2 * rows * (pair + 1))
        for j in range(mp):
            target[j, :, spot, :] = both[:, j]


def gather_kernel(dp, mp, *refs):
    gather_body(dp, mp, *refs[:6], refs[6:15], *refs[15:])


def gather_body(
    dp,
    mp,
    qkv_ref,
    out_ref,
    up_ref,
    down_ref,
    proj_ref,
    table_ref,
    small_refs,
    word_qkv_ref,
    word_out_ref,
    word_up_ref,
    word_down_ref,
    qkv_all,
    qkv_t_all,
    out_all,
    out_t_all,
    up_all,
    up_t_all,
    down_all,
    down_t_all,
    proj_all,
    vecs_all,
    norms_all,
    table_all,
    word_share,
    held,
    tile,
    sends,
    arrivals,
):
    place = Place(dp, mp)
    low = jnp.bfloat16
    i, j = place.i, place.j
    row = 0
    for part in (qkv_ref, out_ref, up_ref, proj_ref):
        for pair in range(part.shape[1] // 256):
            both = [part[:, 256 * pair + 128 * c : 256 * pair + 128 * c + 128] for c in range(2)]
            held[i, j, row : row + 16, :] = jnp.concatenate(both, axis=0).astype(low)
            row += 16
    down_rows = down_ref.shape[0]
    for c in range(2):
        held[i, j, row : row + down_rows, :] = down_ref[:, 128 * c : 128 * c + 128].astype(low)
        row += down_rows
    word_part, char_part = table_ref.shape[1], small_refs[0].shape[1]
    tile[...] = jnp.zeros_like(tile)
    tile[0:8, 0:word_part] = table_ref[...]
    for k in range(4):
        tile[8 + k : 9 + k, 0:word_part] = small_refs[5 + k][...]
        tile[12 + k : 13 + k, 0:char_part] = small_refs[k][...]
    tile[12:13, char_part : 2 * char_part] = small_refs[4][...]
    held[i, j, row : row + 16, :] = tile[...].astype(low)
    place.greet()
    sems = (sends, arrivals)
    wide = place.wide

    def share(step, e):
        return held.at[
            lax.rem(i + dp - step, dp), 2 * lax.rem(place.x + wide - e, wide) + place.core
        ]

    def other_core(step, e):
        return held.at[
            lax.rem(i + dp - step, dp), 2 * lax.rem(place.x + wide - e, wide) + 1 - place.core
        ]

    def along(step):
        return remote(held.at[i, j], held.at[i, j], sems, step - 1, place.along(step))

    def across(step, e):
        index = dp - 1 + step * (wide - 1) + e - 1
        return remote(share(step, 0), share(step, 0), sems, index, place.across(e))

    def over(step, e):
        index = dp - 1 + dp * (wide - 1) + step * wide + e
        return remote(share(step, e), share(step, e), sems, index, place.partner())

    for step in range(1, dp):
        along(step).start()
    for e in range(1, wide):
        across(0, e).start()
    over(0, 0).start()

    rows = word_up_ref.shape[0]
    for t in range(3):
        word_share[rows * t : rows * (t + 1), :] = word_qkv_ref[t].astype(low)
    word_share[3 * rows : 4 * rows, :] = word_out_ref[...].astype(low)
    blocks = word_up_ref.shape[1] // 128
    for c in range(blocks):
        spot = slice((4 + c) * rows, (5 + c) * rows)
        word_share[spot, :] = word_up_ref[:, 128 * c : 128 * c + 128].astype(low)
        spot = slice((4 + blocks + c) * rows, (5 + blocks + c) * rows)
        word_share[spot, :] = word_down_ref[:, 128 * c : 128 * c + 128].astype(low)

    for step in range(1, dp):
        along(step).wait_recv()
        for e in range(1, wide):
            across(step, e).start()
        over(step, 0).start()
    for step in range(dp):
        for e in range(1, wide):
            across(step, e).wait_recv()
            over(step, e).start()
    for step in range(dp):
        for e in range(wide):
            over(step, e).wait_recv()
    for step in range(1, dp):
        along(step).wait_send()
    for step in range(dp):
        for e in range(1, wide):
            across(step, e).wait_send()
        for e in range(wide):
            over(step, e).wait_send()

    count = dp * mp
    row = 0
    for target, target_t in (
        (qkv_all, qkv_t_all),
        (out_all, out_t_all),
        (up_all, up_t_all),
        (proj_all, None),
    ):
        for pair in range(target.shape[1] // 256):
            both = held[:, :, row : row + 16, :].reshape(count, 16, 128).astype(jnp.float32)
            row += 16
            for c in range(2):
                piece = both[:, 8 * c : 8 * c + 8].reshape(8 * count, 128).astype(low)
                spot = slice(256 * pair + 128 * c, 256 * pair + 128 * c + 128)
                target[:, spot] = piece
                if target_t is not None:
                    target_t[spot, :] = piece.T
    for c in range(2):
        piece = held[:, :, row : row + down_rows, :].reshape(count * down_rows, 128)
        row += down_rows
        down_all[:, 128 * c : 128 * c + 128] = piece
        down_t_all[128 * c : 128 * c + 128, :] = piece.T
    small = held[:, :, row : row + 16, :].reshape(count, 16, 128).astype(jnp.float32)
    lane = lax.broadcasted_iota(jnp.int32, (16, 128), 1)
    for part, width in ((word_part, norms_all.shape[1]), (char_part, vecs_all.shape[1])):
        per = 128 // part
        for b in range(width // 128):
            total = small[b * per]
            other = pltpu.roll(total, 128 - part, 1)
            for k in range(1, per):
                piece = small[b * per + k]
                total = jnp.where(lane // part == k, pltpu.roll(piece, part * k, 1), total)
                moved = pltpu.roll(piece, part * (k - 1), 1) if k > 1 else piece
                other = jnp.where(lane // part == k, moved, other)
            cols = slice(128 * b, 128 * b + 128)
            if part == word_part:
                table_all[:, cols] = total[0:8]
                norms_all[:, cols] = total[8:12]
            else:
                vecs_all[0:4, cols] = total[12:16]
                vecs_all[4:5, cols] = other[12:13]
                vecs_all[5:8, cols] = jnp.zeros((3, 128), jnp.float32)


def gather_weights(dp, mp, parts, table, small, word_parts):
    low = jnp.bfloat16
    qkv, out, up, down, proj = parts
    count = dp * mp
    width = qkv.shape[0] * count
    hidden = up.shape[1]
    model = proj.shape[1]
    rows = (qkv.shape[1] + out.shape[1] + up.shape[1] + proj.shape[1]) // 128 * 8
    rows += 2 * down.shape[0] + 16
    word_rows = sum(part.size for part in word_parts) // 128
    copies = dp - 1 + dp * (mp // 2 - 1) + dp * (mp // 2)
    shapes = (
        (width, 3 * width),
        (3 * width, width),
        (width, width),
        (width, width),
        (width, hidden),
        (hidden, width),
        (hidden, width),
        (width, hidden),
        (width, model),
        (8, width),
        (4, model),
        (8, model),
        (word_rows, 128),
    )
    wide = (9, 10, 11)
    arrays = (qkv, out, up, down, proj, table, *small, *word_parts)
    return pl.pallas_call(
        functools.partial(gather_kernel, dp, mp),
        grid=(1,),
        in_specs=[once(array.shape) for array in arrays],
        out_specs=[once(shape) for shape in shapes],
        out_shape=[
            jax.ShapeDtypeStruct(shape, jnp.float32 if k in wide else low)
            for k, shape in enumerate(shapes)
        ],
        scratch_shapes=[
            pltpu.VMEM((dp, mp, rows, 128), low),
            pltpu.VMEM((16, 128), jnp.float32),
            pltpu.SemaphoreType.DMA((copies,)),
            pltpu.SemaphoreType.DMA((copies,)),
        ],
        compiler_params=pltpu.CompilerParams(
            collective_id=0, has_side_effects=True, vmem_limit_bytes=60 * 1024 * 1024
        ),
        name="gather_weights",
    )(*arrays)


def head_rows(rows, masks):
    return jnp.concatenate([rows * masks[h : h + 1] for h in range(CHAR_HEADS)], axis=0)


def gather_diagonal(square, lane_word, chars):
    words = square.shape[1] // chars
    blocks = square.reshape(CHAR_HEADS, words, chars, square.shape[1])
    kept = blocks[:, 0]
    for word in range(1, words):
        kept = jnp.where(lane_word == word, blocks[:, word], kept)
    return kept


def spread_diagonal(kept, word_masks, chars):
    words = kept.shape[2] // chars
    parts = [kept * word_masks[word : word + 1] for word in range(words)]
    return jnp.stack(parts, axis=1)


def norm_strips(values, gain_value, bias_value):
    return strips(lambda strip: apply_norm(strip, gain_value, bias_value), 64, values)


def char_forward_kernel(
    chars,
    chars_ref,
    count_ref,
    qkv_ref,
    out_ref,
    up_ref,
    down_ref,
    ones_ref,
    vecs_ref,
    head_mask_ref,
    word_mask_ref,
    cp_ref,
    probs_ref,
    co_ref,
    y1_ref,
    hidden_ref,
    slope_ref,
    y2_ref,
    pi_ref,
    pooled_ref,
):
    rows, width = chars_ref.shape
    low, wide = jnp.bfloat16, jnp.float32
    lane_word = lax.broadcasted_iota(jnp.int32, (1, 1, GROUP), 2) // chars
    key_slot = lax.broadcasted_iota(jnp.int32, (1, chars, GROUP), 1).astype(wide)
    words = rows // chars
    step = pl.program_id(0)
    counts = count_ref[pl.ds(step * words // 128, 1), :].astype(wide)
    word = lax.broadcasted_iota(jnp.int32, (rows // GROUP, 128), 1) - lax.rem(step * words, 128)
    group = lax.broadcasted_iota(jnp.int32, (rows // GROUP, 128), 0)
    counts = jnp.where(word // (GROUP // chars) == group, counts, 0.0)
    repeats = 128 * chars // GROUP
    spread = jnp.concatenate([word_mask_ref[...].astype(wide)] * repeats, axis=0).astype(low)
    lane_counts = mm(counts.astype(low), spread)
    row_slot = lax.rem(lax.broadcasted_iota(jnp.int32, (GROUP, GROUP), 0), chars).astype(wide)
    masks = head_mask_ref[...]
    word_masks = word_mask_ref[...]
    block = SUB
    parts = up_ref.shape[1] // CHUNK

    def project(s):
        span = slice(s * block, (s + 1) * block)
        states = chars_ref[span, :].astype(wide)
        _, _, normed = norm_strips(states, vecs_ref[0:1, :], vecs_ref[1:2, :])
        cp_ref[span, :] = mm(normed, qkv_ref[...]).astype(low)

    def groups_of(s):
        return [slice(row, row + GROUP) for row in range(s * block, (s + 1) * block, GROUP)]

    scores, probs = {}, {}

    def attend_scores(s):
        scores[s] = []
        for span in groups_of(s):
            keys = head_rows(cp_ref[span, width : 2 * width], masks)
            square = mm(keys, cp_ref[span, 0:width], NT)
            scores[s].append(gather_diagonal(square, lane_word, chars))

    def attend_probs(s):
        probs[s] = []
        for span, score in zip(groups_of(s), scores[s]):
            group = span.start // GROUP
            score = jnp.where(
                key_slot < lane_counts[group : group + 1], score * EXP2_SCALE, NEG_FILL
            )
            powers = jnp.exp2(score - jnp.max(score, axis=1, keepdims=True))
            share = 1.0 / jnp.sum(powers, axis=1, keepdims=True)
            probs[s].append((powers * share).astype(low))
            probs_ref[group] = probs[s][-1].reshape(CHAR_HEADS * chars, GROUP)

    def attend_values(s):
        for span, prob in zip(groups_of(s), probs[s]):
            values = head_rows(cp_ref[span, 2 * width : 3 * width], masks)
            spread = spread_diagonal(prob, word_masks, chars)
            spread = spread.reshape(CHAR_HEADS * GROUP, GROUP)
            co_ref[span, :] = mm(spread, values, TN).astype(low)

    def middle(s):
        span = slice(s * block, (s + 1) * block)
        after_attn = chars_ref[span, :].astype(wide) + mm(co_ref[span, :], out_ref[...])
        y1_ref[span, :] = after_attn
        return norm_strips(after_attn, vecs_ref[2:3, :], vecs_ref[3:4, :])[2]

    def pool_scores(s):
        query = vecs_ref[4:5, :] * EXP2_SCALE
        high, low_part = strips(lambda strip: split_two(strip * query), 64, totals[s])
        return mm(high, ones_ref[...]) + mm(low_part, ones_ref[...])

    def pool(s, scores):
        total = totals[s]
        pooled = []
        for k in range(block // GROUP):
            group = s * block // GROUP + k
            spot = slice(k * GROUP, (k + 1) * GROUP)
            span = slice(s * block + k * GROUP, s * block + (k + 1) * GROUP)
            counts = jnp.broadcast_to(lane_counts[group : group + 1], (GROUP, GROUP)).T
            valid = row_slot < counts
            halves = []
            for half in range(width // GROUP):
                cols = slice(half * GROUP, (half + 1) * GROUP)
                score = jnp.where(valid, scores[spot, cols], NEG_FILL)
                score = score.reshape(GROUP // chars, chars, GROUP)
                powers = jnp.exp2(score - jnp.max(score, axis=1, keepdims=True))
                pi = powers * (1.0 / jnp.sum(powers, axis=1, keepdims=True))
                pi_ref[span, cols] = pi.reshape(GROUP, GROUP).astype(low)
                grid = total[spot, cols].reshape(GROUP // chars, chars, GROUP)
                halves.append(jnp.sum(pi * grid, axis=1))
            pooled.append(jnp.concatenate(halves, axis=1))
        words = block // chars
        pooled_ref[s * words : (s + 1) * words, :] = jnp.concatenate(pooled, axis=0).astype(low)

    count = rows // block
    normed, totals, hiddens = {}, {}, {}

    def up(s, part):
        if part == 0:
            normed[s] = middle(s)
        return mm(normed[s], up_ref[:, part * CHUNK : (part + 1) * CHUNK])

    def activate(s, part, current):
        span, cols = slice(s * block, (s + 1) * block), slice(part * CHUNK, (part + 1) * CHUNK)
        hidden, slope = gelu_low(current)
        hidden_ref[span, cols] = hidden
        slope_ref[span, cols] = slope
        hiddens[s] = hidden

    def down(s, part):
        span, cols = slice(s * block, (s + 1) * block), slice(part * CHUNK, (part + 1) * CHUNK)
        term = mm(hiddens[s], down_ref[cols, :])
        totals[s] = term if part == 0 else totals[s] + term
        if part == parts - 1:
            totals[s] = totals[s] + y1_ref[span, :]
            y2_ref[span, :] = totals[s]

    for first in range(0, count, 2):
        pair = range(first, min(first + 2, count))
        for s in pair:
            project(s)
            attend_scores(s)
        for s in pair:
            attend_probs(s)
            attend_values(s)
        order = [(s, part) for part in range(parts) for s in pair]
        ahead = [up(*order[0])]
        pools = []
        for place, (s, part) in enumerate(order):
            if place + 1 < len(order):
                ahead.append(up(*order[place + 1]))
            activate(s, part, ahead[place])
            down(s, part)
            if part == parts - 1:
                pools.append((s, pool_scores(s)))
                if len(pools) > 1:
                    pool(*pools[-2])
        pool(*pools[-1])


def char_mlp_back_kernel(
    chars,
    exchange,
    y1_ref,
    y2_ref,
    pi_ref,
    grad_pooled_ref,
    hidden_ref,
    slope_ref,
    up_t_ref,
    down_t_ref,
    vecs_ref,
    ones_ref,
    *others,
):
    rows, width = y1_ref.shape
    words = rows // chars
    if exchange is None:
        grad_y1_ref, grad_up_ref, grad_down_t_ref, grad_vecs_ref = others
    else:
        (
            grad_proj_ref,
            word_small_ref,
            word_terms_ref,
            grad_y1_ref,
            char_terms_ref,
            word_qkv_ref,
            word_out_ref,
            word_up_ref,
            word_down_ref,
            grad_up_ref,
            grad_down_t_ref,
            grad_vecs_ref,
            local_ref,
            local_sem,
            one_ref,
            two_ref,
            three_ref,
            sends,
            arrivals,
        ) = others
        place = Place(*exchange)
        totals_word = [
            ScatterSum(
                place,
                word_terms_ref,
                lambda e, row, span: local_ref[e, row, span],
                one_ref,
                two_ref,
                three_ref,
                (sends, arrivals),
                part,
                WORD_PARTS,
            )
            for part in range(WORD_PARTS)
        ]
        own = [
            pltpu.make_async_copy(
                word_terms_ref.at[2 * e + place.core], local_ref.at[e], local_sem.at[e]
            )
            for e in range(place.wide)
        ]
        step, last = pl.program_id(0), pl.num_programs(0) - 1

        @pl.when(step == 0)
        def _():
            place.greet()
            for total in totals_word:
                total.start()
            for copy in own:
                copy.start()

        for part, total in enumerate(totals_word):

            @pl.when(step == (1 + part) * last // 15)
            def _(part=part, total=total):
                if part == 0:
                    for copy in own:
                        copy.wait()
                total.go_across()

            @pl.when(step == (4 + 2 * part) * last // 15)
            def _(total=total):
                total.go_along()

    @pl.when(pl.program_id(0) == 0)
    def _():
        grad_up_ref[...] = jnp.zeros_like(grad_up_ref)
        grad_down_t_ref[...] = jnp.zeros_like(grad_down_t_ref)
        grad_vecs_ref[...] = jnp.zeros_like(grad_vecs_ref)

    low, wide = jnp.bfloat16, jnp.float32
    block = SUB
    count, parts = rows // block, hidden_ref.shape[1] // CHUNK
    query = vecs_ref[4:5, :]
    per = 64 // chars

    def pool_back(s):
        spots = [
            (slice(row, row + 64), slice(row // chars, row // chars + per))
            for row in range(s * block, (s + 1) * block, 64)
        ]
        split = [
            split_two(
                (y2_ref[span, :].reshape(per, chars, width) * grad_pooled_ref[span_words]).reshape(
                    64, width
                )
            )
            for span, span_words in spots
        ]
        high, rest = (jnp.concatenate(side, axis=0) for side in zip(*split))
        grad_pi = mm(high, ones_ref[...]) + mm(rest, ones_ref[...])
        wide_parts, low_parts, query_sum = [], [], None
        for k, (span, span_words) in enumerate(spots):
            pi = pi_ref[span, :].astype(wide).reshape(per, chars, width)
            part = grad_pi[64 * k : 64 * (k + 1)].reshape(per, chars, width)
            inner = jnp.sum(pi * part, axis=1, keepdims=True)
            grad_scores = pi * (part - inner) * HEAD ** (-0.5)
            grid = y2_ref[span, :].reshape(per, chars, width)
            term = fold_rows((grad_scores * grid).reshape(64, width))
            query_sum = term if query_sum is None else query_sum + term
            grad = (pi * grad_pooled_ref[span_words] + grad_scores * query).reshape(64, width)
            wide_parts.append(grad)
            low_parts.append(grad.astype(low))
        grad_vecs_ref[0] += query_sum
        return jnp.concatenate(wide_parts, axis=0), jnp.concatenate(low_parts, axis=0)

    def norm_again(s):
        span = slice(s * block, (s + 1) * block)
        return norm_strips(y1_ref[span, :], vecs_ref[2:3, :], vecs_ref[3:4, :])

    def feed_back(s, branch):
        span = slice(s * block, (s + 1) * block)
        grads, total = [], None
        ahead = mm(branch, down_t_ref[:, 0:CHUNK])
        for part in range(parts):
            cols = slice(part * CHUNK, (part + 1) * CHUNK)
            current = ahead
            if part + 1 < parts:
                ahead = mm(branch, down_t_ref[:, (part + 1) * CHUNK : (part + 2) * CHUNK])
            (grad_pre,) = strips(
                lambda strip, slope: (strip.astype(low) * slope,),
                32,
                current,
                slope_ref[span, cols],
            )
            grads.append(grad_pre)
            term = mm(grad_pre, up_t_ref[cols, :])
            total = term if total is None else total + term
        return grads, total

    def norm_finish(s, grad_normed, unit, inverse, grad_y2):
        span = slice(s * block, (s + 1) * block)
        gain = vecs_ref[2:3, :]
        gain_sum, bias_sum = None, None
        for row in range(0, block, 64):
            spot = slice(row, row + 64)
            part, part_unit = grad_normed[spot], unit[spot]
            one, two = fold_rows(part * part_unit), fold_rows(part)
            gain_sum = one if gain_sum is None else gain_sum + one
            bias_sum = two if bias_sum is None else bias_sum + two
            grad_y1_ref[s * block + row : s * block + row + 64, :] = grad_y2[spot] + norm_back(
                part, part_unit, inverse[spot], gain
            )
        grad_vecs_ref[1] += gain_sum
        grad_vecs_ref[2] += bias_sum

    pooled, norms, grads, totals = {}, {}, {}, {}
    pooled[0] = pool_back(0)
    norms[0] = norm_again(0)
    for s in range(count):
        grads[s], totals[s] = feed_back(s, pooled[s][1])
        if s + 1 < count:
            pooled[s + 1] = pool_back(s + 1)
            norms[s + 1] = norm_again(s + 1)
    branch_t = jnp.concatenate([pooled[s][1] for s in range(count)], axis=0).T
    normed_t = jnp.concatenate([norms[s][2] for s in range(count)], axis=0).T
    for part in range(parts):
        cols = slice(part * CHUNK, (part + 1) * CHUNK)
        grad_down_t_ref[:, cols] += mm(branch_t, hidden_ref[:, cols])
        grad_pre = jnp.concatenate([grads[s][part] for s in range(count)], axis=0)
        grad_up_ref[:, cols] += mm(normed_t, grad_pre)
    for s in range(count):
        norm_finish(s, totals[s], norms[s][0], norms[s][1], pooled[s][0])
    if exchange is None:
        return

    @pl.when(step == last)
    def _():
        low = jnp.bfloat16
        share = hidden_ref.shape[1] // (place.dp * place.mp)
        put_pairs(char_terms_ref, 0, grad_up_ref[...])
        row = hidden_ref.shape[1] // 16
        for c in range(2):
            piece = grad_down_t_ref[128 * c : 128 * c + 128, :].T
            piece = piece.reshape(place.dp, place.mp, share, 128).astype(low)
            for j in range(place.mp):
                char_terms_ref[j, :, row : row + share, :] = piece[:, j]
            row += share
        put_pairs(char_terms_ref, row, grad_proj_ref[...])
        row += grad_proj_ref.shape[1] // 16
        sums = [jnp.sum(grad_vecs_ref[k], axis=0, keepdims=True) for k in range(3)]
        small_row = lax.broadcasted_iota(jnp.int32, (16, 128), 0)
        for b in range(word_small_ref.shape[0]):
            piece = word_small_ref[b]
            if b < 2:
                for k in range(3):
                    piece = jnp.where(
                        small_row == 12 + k, sums[k][:, 128 * b : 128 * b + 128], piece
                    )
            piece = jnp.broadcast_to(piece.astype(low), (place.dp, 16, 128))
            for j in range(place.mp):
                char_terms_ref[j, :, row : row + 16, :] = piece
            row += 16
        for total in totals_word:
            result = total.finish()
        block = word_up_ref.shape[0]
        for t in range(3):
            word_qkv_ref[t] = result(slice(block * t, block * (t + 1)))
        word_out_ref[...] = result(slice(3 * block, 4 * block))
        count = word_up_ref.shape[1] // 128
        for c in range(count):
            cols = slice(128 * c, 128 * c + 128)
            word_up_ref[:, cols] = result(slice((4 + c) * block, (5 + c) * block))
            spot = slice((4 + count + c) * block, (5 + count + c) * block)
            word_down_ref[:, cols] = result(spot)


def char_attn_back_kernel(
    chars,
    exchange,
    chars_ref,
    cp_ref,
    probs_ref,
    co_ref,
    grad_y1_ref,
    qkv_t_ref,
    out_t_ref,
    vecs_ref,
    head_mask_ref,
    word_mask_ref,
    *others,
):
    rows, width = chars_ref.shape
    if exchange is None:
        (
            grad_chars_ref,
            grad_qkv_ref,
            grad_out_ref,
            grad_vecs_ref,
            grad_cp_ref,
            grad_co_ref,
        ) = others
    else:
        (
            early_terms_ref,
            grad_chars_ref,
            share_qkv_ref,
            share_out_ref,
            share_up_ref,
            share_down_ref,
            share_proj_ref,
            share_small_ref,
            share_vecs_ref,
            grad_cp_ref,
            grad_co_ref,
            grad_qkv_ref,
            grad_out_ref,
            grad_vecs_ref,
            local_ref,
            local_sem,
            late_terms_ref,
        ) = others[:17]
        early_refs, late_refs = others[17:22], others[22:27]
        place = Place(*exchange)
        early = ScatterSum(
            place,
            early_terms_ref,
            lambda e, row, span: local_ref[e, row, span],
            *early_refs[:3],
            early_refs[3:],
        )
        late = ScatterSum(
            place,
            late_terms_ref,
            lambda e, row, span: late_terms_ref[2 * e + place.core, row, span],
            *late_refs[:3],
            late_refs[3:],
        )
        own = [
            pltpu.make_async_copy(
                early_terms_ref.at[2 * e + place.core], local_ref.at[e], local_sem.at[e]
            )
            for e in range(place.wide)
        ]
        step, last = pl.program_id(0), pl.num_programs(0) - 1

        @pl.when(step == 0)
        def _():
            place.greet()
            early.start()
            for copy in own:
                copy.start()

        @pl.when(step == last // 15)
        def _():
            for copy in own:
                copy.wait()
            early.go_across()

        @pl.when(step == last // 3)
        def _():
            early.go_along()

    @pl.when(pl.program_id(0) == 0)
    def _():
        grad_qkv_ref[...] = jnp.zeros_like(grad_qkv_ref)
        grad_out_ref[...] = jnp.zeros_like(grad_out_ref)
        grad_vecs_ref[...] = jnp.zeros_like(grad_vecs_ref)

    low, wide = jnp.bfloat16, jnp.float32
    lane_word = lax.broadcasted_iota(jnp.int32, (1, 1, GROUP), 2) // chars
    masks = head_mask_ref[...]
    word_masks = word_mask_ref[...]
    scale = HEAD ** (-0.5)
    block = SUB
    count = rows // block

    def out_back(s):
        span = slice(s * block, (s + 1) * block)
        branch = grad_y1_ref[span, :].astype(low)
        grad_co_ref[span, :] = mm(branch, out_t_ref[...]).astype(low)
        return branch

    def norm_again(s):
        span = slice(s * block, (s + 1) * block)
        return norm_strips(
            chars_ref[span, :].astype(wide), vecs_ref[0:1, :], vecs_ref[1:2, :]
        )

    def side_by_side(spread):
        return jnp.concatenate([spread[h] for h in range(CHAR_HEADS)], axis=1)

    def groups_of(s):
        return [slice(row, row + GROUP) for row in range(s * block, (s + 1) * block, GROUP)]

    grad_probs, grad_scores = {}, {}

    def back_probs(s):
        grad_probs[s] = []
        for span in groups_of(s):
            values = head_rows(cp_ref[span, 2 * width : 3 * width], masks)
            square = mm(values, grad_co_ref[span, :], NT)
            grad_probs[s].append(gather_diagonal(square, lane_word, chars))

    def back_scores(s):
        grad_scores[s] = []
        for span, part in zip(groups_of(s), grad_probs[s]):
            probs = probs_ref[span.start // GROUP].reshape(CHAR_HEADS, chars, GROUP)
            spread = spread_diagonal(probs, word_masks, chars)
            spread = spread.reshape(CHAR_HEADS, GROUP, GROUP)
            grad_values = mm(side_by_side(spread), head_rows(grad_co_ref[span, :], masks))
            grad_cp_ref[span, 2 * width : 3 * width] = grad_values.astype(low)
            probs = probs.astype(wide)
            inner = jnp.sum(part * probs, axis=1, keepdims=True)
            grad_scores[s].append((probs * (part - inner)).astype(low))

    def back_keys(s):
        for span, part in zip(groups_of(s), grad_scores[s]):
            spread = spread_diagonal(part, word_masks, chars)
            spread = spread.reshape(CHAR_HEADS, GROUP, GROUP)
            queries = head_rows(cp_ref[span, 0:width], masks)
            grad_keys = mm(side_by_side(spread), queries) * scale
            grad_cp_ref[span, width : 2 * width] = grad_keys.astype(low)
            keys = head_rows(cp_ref[span, width : 2 * width], masks)
            grad_queries = mm(spread.reshape(CHAR_HEADS * GROUP, GROUP), keys, TN) * scale
            grad_cp_ref[span, 0:width] = grad_queries.astype(low)

    def project_back(s):
        span = slice(s * block, (s + 1) * block)
        return mm(grad_cp_ref[span, :], qkv_t_ref[...])

    def norm_finish(s, grad_normed, unit, inverse):
        gain = vecs_ref[0:1, :]
        gain_sum, bias_sum = None, None
        for row in range(0, block, 64):
            spot, span = slice(row, row + 64), slice(s * block + row, s * block + row + 64)
            part, part_unit = grad_normed[spot], unit[spot]
            one, two = fold_rows(part * part_unit), fold_rows(part)
            gain_sum = one if gain_sum is None else gain_sum + one
            bias_sum = two if bias_sum is None else bias_sum + two
            grad = grad_y1_ref[span, :] + norm_back(part, part_unit, inverse[spot], gain)
            grad_chars_ref[span, :] = grad.astype(low)
        grad_vecs_ref[0] += gain_sum
        grad_vecs_ref[1] += bias_sum

    branches, norms, totals = [], {}, {}
    for s in range(count):
        branches.append(out_back(s))
        back_probs(s)
    norms[0] = norm_again(0)
    for s in range(count):
        back_scores(s)
        back_keys(s)
        if s + 1 < count:
            norms[s + 1] = norm_again(s + 1)
        totals[s] = project_back(s)
    grad_out_ref[...] += mm(co_ref[...].T, jnp.concatenate(branches, axis=0))
    normed_t = jnp.concatenate([norms[s][2] for s in range(count)], axis=0).T
    grad_qkv_ref[...] += mm(normed_t, grad_cp_ref[...])
    for s in range(count):
        norm_finish(s, totals[s], norms[s][0], norms[s][1])
    if exchange is None:
        return

    @pl.when(step == last)
    def _():
        low = jnp.bfloat16
        put_pairs(late_terms_ref, 0, grad_qkv_ref[...])
        row = 3 * width // 16
        put_pairs(late_terms_ref, row, grad_out_ref[...])
        row += width // 16
        sums = [jnp.sum(grad_vecs_ref[k], axis=0, keepdims=True) for k in range(2)]
        small_row = lax.broadcasted_iota(jnp.int32, (16, 128), 0)
        piece = jnp.zeros((16, 128), jnp.float32)
        for k in range(2):
            for b in range(2):
                piece = jnp.where(
                    small_row == 2 * k + b, sums[k][:, 128 * b : 128 * b + 128], piece
                )
        piece = jnp.broadcast_to(piece.astype(low), (place.dp, 16, 128))
        for j in range(place.mp):
            late_terms_ref[j, :, row : row + 16, :] = piece
        late.start()
        result = early.finish()
        row = 0
        for target, share in (
            (share_up_ref, 8),
            (share_down_ref, share_down_ref.shape[0]),
            (share_proj_ref, 8),
            (share_small_ref, 16),
        ):
            for c in range(target.shape[1] // 128):
                target[:, 128 * c : 128 * c + 128] = result(slice(row, row + share))
                row += share
        late.go_across()
        late.go_along()
        result = late.finish()
        row = 0
        for target in (share_qkv_ref, share_out_ref):
            for c in range(target.shape[1] // 128):
                target[:, 128 * c : 128 * c + 128] = result(slice(row, row + 8))
                row += 8
        share_vecs_ref[...] = result(slice(row, row + 16))


def whole(shape):
    return pl.BlockSpec(shape, lambda step: (0,) * len(shape))


def once(shape):
    return pl.BlockSpec(shape, lambda step: (0,) * len(shape), pipeline_mode=pl.Buffered(1))


def blocked(shape):
    return pl.BlockSpec(shape, lambda step: (step,) + (0,) * (len(shape) - 1))


def params(megabytes):
    return pltpu.CompilerParams(
        dimension_semantics=("arbitrary",), vmem_limit_bytes=megabytes * 1024 * 1024
    )


def block_rows(rows, wanted):
    while rows % wanted:
        wanted //= 2
    return wanted


def char_forward(states, counts, weights, chars):
    rows, width = states.shape
    qkv, out, up, down, ones, vecs, head_masks, word_masks = weights
    block = block_rows(rows, 1024)
    words, groups = block // chars, block // GROUP
    low, wide = jnp.bfloat16, jnp.float32
    shapes = (
        ((rows, 3 * width), low),
        ((rows // GROUP, CHAR_HEADS * chars, GROUP), low),
        ((rows, width), low),
        ((rows, width), wide),
        ((rows, up.shape[1]), low),
        ((rows, up.shape[1]), low),
        ((rows, width), wide),
        ((rows, width), low),
        ((rows // chars, width), low),
    )
    blocks = (
        (block, 3 * width),
        (groups, CHAR_HEADS * chars, GROUP),
        (block, width),
        (block, width),
        (block, up.shape[1]),
        (block, up.shape[1]),
        (block, width),
        (block, width),
        (words, width),
    )
    flops = 2 * rows * width * (4 * width + 2 * up.shape[1] + 8 * width)
    return pl.pallas_call(
        functools.partial(char_forward_kernel, chars),
        grid=(rows // block,),
        in_specs=[
            blocked((block, width)),
            whole(counts.shape),
            whole(qkv.shape),
            whole(out.shape),
            whole(up.shape),
            whole(down.shape),
            whole(ones.shape),
            whole(vecs.shape),
            whole(head_masks.shape),
            whole(word_masks.shape),
        ],
        out_specs=[blocked(shape) for shape in blocks],
        out_shape=[jax.ShapeDtypeStruct(shape, kind) for shape, kind in shapes],
        compiler_params=params(56),
        cost_estimate=pl.CostEstimate(
            flops=flops, bytes_accessed=rows * width * 36, transcendentals=rows * width * 5
        ),
        name="char_forward",
    )(states, counts, qkv, out, up, down, ones, vecs, head_masks, word_masks)


def char_mlp_back(y1, y2, pi, grad_pooled, hidden, slope, weights, chars):
    rows, width = y1.shape
    up_t, down_t, vecs, ones = weights
    block = block_rows(rows, 1024)
    hidden_width = hidden.shape[1]
    wide = jnp.float32
    flops = 2 * rows * width * (4 * hidden_width + 2 * width)
    return pl.pallas_call(
        functools.partial(char_mlp_back_kernel, chars, None),
        grid=(rows // block,),
        in_specs=[
            blocked((block, width)),
            blocked((block, width)),
            blocked((block, width)),
            blocked((block // chars, 1, width)),
            blocked((block, hidden_width)),
            blocked((block, hidden_width)),
            whole(up_t.shape),
            whole(down_t.shape),
            whole(vecs.shape),
            whole(ones.shape),
        ],
        out_specs=[
            blocked((block, width)),
            whole((width, hidden_width)),
            whole((width, hidden_width)),
            whole((3, 8, width)),
        ],
        out_shape=[
            jax.ShapeDtypeStruct((rows, width), wide),
            jax.ShapeDtypeStruct((width, hidden_width), wide),
            jax.ShapeDtypeStruct((width, hidden_width), wide),
            jax.ShapeDtypeStruct((3, 8, width), wide),
        ],
        compiler_params=params(56),
        cost_estimate=pl.CostEstimate(
            flops=flops, bytes_accessed=rows * width * 30, transcendentals=0
        ),
        name="char_mlp_back",
    )(y1, y2, pi, grad_pooled, hidden, slope, up_t, down_t, vecs, ones)


def char_attn_back(states, cp, probs, co, grad_y1, weights, chars):
    rows, width = states.shape
    qkv_t, out_t, vecs, head_masks, word_masks = weights
    block = block_rows(rows, 1024)
    low, wide = jnp.bfloat16, jnp.float32
    flops = 2 * rows * width * 18 * width
    return pl.pallas_call(
        functools.partial(char_attn_back_kernel, chars, None),
        grid=(rows // block,),
        in_specs=[
            blocked((block, width)),
            blocked((block, 3 * width)),
            blocked((block // GROUP, CHAR_HEADS * chars, GROUP)),
            blocked((block, width)),
            blocked((block, width)),
            whole(qkv_t.shape),
            whole(out_t.shape),
            whole(vecs.shape),
            whole(head_masks.shape),
            whole(word_masks.shape),
        ],
        out_specs=[
            blocked((block, width)),
            whole((width, 3 * width)),
            whole((width, width)),
            whole((2, 8, width)),
        ],
        out_shape=[
            jax.ShapeDtypeStruct((rows, width), low),
            jax.ShapeDtypeStruct((width, 3 * width), wide),
            jax.ShapeDtypeStruct((width, width), wide),
            jax.ShapeDtypeStruct((2, 8, width), wide),
        ],
        scratch_shapes=[
            pltpu.VMEM((block, 3 * width), low),
            pltpu.VMEM((block, width), low),
        ],
        compiler_params=params(56),
        cost_estimate=pl.CostEstimate(
            flops=flops, bytes_accessed=rows * width * 18, transcendentals=0
        ),
        name="char_attn_back",
    )(states, cp, probs, co, grad_y1, qkv_t, out_t, vecs, head_masks, word_masks)


def char_mlp_back_exchange(
    y1, y2, pi, grad_pooled, hidden, slope, weights, chars, mesh_size, grad_proj, word_small, word_terms
):
    rows, width = y1.shape
    up_t, down_t, vecs, ones = weights
    dp, mp = mesh_size
    block = block_rows(rows, 1024)
    hidden_width = hidden.shape[1]
    low, wide = jnp.bfloat16, jnp.float32
    model = grad_proj.shape[1]
    flops = 2 * rows * width * (4 * hidden_width + 2 * width)
    char_rows = 2 * hidden_width // 16 + model // 16 + 16 * word_small.shape[0]
    n = word_terms.shape[2]
    share = model // dp
    outs = (
        ((rows, width), wide, blocked((block, width))),
        ((mp, dp, char_rows, 128), low, None),
        ((3, share, 128), wide, None),
        ((share, 128), wide, None),
        ((share, model), wide, None),
        ((share, model), wide, None),
    )
    return pl.pallas_call(
        functools.partial(char_mlp_back_kernel, chars, mesh_size),
        grid=(rows // block,),
        in_specs=[
            blocked((block, width)),
            blocked((block, width)),
            blocked((block, width)),
            blocked((block // chars, 1, width)),
            blocked((block, hidden_width)),
            blocked((block, hidden_width)),
            whole(up_t.shape),
            whole(down_t.shape),
            whole(vecs.shape),
            whole(ones.shape),
            whole(grad_proj.shape),
            whole(word_small.shape),
            pl.BlockSpec(memory_space=pl.ANY),
        ],
        out_specs=[spec or whole(shape) for shape, _, spec in outs],
        out_shape=[jax.ShapeDtypeStruct(shape, kind) for shape, kind, _ in outs],
        scratch_shapes=[
            pltpu.VMEM((width, hidden_width), wide),
            pltpu.VMEM((width, hidden_width), wide),
            pltpu.VMEM((3, 8, width), wide),
            pltpu.VMEM((mp // 2, dp, n, 128), low),
            pltpu.SemaphoreType.DMA((mp // 2,)),
        ]
        + scatter_scratch(dp, mp, n, WORD_PARTS),
        compiler_params=pltpu.CompilerParams(
            dimension_semantics=("arbitrary",),
            vmem_limit_bytes=60 * 1024 * 1024,
            collective_id=1,
            has_side_effects=True,
        ),
        cost_estimate=pl.CostEstimate(
            flops=flops, bytes_accessed=rows * width * 30, transcendentals=0
        ),
        name="char_mlp_back",
    )(
        y1, y2, pi, grad_pooled, hidden, slope, up_t, down_t, vecs, ones,
        grad_proj, word_small, word_terms,
    )


def char_attn_back_exchange(
    states, cp, probs, co, grad_y1, weights, chars, mesh_size, early_terms, hidden_width, model
):
    rows, width = states.shape
    qkv_t, out_t, vecs, head_masks, word_masks = weights
    dp, mp = mesh_size
    count = dp * mp
    block = block_rows(rows, 1024)
    low, wide = jnp.bfloat16, jnp.float32
    flops = 2 * rows * width * 18 * width
    n = early_terms.shape[2]
    late = 4 * width // 16 + 16
    outs = (
        ((rows, width), low, blocked((block, width))),
        ((width // count, 3 * width), wide, None),
        ((width // count, width), wide, None),
        ((width // count, hidden_width), wide, None),
        ((hidden_width // count, width), wide, None),
        ((width // count, model), wide, None),
        ((16, model), wide, None),
        ((16, 128), wide, None),
    )
    return pl.pallas_call(
        functools.partial(char_attn_back_kernel, chars, mesh_size),
        grid=(rows // block,),
        in_specs=[
            blocked((block, width)),
            blocked((block, 3 * width)),
            blocked((block // GROUP, CHAR_HEADS * chars, GROUP)),
            blocked((block, width)),
            blocked((block, width)),
            whole(qkv_t.shape),
            whole(out_t.shape),
            whole(vecs.shape),
            whole(head_masks.shape),
            whole(word_masks.shape),
            pl.BlockSpec(memory_space=pl.ANY),
        ],
        out_specs=[spec or whole(shape) for shape, _, spec in outs],
        out_shape=[jax.ShapeDtypeStruct(shape, kind) for shape, kind, _ in outs],
        scratch_shapes=[
            pltpu.VMEM((block, 3 * width), low),
            pltpu.VMEM((block, width), low),
            pltpu.VMEM((width, 3 * width), wide),
            pltpu.VMEM((width, width), wide),
            pltpu.VMEM((2, 8, width), wide),
            pltpu.VMEM((mp // 2, dp, n, 128), low),
            pltpu.SemaphoreType.DMA((mp // 2,)),
            pltpu.VMEM((mp, dp, late, 128), low),
        ]
        + scatter_scratch(dp, mp, n)
        + scatter_scratch(dp, mp, late),
        compiler_params=pltpu.CompilerParams(
            dimension_semantics=("arbitrary",),
            vmem_limit_bytes=56 * 1024 * 1024,
            collective_id=2,
            has_side_effects=True,
        ),
        cost_estimate=pl.CostEstimate(
            flops=flops, bytes_accessed=rows * width * 18, transcendentals=0
        ),
        name="char_attn_back",
    )(states, cp, probs, co, grad_y1, qkv_t, out_t, vecs, head_masks, word_masks, early_terms)


def share_kernel(large_count, places_ref, large_ref, *refs):
    shares, refs = refs[:SHARES], refs[SHARES:]
    small_ref, vecs_ref, large_out_ref, *targets = refs[: 3 + SHARES + 10]
    sems = refs[-1]
    size = large_ref.shape[0] // large_count
    copies = [
        pltpu.make_async_copy(
            large_ref.at[pl.ds(k * size, size)], large_out_ref.at[pl.ds(k * size, size)], sems.at[k]
        )
        for k in range(large_count)
    ]
    for copy in copies:
        copy.start()
    for source, target in zip(shares, targets):
        target[...] = source[...]
    table_out, word_outs, char_outs = targets[SHARES], targets[SHARES + 1 : SHARES + 5], targets[SHARES + 5 :]
    model, width = small_ref.shape[1], 2 * vecs_ref.shape[1]
    word_part, char_part = table_out.shape[1], char_outs[0].shape[1]
    words = pltpu.roll(small_ref[...], places_ref[0], 1)
    table_out[...] = words[0:8, 0:word_part]
    for k, target in enumerate(word_outs):
        target[...] = words[8 + k : 9 + k, 0:word_part]
    early = small_ref[12:15, 0:width]
    late = jnp.concatenate([vecs_ref[0:1, :], vecs_ref[1:2, :]], axis=1)
    late_two = jnp.concatenate([vecs_ref[2:3, :], vecs_ref[3:4, :]], axis=1)
    rows = jnp.concatenate([early, late, late_two, jnp.zeros((3, width), jnp.float32)], axis=0)
    rows = pltpu.roll(rows, places_ref[1], 1)
    for k, target in enumerate(char_outs):
        target[...] = rows[k : k + 1, 0:char_part]
    for copy in copies:
        copy.wait()


def hand_out(places, large, shares, small, vecs, word_part, char_part):
    wide = jnp.float32
    outs = [(share.shape, wide) for share in shares]
    outs += [((8, word_part), wide)] + [((1, word_part), wide)] * 4 + [((1, char_part), wide)] * 5
    anywhere = pl.BlockSpec(memory_space=pl.ANY)
    count = 8
    return pl.pallas_call(
        functools.partial(share_kernel, count),
        grid=(1,),
        in_specs=[pl.BlockSpec(memory_space=pltpu.SMEM), anywhere]
        + [once(array.shape) for array in (*shares, small, vecs)],
        out_specs=[anywhere] + [once(shape) for shape, _ in outs],
        out_shape=[jax.ShapeDtypeStruct(large.shape, large.dtype)]
        + [jax.ShapeDtypeStruct(shape, kind) for shape, kind in outs],
        scratch_shapes=[pltpu.SemaphoreType.DMA((count,))],
        compiler_params=params(60),
        name="hand_out",
    )(places, large, *shares, small, vecs)


def word_kernel(
    pooled_ref,
    words_ref,
    cotangent_ref,
    language_ref,
    table_ref,
    proj_ref,
    weights_ref,
    norms_ref,
    head_mask_ref,
    layer_ref,
    grad_words_ref,
    terms_ref,
    grad_proj_ref,
    grad_pooled_ref,
    small_ref,
    residual_ref,
    normed_one_ref,
    packed_ref,
    probs_ref,
    mixed_ref,
    middle_ref,
    normed_two_ref,
    hidden_ref,
    slope_ref,
    total_ref,
    grad_keys_ref,
    grad_values_ref,
    sums_ref,
):
    low, wide = jnp.bfloat16, jnp.float32
    length, model = words_ref.shape
    dp, mp = weights_ref.shape[:2]
    share = model // dp
    row_block, large = 256, 512
    blocks = length // row_block
    hidden_width = hidden_ref.shape[1]
    up_blocks = hidden_width // mp // 128
    scale = HEAD ** (-0.5)
    up_base, down_base = 4 * share, (4 + up_blocks) * share

    def weight(base):
        pieces = [
            weights_ref[:, j, pl.ds(base, share), :].reshape(model, 128) for j in range(mp)
        ]
        return jnp.concatenate(pieces, axis=1)

    def wide_weight(base, j):
        pieces = [
            weights_ref[:, j, base + c * share : base + (c + 1) * share, :].reshape(model, 128)
            for c in range(up_blocks)
        ]
        return jnp.concatenate(pieces, axis=1)

    def put(base, grad):
        for j in range(mp):
            piece = grad[:, 128 * j : 128 * j + 128].reshape(dp, share, 128).astype(low)
            terms_ref[j, :, pl.ds(base, share), :] = piece

    def put_wide(base, j, grad):
        for c in range(up_blocks):
            piece = grad[:, 128 * c : 128 * c + 128].reshape(dp, share, 128).astype(low)
            terms_ref[j, :, base + c * share : base + (c + 1) * share, :] = piece

    def norm(k):
        return norms_ref[k : k + 1, :]

    sums_ref[...] = jnp.zeros_like(sums_ref)
    language = language_ref[0]

    spans = [slice(row, row + large) for row in range(0, length, large)]
    for span in spans:
        residual = words_ref[span, :].astype(wide) + mm(pooled_ref[span, :], proj_ref[...])
        residual = residual + table_ref[pl.ds(language, 1), :]
        residual_ref[span, :] = residual
        normed_one_ref[span, :] = norm_strips(residual, norm(0), norm(1))[2]

    @pl.loop(0, 3)
    def _(t):
        whole_weight = weight(pl.multiple_of(t * share, share))
        for span in spans:
            packed_ref[t, span, :] = mm(normed_one_ref[span, :], whole_weight).astype(low)

    causal = lax.broadcasted_iota(jnp.int32, (row_block, row_block), 0) <= (
        lax.broadcasted_iota(jnp.int32, (row_block, row_block), 1)
    )

    @pl.loop(0, model // 128)
    def _(pair):
        lanes = pl.ds(pl.multiple_of(pair * 128, 128), 128)
        values_t = packed_ref[2, :, lanes].T

        def scores_of(block, h):
            stop = (block + 1) * row_block
            queries = packed_ref[0, block * row_block : stop, lanes]
            keys = packed_ref[1, 0:stop, lanes] * head_mask_ref[h : h + 1, 0:128]
            return mm(keys, queries, NT)

        order = [(block, h) for block in range(blocks) for h in range(2)]
        ahead = scores_of(*order[0])
        mixed = []
        for place, (block, h) in enumerate(order):
            scores = ahead * EXP2_SCALE
            if place + 1 < len(order):
                ahead = scores_of(*order[place + 1])
            stop = (block + 1) * row_block
            first = block * (block + 1) // 2 * row_block
            near = jnp.where(causal, scores[stop - row_block :], NEG_FILL)
            scores = jnp.concatenate([scores[: stop - row_block], near]) if block else near
            powers = jnp.exp2(scores - jnp.max(scores, axis=0, keepdims=True))
            probs = powers * (1.0 / jnp.sum(powers, axis=0, keepdims=True))
            probs = probs.astype(low)
            probs_ref[2 * pair + h, first : first + stop, :] = probs
            mixed.append(mm(values_t[HEAD * h : HEAD * (h + 1), 0:stop], probs))
            if h == 1:
                both = jnp.concatenate(mixed, axis=0).T.astype(low)
                mixed_ref[block * row_block : stop, lanes] = both
                mixed = []

    out_t = weight(3 * share)
    for span in spans:
        middle = residual_ref[span, :] + mm(mixed_ref[span, :], out_t, NT)
        middle_ref[span, :] = middle
        total_ref[span, :] = middle
        normed_two_ref[span, :] = norm_strips(middle, norm(2), norm(3))[2]

    def columns_of(j):
        return pl.ds(pl.multiple_of(j * 128 * up_blocks, 128 * up_blocks), 128 * up_blocks)

    @pl.loop(0, mp)
    def _(j):
        up, down = wide_weight(up_base, j), wide_weight(down_base, j)
        before = [mm(normed_two_ref[span, :], up) for span in spans]
        for span, part in zip(spans, before):
            hidden, slope = gelu_low(part)
            hidden_ref[span, columns_of(j)] = hidden
            slope_ref[span, columns_of(j)] = slope
            total_ref[span, :] += mm(hidden, down, NT)

    for span in spans:
        layer_ref[span, :] = total_ref[span, :].astype(low)
        total_ref[span, :] = jnp.zeros((large, model), wide)

    cotangent_t = cotangent_ref[...].T
    normed_t = normed_two_ref[...].T

    @pl.loop(0, mp)
    def _(j):
        up, down = wide_weight(up_base, j), wide_weight(down_base, j)
        before = [mm(cotangent_ref[span, :], down) for span in spans]
        put_wide(down_base, j, mm(cotangent_t, hidden_ref[:, columns_of(j)]))
        for span, part in zip(spans, before):
            (grad_pre,) = strips(
                lambda strip, slope: (strip.astype(low) * slope,),
                32,
                part,
                slope_ref[span, columns_of(j)],
            )
            slope_ref[span, columns_of(j)] = grad_pre
            total_ref[span, :] += mm(grad_pre, up, NT)
        put_wide(up_base, j, mm(normed_t, slope_ref[:, columns_of(j)]))

    for span in spans:

        def finish(part, middle, cotangent):
            unit, inverse = standardize(middle)
            sums_ref[2] += fold_rows(part * unit)
            sums_ref[3] += fold_rows(part)
            grad = cotangent.astype(wide) + norm_back(part, unit, inverse, norm(2))
            return grad, grad.astype(low)

        grad_middle, branch = strips(
            finish, 64, total_ref[span, :], middle_ref[span, :], cotangent_ref[span, :]
        )
        middle_ref[span, :] = grad_middle
        normed_two_ref[span, :] = branch
    put(3 * share, mm(normed_two_ref[...].T, mixed_ref[...]))
    for span in spans:
        mixed_ref[span, :] = mm(normed_two_ref[span, :], out_t).astype(low)


    @pl.loop(0, model // 128)
    def _(pair):
        lanes = pl.ds(pl.multiple_of(pair * 128, 128), 128)
        grad_keys_ref[...] = jnp.zeros_like(grad_keys_ref)
        grad_values_ref[...] = jnp.zeros_like(grad_values_ref)
        keys_t = packed_ref[1, :, lanes].T

        def grad_probs_of(block, h):
            stop = (block + 1) * row_block
            grad_mixed = mixed_ref[block * row_block : stop, lanes]
            values = packed_ref[2, 0:stop, lanes] * head_mask_ref[h : h + 1, 0:128]
            return mm(values, grad_mixed, NT)

        order = [(block, h) for block in range(blocks) for h in range(2)]
        ahead = grad_probs_of(*order[0])
        sides = []
        for place, (block, h) in enumerate(order):
            grad_probs = ahead
            if place + 1 < len(order):
                ahead = grad_probs_of(*order[place + 1])
            stop = (block + 1) * row_block
            span = slice(block * row_block, stop)
            first = block * (block + 1) // 2 * row_block
            probs = probs_ref[2 * pair + h, first : first + stop, :]
            probs_wide = probs.astype(wide)
            inner = jnp.sum(grad_probs * probs_wide, axis=0, keepdims=True)
            grad_scores = (probs_wide * (grad_probs - inner)).astype(low)
            grad_queries = mm(keys_t[HEAD * h : HEAD * (h + 1), 0:stop], grad_scores)
            sides.append((probs, grad_scores, grad_queries))
            if h == 1:
                probs, grad_scores, grad_queries = (list(side) for side in zip(*sides))
                sides = []
                masks = [head_mask_ref[k : k + 1, 0:128] for k in range(2)]
                grad_mixed, queries = mixed_ref[span, lanes], packed_ref[0, span, lanes]
                grad_values_ref[0:stop, :] += mm(
                    jnp.concatenate(probs, axis=1),
                    jnp.concatenate([grad_mixed * mask for mask in masks], axis=0),
                )
                grad_keys_ref[0:stop, :] += mm(
                    jnp.concatenate(grad_scores, axis=1),
                    jnp.concatenate([queries * mask for mask in masks], axis=0),
                )
                both = jnp.concatenate(grad_queries, axis=0) * scale
                packed_ref[0, span, lanes] = both.T.astype(low)
        packed_ref[1, :, lanes] = (grad_keys_ref[...] * scale).astype(low)
        packed_ref[2, :, lanes] = grad_values_ref[...].astype(low)

    normed_t = normed_one_ref[...].T
    for span in spans:
        total_ref[span, :] = jnp.zeros((large, model), wide)

    @pl.loop(0, 3)
    def _(t):
        base = pl.multiple_of(t * share, share)
        put(base, mm(normed_t, packed_ref[t]))
        whole_weight = weight(base)
        for span in spans:
            total_ref[span, :] += mm(packed_ref[t, span, :], whole_weight, NT)

    for span in spans:

        def finish(part, residual, grad_middle):
            unit, inverse = standardize(residual)
            sums_ref[0] += fold_rows(part * unit)
            sums_ref[1] += fold_rows(part)
            grad = grad_middle + norm_back(part, unit, inverse, norm(0))
            sums_ref[4] += fold_rows(grad)
            return (grad.astype(low),)

        (grad,) = strips(finish, 64, total_ref[span, :], residual_ref[span, :], middle_ref[span, :])
        grad_words_ref[span, :] = grad
        grad_pooled_ref[span] = mm(grad, proj_ref[...], NT)[:, None, :]

    grad_proj_ref[...] = mm(pooled_ref[...].T, grad_words_ref[...])

    sums = [jnp.sum(sums_ref[k], axis=0, keepdims=True) for k in range(5)]
    small_row = lax.broadcasted_iota(jnp.int32, (8, 128), 0)
    for b in range(model // 128):
        cols = slice(128 * b, 128 * b + 128)
        small_ref[b, 0:8, :] = jnp.where(small_row == language, sums[4][:, cols], 0.0)
        piece = jnp.zeros((8, 128), wide)
        for k in range(4):
            piece = jnp.where(small_row == k, sums[k][:, cols], piece)
        small_ref[b, 8:16, :] = piece


def word_layer_kernel(pooled, words, cotangent, language, table, proj, weights, norms, head_masks):
    low, wide = jnp.bfloat16, jnp.float32
    length, model = words.shape
    width = pooled.shape[1]
    dp, mp, n = weights.shape[:3]
    hidden_width = (n * dp // model - 4) // 2 * 128 * mp
    blocks = length // 256
    heads = model // HEAD
    arrays = (pooled, words, cotangent, language, table, proj, weights, norms, head_masks)
    outs = (
        ((length, model), low),
        ((length, model), low),
        ((mp, dp, n, 128), low),
        ((width, model), wide),
        ((length, 1, width), wide),
        ((model // 128, 16, 128), wide),
    )
    return pl.pallas_call(
        word_kernel,
        grid=(1,),
        in_specs=[
            pl.BlockSpec(memory_space=pltpu.SMEM) if array is language else once(array.shape)
            for array in arrays
        ],
        out_specs=[once(shape) for shape, _ in outs],
        out_shape=[jax.ShapeDtypeStruct(shape, kind) for shape, kind in outs],
        scratch_shapes=[
            pltpu.VMEM((length, model), wide),
            pltpu.VMEM((length, model), low),
            pltpu.VMEM((3, length, model), low),
            pltpu.VMEM((heads, blocks * (blocks + 1) // 2 * 256, 256), low),
            pltpu.VMEM((length, model), low),
            pltpu.VMEM((length, model), wide),
            pltpu.VMEM((length, model), low),
            pltpu.VMEM((length, hidden_width), low),
            pltpu.VMEM((length, hidden_width), low),
            pltpu.VMEM((length, model), wide),
            pltpu.VMEM((length, 128), wide),
            pltpu.VMEM((length, 128), wide),
            pltpu.VMEM((5, 8, model), wide),
        ],
        compiler_params=pltpu.CompilerParams(vmem_limit_bytes=62 * 1024 * 1024),
        cost_estimate=pl.CostEstimate(
            flops=40 * 10**9, bytes_accessed=20 * 2**20, transcendentals=10**7
        ),
        name="word_layer",
    )(*arrays)


def attend_forward(queries, key_block, values, allowed):
    scores = low_sum("bqhd,bkhd->bhqk", queries, key_block) * HEAD ** (-0.5)
    scores = jnp.where(allowed, scores, NEG_FILL)
    row_max = jnp.max(scores, axis=-1, keepdims=True)
    powers = jnp.exp(scores - row_max)
    row_total = jnp.sum(powers, axis=-1, keepdims=True)
    attn_probs = (powers / row_total).astype(jnp.bfloat16)
    attn_mixed = low_sum("bhqk,bkhd->bqhd", attn_probs, values).astype(jnp.bfloat16)
    return (attn_mixed, row_max + jnp.log(row_total))


def attend_backward(queries, key_block, values, allowed, log_total, grad_mixed):
    scale = HEAD ** (-0.5)
    scores = low_sum("bqhd,bkhd->bhqk", queries, key_block) * scale
    attn_probs = jnp.where(allowed, jnp.exp(scores - log_total), 0.0)
    grad_probs = low_sum("bqhd,bkhd->bhqk", grad_mixed, values)
    grad_values = low_sum("bhqk,bqhd->bkhd", attn_probs.astype(jnp.bfloat16), grad_mixed)
    inner_sum = jnp.sum(grad_probs * attn_probs, axis=-1, keepdims=True)
    grad_scores = (attn_probs * (grad_probs - inner_sum)).astype(jnp.bfloat16)
    grad_queries = low_sum("bhqk,bkhd->bqhd", grad_scores, key_block) * scale
    grad_keys = low_sum("bhqk,bqhd->bkhd", grad_scores, queries) * scale
    return (grad_queries, grad_keys, grad_values)


def word_layer(residual, grad_rows, weights, norms, mp_size, mp_index):
    qkv, out_t, up, down_t = weights
    gain_one, bias_one, gain_two, bias_two = norms
    rows, width = residual.shape
    low = jnp.bfloat16
    sequences, length = max(1, rows // LEN), min(rows, LEN)
    share = LEN // length
    groups = [[a * share + b for b in range(share)] for a in range(mp_size // share)]
    unit_one, inverse_one, normed_one = apply_norm(residual, gain_one, bias_one)
    packed = low_sum("rd,tdc->trc", normed_one, qkv).astype(low)
    packed = packed.reshape(3, sequences, length, width // HEAD, HEAD)
    keys = packed[1:]
    start = 0
    if share > 1:
        keys = lax.all_gather(keys, "mp", axis=2, tiled=True, axis_index_groups=groups)
        start = lax.rem(mp_index, share) * length
    allowed = (
        lax.broadcasted_iota(jnp.int32, (length, LEN), 1)
        <= lax.broadcasted_iota(jnp.int32, (length, LEN), 0) + start
    )[None, None]
    mixed, log_total = attend_forward(packed[0], keys[0], keys[1], allowed)
    mixed_rows = mixed.reshape(rows, width)
    middle = residual + mm(mixed_rows, out_t, NT)
    unit_two, inverse_two, normed_two = apply_norm(middle, gain_two, bias_two)
    hidden, slope = gelu_pair(matmul(normed_two, up))
    hidden = hidden.astype(low)
    layer_output = (middle + mm(hidden, down_t, NT)).astype(low)
    grad_wide = grad_rows.astype(jnp.float32)
    grad_down_t = mm(grad_rows, hidden, TN)
    grad_pre = (matmul(grad_rows, down_t) * slope).astype(low)
    grad_up = mm(normed_two, grad_pre, TN)
    grad_normed = mm(grad_pre, up, NT)
    grad_gain_two = jnp.sum(grad_normed * unit_two, axis=0)
    grad_bias_two = jnp.sum(grad_normed, axis=0)
    grad_middle = grad_wide + norm_back(grad_normed, unit_two, inverse_two, gain_two)
    branch = grad_middle.astype(low)
    grad_out_t = mm(branch, mixed_rows, TN)
    grad_mixed = matmul(branch, out_t).astype(low).reshape(sequences, length, -1, HEAD)
    grad_queries, grad_keys, grad_values = attend_backward(
        packed[0], keys[0], keys[1], allowed, log_total, grad_mixed
    )
    grad_keys = jnp.stack((grad_keys, grad_values), axis=0)
    if share > 1:
        grad_keys = lax.psum_scatter(
            grad_keys, "mp", scatter_dimension=2, tiled=True, axis_index_groups=groups
        )
    grad_packed = jnp.concatenate((grad_queries[None], grad_keys), axis=0)
    grad_packed = grad_packed.reshape(3, rows, width).astype(low)
    grad_qkv = low_sum("rd,trc->tdc", normed_one, grad_packed)
    grad_normed = low_sum("trc,tdc->rd", grad_packed, qkv)
    grad_gain_one = jnp.sum(grad_normed * unit_one, axis=0)
    grad_bias_one = jnp.sum(grad_normed, axis=0)
    grad_residual = grad_middle + norm_back(grad_normed, unit_one, inverse_one, gain_one)
    return (
        layer_output,
        grad_residual,
        (grad_qkv, grad_out_t, grad_up, grad_down_t),
        (grad_gain_one, grad_bias_one, grad_gain_two, grad_bias_two),
    )


def mask_constants(width, chars):
    head, word = np.arange(width) // HEAD, np.arange(GROUP) // chars
    head_masks = head[None] == np.arange(8)[:, None]
    word_masks = word[None] == np.arange(GROUP // chars)[:, None]
    ones = head[:, None] == head[None]
    return tuple(jnp.asarray(mask.astype(ml_dtypes.bfloat16)) for mask in (head_masks, word_masks, ones))


def blocks_of(array, count):
    return array.reshape(count, -1)


def shards_general(
    char_states,
    word_states,
    char_counts,
    language_group,
    output_grad,
    char_norm_gain,
    char_norm_bias,
    char_qkv,
    char_out,
    char_mlp_gain,
    char_mlp_bias,
    char_up,
    char_down,
    pool_query,
    char_proj,
    language_table,
    word_norm_gain,
    word_norm_bias,
    word_qkv,
    word_out,
    word_mlp_gain,
    word_mlp_bias,
    word_up,
    word_down,
):
    low, wide = jnp.bfloat16, jnp.float32
    dp_size, mp_size = lax.axis_size("dp"), lax.axis_size("mp")
    mp_index = lax.axis_index("mp")
    devices = dp_size * mp_size
    word_count, chars, width = char_states.shape
    model = word_states.shape[1]
    langs = language_table.shape[0]

    char_parts = (
        char_qkv,
        char_out,
        char_up,
        char_down,
        char_proj,
        char_norm_gain,
        char_norm_bias,
        char_mlp_gain,
        char_mlp_bias,
        pool_query,
        word_norm_gain,
        word_norm_bias,
        word_mlp_gain,
        word_mlp_bias,
        language_table.T,
    )
    flat = jnp.concatenate([part.astype(low).reshape(-1) for part in char_parts])
    flat_size = flat.shape[0]
    flat = jnp.pad(flat, (0, -flat_size % 2048))
    full = lax.all_gather(flat, BOTH, axis=0, tiled=False)
    unpacked, start = [], 0
    for part in char_parts:
        stop = start + part.size
        piece = full[:, start:stop].reshape((devices * part.shape[0],) + part.shape[1:])
        unpacked.append(piece)
        start = stop
    (
        qkv_char,
        out_char,
        up_char,
        down_char,
        proj_char,
        gain_attn,
        bias_attn,
        gain_mlp,
        bias_mlp,
        query_pool,
        gain_one,
        bias_one,
        gain_two,
        bias_two,
        table_t,
    ) = unpacked

    word_parts = (word_qkv, word_out.T, word_up, word_down.T)
    word_flat = jnp.concatenate([part.astype(low).reshape(-1, 128) for part in word_parts])
    word_full = lax.all_gather(word_flat, BOTH, axis=0, tiled=False)
    word_full = word_full.reshape(dp_size, mp_size, word_flat.shape[0], 128)
    word_weights, start = [], 0
    for part in word_parts:
        stop = start + part.size // 128
        piece = word_full[:, :, start:stop].reshape((dp_size, mp_size) + part.shape)
        if part.ndim == 3:
            piece = piece.transpose(2, 0, 3, 1, 4).reshape(3, model, model)
        else:
            piece = piece.transpose(0, 2, 1, 3)
            piece = piece.reshape(dp_size * part.shape[0], mp_size * part.shape[1])
        word_weights.append(piece)
        start = stop

    rows = word_count * chars
    states = char_states.reshape(rows, width)
    counts = char_counts.reshape(-1, 128)
    head_masks, word_masks, ones = mask_constants(width, chars)
    zero = jnp.zeros_like(gain_attn)
    vecs = jnp.stack(
        (gain_attn, bias_attn, gain_mlp, bias_mlp, query_pool, zero, zero, zero)
    ).astype(wide)
    cp, probs, co, y1, hidden, slope, y2, pi, pooled = char_forward(
        states,
        counts,
        (qkv_char, out_char, up_char, down_char, ones, vecs, head_masks, word_masks),
        chars,
    )

    sequences = max(1, word_count // LEN)
    first = (mp_index * word_count) // LEN
    language = lax.dynamic_slice_in_dim(language_group, first, sequences)
    language_hot = (language[:, None] == jnp.arange(langs)[None]).astype(wide)
    language_rows = jnp.sum(language_hot[:, :, None] * table_t.T.astype(wide)[None], axis=1)
    residual = word_states.astype(wide) + matmul(pooled, proj_char)
    residual = (
        residual.reshape(sequences, -1, model) + language_rows[:, None, :]
    ).reshape(word_count, model)
    norms = tuple(value.astype(wide) for value in (gain_one, bias_one, gain_two, bias_two))
    layer_output, grad_residual, word_grads, word_norm_grads = word_layer(
        residual, output_grad, word_weights, norms, mp_size, mp_index
    )
    grad_words = grad_residual.astype(low)
    sequence_grads = jnp.sum(grad_residual.reshape(sequences, -1, model), axis=1)
    grad_table = jnp.sum(language_hot[:, :, None] * sequence_grads[:, None, :], axis=0)

    pieces = []
    for part, grad in zip(word_parts, word_grads):
        if part.ndim == 3:
            grad = grad.reshape(3, dp_size, part.shape[1], mp_size, part.shape[2])
            grad = grad.transpose(3, 1, 0, 2, 4)
        else:
            grad = grad.reshape(dp_size, part.shape[0], mp_size, part.shape[1])
            grad = grad.transpose(2, 0, 1, 3)
        pieces.append(grad.astype(low).reshape(mp_size, dp_size, -1, 128))
    word_terms = jnp.concatenate(pieces, axis=2)
    word_terms = lax.psum_scatter(word_terms, "mp", scatter_dimension=0, tiled=True)
    word_terms = lax.psum_scatter(word_terms[0], "dp", scatter_dimension=0, tiled=True)[0]
    word_shares, start = [], 0
    for part in word_parts:
        stop = start + part.size // 128
        word_shares.append(word_terms[start:stop].reshape(part.shape).astype(wide))
        start = stop

    grad_proj = mm(pooled, grad_words, TN)
    grad_pooled = mm(grad_words, proj_char, NT).reshape(word_count, 1, width)
    grad_y1, grad_up, grad_down_t, mlp_vecs = char_mlp_back(
        y1, y2, pi, grad_pooled, hidden, slope, (up_char.T, down_char.T, vecs, ones), chars
    )
    mlp_vecs = jnp.sum(mlp_vecs, axis=1)
    early = (
        grad_up,
        grad_down_t.T,
        grad_proj,
        mlp_vecs[0],
        mlp_vecs[1],
        mlp_vecs[2],
        word_norm_grads[0],
        word_norm_grads[1],
        word_norm_grads[2],
        word_norm_grads[3],
        grad_table.T,
    )
    early_terms = jnp.concatenate([blocks_of(part, devices) for part in early], axis=1)
    early_size = early_terms.shape[1]
    early_terms = jnp.pad(early_terms, ((0, 0), (0, -early_size % 1024)))
    early_terms = lax.psum_scatter(early_terms, BOTH, scatter_dimension=0, tiled=True)[0]
    grad_chars, grad_qkv, grad_out, attn_vecs = char_attn_back(
        states, cp, probs, co, grad_y1, (qkv_char.T, out_char.T, vecs, head_masks, word_masks), chars
    )
    attn_vecs = jnp.sum(attn_vecs, axis=1)
    late = (grad_qkv, grad_out, attn_vecs[0], attn_vecs[1])
    late_terms = jnp.concatenate([blocks_of(part, devices) for part in late], axis=1)
    late_terms = jnp.pad(late_terms, ((0, 0), (0, -late_terms.shape[1] % 1024)))
    late_terms = lax.psum_scatter(late_terms, BOTH, scatter_dimension=0, tiled=True)[0]

    def take(terms, parts):
        shares, start = [], 0
        for part in parts:
            stop = start + part.size // devices
            shape = (part.shape[0] // devices,) + part.shape[1:]
            shares.append(terms[start:stop].reshape(shape))
            start = stop
        return shares

    (
        g_up,
        g_down,
        g_proj,
        g_query,
        g_gain_mlp,
        g_bias_mlp,
        g_gain_one,
        g_bias_one,
        g_gain_two,
        g_bias_two,
        g_table_t,
    ) = take(early_terms, early)
    g_qkv, g_out, g_gain_attn, g_bias_attn = take(late_terms, late)
    return (
        layer_output,
        grad_chars.reshape(char_states.shape),
        grad_words,
        g_gain_attn,
        g_bias_attn,
        g_qkv,
        g_out,
        g_gain_mlp,
        g_bias_mlp,
        g_up,
        g_down,
        g_query,
        g_proj,
        g_table_t.T,
        g_gain_one,
        g_bias_one,
        word_shares[0],
        word_shares[1].T,
        g_gain_two,
        g_bias_two,
        word_shares[2],
        word_shares[3].T,
    )


def fits(dp, mp, words, model, width, chars, hidden_width, langs):
    count = dp * mp
    return (
        words == LEN
        and mp % 2 == 0
        and model == 128 * mp
        and model // dp % 16 == 0
        and width == 256
        and width == 8 * count
        and hidden_width % (16 * count) == 0
        and GROUP % chars == 0
        and langs == 8
    )


def shards(*arrays):
    char_states, word_states = arrays[:2]
    dp, mp = lax.axis_size("dp"), lax.axis_size("mp")
    words, chars, width = char_states.shape
    model, hidden_width = word_states.shape[1], arrays[11].shape[1]
    if not fits(dp, mp, words, model, width, chars, hidden_width, arrays[15].shape[0]):
        return shards_general(*arrays)
    return shards_whole(*arrays)


def shards_whole(
    char_states,
    word_states,
    char_counts,
    language_group,
    output_grad,
    char_norm_gain,
    char_norm_bias,
    char_qkv,
    char_out,
    char_mlp_gain,
    char_mlp_bias,
    char_up,
    char_down,
    pool_query,
    char_proj,
    language_table,
    word_norm_gain,
    word_norm_bias,
    word_qkv,
    word_out,
    word_mlp_gain,
    word_mlp_bias,
    word_up,
    word_down,
):
    low, wide = jnp.bfloat16, jnp.float32
    dp, mp = lax.axis_size("dp"), lax.axis_size("mp")
    count = dp * mp
    index = lax.axis_index("dp") * mp + lax.axis_index("mp")
    words, chars, width = char_states.shape
    model = word_states.shape[1]
    langs = language_table.shape[0]
    hidden_width = char_up.shape[1]
    small = (char_norm_gain, char_norm_bias, char_mlp_gain, char_mlp_bias, pool_query)
    small += (word_norm_gain, word_norm_bias, word_mlp_gain, word_mlp_bias)
    (
        qkv,
        qkv_t,
        out,
        out_t,
        up,
        up_t,
        down,
        down_t,
        proj,
        vecs,
        norms,
        table,
        word_share,
    ) = gather_weights(
        dp,
        mp,
        (char_qkv, char_out, char_up, char_down, char_proj),
        language_table,
        tuple(value[None] for value in small),
        (word_qkv, word_out.T, word_up, word_down.T),
    )
    word_weights = lax.all_gather(word_share, BOTH, axis=0, tiled=False)
    word_weights = word_weights.reshape(dp, mp, word_share.shape[0], 128)
    char_share, word_part = width // count, model // count

    rows = words * chars
    states = char_states.reshape(rows, width)
    counts = char_counts.reshape(-1, 128)
    head_masks, word_masks, ones = mask_constants(width, chars)
    cp, probs, co, y1, hidden, slope, y2, pi, pooled = char_forward(
        states,
        counts,
        (qkv, out, up, down, ones, vecs, head_masks, word_masks),
        chars,
    )

    language = lax.dynamic_slice_in_dim(language_group, lax.axis_index("mp"), 1)
    layer_output, grad_words, word_terms, grad_proj, grad_pooled, small_terms = word_layer_kernel(
        pooled,
        word_states,
        output_grad,
        language,
        table,
        proj,
        word_weights,
        norms,
        head_masks,
    )

    grad_y1, char_terms, g_word_qkv, g_word_out, g_word_up, g_word_down = char_mlp_back_exchange(
        y1, y2, pi, grad_pooled, hidden, slope, (up_t, down_t, vecs, ones), chars, (dp, mp),
        grad_proj, small_terms, word_terms,
    )
    grad_chars, g_qkv, g_out, g_up, g_down, g_proj, g_small, g_vecs = char_attn_back_exchange(
        states, cp, probs, co, grad_y1, (qkv_t, out_t, vecs, head_masks, word_masks), chars,
        (dp, mp), char_terms, hidden_width, model,
    )
    places = jnp.stack(((model - index * word_part) % model, (width - index * char_share) % width))
    shares = (
        g_qkv, g_out, g_up, g_down, g_proj, g_word_qkv, g_word_out, g_word_up, g_word_down,
    )
    grad_chars, *shares = hand_out(
        places, grad_chars, shares, g_small, g_vecs, word_part, char_share
    )
    g_qkv, g_out, g_up, g_down, g_proj, g_word_qkv, g_word_out, g_word_up, g_word_down = shares[:9]
    g_table, *small_shares = shares[9:]
    norm_shares = [value[0] for value in small_shares]
    return (
        layer_output,
        grad_chars.reshape(char_states.shape),
        grad_words,
        norm_shares[7],
        norm_shares[8],
        g_qkv,
        g_out,
        norm_shares[5],
        norm_shares[6],
        g_up,
        g_down,
        norm_shares[4],
        g_proj,
        g_table,
        norm_shares[0],
        norm_shares[1],
        g_word_qkv,
        g_word_out.T,
        norm_shares[2],
        norm_shares[3],
        g_word_up,
        g_word_down.T,
    )


def solution(mesh):
    vector, rows = P(BOTH), P(BOTH, None)
    cube = P(BOTH, None, None)
    table = P(None, BOTH)
    words = (P(None, "dp", "mp"), P("mp", "dp"), P("dp", "mp"), P("mp", "dp"))
    char_weights = (
        vector, vector, rows, rows, vector, vector, rows, rows, vector, rows, table,
    )
    weights = char_weights + (
        vector, vector, words[0], words[1], vector, vector, words[2], words[3],
    )
    return jax.shard_map(
        shards,
        mesh=mesh,
        in_specs=(cube, rows, vector, P("dp"), rows) + weights,
        out_specs=(rows, cube, rows) + weights,
        check_vma=False,
    )
```

```python
import functools

import jax
import jax.numpy as jnp
import ml_dtypes
import numpy as np
from jax import lax
from jax.experimental import pallas as pl
from jax.experimental.pallas import tpu as pltpu
from jax.sharding import PartitionSpec as P

HEAD = 64
CHAR_HEADS = 4
LEN = 1024
GROUP = 128
SUB = 1024
CHUNK = 512
SHARES = 9
WORD_PARTS = 4


NORM_EPS = 1e-05
NEG_FILL = -1000000000.0
BOTH = ("dp", "mp")
MESH = pl.DeviceIdType.MESH

LOGIT = (
    0.7978697123195114,
    0.036392286136226214,
    -8.782649734580825e-05,
    -3.669345726473906e-05,
    1.4250064727244771e-06,
)

EXP2_SCALE = HEAD ** (-0.5) * 1.4426950408889634
NN = (((1,), (0,)), ((), ()))
NT = (((1,), (1,)), ((), ()))
TN = (((0,), (0,)), ((), ()))


def mm(first_arg, second_arg, dims=NN):
    return lax.dot_general(first_arg, second_arg, dims, preferred_element_type=jnp.float32)


def matmul(first_arg, second_arg):
    return jnp.dot(first_arg, second_arg, preferred_element_type=jnp.float32)


def low_sum(pattern, first_arg, second_arg):
    return jnp.einsum(pattern, first_arg, second_arg, preferred_element_type=jnp.float32)


def standardize(values):
    centred = values - jnp.mean(values, axis=-1, keepdims=True)
    inverse = lax.rsqrt(jnp.mean(centred * centred, axis=-1, keepdims=True) + NORM_EPS)
    return (centred * inverse, inverse)


def apply_norm(values, gain_value, bias_value):
    unit_rows, inverse = standardize(values)
    normed = (unit_rows * gain_value + bias_value).astype(jnp.bfloat16)
    return (unit_rows, inverse, normed)


def norm_back(grad_out, unit_rows, inverse, gain_value):
    grad_unit = grad_out * gain_value
    inner_sum = jnp.mean(grad_unit * unit_rows, axis=-1, keepdims=True)
    return inverse * (
        grad_unit - jnp.mean(grad_unit, axis=-1, keepdims=True) - unit_rows * inner_sum
    )


def gelu_pair(values):
    square = values * values
    logit = square * LOGIT[4] + LOGIT[3]
    for term in LOGIT[2::-1]:
        logit = logit * square + term
    normal = jnp.tanh(logit * values) * 0.5 + 0.5
    density = jnp.exp2(square * -0.7213475204444817 - 1.3257480647361593)
    return (values * normal, values * density + normal)


def strips(function, size, *arrays):
    parts = [
        function(*(array[row : row + size] for array in arrays))
        for row in range(0, arrays[0].shape[0], size)
    ]
    return tuple(jnp.concatenate(part, axis=0) for part in zip(*parts))


def gelu_low(values):
    return strips(
        lambda strip: gelu_pair(strip.astype(jnp.bfloat16)), 64 * 256 // values.shape[1], values
    )


def split_two(values):
    high = values.astype(jnp.bfloat16)
    return (high, (values - high.astype(jnp.float32)).astype(jnp.bfloat16))


def fold_rows(values):
    return jnp.sum(values.reshape(values.shape[0] // 8, 8, values.shape[1]), axis=0)


class Place:
    def __init__(self, dp, mp):
        self.dp, self.mp, self.wide = dp, mp, mp // 2
        self.i, self.j = lax.axis_index("dp"), lax.axis_index("mp")
        self.x, self.core = self.j // 2, lax.rem(self.j, 2)

    def partner(self):
        return (self.i, 2 * self.x + 1 - self.core)

    def across(self, step):
        return (self.i, 2 * lax.rem(self.x + step, self.wide) + self.core)

    def along(self, step):
        return (lax.rem(self.i + step, self.dp), self.j)

    def greet(self):
        barrier = pltpu.get_barrier_semaphore()
        others = [self.partner()]
        others += [self.across(step) for step in range(1, self.wide)]
        others += [self.along(step) for step in range(1, self.dp)]
        for other in others:
            pl.semaphore_signal(barrier, inc=1, device_id=other, device_id_type=MESH)
        pl.semaphore_wait(barrier, len(others))


def remote(source, target, sems, index, device):
    return pltpu.make_async_remote_copy(
        src_ref=source,
        dst_ref=target,
        send_sem=sems[0].at[index],
        recv_sem=sems[1].at[index],
        device_id=device,
        device_id_type=MESH,
    )


class ScatterSum:
    def __init__(self, place, blocks, local, one, two, three, sems, part=0, parts=1):
        self.place, self.blocks, self.local = place, blocks, local
        self.one, self.two, self.three, self.sems = one, two, three, sems
        size = blocks.shape[2] // parts
        self.span = slice(part * size, (part + 1) * size)
        self.sem = part * copies_of(place.dp, place.mp)

    def first(self):
        place = self.place
        return [
            remote(
                self.blocks.at[2 * e + 1 - place.core, :, self.span],
                self.one.at[e, :, self.span],
                self.sems,
                self.sem + e,
                place.partner(),
            )
            for e in range(place.wide)
        ]

    def second(self):
        place = self.place
        return [
            remote(
                self.one.at[lax.rem(place.x + step, place.wide), :, self.span],
                self.two.at[step - 1, :, self.span],
                self.sems,
                self.sem + place.wide + step - 1,
                place.across(step),
            )
            for step in range(1, place.wide)
        ]

    def third(self):
        place = self.place
        return [
            remote(
                self.one.at[place.x, lax.rem(place.i + step, place.dp), self.span],
                self.three.at[step - 1, self.span],
                self.sems,
                self.sem + 2 * place.wide - 1 + step - 1,
                place.along(step),
            )
            for step in range(1, place.dp)
        ]

    def start(self):
        for copy in self.first():
            copy.start()

    def go_across(self):
        place, span = self.place, self.span
        for copy in self.first():
            copy.wait()

        @pl.loop(0, place.dp)
        def _(row):
            for e in range(place.wide):
                own = self.local(e, row, span).astype(jnp.float32)
                total = self.one[e, row, span].astype(jnp.float32) + own
                self.one[e, row, span] = total.astype(jnp.bfloat16)

        for copy in self.second():
            copy.start()

    def go_along(self):
        place, span = self.place, self.span
        for copy in self.second():
            copy.wait()

        @pl.loop(0, place.dp)
        def _(row):
            total = self.one[place.x, row, span].astype(jnp.float32)
            for step in range(1, place.wide):
                total = total + self.two[step - 1, row, span].astype(jnp.float32)
            self.one[place.x, row, span] = total.astype(jnp.bfloat16)

        for copy in self.third():
            copy.start()

    def finish(self):
        place = self.place
        for copy in self.third():
            copy.wait()

        def own(rows):
            total = self.one[place.x, place.i, rows].astype(jnp.float32)
            for step in range(1, place.dp):
                total = total + self.three[step - 1, rows].astype(jnp.float32)
            return total

        return own


def copies_of(dp, mp):
    return 2 * (mp // 2) - 1 + dp - 1


def scatter_scratch(dp, mp, n, parts=1):
    wide = mp // 2
    copies = copies_of(dp, mp) * parts
    return [
        pltpu.VMEM((wide, dp, n, 128), jnp.bfloat16),
        pltpu.VMEM((max(1, wide - 1), dp, n, 128), jnp.bfloat16),
        pltpu.VMEM((dp - 1, n, 128), jnp.bfloat16),
        pltpu.SemaphoreType.DMA((copies,)),
        pltpu.SemaphoreType.DMA((copies,)),
    ]


def put_pairs(target, first_row, columns):
    mp, dp = target.shape[0], target.shape[1]
    rows = columns.shape[0] // (mp * dp)
    for pair in range(columns.shape[1] // 256):
        both = [
            columns[:, 256 * pair + 128 * c : 256 * pair + 128 * c + 128].reshape(
                dp, mp, rows, 128
            )
            for c in range(2)
        ]
        both = jnp.concatenate(both, axis=2).astype(jnp.bfloat16)
        spot = slice(first_row + 2 * rows * pair, first_row + 2 * rows * (pair + 1))
        for j in range(mp):
            target[j, :, spot, :] = both[:, j]


def gather_kernel(dp, mp, *refs):
    gather_body(dp, mp, *refs[:6], refs[6:15], *refs[15:])


def gather_body(
    dp,
    mp,
    qkv_ref,
    out_ref,
    up_ref,
    down_ref,
    proj_ref,
    table_ref,
    small_refs,
    word_qkv_ref,
    word_out_ref,
    word_up_ref,
    word_down_ref,
    qkv_all,
    qkv_t_all,
    out_all,
    out_t_all,
    up_all,
    up_t_all,
    down_all,
    down_t_all,
    proj_all,
    vecs_all,
    norms_all,
    table_all,
    word_share,
    held,
    tile,
    sends,
    arrivals,
):
    place = Place(dp, mp)
    low = jnp.bfloat16
    i, j = place.i, place.j
    row = 0
    for part in (qkv_ref, out_ref, up_ref, proj_ref):
        for pair in range(part.shape[1] // 256):
            both = [part[:, 256 * pair + 128 * c : 256 * pair + 128 * c + 128] for c in range(2)]
            held[i, j, row : row + 16, :] = jnp.concatenate(both, axis=0).astype(low)
            row += 16
    down_rows = down_ref.shape[0]
    for c in range(2):
        held[i, j, row : row + down_rows, :] = down_ref[:, 128 * c : 128 * c + 128].astype(low)
        row += down_rows
    word_part, char_part = table_ref.shape[1], small_refs[0].shape[1]
    tile[...] = jnp.zeros_like(tile)
    tile[0:8, 0:word_part] = table_ref[...]
    for k in range(4):
        tile[8 + k : 9 + k, 0:word_part] = small_refs[5 + k][...]
        tile[12 + k : 13 + k, 0:char_part] = small_refs[k][...]
    tile[12:13, char_part : 2 * char_part] = small_refs[4][...]
    held[i, j, row : row + 16, :] = tile[...].astype(low)
    place.greet()
    sems = (sends, arrivals)
    wide = place.wide

    def share(step, e):
        return held.at[
            lax.rem(i + dp - step, dp), 2 * lax.rem(place.x + wide - e, wide) + place.core
        ]

    def other_core(step, e):
        return held.at[
            lax.rem(i + dp - step, dp), 2 * lax.rem(place.x + wide - e, wide) + 1 - place.core
        ]

    def along(step):
        return remote(held.at[i, j], held.at[i, j], sems, step - 1, place.along(step))

    def across(step, e):
        index = dp - 1 + step * (wide - 1) + e - 1
        return remote(share(step, 0), share(step, 0), sems, index, place.across(e))

    def over(step, e):
        index = dp - 1 + dp * (wide - 1) + step * wide + e
        return remote(share(step, e), share(step, e), sems, index, place.partner())

    for step in range(1, dp):
        along(step).start()
    for e in range(1, wide):
        across(0, e).start()
    over(0, 0).start()

    rows = word_up_ref.shape[0]
    for t in range(3):
        word_share[rows * t : rows * (t + 1), :] = word_qkv_ref[t].astype(low)
    word_share[3 * rows : 4 * rows, :] = word_out_ref[...].astype(low)
    blocks = word_up_ref.shape[1] // 128
    for c in range(blocks):
        spot = slice((4 + c) * rows, (5 + c) * rows)
        word_share[spot, :] = word_up_ref[:, 128 * c : 128 * c + 128].astype(low)
        spot = slice((4 + blocks + c) * rows, (5 + blocks + c) * rows)
        word_share[spot, :] = word_down_ref[:, 128 * c : 128 * c + 128].astype(low)

    for step in range(1, dp):
        along(step).wait_recv()
        for e in range(1, wide):
            across(step, e).start()
        over(step, 0).start()
    for step in range(dp):
        for e in range(1, wide):
            across(step, e).wait_recv()
            over(step, e).start()
    for step in range(dp):
        for e in range(wide):
            over(step, e).wait_recv()
    for step in range(1, dp):
        along(step).wait_send()
    for step in range(dp):
        for e in range(1, wide):
            across(step, e).wait_send()
        for e in range(wide):
            over(step, e).wait_send()

    count = dp * mp
    row = 0
    for target, target_t in (
        (qkv_all, qkv_t_all),
        (out_all, out_t_all),
        (up_all, up_t_all),
        (proj_all, None),
    ):
        for pair in range(target.shape[1] // 256):
            both = held[:, :, row : row + 16, :].reshape(count, 16, 128).astype(jnp.float32)
            row += 16
            for c in range(2):
                piece = both[:, 8 * c : 8 * c + 8].reshape(8 * count, 128).astype(low)
                spot = slice(256 * pair + 128 * c, 256 * pair + 128 * c + 128)
                target[:, spot] = piece
                if target_t is not None:
                    target_t[spot, :] = piece.T
    for c in range(2):
        piece = held[:, :, row : row + down_rows, :].reshape(count * down_rows, 128)
        row += down_rows
        down_all[:, 128 * c : 128 * c + 128] = piece
        down_t_all[128 * c : 128 * c + 128, :] = piece.T
    small = held[:, :, row : row + 16, :].reshape(count, 16, 128).astype(jnp.float32)
    lane = lax.broadcasted_iota(jnp.int32, (16, 128), 1)
    for part, width in ((word_part, norms_all.shape[1]), (char_part, vecs_all.shape[1])):
        per = 128 // part
        for b in range(width // 128):
            total = small[b * per]
            other = pltpu.roll(total, 128 - part, 1)
            for k in range(1, per):
                piece = small[b * per + k]
                total = jnp.where(lane // part == k, pltpu.roll(piece, part * k, 1), total)
                moved = pltpu.roll(piece, part * (k - 1), 1) if k > 1 else piece
                other = jnp.where(lane // part == k, moved, other)
            cols = slice(128 * b, 128 * b + 128)
            if part == word_part:
                table_all[:, cols] = total[0:8]
                norms_all[:, cols] = total[8:12]
            else:
                vecs_all[0:4, cols] = total[12:16]
                vecs_all[4:5, cols] = other[12:13]
                vecs_all[5:8, cols] = jnp.zeros((3, 128), jnp.float32)


def gather_weights(dp, mp, parts, table, small, word_parts):
    low = jnp.bfloat16
    qkv, out, up, down, proj = parts
    count = dp * mp
    width = qkv.shape[0] * count
    hidden = up.shape[1]
    model = proj.shape[1]
    rows = (qkv.shape[1] + out.shape[1] + up.shape[1] + proj.shape[1]) // 128 * 8
    rows += 2 * down.shape[0] + 16
    word_rows = sum(part.size for part in word_parts) // 128
    copies = dp - 1 + dp * (mp // 2 - 1) + dp * (mp // 2)
    shapes = (
        (width, 3 * width),
        (3 * width, width),
        (width, width),
        (width, width),
        (width, hidden),
        (hidden, width),
        (hidden, width),
        (width, hidden),
        (width, model),
        (8, width),
        (4, model),
        (8, model),
        (word_rows, 128),
    )
    wide = (9, 10, 11)
    arrays = (qkv, out, up, down, proj, table, *small, *word_parts)
    return pl.pallas_call(
        functools.partial(gather_kernel, dp, mp),
        grid=(1,),
        in_specs=[once(array.shape) for array in arrays],
        out_specs=[once(shape) for shape in shapes],
        out_shape=[
            jax.ShapeDtypeStruct(shape, jnp.float32 if k in wide else low)
            for k, shape in enumerate(shapes)
        ],
        scratch_shapes=[
            pltpu.VMEM((dp, mp, rows, 128), low),
            pltpu.VMEM((16, 128), jnp.float32),
            pltpu.SemaphoreType.DMA((copies,)),
            pltpu.SemaphoreType.DMA((copies,)),
        ],
        compiler_params=pltpu.CompilerParams(
            collective_id=0, has_side_effects=True, vmem_limit_bytes=60 * 1024 * 1024
        ),
        name="gather_weights",
    )(*arrays)


def head_rows(rows, masks):
    return jnp.concatenate([rows * masks[h : h + 1] for h in range(CHAR_HEADS)], axis=0)


def gather_diagonal(square, lane_word, chars):
    words = square.shape[1] // chars
    blocks = square.reshape(CHAR_HEADS, words, chars, square.shape[1])
    kept = blocks[:, 0]
    for word in range(1, words):
        kept = jnp.where(lane_word == word, blocks[:, word], kept)
    return kept


def spread_diagonal(kept, word_masks, chars):
    words = kept.shape[2] // chars
    parts = [kept * word_masks[word : word + 1] for word in range(words)]
    return jnp.stack(parts, axis=1)


def norm_strips(values, gain_value, bias_value):
    return strips(lambda strip: apply_norm(strip, gain_value, bias_value), 64, values)


def char_forward_kernel(
    chars,
    chars_ref,
    count_ref,
    qkv_ref,
    out_ref,
    up_ref,
    down_ref,
    ones_ref,
    vecs_ref,
    head_mask_ref,
    word_mask_ref,
    cp_ref,
    probs_ref,
    co_ref,
    y1_ref,
    hidden_ref,
    slope_ref,
    y2_ref,
    pi_ref,
    pooled_ref,
):
    rows, width = chars_ref.shape
    low, wide = jnp.bfloat16, jnp.float32
    lane_word = lax.broadcasted_iota(jnp.int32, (1, 1, GROUP), 2) // chars
    key_slot = lax.broadcasted_iota(jnp.int32, (1, chars, GROUP), 1).astype(wide)
    words = rows // chars
    step = pl.program_id(0)
    counts = count_ref[pl.ds(step * words // 128, 1), :].astype(wide)
    word = lax.broadcasted_iota(jnp.int32, (rows // GROUP, 128), 1) - lax.rem(step * words, 128)
    group = lax.broadcasted_iota(jnp.int32, (rows // GROUP, 128), 0)
    counts = jnp.where(word // (GROUP // chars) == group, counts, 0.0)
    repeats = 128 * chars // GROUP
    spread = jnp.concatenate([word_mask_ref[...].astype(wide)] * repeats, axis=0).astype(low)
    lane_counts = mm(counts.astype(low), spread)
    row_slot = lax.rem(lax.broadcasted_iota(jnp.int32, (GROUP, GROUP), 0), chars).astype(wide)
    masks = head_mask_ref[...]
    word_masks = word_mask_ref[...]
    block = SUB
    parts = up_ref.shape[1] // CHUNK

    def project(s):
        span = slice(s * block, (s + 1) * block)
        states = chars_ref[span, :].astype(wide)
        _, _, normed = norm_strips(states, vecs_ref[0:1, :], vecs_ref[1:2, :])
        cp_ref[span, :] = mm(normed, qkv_ref[...]).astype(low)

    def groups_of(s):
        return [slice(row, row + GROUP) for row in range(s * block, (s + 1) * block, GROUP)]

    scores, probs = {}, {}

    def attend_scores(s):
        scores[s] = []
        for span in groups_of(s):
            keys = head_rows(cp_ref[span, width : 2 * width], masks)
            square = mm(keys, cp_ref[span, 0:width], NT)
            scores[s].append(gather_diagonal(square, lane_word, chars))

    def attend_probs(s):
        probs[s] = []
        for span, score in zip(groups_of(s), scores[s]):
            group = span.start // GROUP
            score = jnp.where(
                key_slot < lane_counts[group : group + 1], score * EXP2_SCALE, NEG_FILL
            )
            powers = jnp.exp2(score - jnp.max(score, axis=1, keepdims=True))
            share = 1.0 / jnp.sum(powers, axis=1, keepdims=True)
            probs[s].append((powers * share).astype(low))
            probs_ref[group] = probs[s][-1].reshape(CHAR_HEADS * chars, GROUP)

    def attend_values(s):
        for span, prob in zip(groups_of(s), probs[s]):
            values = head_rows(cp_ref[span, 2 * width : 3 * width], masks)
            spread = spread_diagonal(prob, word_masks, chars)
            spread = spread.reshape(CHAR_HEADS * GROUP, GROUP)
            co_ref[span, :] = mm(spread, values, TN).astype(low)

    def middle(s):
        span = slice(s * block, (s + 1) * block)
        after_attn = chars_ref[span, :].astype(wide) + mm(co_ref[span, :], out_ref[...])
        y1_ref[span, :] = after_attn
        return norm_strips(after_attn, vecs_ref[2:3, :], vecs_ref[3:4, :])[2]

    def pool_scores(s):
        query = vecs_ref[4:5, :] * EXP2_SCALE
        high, low_part = strips(lambda strip: split_two(strip * query), 64, totals[s])
        return mm(high, ones_ref[...]) + mm(low_part, ones_ref[...])

    def pool(s, scores):
        total = totals[s]
        pooled = []
        for k in range(block // GROUP):
            group = s * block // GROUP + k
            spot = slice(k * GROUP, (k + 1) * GROUP)
            span = slice(s * block + k * GROUP, s * block + (k + 1) * GROUP)
            counts = jnp.broadcast_to(lane_counts[group : group + 1], (GROUP, GROUP)).T
            valid = row_slot < counts
            halves = []
            for half in range(width // GROUP):
                cols = slice(half * GROUP, (half + 1) * GROUP)
                score = jnp.where(valid, scores[spot, cols], NEG_FILL)
                score = score.reshape(GROUP // chars, chars, GROUP)
                powers = jnp.exp2(score - jnp.max(score, axis=1, keepdims=True))
                pi = powers * (1.0 / jnp.sum(powers, axis=1, keepdims=True))
                pi_ref[span, cols] = pi.reshape(GROUP, GROUP).astype(low)
                grid = total[spot, cols].reshape(GROUP // chars, chars, GROUP)
                halves.append(jnp.sum(pi * grid, axis=1))
            pooled.append(jnp.concatenate(halves, axis=1))
        words = block // chars
        pooled_ref[s * words : (s + 1) * words, :] = jnp.concatenate(pooled, axis=0).astype(low)

    count = rows // block
    normed, totals, hiddens = {}, {}, {}

    def up(s, part):
        if part == 0:
            normed[s] = middle(s)
        return mm(normed[s], up_ref[:, part * CHUNK : (part + 1) * CHUNK])

    def activate(s, part, current):
        span, cols = slice(s * block, (s + 1) * block), slice(part * CHUNK, (part + 1) * CHUNK)
        hidden, slope = gelu_low(current)
        hidden_ref[span, cols] = hidden
        slope_ref[span, cols] = slope
        hiddens[s] = hidden

    def down(s, part):
        span, cols = slice(s * block, (s + 1) * block), slice(part * CHUNK, (part + 1) * CHUNK)
        term = mm(hiddens[s], down_ref[cols, :])
        totals[s] = term if part == 0 else totals[s] + term
        if part == parts - 1:
            totals[s] = totals[s] + y1_ref[span, :]
            y2_ref[span, :] = totals[s]

    for first in range(0, count, 2):
        pair = range(first, min(first + 2, count))
        for s in pair:
            project(s)
            attend_scores(s)
        for s in pair:
            attend_probs(s)
            attend_values(s)
        order = [(s, part) for part in range(parts) for s in pair]
        ahead = [up(*order[0])]
        pools = []
        for place, (s, part) in enumerate(order):
            if place + 1 < len(order):
                ahead.append(up(*order[place + 1]))
            activate(s, part, ahead[place])
            down(s, part)
            if part == parts - 1:
                pools.append((s, pool_scores(s)))
                if len(pools) > 1:
                    pool(*pools[-2])
        pool(*pools[-1])


def char_mlp_back_kernel(
    chars,
    exchange,
    y1_ref,
    y2_ref,
    pi_ref,
    grad_pooled_ref,
    hidden_ref,
    slope_ref,
    up_t_ref,
    down_t_ref,
    vecs_ref,
    ones_ref,
    *others,
):
    rows, width = y1_ref.shape
    words = rows // chars
    if exchange is None:
        grad_y1_ref, grad_up_ref, grad_down_t_ref, grad_vecs_ref = others
    else:
        (
            grad_proj_ref,
            word_small_ref,
            word_terms_ref,
            grad_y1_ref,
            char_terms_ref,
            word_qkv_ref,
            word_out_ref,
            word_up_ref,
            word_down_ref,
            grad_up_ref,
            grad_down_t_ref,
            grad_vecs_ref,
            local_ref,
            local_sem,
            one_ref,
            two_ref,
            three_ref,
            sends,
            arrivals,
        ) = others
        place = Place(*exchange)
        totals_word = [
            ScatterSum(
                place,
                word_terms_ref,
                lambda e, row, span: local_ref[e, row, span],
                one_ref,
                two_ref,
                three_ref,
                (sends, arrivals),
                part,
                WORD_PARTS,
            )
            for part in range(WORD_PARTS)
        ]
        own = [
            pltpu.make_async_copy(
                word_terms_ref.at[2 * e + place.core], local_ref.at[e], local_sem.at[e]
            )
            for e in range(place.wide)
        ]
        step, last = pl.program_id(0), pl.num_programs(0) - 1

        @pl.when(step == 0)
        def _():
            place.greet()
            for total in totals_word:
                total.start()
            for copy in own:
                copy.start()

        for part, total in enumerate(totals_word):

            @pl.when(step == (1 + part) * last // 15)
            def _(part=part, total=total):
                if part == 0:
                    for copy in own:
                        copy.wait()
                total.go_across()

            @pl.when(step == (4 + 2 * part) * last // 15)
            def _(total=total):
                total.go_along()

    @pl.when(pl.program_id(0) == 0)
    def _():
        grad_up_ref[...] = jnp.zeros_like(grad_up_ref)
        grad_down_t_ref[...] = jnp.zeros_like(grad_down_t_ref)
        grad_vecs_ref[...] = jnp.zeros_like(grad_vecs_ref)

    low, wide = jnp.bfloat16, jnp.float32
    block = SUB
    count, parts = rows // block, hidden_ref.shape[1] // CHUNK
    query = vecs_ref[4:5, :]
    per = 64 // chars

    def pool_back(s):
        spots = [
            (slice(row, row + 64), slice(row // chars, row // chars + per))
            for row in range(s * block, (s + 1) * block, 64)
        ]
        split = [
            split_two(
                (y2_ref[span, :].reshape(per, chars, width) * grad_pooled_ref[span_words]).reshape(
                    64, width
                )
            )
            for span, span_words in spots
        ]
        high, rest = (jnp.concatenate(side, axis=0) for side in zip(*split))
        grad_pi = mm(high, ones_ref[...]) + mm(rest, ones_ref[...])
        wide_parts, low_parts, query_sum = [], [], None
        for k, (span, span_words) in enumerate(spots):
            pi = pi_ref[span, :].astype(wide).reshape(per, chars, width)
            part = grad_pi[64 * k : 64 * (k + 1)].reshape(per, chars, width)
            inner = jnp.sum(pi * part, axis=1, keepdims=True)
            grad_scores = pi * (part - inner) * HEAD ** (-0.5)
            grid = y2_ref[span, :].reshape(per, chars, width)
            term = fold_rows((grad_scores * grid).reshape(64, width))
            query_sum = term if query_sum is None else query_sum + term
            grad = (pi * grad_pooled_ref[span_words] + grad_scores * query).reshape(64, width)
            wide_parts.append(grad)
            low_parts.append(grad.astype(low))
        grad_vecs_ref[0] += query_sum
        return jnp.concatenate(wide_parts, axis=0), jnp.concatenate(low_parts, axis=0)

    def norm_again(s):
        span = slice(s * block, (s + 1) * block)
        return norm_strips(y1_ref[span, :], vecs_ref[2:3, :], vecs_ref[3:4, :])

    def feed_back(s, branch):
        span = slice(s * block, (s + 1) * block)
        grads, total = [], None
        ahead = mm(branch, down_t_ref[:, 0:CHUNK])
        for part in range(parts):
            cols = slice(part * CHUNK, (part + 1) * CHUNK)
            current = ahead
            if part + 1 < parts:
                ahead = mm(branch, down_t_ref[:, (part + 1) * CHUNK : (part + 2) * CHUNK])
            (grad_pre,) = strips(
                lambda strip, slope: (strip.astype(low) * slope,),
                32,
                current,
                slope_ref[span, cols],
            )
            grads.append(grad_pre)
            term = mm(grad_pre, up_t_ref[cols, :])
            total = term if total is None else total + term
        return grads, total

    def norm_finish(rows_done, sums):
        s, row = rows_done // block, rows_done % block
        spot = slice(row, row + 64)
        part, (unit, inverse, _), grad = totals[s][spot], norms[s], pooled[s][0][spot]
        part_unit = unit[spot]
        terms = (fold_rows(part * part_unit), fold_rows(part))
        grad_y1_ref[rows_done : rows_done + 64, :] = grad + norm_back(
            part, part_unit, inverse[spot], vecs_ref[2:3, :]
        )
        return terms if sums is None else tuple(a + b for a, b in zip(sums, terms))

    pooled, norms, grads, totals = {}, {}, {}, {}
    pooled[0] = pool_back(0)
    norms[0] = norm_again(0)
    for s in range(count):
        grads[s], totals[s] = feed_back(s, pooled[s][1])
        if s + 1 < count:
            pooled[s + 1] = pool_back(s + 1)
            norms[s + 1] = norm_again(s + 1)
    branch_t = jnp.concatenate([pooled[s][1] for s in range(count)], axis=0).T
    normed_t = jnp.concatenate([norms[s][2] for s in range(count)], axis=0).T
    sums, done = None, 0
    steps = 2 * hidden_ref.shape[1] // width
    for k in range(steps):
        cols = slice(k // 2 * width, (k // 2 + 1) * width)
        if k % 2 == 0:
            grad_down_t_ref[:, cols] += mm(branch_t, hidden_ref[:, cols])
        else:
            part, first = cols.start // CHUNK, cols.start % CHUNK
            grad_pre = [grads[s][part][:, first : first + width] for s in range(count)]
            grad_up_ref[:, cols] += mm(normed_t, jnp.concatenate(grad_pre, axis=0))
        while done < (k + 1) * rows // steps:
            sums = norm_finish(done, sums)
            done += 64
    grad_vecs_ref[1] += sums[0]
    grad_vecs_ref[2] += sums[1]
    if exchange is None:
        return

    @pl.when(step == last)
    def _():
        low = jnp.bfloat16
        share = hidden_ref.shape[1] // (place.dp * place.mp)
        put_pairs(char_terms_ref, 0, grad_up_ref[...])
        row = hidden_ref.shape[1] // 16
        for c in range(2):
            piece = grad_down_t_ref[128 * c : 128 * c + 128, :].T
            piece = piece.reshape(place.dp, place.mp, share, 128).astype(low)
            for j in range(place.mp):
                char_terms_ref[j, :, row : row + share, :] = piece[:, j]
            row += share
        put_pairs(char_terms_ref, row, grad_proj_ref[...])
        row += grad_proj_ref.shape[1] // 16
        sums = [jnp.sum(grad_vecs_ref[k], axis=0, keepdims=True) for k in range(3)]
        small_row = lax.broadcasted_iota(jnp.int32, (16, 128), 0)
        for b in range(word_small_ref.shape[0]):
            piece = word_small_ref[b]
            if b < 2:
                for k in range(3):
                    piece = jnp.where(
                        small_row == 12 + k, sums[k][:, 128 * b : 128 * b + 128], piece
                    )
            piece = jnp.broadcast_to(piece.astype(low), (place.dp, 16, 128))
            for j in range(place.mp):
                char_terms_ref[j, :, row : row + 16, :] = piece
            row += 16
        for total in totals_word:
            result = total.finish()
        block = word_up_ref.shape[0]
        for t in range(3):
            word_qkv_ref[t] = result(slice(block * t, block * (t + 1)))
        word_out_ref[...] = result(slice(3 * block, 4 * block))
        count = word_up_ref.shape[1] // 128
        for c in range(count):
            cols = slice(128 * c, 128 * c + 128)
            word_up_ref[:, cols] = result(slice((4 + c) * block, (5 + c) * block))
            spot = slice((4 + count + c) * block, (5 + count + c) * block)
            word_down_ref[:, cols] = result(spot)


def char_attn_back_kernel(
    chars,
    exchange,
    chars_ref,
    cp_ref,
    probs_ref,
    co_ref,
    grad_y1_ref,
    qkv_t_ref,
    out_t_ref,
    vecs_ref,
    head_mask_ref,
    word_mask_ref,
    *others,
):
    rows, width = chars_ref.shape
    if exchange is None:
        (
            grad_chars_ref,
            grad_qkv_ref,
            grad_out_ref,
            grad_vecs_ref,
            grad_cp_ref,
            grad_co_ref,
        ) = others
    else:
        (
            early_terms_ref,
            grad_chars_ref,
            share_qkv_ref,
            share_out_ref,
            share_up_ref,
            share_down_ref,
            share_proj_ref,
            share_small_ref,
            share_vecs_ref,
            grad_cp_ref,
            grad_co_ref,
            grad_qkv_ref,
            grad_out_ref,
            grad_vecs_ref,
            local_ref,
            local_sem,
            late_terms_ref,
        ) = others[:17]
        early_refs, late_refs = others[17:22], others[22:27]
        place = Place(*exchange)
        early = ScatterSum(
            place,
            early_terms_ref,
            lambda e, row, span: local_ref[e, row, span],
            *early_refs[:3],
            early_refs[3:],
        )
        late = ScatterSum(
            place,
            late_terms_ref,
            lambda e, row, span: late_terms_ref[2 * e + place.core, row, span],
            *late_refs[:3],
            late_refs[3:],
        )
        own = [
            pltpu.make_async_copy(
                early_terms_ref.at[2 * e + place.core], local_ref.at[e], local_sem.at[e]
            )
            for e in range(place.wide)
        ]
        step, last = pl.program_id(0), pl.num_programs(0) - 1

        @pl.when(step == 0)
        def _():
            place.greet()
            early.start()
            for copy in own:
                copy.start()

        @pl.when(step == last // 15)
        def _():
            for copy in own:
                copy.wait()
            early.go_across()

        @pl.when(step == last // 3)
        def _():
            early.go_along()

    @pl.when(pl.program_id(0) == 0)
    def _():
        grad_qkv_ref[...] = jnp.zeros_like(grad_qkv_ref)
        grad_out_ref[...] = jnp.zeros_like(grad_out_ref)
        grad_vecs_ref[...] = jnp.zeros_like(grad_vecs_ref)

    low, wide = jnp.bfloat16, jnp.float32
    lane_word = lax.broadcasted_iota(jnp.int32, (1, 1, GROUP), 2) // chars
    masks = head_mask_ref[...]
    word_masks = word_mask_ref[...]
    scale = HEAD ** (-0.5)
    block = SUB
    count = rows // block

    def out_back(s):
        span = slice(s * block, (s + 1) * block)
        branch = grad_y1_ref[span, :].astype(low)
        grad_co_ref[span, :] = mm(branch, out_t_ref[...]).astype(low)
        return branch

    def norm_again(s):
        span = slice(s * block, (s + 1) * block)
        return norm_strips(
            chars_ref[span, :].astype(wide), vecs_ref[0:1, :], vecs_ref[1:2, :]
        )

    def side_by_side(spread):
        return jnp.concatenate([spread[h] for h in range(CHAR_HEADS)], axis=1)

    def groups_of(s):
        return [slice(row, row + GROUP) for row in range(s * block, (s + 1) * block, GROUP)]

    grad_probs, grad_scores = {}, {}

    def back_probs(s):
        grad_probs[s] = []
        for span in groups_of(s):
            values = head_rows(cp_ref[span, 2 * width : 3 * width], masks)
            square = mm(values, grad_co_ref[span, :], NT)
            grad_probs[s].append(gather_diagonal(square, lane_word, chars))

    def back_scores(s):
        grad_scores[s] = []
        for span, part in zip(groups_of(s), grad_probs[s]):
            probs = probs_ref[span.start // GROUP].reshape(CHAR_HEADS, chars, GROUP)
            spread = spread_diagonal(probs, word_masks, chars)
            spread = spread.reshape(CHAR_HEADS, GROUP, GROUP)
            grad_values = mm(side_by_side(spread), head_rows(grad_co_ref[span, :], masks))
            grad_cp_ref[span, 2 * width : 3 * width] = grad_values.astype(low)
            probs = probs.astype(wide)
            inner = jnp.sum(part * probs, axis=1, keepdims=True)
            grad_scores[s].append((probs * (part - inner)).astype(low))

    def back_keys(s):
        for span, part in zip(groups_of(s), grad_scores[s]):
            spread = spread_diagonal(part, word_masks, chars)
            spread = spread.reshape(CHAR_HEADS, GROUP, GROUP)
            queries = head_rows(cp_ref[span, 0:width], masks)
            grad_keys = mm(side_by_side(spread), queries) * scale
            grad_cp_ref[span, width : 2 * width] = grad_keys.astype(low)
            keys = head_rows(cp_ref[span, width : 2 * width], masks)
            grad_queries = mm(spread.reshape(CHAR_HEADS * GROUP, GROUP), keys, TN) * scale
            grad_cp_ref[span, 0:width] = grad_queries.astype(low)

    def project_back(s):
        span = slice(s * block, (s + 1) * block)
        return mm(grad_cp_ref[span, :], qkv_t_ref[...])

    def norm_finish(rows_done, sums):
        s, row = rows_done // block, rows_done % block
        spot, span = slice(row, row + 64), slice(rows_done, rows_done + 64)
        part, (unit, inverse, _) = totals[s][spot], norms[s]
        part_unit = unit[spot]
        terms = (fold_rows(part * part_unit), fold_rows(part))
        grad = grad_y1_ref[span, :] + norm_back(
            part, part_unit, inverse[spot], vecs_ref[0:1, :]
        )
        grad_chars_ref[span, :] = grad.astype(low)
        return terms if sums is None else tuple(a + b for a, b in zip(sums, terms))

    branches, norms, totals = [], {}, {}
    for s in range(count):
        branches.append(out_back(s))
        back_probs(s)
    norms[0] = norm_again(0)
    for s in range(count):
        back_scores(s)
        back_keys(s)
        if s + 1 < count:
            norms[s + 1] = norm_again(s + 1)
        totals[s] = project_back(s)
    normed_t = jnp.concatenate([norms[s][2] for s in range(count)], axis=0).T
    sums, done = None, 0
    for k in range(4):
        if k == 3:
            grad_out_ref[...] += mm(co_ref[...].T, jnp.concatenate(branches, axis=0))
        else:
            cols = slice(k * width, (k + 1) * width)
            grad_qkv_ref[:, cols] += mm(normed_t, grad_cp_ref[:, cols])
        while done < (k + 1) * rows // 4:
            sums = norm_finish(done, sums)
            done += 64
    grad_vecs_ref[0] += sums[0]
    grad_vecs_ref[1] += sums[1]
    if exchange is None:
        return

    @pl.when(step == last)
    def _():
        low = jnp.bfloat16
        put_pairs(late_terms_ref, 0, grad_qkv_ref[...])
        row = 3 * width // 16
        put_pairs(late_terms_ref, row, grad_out_ref[...])
        row += width // 16
        sums = [jnp.sum(grad_vecs_ref[k], axis=0, keepdims=True) for k in range(2)]
        small_row = lax.broadcasted_iota(jnp.int32, (16, 128), 0)
        piece = jnp.zeros((16, 128), jnp.float32)
        for k in range(2):
            for b in range(2):
                piece = jnp.where(
                    small_row == 2 * k + b, sums[k][:, 128 * b : 128 * b + 128], piece
                )
        piece = jnp.broadcast_to(piece.astype(low), (place.dp, 16, 128))
        for j in range(place.mp):
            late_terms_ref[j, :, row : row + 16, :] = piece
        late.start()
        result = early.finish()
        row = 0
        for target, share in (
            (share_up_ref, 8),
            (share_down_ref, share_down_ref.shape[0]),
            (share_proj_ref, 8),
            (share_small_ref, 16),
        ):
            for c in range(target.shape[1] // 128):
                target[:, 128 * c : 128 * c + 128] = result(slice(row, row + share))
                row += share
        late.go_across()
        late.go_along()
        result = late.finish()
        row = 0
        for target in (share_qkv_ref, share_out_ref):
            for c in range(target.shape[1] // 128):
                target[:, 128 * c : 128 * c + 128] = result(slice(row, row + 8))
                row += 8
        share_vecs_ref[...] = result(slice(row, row + 16))


def whole(shape):
    return pl.BlockSpec(shape, lambda step: (0,) * len(shape))


def once(shape):
    return pl.BlockSpec(shape, lambda step: (0,) * len(shape), pipeline_mode=pl.Buffered(1))


def blocked(shape):
    return pl.BlockSpec(shape, lambda step: (step,) + (0,) * (len(shape) - 1))


def params(megabytes):
    return pltpu.CompilerParams(
        dimension_semantics=("arbitrary",), vmem_limit_bytes=megabytes * 1024 * 1024
    )


def block_rows(rows, wanted):
    while rows % wanted:
        wanted //= 2
    return wanted


def char_forward(states, counts, weights, chars):
    rows, width = states.shape
    qkv, out, up, down, ones, vecs, head_masks, word_masks = weights
    block = block_rows(rows, 1024)
    words, groups = block // chars, block // GROUP
    low, wide = jnp.bfloat16, jnp.float32
    shapes = (
        ((rows, 3 * width), low),
        ((rows // GROUP, CHAR_HEADS * chars, GROUP), low),
        ((rows, width), low),
        ((rows, width), wide),
        ((rows, up.shape[1]), low),
        ((rows, up.shape[1]), low),
        ((rows, width), wide),
        ((rows, width), low),
        ((rows // chars, width), low),
    )
    blocks = (
        (block, 3 * width),
        (groups, CHAR_HEADS * chars, GROUP),
        (block, width),
        (block, width),
        (block, up.shape[1]),
        (block, up.shape[1]),
        (block, width),
        (block, width),
        (words, width),
    )
    flops = 2 * rows * width * (4 * width + 2 * up.shape[1] + 8 * width)
    return pl.pallas_call(
        functools.partial(char_forward_kernel, chars),
        grid=(rows // block,),
        in_specs=[
            blocked((block, width)),
            whole(counts.shape),
            whole(qkv.shape),
            whole(out.shape),
            whole(up.shape),
            whole(down.shape),
            whole(ones.shape),
            whole(vecs.shape),
            whole(head_masks.shape),
            whole(word_masks.shape),
        ],
        out_specs=[blocked(shape) for shape in blocks],
        out_shape=[jax.ShapeDtypeStruct(shape, kind) for shape, kind in shapes],
        compiler_params=params(56),
        cost_estimate=pl.CostEstimate(
            flops=flops, bytes_accessed=rows * width * 36, transcendentals=rows * width * 5
        ),
        name="char_forward",
    )(states, counts, qkv, out, up, down, ones, vecs, head_masks, word_masks)


def char_mlp_back(y1, y2, pi, grad_pooled, hidden, slope, weights, chars):
    rows, width = y1.shape
    up_t, down_t, vecs, ones = weights
    block = block_rows(rows, 1024)
    hidden_width = hidden.shape[1]
    wide = jnp.float32
    flops = 2 * rows * width * (4 * hidden_width + 2 * width)
    return pl.pallas_call(
        functools.partial(char_mlp_back_kernel, chars, None),
        grid=(rows // block,),
        in_specs=[
            blocked((block, width)),
            blocked((block, width)),
            blocked((block, width)),
            blocked((block // chars, 1, width)),
            blocked((block, hidden_width)),
            blocked((block, hidden_width)),
            whole(up_t.shape),
            whole(down_t.shape),
            whole(vecs.shape),
            whole(ones.shape),
        ],
        out_specs=[
            blocked((block, width)),
            whole((width, hidden_width)),
            whole((width, hidden_width)),
            whole((3, 8, width)),
        ],
        out_shape=[
            jax.ShapeDtypeStruct((rows, width), wide),
            jax.ShapeDtypeStruct((width, hidden_width), wide),
            jax.ShapeDtypeStruct((width, hidden_width), wide),
            jax.ShapeDtypeStruct((3, 8, width), wide),
        ],
        compiler_params=params(56),
        cost_estimate=pl.CostEstimate(
            flops=flops, bytes_accessed=rows * width * 30, transcendentals=0
        ),
        name="char_mlp_back",
    )(y1, y2, pi, grad_pooled, hidden, slope, up_t, down_t, vecs, ones)


def char_attn_back(states, cp, probs, co, grad_y1, weights, chars):
    rows, width = states.shape
    qkv_t, out_t, vecs, head_masks, word_masks = weights
    block = block_rows(rows, 1024)
    low, wide = jnp.bfloat16, jnp.float32
    flops = 2 * rows * width * 18 * width
    return pl.pallas_call(
        functools.partial(char_attn_back_kernel, chars, None),
        grid=(rows // block,),
        in_specs=[
            blocked((block, width)),
            blocked((block, 3 * width)),
            blocked((block // GROUP, CHAR_HEADS * chars, GROUP)),
            blocked((block, width)),
            blocked((block, width)),
            whole(qkv_t.shape),
            whole(out_t.shape),
            whole(vecs.shape),
            whole(head_masks.shape),
            whole(word_masks.shape),
        ],
        out_specs=[
            blocked((block, width)),
            whole((width, 3 * width)),
            whole((width, width)),
            whole((2, 8, width)),
        ],
        out_shape=[
            jax.ShapeDtypeStruct((rows, width), low),
            jax.ShapeDtypeStruct((width, 3 * width), wide),
            jax.ShapeDtypeStruct((width, width), wide),
            jax.ShapeDtypeStruct((2, 8, width), wide),
        ],
        scratch_shapes=[
            pltpu.VMEM((block, 3 * width), low),
            pltpu.VMEM((block, width), low),
        ],
        compiler_params=params(56),
        cost_estimate=pl.CostEstimate(
            flops=flops, bytes_accessed=rows * width * 18, transcendentals=0
        ),
        name="char_attn_back",
    )(states, cp, probs, co, grad_y1, qkv_t, out_t, vecs, head_masks, word_masks)


def char_mlp_back_exchange(
    y1, y2, pi, grad_pooled, hidden, slope, weights, chars, mesh_size, grad_proj, word_small, word_terms
):
    rows, width = y1.shape
    up_t, down_t, vecs, ones = weights
    dp, mp = mesh_size
    block = block_rows(rows, 1024)
    hidden_width = hidden.shape[1]
    low, wide = jnp.bfloat16, jnp.float32
    model = grad_proj.shape[1]
    flops = 2 * rows * width * (4 * hidden_width + 2 * width)
    char_rows = 2 * hidden_width // 16 + model // 16 + 16 * word_small.shape[0]
    n = word_terms.shape[2]
    share = model // dp
    outs = (
        ((rows, width), wide, blocked((block, width))),
        ((mp, dp, char_rows, 128), low, None),
        ((3, share, 128), wide, None),
        ((share, 128), wide, None),
        ((share, model), wide, None),
        ((share, model), wide, None),
    )
    return pl.pallas_call(
        functools.partial(char_mlp_back_kernel, chars, mesh_size),
        grid=(rows // block,),
        in_specs=[
            blocked((block, width)),
            blocked((block, width)),
            blocked((block, width)),
            blocked((block // chars, 1, width)),
            blocked((block, hidden_width)),
            blocked((block, hidden_width)),
            whole(up_t.shape),
            whole(down_t.shape),
            whole(vecs.shape),
            whole(ones.shape),
            whole(grad_proj.shape),
            whole(word_small.shape),
            pl.BlockSpec(memory_space=pl.ANY),
        ],
        out_specs=[spec or whole(shape) for shape, _, spec in outs],
        out_shape=[jax.ShapeDtypeStruct(shape, kind) for shape, kind, _ in outs],
        scratch_shapes=[
            pltpu.VMEM((width, hidden_width), wide),
            pltpu.VMEM((width, hidden_width), wide),
            pltpu.VMEM((3, 8, width), wide),
            pltpu.VMEM((mp // 2, dp, n, 128), low),
            pltpu.SemaphoreType.DMA((mp // 2,)),
        ]
        + scatter_scratch(dp, mp, n, WORD_PARTS),
        compiler_params=pltpu.CompilerParams(
            dimension_semantics=("arbitrary",),
            vmem_limit_bytes=60 * 1024 * 1024,
            collective_id=1,
            has_side_effects=True,
        ),
        cost_estimate=pl.CostEstimate(
            flops=flops, bytes_accessed=rows * width * 30, transcendentals=0
        ),
        name="char_mlp_back",
    )(
        y1, y2, pi, grad_pooled, hidden, slope, up_t, down_t, vecs, ones,
        grad_proj, word_small, word_terms,
    )


def char_attn_back_exchange(
    states, cp, probs, co, grad_y1, weights, chars, mesh_size, early_terms, hidden_width, model
):
    rows, width = states.shape
    qkv_t, out_t, vecs, head_masks, word_masks = weights
    dp, mp = mesh_size
    count = dp * mp
    block = block_rows(rows, 1024)
    low, wide = jnp.bfloat16, jnp.float32
    flops = 2 * rows * width * 18 * width
    n = early_terms.shape[2]
    late = 4 * width // 16 + 16
    outs = (
        ((rows, width), low, blocked((block, width))),
        ((width // count, 3 * width), wide, None),
        ((width // count, width), wide, None),
        ((width // count, hidden_width), wide, None),
        ((hidden_width // count, width), wide, None),
        ((width // count, model), wide, None),
        ((16, model), wide, None),
        ((16, 128), wide, None),
    )
    return pl.pallas_call(
        functools.partial(char_attn_back_kernel, chars, mesh_size),
        grid=(rows // block,),
        in_specs=[
            blocked((block, width)),
            blocked((block, 3 * width)),
            blocked((block // GROUP, CHAR_HEADS * chars, GROUP)),
            blocked((block, width)),
            blocked((block, width)),
            whole(qkv_t.shape),
            whole(out_t.shape),
            whole(vecs.shape),
            whole(head_masks.shape),
            whole(word_masks.shape),
            pl.BlockSpec(memory_space=pl.ANY),
        ],
        out_specs=[spec or whole(shape) for shape, _, spec in outs],
        out_shape=[jax.ShapeDtypeStruct(shape, kind) for shape, kind, _ in outs],
        scratch_shapes=[
            pltpu.VMEM((block, 3 * width), low),
            pltpu.VMEM((block, width), low),
            pltpu.VMEM((width, 3 * width), wide),
            pltpu.VMEM((width, width), wide),
            pltpu.VMEM((2, 8, width), wide),
            pltpu.VMEM((mp // 2, dp, n, 128), low),
            pltpu.SemaphoreType.DMA((mp // 2,)),
            pltpu.VMEM((mp, dp, late, 128), low),
        ]
        + scatter_scratch(dp, mp, n)
        + scatter_scratch(dp, mp, late),
        compiler_params=pltpu.CompilerParams(
            dimension_semantics=("arbitrary",),
            vmem_limit_bytes=56 * 1024 * 1024,
            collective_id=2,
            has_side_effects=True,
        ),
        cost_estimate=pl.CostEstimate(
            flops=flops, bytes_accessed=rows * width * 18, transcendentals=0
        ),
        name="char_attn_back",
    )(states, cp, probs, co, grad_y1, qkv_t, out_t, vecs, head_masks, word_masks, early_terms)


def share_kernel(places_ref, large_ref, *refs):
    shares, refs = refs[:SHARES], refs[SHARES:]
    small_ref, vecs_ref, large_out_ref, *targets = refs
    large_out_ref[...] = large_ref[...]

    @pl.when(pl.program_id(0) == 0)
    def _():
        for source, target in zip(shares, targets):
            target[...] = source[...]
        table_out, *small_outs = targets[SHARES:]
        word_outs, char_outs = small_outs[:4], small_outs[4:]
        width = 2 * vecs_ref.shape[1]
        word_part, char_part = table_out.shape[1], char_outs[0].shape[1]
        words = pltpu.roll(small_ref[...], places_ref[0], 1)
        table_out[...] = words[0:8, 0:word_part]
        for k, target in enumerate(word_outs):
            target[...] = words[8 + k : 9 + k, 0:word_part]
        early = small_ref[12:15, 0:width]
        late = jnp.concatenate([vecs_ref[0:1, :], vecs_ref[1:2, :]], axis=1)
        late_two = jnp.concatenate([vecs_ref[2:3, :], vecs_ref[3:4, :]], axis=1)
        rows = jnp.concatenate([early, late, late_two, jnp.zeros((3, width), jnp.float32)], axis=0)
        rows = pltpu.roll(rows, places_ref[1], 1)
        for k, target in enumerate(char_outs):
            target[...] = rows[k : k + 1, 0:char_part]


def hand_out(places, large, shares, small, vecs, word_part, char_part):
    wide = jnp.float32
    outs = [(share.shape, wide) for share in shares]
    outs += [((8, word_part), wide)] + [((1, word_part), wide)] * 4 + [((1, char_part), wide)] * 5
    block = blocked((block_rows(large.shape[0], 2048), large.shape[1]))
    return pl.pallas_call(
        share_kernel,
        grid=(large.shape[0] // block.block_shape[0],),
        in_specs=[pl.BlockSpec(memory_space=pltpu.SMEM), block]
        + [once(array.shape) for array in (*shares, small, vecs)],
        out_specs=[block] + [once(shape) for shape, _ in outs],
        out_shape=[jax.ShapeDtypeStruct(large.shape, large.dtype)]
        + [jax.ShapeDtypeStruct(shape, kind) for shape, kind in outs],
        compiler_params=params(60),
        name="hand_out",
    )(places, large, *shares, small, vecs)


def word_kernel(
    pooled_ref,
    words_ref,
    cotangent_ref,
    language_ref,
    table_ref,
    proj_ref,
    weights_ref,
    norms_ref,
    head_mask_ref,
    layer_ref,
    grad_words_ref,
    terms_ref,
    grad_proj_ref,
    grad_pooled_ref,
    small_ref,
    residual_ref,
    normed_one_ref,
    packed_ref,
    probs_ref,
    mixed_ref,
    middle_ref,
    normed_two_ref,
    hidden_ref,
    slope_ref,
    total_ref,
    grad_keys_ref,
    grad_values_ref,
    sums_ref,
):
    low, wide = jnp.bfloat16, jnp.float32
    length, model = words_ref.shape
    dp, mp = weights_ref.shape[:2]
    share = model // dp
    row_block, large = 256, 1024
    blocks = length // row_block
    hidden_width = hidden_ref.shape[1]
    up_blocks = hidden_width // mp // 128
    scale = HEAD ** (-0.5)
    up_base, down_base = 4 * share, (4 + up_blocks) * share

    def weight(base):
        pieces = [
            weights_ref[:, j, pl.ds(base, share), :].reshape(model, 128) for j in range(mp)
        ]
        return jnp.concatenate(pieces, axis=1)

    def wide_weight(base, j):
        pieces = [
            weights_ref[:, j, base + c * share : base + (c + 1) * share, :].reshape(model, 128)
            for c in range(up_blocks)
        ]
        return jnp.concatenate(pieces, axis=1)

    def put(base, grad):
        for j in range(mp):
            piece = grad[:, 128 * j : 128 * j + 128].reshape(dp, share, 128).astype(low)
            terms_ref[j, :, pl.ds(base, share), :] = piece

    def put_wide(base, j, grad):
        for c in range(up_blocks):
            piece = grad[:, 128 * c : 128 * c + 128].reshape(dp, share, 128).astype(low)
            terms_ref[j, :, base + c * share : base + (c + 1) * share, :] = piece

    def norm(k):
        return norms_ref[k : k + 1, :]

    sums_ref[...] = jnp.zeros_like(sums_ref)
    language = language_ref[0]

    spans = [slice(row, row + large) for row in range(0, length, large)]
    for span in spans:
        residual = words_ref[span, :].astype(wide) + mm(pooled_ref[span, :], proj_ref[...])
        residual = residual + table_ref[pl.ds(language, 1), :]
        residual_ref[span, :] = residual
        normed_one_ref[span, :] = norm_strips(residual, norm(0), norm(1))[2]

    @pl.loop(0, 3)
    def _(t):
        whole_weight = weight(pl.multiple_of(t * share, share))
        for span in spans:
            packed_ref[t, span, :] = mm(normed_one_ref[span, :], whole_weight).astype(low)

    causal = lax.broadcasted_iota(jnp.int32, (row_block, row_block), 0) <= (
        lax.broadcasted_iota(jnp.int32, (row_block, row_block), 1)
    )

    @pl.loop(0, model // 128)
    def _(pair):
        lanes = pl.ds(pl.multiple_of(pair * 128, 128), 128)
        values_t = packed_ref[2, :, lanes].T

        def scores_of(block, h):
            stop = (block + 1) * row_block
            queries = packed_ref[0, block * row_block : stop, lanes]
            keys = packed_ref[1, 0:stop, lanes] * head_mask_ref[h : h + 1, 0:128]
            return mm(keys, queries, NT)

        order = [(block, h) for block in range(blocks) for h in range(2)]
        ahead = scores_of(*order[0])
        mixed = []
        for place, (block, h) in enumerate(order):
            scores = ahead * EXP2_SCALE
            if place + 1 < len(order):
                ahead = scores_of(*order[place + 1])
            stop = (block + 1) * row_block
            first = block * (block + 1) // 2 * row_block
            near = jnp.where(causal, scores[stop - row_block :], NEG_FILL)
            scores = jnp.concatenate([scores[: stop - row_block], near]) if block else near
            powers = jnp.exp2(scores - jnp.max(scores, axis=0, keepdims=True))
            probs = powers * (1.0 / jnp.sum(powers, axis=0, keepdims=True))
            probs = probs.astype(low)
            probs_ref[2 * pair + h, first : first + stop, :] = probs
            mixed.append(mm(values_t[HEAD * h : HEAD * (h + 1), 0:stop], probs))
            if h == 1:
                both = jnp.concatenate(mixed, axis=0).T.astype(low)
                mixed_ref[block * row_block : stop, lanes] = both
                mixed = []

    out_t = weight(3 * share)
    for span in spans:
        middle = residual_ref[span, :] + mm(mixed_ref[span, :], out_t, NT)
        middle_ref[span, :] = middle
        total_ref[span, :] = middle
        normed_two_ref[span, :] = norm_strips(middle, norm(2), norm(3))[2]

    def columns_of(j):
        return pl.ds(pl.multiple_of(j * 128 * up_blocks, 128 * up_blocks), 128 * up_blocks)

    @pl.loop(0, mp)
    def _(j):
        up, down = wide_weight(up_base, j), wide_weight(down_base, j)
        before = [mm(normed_two_ref[span, :], up) for span in spans]
        for span, part in zip(spans, before):
            hidden, slope = gelu_low(part)
            hidden_ref[span, columns_of(j)] = hidden
            slope_ref[span, columns_of(j)] = slope
            total_ref[span, :] += mm(hidden, down, NT)

    for span in spans:
        layer_ref[span, :] = total_ref[span, :].astype(low)
        total_ref[span, :] = jnp.zeros((large, model), wide)

    cotangent_t = cotangent_ref[...].T
    normed_t = normed_two_ref[...].T

    @pl.loop(0, mp)
    def _(j):
        up, down = wide_weight(up_base, j), wide_weight(down_base, j)
        before = [mm(cotangent_ref[span, :], down) for span in spans]
        put_wide(down_base, j, mm(cotangent_t, hidden_ref[:, columns_of(j)]))
        for span, part in zip(spans, before):
            (grad_pre,) = strips(
                lambda strip, slope: (strip.astype(low) * slope,),
                32,
                part,
                slope_ref[span, columns_of(j)],
            )
            slope_ref[span, columns_of(j)] = grad_pre
            total_ref[span, :] += mm(grad_pre, up, NT)
        put_wide(up_base, j, mm(normed_t, slope_ref[:, columns_of(j)]))

    for span in spans:

        def finish(part, middle, cotangent):
            unit, inverse = standardize(middle)
            sums_ref[2] += fold_rows(part * unit)
            sums_ref[3] += fold_rows(part)
            grad = cotangent.astype(wide) + norm_back(part, unit, inverse, norm(2))
            return grad, grad.astype(low)

        grad_middle, branch = strips(
            finish, 64, total_ref[span, :], middle_ref[span, :], cotangent_ref[span, :]
        )
        middle_ref[span, :] = grad_middle
        normed_two_ref[span, :] = branch
    put(3 * share, mm(normed_two_ref[...].T, mixed_ref[...]))
    for span in spans:
        mixed_ref[span, :] = mm(normed_two_ref[span, :], out_t).astype(low)


    @pl.loop(0, model // 128)
    def _(pair):
        lanes = pl.ds(pl.multiple_of(pair * 128, 128), 128)
        grad_keys_ref[...] = jnp.zeros_like(grad_keys_ref)
        grad_values_ref[...] = jnp.zeros_like(grad_values_ref)
        keys_t = packed_ref[1, :, lanes].T

        def grad_probs_of(block, h):
            stop = (block + 1) * row_block
            grad_mixed = mixed_ref[block * row_block : stop, lanes]
            values = packed_ref[2, 0:stop, lanes] * head_mask_ref[h : h + 1, 0:128]
            return mm(values, grad_mixed, NT)

        order = [(block, h) for block in range(blocks) for h in range(2)]
        ahead = grad_probs_of(*order[0])
        sides = []
        for place, (block, h) in enumerate(order):
            grad_probs = ahead
            if place + 1 < len(order):
                ahead = grad_probs_of(*order[place + 1])
            stop = (block + 1) * row_block
            span = slice(block * row_block, stop)
            first = block * (block + 1) // 2 * row_block
            probs = probs_ref[2 * pair + h, first : first + stop, :]
            probs_wide = probs.astype(wide)
            inner = jnp.sum(grad_probs * probs_wide, axis=0, keepdims=True)
            grad_scores = (probs_wide * (grad_probs - inner)).astype(low)
            grad_queries = mm(keys_t[HEAD * h : HEAD * (h + 1), 0:stop], grad_scores)
            sides.append((probs, grad_scores, grad_queries))
            if h == 1:
                probs, grad_scores, grad_queries = (list(side) for side in zip(*sides))
                sides = []
                masks = [head_mask_ref[k : k + 1, 0:128] for k in range(2)]
                grad_mixed, queries = mixed_ref[span, lanes], packed_ref[0, span, lanes]
                grad_values_ref[0:stop, :] += mm(
                    jnp.concatenate(probs, axis=1),
                    jnp.concatenate([grad_mixed * mask for mask in masks], axis=0),
                )
                grad_keys_ref[0:stop, :] += mm(
                    jnp.concatenate(grad_scores, axis=1),
                    jnp.concatenate([queries * mask for mask in masks], axis=0),
                )
                both = jnp.concatenate(grad_queries, axis=0) * scale
                packed_ref[0, span, lanes] = both.T.astype(low)
        packed_ref[1, :, lanes] = (grad_keys_ref[...] * scale).astype(low)
        packed_ref[2, :, lanes] = grad_values_ref[...].astype(low)

    normed_t = normed_one_ref[...].T
    for span in spans:
        total_ref[span, :] = jnp.zeros((large, model), wide)

    @pl.loop(0, 3)
    def _(t):
        base = pl.multiple_of(t * share, share)
        put(base, mm(normed_t, packed_ref[t]))
        whole_weight = weight(base)
        for span in spans:
            total_ref[span, :] += mm(packed_ref[t, span, :], whole_weight, NT)

    for span in spans:

        def finish(part, residual, grad_middle):
            unit, inverse = standardize(residual)
            sums_ref[0] += fold_rows(part * unit)
            sums_ref[1] += fold_rows(part)
            grad = grad_middle + norm_back(part, unit, inverse, norm(0))
            sums_ref[4] += fold_rows(grad)
            return (grad.astype(low),)

        (grad,) = strips(finish, 64, total_ref[span, :], residual_ref[span, :], middle_ref[span, :])
        grad_words_ref[span, :] = grad
        grad_pooled_ref[span] = mm(grad, proj_ref[...], NT)[:, None, :]

    grad_proj_ref[...] = mm(pooled_ref[...].T, grad_words_ref[...])

    sums = [jnp.sum(sums_ref[k], axis=0, keepdims=True) for k in range(5)]
    small_row = lax.broadcasted_iota(jnp.int32, (8, 128), 0)
    for b in range(model // 128):
        cols = slice(128 * b, 128 * b + 128)
        small_ref[b, 0:8, :] = jnp.where(small_row == language, sums[4][:, cols], 0.0)
        piece = jnp.zeros((8, 128), wide)
        for k in range(4):
            piece = jnp.where(small_row == k, sums[k][:, cols], piece)
        small_ref[b, 8:16, :] = piece


def word_layer_kernel(pooled, words, cotangent, language, table, proj, weights, norms, head_masks):
    low, wide = jnp.bfloat16, jnp.float32
    length, model = words.shape
    width = pooled.shape[1]
    dp, mp, n = weights.shape[:3]
    hidden_width = (n * dp // model - 4) // 2 * 128 * mp
    blocks = length // 256
    heads = model // HEAD
    arrays = (pooled, words, cotangent, language, table, proj, weights, norms, head_masks)
    outs = (
        ((length, model), low),
        ((length, model), low),
        ((mp, dp, n, 128), low),
        ((width, model), wide),
        ((length, 1, width), wide),
        ((model // 128, 16, 128), wide),
    )
    return pl.pallas_call(
        word_kernel,
        grid=(1,),
        in_specs=[
            pl.BlockSpec(memory_space=pltpu.SMEM) if array is language else once(array.shape)
            for array in arrays
        ],
        out_specs=[once(shape) for shape, _ in outs],
        out_shape=[jax.ShapeDtypeStruct(shape, kind) for shape, kind in outs],
        scratch_shapes=[
            pltpu.VMEM((length, model), wide),
            pltpu.VMEM((length, model), low),
            pltpu.VMEM((3, length, model), low),
            pltpu.VMEM((heads, blocks * (blocks + 1) // 2 * 256, 256), low),
            pltpu.VMEM((length, model), low),
            pltpu.VMEM((length, model), wide),
            pltpu.VMEM((length, model), low),
            pltpu.VMEM((length, hidden_width), low),
            pltpu.VMEM((length, hidden_width), low),
            pltpu.VMEM((length, model), wide),
            pltpu.VMEM((length, 128), wide),
            pltpu.VMEM((length, 128), wide),
            pltpu.VMEM((5, 8, model), wide),
        ],
        compiler_params=pltpu.CompilerParams(vmem_limit_bytes=62 * 1024 * 1024),
        cost_estimate=pl.CostEstimate(
            flops=40 * 10**9, bytes_accessed=20 * 2**20, transcendentals=10**7
        ),
        name="word_layer",
    )(*arrays)


def attend_forward(queries, key_block, values, allowed):
    scores = low_sum("bqhd,bkhd->bhqk", queries, key_block) * HEAD ** (-0.5)
    scores = jnp.where(allowed, scores, NEG_FILL)
    row_max = jnp.max(scores, axis=-1, keepdims=True)
    powers = jnp.exp(scores - row_max)
    row_total = jnp.sum(powers, axis=-1, keepdims=True)
    attn_probs = (powers / row_total).astype(jnp.bfloat16)
    attn_mixed = low_sum("bhqk,bkhd->bqhd", attn_probs, values).astype(jnp.bfloat16)
    return (attn_mixed, row_max + jnp.log(row_total))


def attend_backward(queries, key_block, values, allowed, log_total, grad_mixed):
    scale = HEAD ** (-0.5)
    scores = low_sum("bqhd,bkhd->bhqk", queries, key_block) * scale
    attn_probs = jnp.where(allowed, jnp.exp(scores - log_total), 0.0)
    grad_probs = low_sum("bqhd,bkhd->bhqk", grad_mixed, values)
    grad_values = low_sum("bhqk,bqhd->bkhd", attn_probs.astype(jnp.bfloat16), grad_mixed)
    inner_sum = jnp.sum(grad_probs * attn_probs, axis=-1, keepdims=True)
    grad_scores = (attn_probs * (grad_probs - inner_sum)).astype(jnp.bfloat16)
    grad_queries = low_sum("bhqk,bkhd->bqhd", grad_scores, key_block) * scale
    grad_keys = low_sum("bhqk,bqhd->bkhd", grad_scores, queries) * scale
    return (grad_queries, grad_keys, grad_values)


def word_layer(residual, grad_rows, weights, norms, mp_size, mp_index):
    qkv, out_t, up, down_t = weights
    gain_one, bias_one, gain_two, bias_two = norms
    rows, width = residual.shape
    low = jnp.bfloat16
    sequences, length = max(1, rows // LEN), min(rows, LEN)
    share = LEN // length
    groups = [[a * share + b for b in range(share)] for a in range(mp_size // share)]
    unit_one, inverse_one, normed_one = apply_norm(residual, gain_one, bias_one)
    packed = low_sum("rd,tdc->trc", normed_one, qkv).astype(low)
    packed = packed.reshape(3, sequences, length, width // HEAD, HEAD)
    keys = packed[1:]
    start = 0
    if share > 1:
        keys = lax.all_gather(keys, "mp", axis=2, tiled=True, axis_index_groups=groups)
        start = lax.rem(mp_index, share) * length
    allowed = (
        lax.broadcasted_iota(jnp.int32, (length, LEN), 1)
        <= lax.broadcasted_iota(jnp.int32, (length, LEN), 0) + start
    )[None, None]
    mixed, log_total = attend_forward(packed[0], keys[0], keys[1], allowed)
    mixed_rows = mixed.reshape(rows, width)
    middle = residual + mm(mixed_rows, out_t, NT)
    unit_two, inverse_two, normed_two = apply_norm(middle, gain_two, bias_two)
    hidden, slope = gelu_pair(matmul(normed_two, up))
    hidden = hidden.astype(low)
    layer_output = (middle + mm(hidden, down_t, NT)).astype(low)
    grad_wide = grad_rows.astype(jnp.float32)
    grad_down_t = mm(grad_rows, hidden, TN)
    grad_pre = (matmul(grad_rows, down_t) * slope).astype(low)
    grad_up = mm(normed_two, grad_pre, TN)
    grad_normed = mm(grad_pre, up, NT)
    grad_gain_two = jnp.sum(grad_normed * unit_two, axis=0)
    grad_bias_two = jnp.sum(grad_normed, axis=0)
    grad_middle = grad_wide + norm_back(grad_normed, unit_two, inverse_two, gain_two)
    branch = grad_middle.astype(low)
    grad_out_t = mm(branch, mixed_rows, TN)
    grad_mixed = matmul(branch, out_t).astype(low).reshape(sequences, length, -1, HEAD)
    grad_queries, grad_keys, grad_values = attend_backward(
        packed[0], keys[0], keys[1], allowed, log_total, grad_mixed
    )
    grad_keys = jnp.stack((grad_keys, grad_values), axis=0)
    if share > 1:
        grad_keys = lax.psum_scatter(
            grad_keys, "mp", scatter_dimension=2, tiled=True, axis_index_groups=groups
        )
    grad_packed = jnp.concatenate((grad_queries[None], grad_keys), axis=0)
    grad_packed = grad_packed.reshape(3, rows, width).astype(low)
    grad_qkv = low_sum("rd,trc->tdc", normed_one, grad_packed)
    grad_normed = low_sum("trc,tdc->rd", grad_packed, qkv)
    grad_gain_one = jnp.sum(grad_normed * unit_one, axis=0)
    grad_bias_one = jnp.sum(grad_normed, axis=0)
    grad_residual = grad_middle + norm_back(grad_normed, unit_one, inverse_one, gain_one)
    return (
        layer_output,
        grad_residual,
        (grad_qkv, grad_out_t, grad_up, grad_down_t),
        (grad_gain_one, grad_bias_one, grad_gain_two, grad_bias_two),
    )


def mask_constants(width, chars):
    head, word = np.arange(width) // HEAD, np.arange(GROUP) // chars
    head_masks = head[None] == np.arange(8)[:, None]
    word_masks = word[None] == np.arange(GROUP // chars)[:, None]
    ones = head[:, None] == head[None]
    return tuple(jnp.asarray(mask.astype(ml_dtypes.bfloat16)) for mask in (head_masks, word_masks, ones))


def blocks_of(array, count):
    return array.reshape(count, -1)


def shards_general(
    char_states,
    word_states,
    char_counts,
    language_group,
    output_grad,
    char_norm_gain,
    char_norm_bias,
    char_qkv,
    char_out,
    char_mlp_gain,
    char_mlp_bias,
    char_up,
    char_down,
    pool_query,
    char_proj,
    language_table,
    word_norm_gain,
    word_norm_bias,
    word_qkv,
    word_out,
    word_mlp_gain,
    word_mlp_bias,
    word_up,
    word_down,
):
    low, wide = jnp.bfloat16, jnp.float32
    dp_size, mp_size = lax.axis_size("dp"), lax.axis_size("mp")
    mp_index = lax.axis_index("mp")
    devices = dp_size * mp_size
    word_count, chars, width = char_states.shape
    model = word_states.shape[1]
    langs = language_table.shape[0]

    char_parts = (
        char_qkv,
        char_out,
        char_up,
        char_down,
        char_proj,
        char_norm_gain,
        char_norm_bias,
        char_mlp_gain,
        char_mlp_bias,
        pool_query,
        word_norm_gain,
        word_norm_bias,
        word_mlp_gain,
        word_mlp_bias,
        language_table.T,
    )
    flat = jnp.concatenate([part.astype(low).reshape(-1) for part in char_parts])
    flat_size = flat.shape[0]
    flat = jnp.pad(flat, (0, -flat_size % 2048))
    full = lax.all_gather(flat, BOTH, axis=0, tiled=False)
    unpacked, start = [], 0
    for part in char_parts:
        stop = start + part.size
        piece = full[:, start:stop].reshape((devices * part.shape[0],) + part.shape[1:])
        unpacked.append(piece)
        start = stop
    (
        qkv_char,
        out_char,
        up_char,
        down_char,
        proj_char,
        gain_attn,
        bias_attn,
        gain_mlp,
        bias_mlp,
        query_pool,
        gain_one,
        bias_one,
        gain_two,
        bias_two,
        table_t,
    ) = unpacked

    word_parts = (word_qkv, word_out.T, word_up, word_down.T)
    word_flat = jnp.concatenate([part.astype(low).reshape(-1, 128) for part in word_parts])
    word_full = lax.all_gather(word_flat, BOTH, axis=0, tiled=False)
    word_full = word_full.reshape(dp_size, mp_size, word_flat.shape[0], 128)
    word_weights, start = [], 0
    for part in word_parts:
        stop = start + part.size // 128
        piece = word_full[:, :, start:stop].reshape((dp_size, mp_size) + part.shape)
        if part.ndim == 3:
            piece = piece.transpose(2, 0, 3, 1, 4).reshape(3, model, model)
        else:
            piece = piece.transpose(0, 2, 1, 3)
            piece = piece.reshape(dp_size * part.shape[0], mp_size * part.shape[1])
        word_weights.append(piece)
        start = stop

    rows = word_count * chars
    states = char_states.reshape(rows, width)
    counts = char_counts.reshape(-1, 128)
    head_masks, word_masks, ones = mask_constants(width, chars)
    zero = jnp.zeros_like(gain_attn)
    vecs = jnp.stack(
        (gain_attn, bias_attn, gain_mlp, bias_mlp, query_pool, zero, zero, zero)
    ).astype(wide)
    cp, probs, co, y1, hidden, slope, y2, pi, pooled = char_forward(
        states,
        counts,
        (qkv_char, out_char, up_char, down_char, ones, vecs, head_masks, word_masks),
        chars,
    )

    sequences = max(1, word_count // LEN)
    first = (mp_index * word_count) // LEN
    language = lax.dynamic_slice_in_dim(language_group, first, sequences)
    language_hot = (language[:, None] == jnp.arange(langs)[None]).astype(wide)
    language_rows = jnp.sum(language_hot[:, :, None] * table_t.T.astype(wide)[None], axis=1)
    residual = word_states.astype(wide) + matmul(pooled, proj_char)
    residual = (
        residual.reshape(sequences, -1, model) + language_rows[:, None, :]
    ).reshape(word_count, model)
    norms = tuple(value.astype(wide) for value in (gain_one, bias_one, gain_two, bias_two))
    layer_output, grad_residual, word_grads, word_norm_grads = word_layer(
        residual, output_grad, word_weights, norms, mp_size, mp_index
    )
    grad_words = grad_residual.astype(low)
    sequence_grads = jnp.sum(grad_residual.reshape(sequences, -1, model), axis=1)
    grad_table = jnp.sum(language_hot[:, :, None] * sequence_grads[:, None, :], axis=0)

    pieces = []
    for part, grad in zip(word_parts, word_grads):
        if part.ndim == 3:
            grad = grad.reshape(3, dp_size, part.shape[1], mp_size, part.shape[2])
            grad = grad.transpose(3, 1, 0, 2, 4)
        else:
            grad = grad.reshape(dp_size, part.shape[0], mp_size, part.shape[1])
            grad = grad.transpose(2, 0, 1, 3)
        pieces.append(grad.astype(low).reshape(mp_size, dp_size, -1, 128))
    word_terms = jnp.concatenate(pieces, axis=2)
    word_terms = lax.psum_scatter(word_terms, "mp", scatter_dimension=0, tiled=True)
    word_terms = lax.psum_scatter(word_terms[0], "dp", scatter_dimension=0, tiled=True)[0]
    word_shares, start = [], 0
    for part in word_parts:
        stop = start + part.size // 128
        word_shares.append(word_terms[start:stop].reshape(part.shape).astype(wide))
        start = stop

    grad_proj = mm(pooled, grad_words, TN)
    grad_pooled = mm(grad_words, proj_char, NT).reshape(word_count, 1, width)
    grad_y1, grad_up, grad_down_t, mlp_vecs = char_mlp_back(
        y1, y2, pi, grad_pooled, hidden, slope, (up_char.T, down_char.T, vecs, ones), chars
    )
    mlp_vecs = jnp.sum(mlp_vecs, axis=1)
    early = (
        grad_up,
        grad_down_t.T,
        grad_proj,
        mlp_vecs[0],
        mlp_vecs[1],
        mlp_vecs[2],
        word_norm_grads[0],
        word_norm_grads[1],
        word_norm_grads[2],
        word_norm_grads[3],
        grad_table.T,
    )
    early_terms = jnp.concatenate([blocks_of(part, devices) for part in early], axis=1)
    early_size = early_terms.shape[1]
    early_terms = jnp.pad(early_terms, ((0, 0), (0, -early_size % 1024)))
    early_terms = lax.psum_scatter(early_terms, BOTH, scatter_dimension=0, tiled=True)[0]
    grad_chars, grad_qkv, grad_out, attn_vecs = char_attn_back(
        states, cp, probs, co, grad_y1, (qkv_char.T, out_char.T, vecs, head_masks, word_masks), chars
    )
    attn_vecs = jnp.sum(attn_vecs, axis=1)
    late = (grad_qkv, grad_out, attn_vecs[0], attn_vecs[1])
    late_terms = jnp.concatenate([blocks_of(part, devices) for part in late], axis=1)
    late_terms = jnp.pad(late_terms, ((0, 0), (0, -late_terms.shape[1] % 1024)))
    late_terms = lax.psum_scatter(late_terms, BOTH, scatter_dimension=0, tiled=True)[0]

    def take(terms, parts):
        shares, start = [], 0
        for part in parts:
            stop = start + part.size // devices
            shape = (part.shape[0] // devices,) + part.shape[1:]
            shares.append(terms[start:stop].reshape(shape))
            start = stop
        return shares

    (
        g_up,
        g_down,
        g_proj,
        g_query,
        g_gain_mlp,
        g_bias_mlp,
        g_gain_one,
        g_bias_one,
        g_gain_two,
        g_bias_two,
        g_table_t,
    ) = take(early_terms, early)
    g_qkv, g_out, g_gain_attn, g_bias_attn = take(late_terms, late)
    return (
        layer_output,
        grad_chars.reshape(char_states.shape),
        grad_words,
        g_gain_attn,
        g_bias_attn,
        g_qkv,
        g_out,
        g_gain_mlp,
        g_bias_mlp,
        g_up,
        g_down,
        g_query,
        g_proj,
        g_table_t.T,
        g_gain_one,
        g_bias_one,
        word_shares[0],
        word_shares[1].T,
        g_gain_two,
        g_bias_two,
        word_shares[2],
        word_shares[3].T,
    )


def fits(dp, mp, words, model, width, chars, hidden_width, langs):
    count = dp * mp
    return (
        words == LEN
        and mp % 2 == 0
        and model == 128 * mp
        and model // dp % 16 == 0
        and width == 256
        and width == 8 * count
        and hidden_width % (16 * count) == 0
        and GROUP % chars == 0
        and langs == 8
    )


def shards(*arrays):
    char_states, word_states = arrays[:2]
    dp, mp = lax.axis_size("dp"), lax.axis_size("mp")
    words, chars, width = char_states.shape
    model, hidden_width = word_states.shape[1], arrays[11].shape[1]
    if not fits(dp, mp, words, model, width, chars, hidden_width, arrays[15].shape[0]):
        return shards_general(*arrays)
    return shards_whole(*arrays)


def shards_whole(
    char_states,
    word_states,
    char_counts,
    language_group,
    output_grad,
    char_norm_gain,
    char_norm_bias,
    char_qkv,
    char_out,
    char_mlp_gain,
    char_mlp_bias,
    char_up,
    char_down,
    pool_query,
    char_proj,
    language_table,
    word_norm_gain,
    word_norm_bias,
    word_qkv,
    word_out,
    word_mlp_gain,
    word_mlp_bias,
    word_up,
    word_down,
):
    low, wide = jnp.bfloat16, jnp.float32
    dp, mp = lax.axis_size("dp"), lax.axis_size("mp")
    count = dp * mp
    index = lax.axis_index("dp") * mp + lax.axis_index("mp")
    words, chars, width = char_states.shape
    model = word_states.shape[1]
    langs = language_table.shape[0]
    hidden_width = char_up.shape[1]
    small = (char_norm_gain, char_norm_bias, char_mlp_gain, char_mlp_bias, pool_query)
    small += (word_norm_gain, word_norm_bias, word_mlp_gain, word_mlp_bias)
    (
        qkv,
        qkv_t,
        out,
        out_t,
        up,
        up_t,
        down,
        down_t,
        proj,
        vecs,
        norms,
        table,
        word_share,
    ) = gather_weights(
        dp,
        mp,
        (char_qkv, char_out, char_up, char_down, char_proj),
        language_table,
        tuple(value[None] for value in small),
        (word_qkv, word_out.T, word_up, word_down.T),
    )
    word_weights = lax.all_gather(word_share, BOTH, axis=0, tiled=False)
    word_weights = word_weights.reshape(dp, mp, word_share.shape[0], 128)
    char_share, word_part = width // count, model // count

    rows = words * chars
    states = char_states.reshape(rows, width)
    counts = char_counts.reshape(-1, 128)
    head_masks, word_masks, ones = mask_constants(width, chars)
    cp, probs, co, y1, hidden, slope, y2, pi, pooled = char_forward(
        states,
        counts,
        (qkv, out, up, down, ones, vecs, head_masks, word_masks),
        chars,
    )

    language = lax.dynamic_slice_in_dim(language_group, lax.axis_index("mp"), 1)
    layer_output, grad_words, word_terms, grad_proj, grad_pooled, small_terms = word_layer_kernel(
        pooled,
        word_states,
        output_grad,
        language,
        table,
        proj,
        word_weights,
        norms,
        head_masks,
    )

    grad_y1, char_terms, g_word_qkv, g_word_out, g_word_up, g_word_down = char_mlp_back_exchange(
        y1, y2, pi, grad_pooled, hidden, slope, (up_t, down_t, vecs, ones), chars, (dp, mp),
        grad_proj, small_terms, word_terms,
    )
    grad_chars, g_qkv, g_out, g_up, g_down, g_proj, g_small, g_vecs = char_attn_back_exchange(
        states, cp, probs, co, grad_y1, (qkv_t, out_t, vecs, head_masks, word_masks), chars,
        (dp, mp), char_terms, hidden_width, model,
    )
    places = jnp.stack(((model - index * word_part) % model, (width - index * char_share) % width))
    shares = (
        g_qkv, g_out, g_up, g_down, g_proj, g_word_qkv, g_word_out, g_word_up, g_word_down,
    )
    grad_chars, *shares = hand_out(
        places, grad_chars, shares, g_small, g_vecs, word_part, char_share
    )
    g_qkv, g_out, g_up, g_down, g_proj, g_word_qkv, g_word_out, g_word_up, g_word_down = shares[:9]
    g_table, *small_shares = shares[9:]
    norm_shares = [value[0] for value in small_shares]
    return (
        layer_output,
        grad_chars.reshape(char_states.shape),
        grad_words,
        norm_shares[7],
        norm_shares[8],
        g_qkv,
        g_out,
        norm_shares[5],
        norm_shares[6],
        g_up,
        g_down,
        norm_shares[4],
        g_proj,
        g_table,
        norm_shares[0],
        norm_shares[1],
        g_word_qkv,
        g_word_out.T,
        norm_shares[2],
        norm_shares[3],
        g_word_up,
        g_word_down.T,
    )


def solution(mesh):
    vector, rows = P(BOTH), P(BOTH, None)
    cube = P(BOTH, None, None)
    table = P(None, BOTH)
    words = (P(None, "dp", "mp"), P("mp", "dp"), P("dp", "mp"), P("mp", "dp"))
    char_weights = (
        vector, vector, rows, rows, vector, vector, rows, rows, vector, rows, table,
    )
    weights = char_weights + (
        vector, vector, words[0], words[1], vector, vector, words[2], words[3],
    )
    return jax.shard_map(
        shards,
        mesh=mesh,
        in_specs=(cube, rows, vector, P("dp"), rows) + weights,
        out_specs=(rows, cube, rows) + weights,
        check_vma=False,
    )
```

```python
import functools

import jax
import jax.numpy as jnp
import ml_dtypes
import numpy as np
from jax import lax
from jax.experimental import pallas as pl
from jax.experimental.pallas import tpu as pltpu
from jax.sharding import PartitionSpec as P

HEAD = 64
CHAR_HEADS = 4
LEN = 1024
GROUP = 128
SUB = 1024
CHUNK = 256
SHARES = 9
WORD_PARTS = 4


NORM_EPS = 1e-05
NEG_FILL = -1000000000.0
BOTH = ("dp", "mp")
MESH = pl.DeviceIdType.MESH

LOGIT = (
    0.7978697123195114,
    0.036392286136226214,
    -8.782649734580825e-05,
    -3.669345726473906e-05,
    1.4250064727244771e-06,
)

EXP2_SCALE = HEAD ** (-0.5) * 1.4426950408889634
NN = (((1,), (0,)), ((), ()))
NT = (((1,), (1,)), ((), ()))
TN = (((0,), (0,)), ((), ()))


def mm(first_arg, second_arg, dims=NN):
    return lax.dot_general(first_arg, second_arg, dims, preferred_element_type=jnp.float32)


def matmul(first_arg, second_arg):
    return jnp.dot(first_arg, second_arg, preferred_element_type=jnp.float32)


def low_sum(pattern, first_arg, second_arg):
    return jnp.einsum(pattern, first_arg, second_arg, preferred_element_type=jnp.float32)


def standardize(values):
    centred = values - jnp.mean(values, axis=-1, keepdims=True)
    inverse = lax.rsqrt(jnp.mean(centred * centred, axis=-1, keepdims=True) + NORM_EPS)
    return (centred * inverse, inverse)


def apply_norm(values, gain_value, bias_value):
    unit_rows, inverse = standardize(values)
    normed = (unit_rows * gain_value + bias_value).astype(jnp.bfloat16)
    return (unit_rows, inverse, normed)


def norm_back(grad_out, unit_rows, inverse, gain_value):
    grad_unit = grad_out * gain_value
    inner_sum = jnp.mean(grad_unit * unit_rows, axis=-1, keepdims=True)
    return inverse * (
        grad_unit - jnp.mean(grad_unit, axis=-1, keepdims=True) - unit_rows * inner_sum
    )


def gelu_pair(values):
    square = values * values
    logit = square * LOGIT[4] + LOGIT[3]
    for term in LOGIT[2::-1]:
        logit = logit * square + term
    normal = jnp.tanh(logit * values) * 0.5 + 0.5
    density = jnp.exp2(square * -0.7213475204444817 - 1.3257480647361593)
    return (values * normal, values * density + normal)


def strips(function, size, *arrays):
    parts = [
        function(*(array[row : row + size] for array in arrays))
        for row in range(0, arrays[0].shape[0], size)
    ]
    return tuple(jnp.concatenate(part, axis=0) for part in zip(*parts))


def gelu_low(values):
    return strips(
        lambda strip: gelu_pair(strip.astype(jnp.bfloat16)), 64 * 256 // values.shape[1], values
    )


def split_two(values):
    high = values.astype(jnp.bfloat16)
    return (high, (values - high.astype(jnp.float32)).astype(jnp.bfloat16))


def fold_rows(values):
    return jnp.sum(values.reshape(values.shape[0] // 8, 8, values.shape[1]), axis=0)


class Place:
    def __init__(self, dp, mp):
        self.dp, self.mp, self.wide = dp, mp, mp // 2
        self.i, self.j = lax.axis_index("dp"), lax.axis_index("mp")
        self.x, self.core = self.j // 2, lax.rem(self.j, 2)

    def partner(self):
        return (self.i, 2 * self.x + 1 - self.core)

    def across(self, step):
        return (self.i, 2 * lax.rem(self.x + step, self.wide) + self.core)

    def along(self, step):
        return (lax.rem(self.i + step, self.dp), self.j)

    def greet(self):
        barrier = pltpu.get_barrier_semaphore()
        others = [self.partner()]
        others += [self.across(step) for step in range(1, self.wide)]
        others += [self.along(step) for step in range(1, self.dp)]
        for other in others:
            pl.semaphore_signal(barrier, inc=1, device_id=other, device_id_type=MESH)
        pl.semaphore_wait(barrier, len(others))


def remote(source, target, sems, index, device):
    return pltpu.make_async_remote_copy(
        src_ref=source,
        dst_ref=target,
        send_sem=sems[0].at[index],
        recv_sem=sems[1].at[index],
        device_id=device,
        device_id_type=MESH,
    )


class ScatterSum:
    def __init__(self, place, blocks, local, one, two, three, sems, part=0, parts=1):
        self.place, self.blocks, self.local = place, blocks, local
        self.one, self.two, self.three, self.sems = one, two, three, sems
        size = blocks.shape[2] // parts
        self.span = slice(part * size, (part + 1) * size)
        self.sem = part * copies_of(place.dp, place.mp)

    def first(self):
        place = self.place
        return [
            remote(
                self.blocks.at[2 * e + 1 - place.core, :, self.span],
                self.one.at[e, :, self.span],
                self.sems,
                self.sem + e,
                place.partner(),
            )
            for e in range(place.wide)
        ]

    def second(self):
        place = self.place
        return [
            remote(
                self.one.at[lax.rem(place.x + step, place.wide), :, self.span],
                self.two.at[step - 1, :, self.span],
                self.sems,
                self.sem + place.wide + step - 1,
                place.across(step),
            )
            for step in range(1, place.wide)
        ]

    def third(self):
        place = self.place
        return [
            remote(
                self.one.at[place.x, lax.rem(place.i + step, place.dp), self.span],
                self.three.at[step - 1, self.span],
                self.sems,
                self.sem + 2 * place.wide - 1 + step - 1,
                place.along(step),
            )
            for step in range(1, place.dp)
        ]

    def start(self):
        for copy in self.first():
            copy.start()

    def go_across(self):
        place, span = self.place, self.span
        for copy in self.first():
            copy.wait()

        @pl.loop(0, place.dp)
        def _(row):
            for e in range(place.wide):
                own = self.local(e, row, span).astype(jnp.float32)
                total = self.one[e, row, span].astype(jnp.float32) + own
                self.one[e, row, span] = total.astype(jnp.bfloat16)

        for copy in self.second():
            copy.start()

    def go_along(self):
        place, span = self.place, self.span
        for copy in self.second():
            copy.wait()

        @pl.loop(0, place.dp)
        def _(row):
            total = self.one[place.x, row, span].astype(jnp.float32)
            for step in range(1, place.wide):
                total = total + self.two[step - 1, row, span].astype(jnp.float32)
            self.one[place.x, row, span] = total.astype(jnp.bfloat16)

        for copy in self.third():
            copy.start()

    def finish(self):
        place = self.place
        for copy in self.third():
            copy.wait()

        def own(rows):
            total = self.one[place.x, place.i, rows].astype(jnp.float32)
            for step in range(1, place.dp):
                total = total + self.three[step - 1, rows].astype(jnp.float32)
            return total

        return own


def copies_of(dp, mp):
    return 2 * (mp // 2) - 1 + dp - 1


def scatter_scratch(dp, mp, n, parts=1):
    wide = mp // 2
    copies = copies_of(dp, mp) * parts
    return [
        pltpu.VMEM((wide, dp, n, 128), jnp.bfloat16),
        pltpu.VMEM((max(1, wide - 1), dp, n, 128), jnp.bfloat16),
        pltpu.VMEM((dp - 1, n, 128), jnp.bfloat16),
        pltpu.SemaphoreType.DMA((copies,)),
        pltpu.SemaphoreType.DMA((copies,)),
    ]


def put_pairs(target, first_row, columns):
    mp, dp = target.shape[0], target.shape[1]
    rows = columns.shape[0] // (mp * dp)
    for pair in range(columns.shape[1] // 256):
        both = [
            columns[:, 256 * pair + 128 * c : 256 * pair + 128 * c + 128].reshape(
                dp, mp, rows, 128
            )
            for c in range(2)
        ]
        both = jnp.concatenate(both, axis=2).astype(jnp.bfloat16)
        spot = slice(first_row + 2 * rows * pair, first_row + 2 * rows * (pair + 1))
        for j in range(mp):
            target[j, :, spot, :] = both[:, j]


def gather_kernel(dp, mp, *refs):
    gather_body(dp, mp, *refs[:6], refs[6:15], *refs[15:])


def gather_body(
    dp,
    mp,
    qkv_ref,
    out_ref,
    up_ref,
    down_ref,
    proj_ref,
    table_ref,
    small_refs,
    word_qkv_ref,
    word_out_ref,
    word_up_ref,
    word_down_ref,
    qkv_all,
    qkv_t_all,
    out_all,
    out_t_all,
    up_all,
    up_t_all,
    down_all,
    down_t_all,
    proj_all,
    vecs_all,
    norms_all,
    table_all,
    word_share,
    held,
    tile,
    sends,
    arrivals,
):
    place = Place(dp, mp)
    low = jnp.bfloat16
    i, j = place.i, place.j
    row = 0
    for part in (qkv_ref, out_ref, up_ref, proj_ref):
        for pair in range(part.shape[1] // 256):
            both = [part[:, 256 * pair + 128 * c : 256 * pair + 128 * c + 128] for c in range(2)]
            held[i, j, row : row + 16, :] = jnp.concatenate(both, axis=0).astype(low)
            row += 16
    down_rows = down_ref.shape[0]
    for c in range(2):
        held[i, j, row : row + down_rows, :] = down_ref[:, 128 * c : 128 * c + 128].astype(low)
        row += down_rows
    word_part, char_part = table_ref.shape[1], small_refs[0].shape[1]
    tile[...] = jnp.zeros_like(tile)
    tile[0:8, 0:word_part] = table_ref[...]
    for k in range(4):
        tile[8 + k : 9 + k, 0:word_part] = small_refs[5 + k][...]
        tile[12 + k : 13 + k, 0:char_part] = small_refs[k][...]
    tile[12:13, char_part : 2 * char_part] = small_refs[4][...]
    held[i, j, row : row + 16, :] = tile[...].astype(low)
    place.greet()
    sems = (sends, arrivals)
    wide = place.wide

    def share(step, e):
        return held.at[
            lax.rem(i + dp - step, dp), 2 * lax.rem(place.x + wide - e, wide) + place.core
        ]

    def other_core(step, e):
        return held.at[
            lax.rem(i + dp - step, dp), 2 * lax.rem(place.x + wide - e, wide) + 1 - place.core
        ]

    def along(step):
        return remote(held.at[i, j], held.at[i, j], sems, step - 1, place.along(step))

    def across(step, e):
        index = dp - 1 + step * (wide - 1) + e - 1
        return remote(share(step, 0), share(step, 0), sems, index, place.across(e))

    def over(step, e):
        index = dp - 1 + dp * (wide - 1) + step * wide + e
        return remote(share(step, e), share(step, e), sems, index, place.partner())

    for step in range(1, dp):
        along(step).start()
    for e in range(1, wide):
        across(0, e).start()
    over(0, 0).start()

    rows = word_up_ref.shape[0]
    for t in range(3):
        word_share[rows * t : rows * (t + 1), :] = word_qkv_ref[t].astype(low)
    word_share[3 * rows : 4 * rows, :] = word_out_ref[...].astype(low)
    blocks = word_up_ref.shape[1] // 128
    for c in range(blocks):
        spot = slice((4 + c) * rows, (5 + c) * rows)
        word_share[spot, :] = word_up_ref[:, 128 * c : 128 * c + 128].astype(low)
        spot = slice((4 + blocks + c) * rows, (5 + blocks + c) * rows)
        word_share[spot, :] = word_down_ref[:, 128 * c : 128 * c + 128].astype(low)

    for step in range(1, dp):
        along(step).wait_recv()
        for e in range(1, wide):
            across(step, e).start()
        over(step, 0).start()
    for step in range(dp):
        for e in range(1, wide):
            across(step, e).wait_recv()
            over(step, e).start()
    for step in range(dp):
        for e in range(wide):
            over(step, e).wait_recv()
    for step in range(1, dp):
        along(step).wait_send()
    for step in range(dp):
        for e in range(1, wide):
            across(step, e).wait_send()
        for e in range(wide):
            over(step, e).wait_send()

    count = dp * mp
    row = 0
    for target, target_t in (
        (qkv_all, qkv_t_all),
        (out_all, out_t_all),
        (up_all, up_t_all),
        (proj_all, None),
    ):
        for pair in range(target.shape[1] // 256):
            both = held[:, :, row : row + 16, :].reshape(count, 16, 128).astype(jnp.float32)
            row += 16
            for c in range(2):
                piece = both[:, 8 * c : 8 * c + 8].reshape(8 * count, 128).astype(low)
                spot = slice(256 * pair + 128 * c, 256 * pair + 128 * c + 128)
                target[:, spot] = piece
                if target_t is not None:
                    target_t[spot, :] = piece.T
    for c in range(2):
        piece = held[:, :, row : row + down_rows, :].reshape(count * down_rows, 128)
        row += down_rows
        down_all[:, 128 * c : 128 * c + 128] = piece
        down_t_all[128 * c : 128 * c + 128, :] = piece.T
    small = held[:, :, row : row + 16, :].reshape(count, 16, 128).astype(jnp.float32)
    lane = lax.broadcasted_iota(jnp.int32, (16, 128), 1)
    for part, width in ((word_part, norms_all.shape[1]), (char_part, vecs_all.shape[1])):
        per = 128 // part
        for b in range(width // 128):
            total = small[b * per]
            other = pltpu.roll(total, 128 - part, 1)
            for k in range(1, per):
                piece = small[b * per + k]
                total = jnp.where(lane // part == k, pltpu.roll(piece, part * k, 1), total)
                moved = pltpu.roll(piece, part * (k - 1), 1) if k > 1 else piece
                other = jnp.where(lane // part == k, moved, other)
            cols = slice(128 * b, 128 * b + 128)
            if part == word_part:
                table_all[:, cols] = total[0:8]
                norms_all[:, cols] = total[8:12]
            else:
                vecs_all[0:4, cols] = total[12:16]
                vecs_all[4:5, cols] = other[12:13]
                vecs_all[5:8, cols] = jnp.zeros((3, 128), jnp.float32)


def gather_weights(dp, mp, parts, table, small, word_parts):
    low = jnp.bfloat16
    qkv, out, up, down, proj = parts
    count = dp * mp
    width = qkv.shape[0] * count
    hidden = up.shape[1]
    model = proj.shape[1]
    rows = (qkv.shape[1] + out.shape[1] + up.shape[1] + proj.shape[1]) // 128 * 8
    rows += 2 * down.shape[0] + 16
    word_rows = sum(part.size for part in word_parts) // 128
    copies = dp - 1 + dp * (mp // 2 - 1) + dp * (mp // 2)
    shapes = (
        (width, 3 * width),
        (3 * width, width),
        (width, width),
        (width, width),
        (width, hidden),
        (hidden, width),
        (hidden, width),
        (width, hidden),
        (width, model),
        (8, width),
        (4, model),
        (8, model),
        (word_rows, 128),
    )
    wide = (9, 10, 11)
    arrays = (qkv, out, up, down, proj, table, *small, *word_parts)
    return pl.pallas_call(
        functools.partial(gather_kernel, dp, mp),
        grid=(1,),
        in_specs=[once(array.shape) for array in arrays],
        out_specs=[once(shape) for shape in shapes],
        out_shape=[
            jax.ShapeDtypeStruct(shape, jnp.float32 if k in wide else low)
            for k, shape in enumerate(shapes)
        ],
        scratch_shapes=[
            pltpu.VMEM((dp, mp, rows, 128), low),
            pltpu.VMEM((16, 128), jnp.float32),
            pltpu.SemaphoreType.DMA((copies,)),
            pltpu.SemaphoreType.DMA((copies,)),
        ],
        compiler_params=pltpu.CompilerParams(
            collective_id=0, has_side_effects=True, vmem_limit_bytes=60 * 1024 * 1024
        ),
        name="gather_weights",
    )(*arrays)


def head_rows(rows, masks):
    return jnp.concatenate([rows * masks[h : h + 1] for h in range(CHAR_HEADS)], axis=0)


def gather_diagonal(square, lane_word, chars):
    words = square.shape[1] // chars
    blocks = square.reshape(CHAR_HEADS, words, chars, square.shape[1])
    kept = blocks[:, 0]
    for word in range(1, words):
        kept = jnp.where(lane_word == word, blocks[:, word], kept)
    return kept


def spread_diagonal(kept, word_masks, chars):
    words = kept.shape[2] // chars
    parts = [kept * word_masks[word : word + 1] for word in range(words)]
    return jnp.stack(parts, axis=1)


def norm_strips(values, gain_value, bias_value):
    return strips(lambda strip: apply_norm(strip, gain_value, bias_value), 64, values)


def char_forward_kernel(
    chars,
    chars_ref,
    count_ref,
    qkv_ref,
    out_ref,
    up_ref,
    down_ref,
    ones_ref,
    vecs_ref,
    head_mask_ref,
    word_mask_ref,
    cp_ref,
    probs_ref,
    co_ref,
    y1_ref,
    hidden_ref,
    slope_ref,
    y2_ref,
    pi_ref,
    pooled_ref,
):
    rows, width = chars_ref.shape
    low, wide = jnp.bfloat16, jnp.float32
    lane_word = lax.broadcasted_iota(jnp.int32, (1, 1, GROUP), 2) // chars
    key_slot = lax.broadcasted_iota(jnp.int32, (1, chars, GROUP), 1).astype(wide)
    words = rows // chars
    step = pl.program_id(0)
    counts = count_ref[pl.ds(step * words // 128, 1), :].astype(wide)
    word = lax.broadcasted_iota(jnp.int32, (rows // GROUP, 128), 1) - lax.rem(step * words, 128)
    group = lax.broadcasted_iota(jnp.int32, (rows // GROUP, 128), 0)
    counts = jnp.where(word // (GROUP // chars) == group, counts, 0.0)
    repeats = 128 * chars // GROUP
    spread = jnp.concatenate([word_mask_ref[...].astype(wide)] * repeats, axis=0).astype(low)
    lane_counts = mm(counts.astype(low), spread)
    row_slot = lax.rem(lax.broadcasted_iota(jnp.int32, (GROUP, GROUP), 0), chars).astype(wide)
    masks = head_mask_ref[...]
    word_masks = word_mask_ref[...]
    block = SUB
    parts = up_ref.shape[1] // CHUNK

    def project(s):
        span = slice(s * block, (s + 1) * block)
        states = chars_ref[span, :].astype(wide)
        _, _, normed = norm_strips(states, vecs_ref[0:1, :], vecs_ref[1:2, :])
        cp_ref[span, :] = mm(normed, qkv_ref[...]).astype(low)

    def groups_of(s):
        return [slice(row, row + GROUP) for row in range(s * block, (s + 1) * block, GROUP)]

    scores, probs = {}, {}

    def attend_scores(s):
        scores[s] = []
        for span in groups_of(s):
            keys = head_rows(cp_ref[span, width : 2 * width], masks)
            square = mm(keys, cp_ref[span, 0:width], NT)
            scores[s].append(gather_diagonal(square, lane_word, chars))

    def attend_probs(s):
        probs[s] = []
        for span, score in zip(groups_of(s), scores[s]):
            group = span.start // GROUP
            score = jnp.where(
                key_slot < lane_counts[group : group + 1], score * EXP2_SCALE, NEG_FILL
            )
            powers = jnp.exp2(score - jnp.max(score, axis=1, keepdims=True))
            share = 1.0 / jnp.sum(powers, axis=1, keepdims=True)
            probs[s].append((powers * share).astype(low))
            probs_ref[group] = probs[s][-1].reshape(CHAR_HEADS * chars, GROUP)

    def attend_values(s):
        for span, prob in zip(groups_of(s), probs[s]):
            values = head_rows(cp_ref[span, 2 * width : 3 * width], masks)
            spread = spread_diagonal(prob, word_masks, chars)
            spread = spread.reshape(CHAR_HEADS * GROUP, GROUP)
            co_ref[span, :] = mm(spread, values, TN).astype(low)

    def middle(s):
        span = slice(s * block, (s + 1) * block)
        after_attn = chars_ref[span, :].astype(wide) + mm(co_ref[span, :], out_ref[...])
        y1_ref[span, :] = after_attn
        return norm_strips(after_attn, vecs_ref[2:3, :], vecs_ref[3:4, :])[2]

    def pool_scores(s):
        query = vecs_ref[4:5, :] * EXP2_SCALE
        high, low_part = strips(lambda strip: split_two(strip * query), 64, totals[s])
        return mm(high, ones_ref[...]) + mm(low_part, ones_ref[...])

    def pool(s, scores):
        total = totals[s]
        pooled = []
        for k in range(block // GROUP):
            group = s * block // GROUP + k
            spot = slice(k * GROUP, (k + 1) * GROUP)
            span = slice(s * block + k * GROUP, s * block + (k + 1) * GROUP)
            counts = jnp.broadcast_to(lane_counts[group : group + 1], (GROUP, GROUP)).T
            valid = row_slot < counts
            halves = []
            for half in range(width // GROUP):
                cols = slice(half * GROUP, (half + 1) * GROUP)
                score = jnp.where(valid, scores[spot, cols], NEG_FILL)
                score = score.reshape(GROUP // chars, chars, GROUP)
                powers = jnp.exp2(score - jnp.max(score, axis=1, keepdims=True))
                pi = powers * (1.0 / jnp.sum(powers, axis=1, keepdims=True))
                pi_ref[span, cols] = pi.reshape(GROUP, GROUP).astype(low)
                grid = total[spot, cols].reshape(GROUP // chars, chars, GROUP)
                halves.append(jnp.sum(pi * grid, axis=1))
            pooled.append(jnp.concatenate(halves, axis=1))
        words = block // chars
        pooled_ref[s * words : (s + 1) * words, :] = jnp.concatenate(pooled, axis=0).astype(low)

    count = rows // block
    normed, totals, hiddens = {}, {}, {}

    def up(s, part):
        if part == 0:
            normed[s] = middle(s)
        return mm(normed[s], up_ref[:, part * CHUNK : (part + 1) * CHUNK])

    def activate(s, part, current, half):
        size = block // 2
        first = s * block + half * size
        span, cols = slice(first, first + size), slice(part * CHUNK, (part + 1) * CHUNK)
        hidden, slope = gelu_low(current[half * size : (half + 1) * size])
        hidden_ref[span, cols] = hidden
        slope_ref[span, cols] = slope
        hiddens[s, part, half] = hidden

    def down(s, part):
        span, cols = slice(s * block, (s + 1) * block), slice(part * CHUNK, (part + 1) * CHUNK)
        hidden = jnp.concatenate([hiddens[s, part, half] for half in range(2)], axis=0)
        term = mm(hidden, down_ref[cols, :])
        totals[s] = term if part == 0 else totals[s] + term
        if part == parts - 1:
            totals[s] = totals[s] + y1_ref[span, :]
            y2_ref[span, :] = totals[s]

    for first in range(0, count, 2):
        pair = range(first, min(first + 2, count))
        for s in pair:
            project(s)
            attend_scores(s)
        for s in pair:
            attend_probs(s)
            attend_values(s)
        order = [(s, part) for part in range(parts) for s in pair]
        ahead = [up(*order[0])]
        pools = []
        for place, (s, part) in enumerate(order):
            if place + 1 < len(order):
                ahead.append(up(*order[place + 1]))
            activate(s, part, ahead[place], 0)
            if place > 0:
                down(*order[place - 1])
            activate(s, part, ahead[place], 1)
        down(*order[-1])
        for s in pair:
            pools.append((s, pool_scores(s)))
            if len(pools) > 1:
                pool(*pools[-2])
        pool(*pools[-1])


def char_mlp_back_kernel(
    chars,
    exchange,
    y1_ref,
    y2_ref,
    pi_ref,
    grad_pooled_ref,
    hidden_ref,
    slope_ref,
    up_t_ref,
    down_t_ref,
    vecs_ref,
    ones_ref,
    *others,
):
    rows, width = y1_ref.shape
    words = rows // chars
    if exchange is None:
        grad_y1_ref, grad_up_ref, grad_down_t_ref, grad_vecs_ref = others
    else:
        (
            grad_proj_ref,
            word_small_ref,
            word_terms_ref,
            grad_y1_ref,
            char_terms_ref,
            word_qkv_ref,
            word_out_ref,
            word_up_ref,
            word_down_ref,
            grad_up_ref,
            grad_down_t_ref,
            grad_vecs_ref,
            local_ref,
            local_sem,
            one_ref,
            two_ref,
            three_ref,
            sends,
            arrivals,
        ) = others
        place = Place(*exchange)
        totals_word = [
            ScatterSum(
                place,
                word_terms_ref,
                lambda e, row, span: local_ref[e, row, span],
                one_ref,
                two_ref,
                three_ref,
                (sends, arrivals),
                part,
                WORD_PARTS,
            )
            for part in range(WORD_PARTS)
        ]
        own = [
            pltpu.make_async_copy(
                word_terms_ref.at[2 * e + place.core], local_ref.at[e], local_sem.at[e]
            )
            for e in range(place.wide)
        ]
        step, last = pl.program_id(0), pl.num_programs(0) - 1

        @pl.when(step == 0)
        def _():
            place.greet()
            for total in totals_word:
                total.start()
            for copy in own:
                copy.start()

        for part, total in enumerate(totals_word):

            @pl.when(step == (1 + part) * last // 15)
            def _(part=part, total=total):
                if part == 0:
                    for copy in own:
                        copy.wait()
                total.go_across()

            @pl.when(step == (4 + 2 * part) * last // 15)
            def _(total=total):
                total.go_along()

    @pl.when(pl.program_id(0) == 0)
    def _():
        grad_up_ref[...] = jnp.zeros_like(grad_up_ref)
        grad_down_t_ref[...] = jnp.zeros_like(grad_down_t_ref)
        grad_vecs_ref[...] = jnp.zeros_like(grad_vecs_ref)

    low, wide = jnp.bfloat16, jnp.float32
    block = SUB
    count, parts = rows // block, hidden_ref.shape[1] // CHUNK
    query = vecs_ref[4:5, :]
    per = 64 // chars

    def pool_back(s):
        spots = [
            (slice(row, row + 64), slice(row // chars, row // chars + per))
            for row in range(s * block, (s + 1) * block, 64)
        ]
        split = [
            split_two(
                (y2_ref[span, :].reshape(per, chars, width) * grad_pooled_ref[span_words]).reshape(
                    64, width
                )
            )
            for span, span_words in spots
        ]
        high, rest = (jnp.concatenate(side, axis=0) for side in zip(*split))
        grad_pi = mm(high, ones_ref[...]) + mm(rest, ones_ref[...])
        wide_parts, low_parts, query_sum = [], [], None
        for k, (span, span_words) in enumerate(spots):
            pi = pi_ref[span, :].astype(wide).reshape(per, chars, width)
            part = grad_pi[64 * k : 64 * (k + 1)].reshape(per, chars, width)
            inner = jnp.sum(pi * part, axis=1, keepdims=True)
            grad_scores = pi * (part - inner) * HEAD ** (-0.5)
            grid = y2_ref[span, :].reshape(per, chars, width)
            term = fold_rows((grad_scores * grid).reshape(64, width))
            query_sum = term if query_sum is None else query_sum + term
            grad = (pi * grad_pooled_ref[span_words] + grad_scores * query).reshape(64, width)
            wide_parts.append(grad)
            low_parts.append(grad.astype(low))
        grad_vecs_ref[0] += query_sum
        return jnp.concatenate(wide_parts, axis=0), jnp.concatenate(low_parts, axis=0)

    def feed_back(s, branch):
        first = s * block
        half = block // 2
        total, unit_strips, last_grad = None, [], None
        grads = []

        def norm_some():
            for _ in range(block // 64 // (2 * parts)):
                row = first + 64 * len(unit_strips)
                unit_strips.append(
                    apply_norm(y1_ref[row : row + 64, :], vecs_ref[2:3, :], vecs_ref[3:4, :])
                )

        def slope_back(current, part, k):
            cols = slice(part * CHUNK, (part + 1) * CHUNK)
            (grad_pre,) = strips(
                lambda strip, slope: (strip.astype(low) * slope,),
                64,
                current[k * half : (k + 1) * half],
                slope_ref[first + k * half : first + (k + 1) * half, cols],
            )
            return grad_pre

        def up_back(total, part):
            term = mm(grads[part], up_t_ref[part * CHUNK : (part + 1) * CHUNK, :])
            return term if total is None else total + term

        ahead = mm(branch, down_t_ref[:, 0:CHUNK])
        for part in range(parts):
            current = ahead
            if part + 1 < parts:
                ahead = mm(branch, down_t_ref[:, (part + 1) * CHUNK : (part + 2) * CHUNK])
            norm_some()
            one = slope_back(current, part, 0)
            if part > 0:
                total = up_back(total, part - 1)
            norm_some()
            grads.append(jnp.concatenate([one, slope_back(current, part, 1)], axis=0))
        total = up_back(total, parts - 1)
        norms[s] = tuple(jnp.concatenate(side, axis=0) for side in zip(*unit_strips))
        return grads, total

    def norm_finish(rows_done, sums):
        s, row = rows_done // block, rows_done % block
        spot = slice(row, row + 64)
        part, (unit, inverse, _), grad = totals[s][spot], norms[s], pooled[s][0][spot]
        part_unit = unit[spot]
        terms = (fold_rows(part * part_unit), fold_rows(part))
        grad_y1_ref[rows_done : rows_done + 64, :] = grad + norm_back(
            part, part_unit, inverse[spot], vecs_ref[2:3, :]
        )
        return terms if sums is None else tuple(a + b for a, b in zip(sums, terms))

    pooled, norms, grads, totals = {}, {}, {}, {}
    pooled[0] = pool_back(0)
    for s in range(count):
        grads[s], totals[s] = feed_back(s, pooled[s][1])
        if s + 1 < count:
            pooled[s + 1] = pool_back(s + 1)
    branch_t = jnp.concatenate([pooled[s][1] for s in range(count)], axis=0).T
    normed_t = jnp.concatenate([norms[s][2] for s in range(count)], axis=0).T
    sums, done = None, 0
    steps = 2 * hidden_ref.shape[1] // width
    for k in range(steps):
        cols = slice(k // 2 * width, (k // 2 + 1) * width)
        if k % 2 == 0:
            grad_down_t_ref[:, cols] += mm(branch_t, hidden_ref[:, cols])
        else:
            part, first = cols.start // CHUNK, cols.start % CHUNK
            grad_pre = [grads[s][part][:, first : first + width] for s in range(count)]
            grad_up_ref[:, cols] += mm(normed_t, jnp.concatenate(grad_pre, axis=0))
        while done < (k + 1) * rows // steps:
            sums = norm_finish(done, sums)
            done += 64
    grad_vecs_ref[1] += sums[0]
    grad_vecs_ref[2] += sums[1]
    if exchange is None:
        return

    @pl.when(step == last)
    def _():
        low = jnp.bfloat16
        share = hidden_ref.shape[1] // (place.dp * place.mp)
        put_pairs(char_terms_ref, 0, grad_up_ref[...])
        row = hidden_ref.shape[1] // 16
        for c in range(2):
            piece = grad_down_t_ref[128 * c : 128 * c + 128, :].T
            piece = piece.reshape(place.dp, place.mp, share, 128).astype(low)
            for j in range(place.mp):
                char_terms_ref[j, :, row : row + share, :] = piece[:, j]
            row += share
        put_pairs(char_terms_ref, row, grad_proj_ref[...])
        row += grad_proj_ref.shape[1] // 16
        sums = [jnp.sum(grad_vecs_ref[k], axis=0, keepdims=True) for k in range(3)]
        small_row = lax.broadcasted_iota(jnp.int32, (16, 128), 0)
        for b in range(word_small_ref.shape[0]):
            piece = word_small_ref[b]
            if b < 2:
                for k in range(3):
                    piece = jnp.where(
                        small_row == 12 + k, sums[k][:, 128 * b : 128 * b + 128], piece
                    )
            piece = jnp.broadcast_to(piece.astype(low), (place.dp, 16, 128))
            for j in range(place.mp):
                char_terms_ref[j, :, row : row + 16, :] = piece
            row += 16
        for total in totals_word:
            result = total.finish()
        block = word_up_ref.shape[0]
        for t in range(3):
            word_qkv_ref[t] = result(slice(block * t, block * (t + 1)))
        word_out_ref[...] = result(slice(3 * block, 4 * block))
        count = word_up_ref.shape[1] // 128
        for c in range(count):
            cols = slice(128 * c, 128 * c + 128)
            word_up_ref[:, cols] = result(slice((4 + c) * block, (5 + c) * block))
            spot = slice((4 + count + c) * block, (5 + count + c) * block)
            word_down_ref[:, cols] = result(spot)


def char_attn_back_kernel(
    chars,
    exchange,
    chars_ref,
    cp_ref,
    probs_ref,
    co_ref,
    grad_y1_ref,
    qkv_t_ref,
    out_t_ref,
    vecs_ref,
    head_mask_ref,
    word_mask_ref,
    *others,
):
    rows, width = chars_ref.shape
    if exchange is None:
        (
            grad_chars_ref,
            grad_qkv_ref,
            grad_out_ref,
            grad_vecs_ref,
            grad_cp_ref,
            grad_co_ref,
        ) = others
    else:
        (
            early_terms_ref,
            grad_chars_ref,
            share_qkv_ref,
            share_out_ref,
            share_up_ref,
            share_down_ref,
            share_proj_ref,
            share_small_ref,
            share_vecs_ref,
            grad_cp_ref,
            grad_co_ref,
            grad_qkv_ref,
            grad_out_ref,
            grad_vecs_ref,
            local_ref,
            local_sem,
            late_terms_ref,
        ) = others[:17]
        early_refs, late_refs = others[17:22], others[22:27]
        place = Place(*exchange)
        early = ScatterSum(
            place,
            early_terms_ref,
            lambda e, row, span: local_ref[e, row, span],
            *early_refs[:3],
            early_refs[3:],
        )
        late = ScatterSum(
            place,
            late_terms_ref,
            lambda e, row, span: late_terms_ref[2 * e + place.core, row, span],
            *late_refs[:3],
            late_refs[3:],
        )
        own = [
            pltpu.make_async_copy(
                early_terms_ref.at[2 * e + place.core], local_ref.at[e], local_sem.at[e]
            )
            for e in range(place.wide)
        ]
        step, last = pl.program_id(0), pl.num_programs(0) - 1

        @pl.when(step == 0)
        def _():
            place.greet()
            early.start()
            for copy in own:
                copy.start()

        @pl.when(step == last // 15)
        def _():
            for copy in own:
                copy.wait()
            early.go_across()

        @pl.when(step == last // 3)
        def _():
            early.go_along()

    @pl.when(pl.program_id(0) == 0)
    def _():
        grad_qkv_ref[...] = jnp.zeros_like(grad_qkv_ref)
        grad_out_ref[...] = jnp.zeros_like(grad_out_ref)
        grad_vecs_ref[...] = jnp.zeros_like(grad_vecs_ref)

    low, wide = jnp.bfloat16, jnp.float32
    lane_word = lax.broadcasted_iota(jnp.int32, (1, 1, GROUP), 2) // chars
    masks = head_mask_ref[...]
    word_masks = word_mask_ref[...]
    scale = HEAD ** (-0.5)
    block = SUB
    count = rows // block

    def out_back(s):
        span = slice(s * block, (s + 1) * block)
        branch = grad_y1_ref[span, :].astype(low)
        grad_co_ref[span, :] = mm(branch, out_t_ref[...]).astype(low)
        return branch

    def norm_some(s, k):
        for row in range(s * block + k * GROUP, s * block + (k + 1) * GROUP, 64):
            states = chars_ref[row : row + 64, :].astype(wide)
            unit_strips.append(apply_norm(states, vecs_ref[0:1, :], vecs_ref[1:2, :]))

    def side_by_side(spread):
        return jnp.concatenate([spread[h] for h in range(CHAR_HEADS)], axis=1)

    def groups_of(s):
        return [slice(row, row + GROUP) for row in range(s * block, (s + 1) * block, GROUP)]

    grad_probs, grad_scores = {}, {}

    def back_probs(s):
        grad_probs[s] = []
        for span in groups_of(s):
            values = head_rows(cp_ref[span, 2 * width : 3 * width], masks)
            square = mm(values, grad_co_ref[span, :], NT)
            grad_probs[s].append(gather_diagonal(square, lane_word, chars))

    def back_scores(s):
        grad_scores[s] = []
        for span, part in zip(groups_of(s), grad_probs[s]):
            probs = probs_ref[span.start // GROUP].reshape(CHAR_HEADS, chars, GROUP)
            spread = spread_diagonal(probs, word_masks, chars)
            spread = spread.reshape(CHAR_HEADS, GROUP, GROUP)
            grad_values = mm(side_by_side(spread), head_rows(grad_co_ref[span, :], masks))
            grad_cp_ref[span, 2 * width : 3 * width] = grad_values.astype(low)
            probs = probs.astype(wide)
            inner = jnp.sum(part * probs, axis=1, keepdims=True)
            grad_scores[s].append((probs * (part - inner)).astype(low))

    def back_keys(s):
        for k, (span, part) in enumerate(zip(groups_of(s), grad_scores[s])):
            norm_some(s, k)
            spread = spread_diagonal(part, word_masks, chars)
            spread = spread.reshape(CHAR_HEADS, GROUP, GROUP)
            queries = head_rows(cp_ref[span, 0:width], masks)
            grad_keys = mm(side_by_side(spread), queries) * scale
            grad_cp_ref[span, width : 2 * width] = grad_keys.astype(low)
            keys = head_rows(cp_ref[span, width : 2 * width], masks)
            grad_queries = mm(spread.reshape(CHAR_HEADS * GROUP, GROUP), keys, TN) * scale
            grad_cp_ref[span, 0:width] = grad_queries.astype(low)

    def project_back(s):
        span = slice(s * block, (s + 1) * block)
        return mm(grad_cp_ref[span, :], qkv_t_ref[...])

    def norm_finish(rows_done, sums):
        s, row = rows_done // block, rows_done % block
        spot, span = slice(row, row + 64), slice(rows_done, rows_done + 64)
        part, (unit, inverse, _) = totals[s][spot], norms[s]
        part_unit = unit[spot]
        terms = (fold_rows(part * part_unit), fold_rows(part))
        grad = grad_y1_ref[span, :] + norm_back(
            part, part_unit, inverse[spot], vecs_ref[0:1, :]
        )
        grad_chars_ref[span, :] = grad.astype(low)
        return terms if sums is None else tuple(a + b for a, b in zip(sums, terms))

    branches, norms, totals = [], {}, {}
    for s in range(count):
        branches.append(out_back(s))
        back_probs(s)
    for s in range(count):
        unit_strips = []
        back_scores(s)
        back_keys(s)
        norms[s] = tuple(jnp.concatenate(side, axis=0) for side in zip(*unit_strips))
        totals[s] = project_back(s)
    normed_t = jnp.concatenate([norms[s][2] for s in range(count)], axis=0).T
    sums, done = None, 0
    for k in range(4):
        if k == 3:
            grad_out_ref[...] += mm(co_ref[...].T, jnp.concatenate(branches, axis=0))
        else:
            cols = slice(k * width, (k + 1) * width)
            grad_qkv_ref[:, cols] += mm(normed_t, grad_cp_ref[:, cols])
        while done < (k + 1) * rows // 4:
            sums = norm_finish(done, sums)
            done += 64
    grad_vecs_ref[0] += sums[0]
    grad_vecs_ref[1] += sums[1]
    if exchange is None:
        return

    @pl.when(step == last)
    def _():
        low = jnp.bfloat16
        put_pairs(late_terms_ref, 0, grad_qkv_ref[...])
        row = 3 * width // 16
        put_pairs(late_terms_ref, row, grad_out_ref[...])
        row += width // 16
        sums = [jnp.sum(grad_vecs_ref[k], axis=0, keepdims=True) for k in range(2)]
        small_row = lax.broadcasted_iota(jnp.int32, (16, 128), 0)
        piece = jnp.zeros((16, 128), jnp.float32)
        for k in range(2):
            for b in range(2):
                piece = jnp.where(
                    small_row == 2 * k + b, sums[k][:, 128 * b : 128 * b + 128], piece
                )
        piece = jnp.broadcast_to(piece.astype(low), (place.dp, 16, 128))
        for j in range(place.mp):
            late_terms_ref[j, :, row : row + 16, :] = piece
        late.start()
        result = early.finish()
        row = 0
        for target, share in (
            (share_up_ref, 8),
            (share_down_ref, share_down_ref.shape[0]),
            (share_proj_ref, 8),
            (share_small_ref, 16),
        ):
            for c in range(target.shape[1] // 128):
                target[:, 128 * c : 128 * c + 128] = result(slice(row, row + share))
                row += share
        late.go_across()
        late.go_along()
        result = late.finish()
        row = 0
        for target in (share_qkv_ref, share_out_ref):
            for c in range(target.shape[1] // 128):
                target[:, 128 * c : 128 * c + 128] = result(slice(row, row + 8))
                row += 8
        share_vecs_ref[...] = result(slice(row, row + 16))


def whole(shape):
    return pl.BlockSpec(shape, lambda step: (0,) * len(shape))


def once(shape):
    return pl.BlockSpec(shape, lambda step: (0,) * len(shape), pipeline_mode=pl.Buffered(1))


def blocked(shape):
    return pl.BlockSpec(shape, lambda step: (step,) + (0,) * (len(shape) - 1))


def params(megabytes):
    return pltpu.CompilerParams(
        dimension_semantics=("arbitrary",), vmem_limit_bytes=megabytes * 1024 * 1024
    )


def block_rows(rows, wanted):
    while rows % wanted:
        wanted //= 2
    return wanted


def char_forward(states, counts, weights, chars):
    rows, width = states.shape
    qkv, out, up, down, ones, vecs, head_masks, word_masks = weights
    block = block_rows(rows, 1024)
    words, groups = block // chars, block // GROUP
    low, wide = jnp.bfloat16, jnp.float32
    shapes = (
        ((rows, 3 * width), low),
        ((rows // GROUP, CHAR_HEADS * chars, GROUP), low),
        ((rows, width), low),
        ((rows, width), wide),
        ((rows, up.shape[1]), low),
        ((rows, up.shape[1]), low),
        ((rows, width), wide),
        ((rows, width), low),
        ((rows // chars, width), low),
    )
    blocks = (
        (block, 3 * width),
        (groups, CHAR_HEADS * chars, GROUP),
        (block, width),
        (block, width),
        (block, up.shape[1]),
        (block, up.shape[1]),
        (block, width),
        (block, width),
        (words, width),
    )
    flops = 2 * rows * width * (4 * width + 2 * up.shape[1] + 8 * width)
    return pl.pallas_call(
        functools.partial(char_forward_kernel, chars),
        grid=(rows // block,),
        in_specs=[
            blocked((block, width)),
            whole(counts.shape),
            whole(qkv.shape),
            whole(out.shape),
            whole(up.shape),
            whole(down.shape),
            whole(ones.shape),
            whole(vecs.shape),
            whole(head_masks.shape),
            whole(word_masks.shape),
        ],
        out_specs=[blocked(shape) for shape in blocks],
        out_shape=[jax.ShapeDtypeStruct(shape, kind) for shape, kind in shapes],
        compiler_params=params(56),
        cost_estimate=pl.CostEstimate(
            flops=flops, bytes_accessed=rows * width * 36, transcendentals=rows * width * 5
        ),
        name="char_forward",
    )(states, counts, qkv, out, up, down, ones, vecs, head_masks, word_masks)


def char_mlp_back(y1, y2, pi, grad_pooled, hidden, slope, weights, chars):
    rows, width = y1.shape
    up_t, down_t, vecs, ones = weights
    block = block_rows(rows, 1024)
    hidden_width = hidden.shape[1]
    wide = jnp.float32
    flops = 2 * rows * width * (4 * hidden_width + 2 * width)
    return pl.pallas_call(
        functools.partial(char_mlp_back_kernel, chars, None),
        grid=(rows // block,),
        in_specs=[
            blocked((block, width)),
            blocked((block, width)),
            blocked((block, width)),
            blocked((block // chars, 1, width)),
            blocked((block, hidden_width)),
            blocked((block, hidden_width)),
            whole(up_t.shape),
            whole(down_t.shape),
            whole(vecs.shape),
            whole(ones.shape),
        ],
        out_specs=[
            blocked((block, width)),
            whole((width, hidden_width)),
            whole((width, hidden_width)),
            whole((3, 8, width)),
        ],
        out_shape=[
            jax.ShapeDtypeStruct((rows, width), wide),
            jax.ShapeDtypeStruct((width, hidden_width), wide),
            jax.ShapeDtypeStruct((width, hidden_width), wide),
            jax.ShapeDtypeStruct((3, 8, width), wide),
        ],
        compiler_params=params(56),
        cost_estimate=pl.CostEstimate(
            flops=flops, bytes_accessed=rows * width * 30, transcendentals=0
        ),
        name="char_mlp_back",
    )(y1, y2, pi, grad_pooled, hidden, slope, up_t, down_t, vecs, ones)


def char_attn_back(states, cp, probs, co, grad_y1, weights, chars):
    rows, width = states.shape
    qkv_t, out_t, vecs, head_masks, word_masks = weights
    block = block_rows(rows, 1024)
    low, wide = jnp.bfloat16, jnp.float32
    flops = 2 * rows * width * 18 * width
    return pl.pallas_call(
        functools.partial(char_attn_back_kernel, chars, None),
        grid=(rows // block,),
        in_specs=[
            blocked((block, width)),
            blocked((block, 3 * width)),
            blocked((block // GROUP, CHAR_HEADS * chars, GROUP)),
            blocked((block, width)),
            blocked((block, width)),
            whole(qkv_t.shape),
            whole(out_t.shape),
            whole(vecs.shape),
            whole(head_masks.shape),
            whole(word_masks.shape),
        ],
        out_specs=[
            blocked((block, width)),
            whole((width, 3 * width)),
            whole((width, width)),
            whole((2, 8, width)),
        ],
        out_shape=[
            jax.ShapeDtypeStruct((rows, width), low),
            jax.ShapeDtypeStruct((width, 3 * width), wide),
            jax.ShapeDtypeStruct((width, width), wide),
            jax.ShapeDtypeStruct((2, 8, width), wide),
        ],
        scratch_shapes=[
            pltpu.VMEM((block, 3 * width), low),
            pltpu.VMEM((block, width), low),
        ],
        compiler_params=params(56),
        cost_estimate=pl.CostEstimate(
            flops=flops, bytes_accessed=rows * width * 18, transcendentals=0
        ),
        name="char_attn_back",
    )(states, cp, probs, co, grad_y1, qkv_t, out_t, vecs, head_masks, word_masks)


def char_mlp_back_exchange(
    y1, y2, pi, grad_pooled, hidden, slope, weights, chars, mesh_size, grad_proj, word_small, word_terms
):
    rows, width = y1.shape
    up_t, down_t, vecs, ones = weights
    dp, mp = mesh_size
    block = block_rows(rows, 1024)
    hidden_width = hidden.shape[1]
    low, wide = jnp.bfloat16, jnp.float32
    model = grad_proj.shape[1]
    flops = 2 * rows * width * (4 * hidden_width + 2 * width)
    char_rows = 2 * hidden_width // 16 + model // 16 + 16 * word_small.shape[0]
    n = word_terms.shape[2]
    share = model // dp
    outs = (
        ((rows, width), wide, blocked((block, width))),
        ((mp, dp, char_rows, 128), low, None),
        ((3, share, 128), wide, None),
        ((share, 128), wide, None),
        ((share, model), wide, None),
        ((share, model), wide, None),
    )
    return pl.pallas_call(
        functools.partial(char_mlp_back_kernel, chars, mesh_size),
        grid=(rows // block,),
        in_specs=[
            blocked((block, width)),
            blocked((block, width)),
            blocked((block, width)),
            blocked((block // chars, 1, width)),
            blocked((block, hidden_width)),
            blocked((block, hidden_width)),
            whole(up_t.shape),
            whole(down_t.shape),
            whole(vecs.shape),
            whole(ones.shape),
            whole(grad_proj.shape),
            whole(word_small.shape),
            pl.BlockSpec(memory_space=pl.ANY),
        ],
        out_specs=[spec or whole(shape) for shape, _, spec in outs],
        out_shape=[jax.ShapeDtypeStruct(shape, kind) for shape, kind, _ in outs],
        scratch_shapes=[
            pltpu.VMEM((width, hidden_width), wide),
            pltpu.VMEM((width, hidden_width), wide),
            pltpu.VMEM((3, 8, width), wide),
            pltpu.VMEM((mp // 2, dp, n, 128), low),
            pltpu.SemaphoreType.DMA((mp // 2,)),
        ]
        + scatter_scratch(dp, mp, n, WORD_PARTS),
        compiler_params=pltpu.CompilerParams(
            dimension_semantics=("arbitrary",),
            vmem_limit_bytes=60 * 1024 * 1024,
            collective_id=1,
            has_side_effects=True,
        ),
        cost_estimate=pl.CostEstimate(
            flops=flops, bytes_accessed=rows * width * 30, transcendentals=0
        ),
        name="char_mlp_back",
    )(
        y1, y2, pi, grad_pooled, hidden, slope, up_t, down_t, vecs, ones,
        grad_proj, word_small, word_terms,
    )


def char_attn_back_exchange(
    states, cp, probs, co, grad_y1, weights, chars, mesh_size, early_terms, hidden_width, model
):
    rows, width = states.shape
    qkv_t, out_t, vecs, head_masks, word_masks = weights
    dp, mp = mesh_size
    count = dp * mp
    block = block_rows(rows, 1024)
    low, wide = jnp.bfloat16, jnp.float32
    flops = 2 * rows * width * 18 * width
    n = early_terms.shape[2]
    late = 4 * width // 16 + 16
    outs = (
        ((rows, width), low, blocked((block, width))),
        ((width // count, 3 * width), wide, None),
        ((width // count, width), wide, None),
        ((width // count, hidden_width), wide, None),
        ((hidden_width // count, width), wide, None),
        ((width // count, model), wide, None),
        ((16, model), wide, None),
        ((16, 128), wide, None),
    )
    return pl.pallas_call(
        functools.partial(char_attn_back_kernel, chars, mesh_size),
        grid=(rows // block,),
        in_specs=[
            blocked((block, width)),
            blocked((block, 3 * width)),
            blocked((block // GROUP, CHAR_HEADS * chars, GROUP)),
            blocked((block, width)),
            blocked((block, width)),
            whole(qkv_t.shape),
            whole(out_t.shape),
            whole(vecs.shape),
            whole(head_masks.shape),
            whole(word_masks.shape),
            pl.BlockSpec(memory_space=pl.ANY),
        ],
        out_specs=[spec or whole(shape) for shape, _, spec in outs],
        out_shape=[jax.ShapeDtypeStruct(shape, kind) for shape, kind, _ in outs],
        scratch_shapes=[
            pltpu.VMEM((block, 3 * width), low),
            pltpu.VMEM((block, width), low),
            pltpu.VMEM((width, 3 * width), wide),
            pltpu.VMEM((width, width), wide),
            pltpu.VMEM((2, 8, width), wide),
            pltpu.VMEM((mp // 2, dp, n, 128), low),
            pltpu.SemaphoreType.DMA((mp // 2,)),
            pltpu.VMEM((mp, dp, late, 128), low),
        ]
        + scatter_scratch(dp, mp, n)
        + scatter_scratch(dp, mp, late),
        compiler_params=pltpu.CompilerParams(
            dimension_semantics=("arbitrary",),
            vmem_limit_bytes=56 * 1024 * 1024,
            collective_id=2,
            has_side_effects=True,
        ),
        cost_estimate=pl.CostEstimate(
            flops=flops, bytes_accessed=rows * width * 18, transcendentals=0
        ),
        name="char_attn_back",
    )(states, cp, probs, co, grad_y1, qkv_t, out_t, vecs, head_masks, word_masks, early_terms)


def share_kernel(places_ref, large_ref, *refs):
    shares, refs = refs[:SHARES], refs[SHARES:]
    small_ref, vecs_ref, large_out_ref, *targets = refs
    large_out_ref[...] = large_ref[...]

    @pl.when(pl.program_id(0) == 0)
    def _():
        for source, target in zip(shares, targets):
            target[...] = source[...]
        table_out, *small_outs = targets[SHARES:]
        word_outs, char_outs = small_outs[:4], small_outs[4:]
        width = 2 * vecs_ref.shape[1]
        word_part, char_part = table_out.shape[1], char_outs[0].shape[1]
        words = pltpu.roll(small_ref[...], places_ref[0], 1)
        table_out[...] = words[0:8, 0:word_part]
        for k, target in enumerate(word_outs):
            target[...] = words[8 + k : 9 + k, 0:word_part]
        early = small_ref[12:15, 0:width]
        late = jnp.concatenate([vecs_ref[0:1, :], vecs_ref[1:2, :]], axis=1)
        late_two = jnp.concatenate([vecs_ref[2:3, :], vecs_ref[3:4, :]], axis=1)
        rows = jnp.concatenate([early, late, late_two, jnp.zeros((3, width), jnp.float32)], axis=0)
        rows = pltpu.roll(rows, places_ref[1], 1)
        for k, target in enumerate(char_outs):
            target[...] = rows[k : k + 1, 0:char_part]


def hand_out(places, large, shares, small, vecs, word_part, char_part):
    wide = jnp.float32
    outs = [(share.shape, wide) for share in shares]
    outs += [((8, word_part), wide)] + [((1, word_part), wide)] * 4 + [((1, char_part), wide)] * 5
    block = blocked((block_rows(large.shape[0], 2048), large.shape[1]))
    return pl.pallas_call(
        share_kernel,
        grid=(large.shape[0] // block.block_shape[0],),
        in_specs=[pl.BlockSpec(memory_space=pltpu.SMEM), block]
        + [once(array.shape) for array in (*shares, small, vecs)],
        out_specs=[block] + [once(shape) for shape, _ in outs],
        out_shape=[jax.ShapeDtypeStruct(large.shape, large.dtype)]
        + [jax.ShapeDtypeStruct(shape, kind) for shape, kind in outs],
        compiler_params=params(60),
        name="hand_out",
    )(places, large, *shares, small, vecs)


def word_kernel(
    pooled_ref,
    words_ref,
    cotangent_ref,
    language_ref,
    table_ref,
    proj_ref,
    weights_ref,
    norms_ref,
    head_mask_ref,
    layer_ref,
    grad_words_ref,
    terms_ref,
    grad_proj_ref,
    grad_pooled_ref,
    small_ref,
    residual_ref,
    normed_one_ref,
    packed_ref,
    probs_ref,
    mixed_ref,
    middle_ref,
    normed_two_ref,
    hidden_ref,
    slope_ref,
    total_ref,
    grad_keys_ref,
    grad_values_ref,
    sums_ref,
):
    low, wide = jnp.bfloat16, jnp.float32
    length, model = words_ref.shape
    dp, mp = weights_ref.shape[:2]
    share = model // dp
    row_block, large = 256, 1024
    blocks = length // row_block
    hidden_width = hidden_ref.shape[1]
    up_blocks = hidden_width // mp // 128
    scale = HEAD ** (-0.5)
    up_base, down_base = 4 * share, (4 + up_blocks) * share

    def weight(base):
        pieces = [
            weights_ref[:, j, pl.ds(base, share), :].reshape(model, 128) for j in range(mp)
        ]
        return jnp.concatenate(pieces, axis=1)

    def wide_weight(base, j, half):
        pieces = [
            weights_ref[:, j, base + c * share : base + (c + 1) * share, :].reshape(model, 128)
            for c in range(half * up_blocks // 2, (half + 1) * up_blocks // 2)
        ]
        return jnp.concatenate(pieces, axis=1)

    def put(base, grad):
        for j in range(mp):
            piece = grad[:, 128 * j : 128 * j + 128].reshape(dp, share, 128).astype(low)
            terms_ref[j, :, pl.ds(base, share), :] = piece

    def put_wide(base, j, half, grad):
        first = half * up_blocks // 2
        for c in range(first, first + up_blocks // 2):
            piece = grad[:, 128 * (c - first) : 128 * (c - first) + 128]
            piece = piece.reshape(dp, share, 128).astype(low)
            terms_ref[j, :, base + c * share : base + (c + 1) * share, :] = piece

    def norm(k):
        return norms_ref[k : k + 1, :]

    sums_ref[...] = jnp.zeros_like(sums_ref)
    language = language_ref[0]

    spans = [slice(row, row + large) for row in range(0, length, large)]
    for span in spans:
        residual = words_ref[span, :].astype(wide) + mm(pooled_ref[span, :], proj_ref[...])
        residual = residual + table_ref[pl.ds(language, 1), :]
        residual_ref[span, :] = residual
        normed_one_ref[span, :] = norm_strips(residual, norm(0), norm(1))[2]

    @pl.loop(0, 3)
    def _(t):
        whole_weight = weight(pl.multiple_of(t * share, share))
        for span in spans:
            packed_ref[t, span, :] = mm(normed_one_ref[span, :], whole_weight).astype(low)

    causal = lax.broadcasted_iota(jnp.int32, (row_block, row_block), 0) <= (
        lax.broadcasted_iota(jnp.int32, (row_block, row_block), 1)
    )

    @pl.loop(0, model // 128)
    def _(pair):
        lanes = pl.ds(pl.multiple_of(pair * 128, 128), 128)
        values_t = packed_ref[2, :, lanes].T

        def scores_of(block, h):
            stop = (block + 1) * row_block
            queries = packed_ref[0, block * row_block : stop, lanes]
            keys = packed_ref[1, 0:stop, lanes] * head_mask_ref[h : h + 1, 0:128]
            return mm(keys, queries, NT)

        order = [(block, h) for block in range(blocks) for h in range(2)]
        ahead = scores_of(*order[0])
        mixed = []
        for place, (block, h) in enumerate(order):
            scores = ahead * EXP2_SCALE
            if place + 1 < len(order):
                ahead = scores_of(*order[place + 1])
            stop = (block + 1) * row_block
            first = block * (block + 1) // 2 * row_block
            near = jnp.where(causal, scores[stop - row_block :], NEG_FILL)
            scores = jnp.concatenate([scores[: stop - row_block], near]) if block else near
            powers = jnp.exp2(scores - jnp.max(scores, axis=0, keepdims=True))
            probs = powers * (1.0 / jnp.sum(powers, axis=0, keepdims=True))
            probs = probs.astype(low)
            probs_ref[2 * pair + h, first : first + stop, :] = probs
            mixed.append(mm(values_t[HEAD * h : HEAD * (h + 1), 0:stop], probs))
            if h == 1:
                both = jnp.concatenate(mixed, axis=0).T.astype(low)
                mixed_ref[block * row_block : stop, lanes] = both
                mixed = []

    out_t = weight(3 * share)
    for span in spans:
        middle = residual_ref[span, :] + mm(mixed_ref[span, :], out_t, NT)
        middle_ref[span, :] = middle
        total_ref[span, :] = middle
        normed_two_ref[span, :] = norm_strips(middle, norm(2), norm(3))[2]

    def columns_of(j, half):
        size = 64 * up_blocks
        return pl.ds(pl.multiple_of((2 * j + half) * size, size), size)

    @pl.loop(0, mp)
    def _(j):
        for span in spans:
            before = [mm(normed_two_ref[span, :], wide_weight(up_base, j, h)) for h in range(2)]
            for h in range(2):
                hidden, slope = gelu_low(before[h])
                hidden_ref[span, columns_of(j, h)] = hidden
                slope_ref[span, columns_of(j, h)] = slope
                total_ref[span, :] += mm(hidden, wide_weight(down_base, j, h), NT)

    for span in spans:
        layer_ref[span, :] = total_ref[span, :].astype(low)
        total_ref[span, :] = jnp.zeros((large, model), wide)

    cotangent_t = cotangent_ref[...].T
    normed_t = normed_two_ref[...].T

    @pl.loop(0, mp)
    def _(j):
        for h in range(2):
            cols = columns_of(j, h)
            for span in spans:
                before = mm(cotangent_ref[span, :], wide_weight(down_base, j, h))
                (grad_pre,) = strips(
                    lambda strip, slope: (strip.astype(low) * slope,),
                    64,
                    before,
                    slope_ref[span, cols],
                )
                slope_ref[span, cols] = grad_pre
                total_ref[span, :] += mm(grad_pre, wide_weight(up_base, j, h), NT)
            put_wide(down_base, j, h, mm(cotangent_t, hidden_ref[:, cols]))
            put_wide(up_base, j, h, mm(normed_t, slope_ref[:, cols]))

    for span in spans:

        def finish(part, middle, cotangent):
            unit, inverse = standardize(middle)
            sums_ref[2] += fold_rows(part * unit)
            sums_ref[3] += fold_rows(part)
            grad = cotangent.astype(wide) + norm_back(part, unit, inverse, norm(2))
            return grad, grad.astype(low)

        grad_middle, branch = strips(
            finish, 64, total_ref[span, :], middle_ref[span, :], cotangent_ref[span, :]
        )
        middle_ref[span, :] = grad_middle
        normed_two_ref[span, :] = branch
    put(3 * share, mm(normed_two_ref[...].T, mixed_ref[...]))
    for span in spans:
        mixed_ref[span, :] = mm(normed_two_ref[span, :], out_t).astype(low)


    @pl.loop(0, model // 128)
    def _(pair):
        lanes = pl.ds(pl.multiple_of(pair * 128, 128), 128)
        grad_keys_ref[...] = jnp.zeros_like(grad_keys_ref)
        grad_values_ref[...] = jnp.zeros_like(grad_values_ref)
        keys_t = packed_ref[1, :, lanes].T

        def grad_probs_of(block, h):
            stop = (block + 1) * row_block
            grad_mixed = mixed_ref[block * row_block : stop, lanes]
            values = packed_ref[2, 0:stop, lanes] * head_mask_ref[h : h + 1, 0:128]
            return mm(values, grad_mixed, NT)

        order = [(block, h) for block in range(blocks) for h in range(2)]
        ahead = grad_probs_of(*order[0])
        sides = []
        for place, (block, h) in enumerate(order):
            grad_probs = ahead
            if place + 1 < len(order):
                ahead = grad_probs_of(*order[place + 1])
            stop = (block + 1) * row_block
            span = slice(block * row_block, stop)
            first = block * (block + 1) // 2 * row_block
            probs = probs_ref[2 * pair + h, first : first + stop, :]
            probs_wide = probs.astype(wide)
            inner = jnp.sum(grad_probs * probs_wide, axis=0, keepdims=True)
            grad_scores = (probs_wide * (grad_probs - inner)).astype(low)
            grad_queries = mm(keys_t[HEAD * h : HEAD * (h + 1), 0:stop], grad_scores)
            sides.append((probs, grad_scores, grad_queries))
            if h == 1:
                probs, grad_scores, grad_queries = (list(side) for side in zip(*sides))
                sides = []
                masks = [head_mask_ref[k : k + 1, 0:128] for k in range(2)]
                grad_mixed, queries = mixed_ref[span, lanes], packed_ref[0, span, lanes]
                grad_values_ref[0:stop, :] += mm(
                    jnp.concatenate(probs, axis=1),
                    jnp.concatenate([grad_mixed * mask for mask in masks], axis=0),
                )
                grad_keys_ref[0:stop, :] += mm(
                    jnp.concatenate(grad_scores, axis=1),
                    jnp.concatenate([queries * mask for mask in masks], axis=0),
                )
                both = jnp.concatenate(grad_queries, axis=0) * scale
                packed_ref[0, span, lanes] = both.T.astype(low)
        packed_ref[1, :, lanes] = (grad_keys_ref[...] * scale).astype(low)
        packed_ref[2, :, lanes] = grad_values_ref[...].astype(low)

    normed_t = normed_one_ref[...].T
    for span in spans:
        total_ref[span, :] = jnp.zeros((large, model), wide)

    @pl.loop(0, 3)
    def _(t):
        base = pl.multiple_of(t * share, share)
        put(base, mm(normed_t, packed_ref[t]))
        whole_weight = weight(base)
        for span in spans:
            total_ref[span, :] += mm(packed_ref[t, span, :], whole_weight, NT)

    for span in spans:

        def finish(part, residual, grad_middle):
            unit, inverse = standardize(residual)
            sums_ref[0] += fold_rows(part * unit)
            sums_ref[1] += fold_rows(part)
            grad = grad_middle + norm_back(part, unit, inverse, norm(0))
            sums_ref[4] += fold_rows(grad)
            return (grad.astype(low),)

        (grad,) = strips(finish, 64, total_ref[span, :], residual_ref[span, :], middle_ref[span, :])
        grad_words_ref[span, :] = grad
        grad_pooled_ref[span] = mm(grad, proj_ref[...], NT)[:, None, :]

    grad_proj_ref[...] = mm(pooled_ref[...].T, grad_words_ref[...])

    sums = [jnp.sum(sums_ref[k], axis=0, keepdims=True) for k in range(5)]
    small_row = lax.broadcasted_iota(jnp.int32, (8, 128), 0)
    for b in range(model // 128):
        cols = slice(128 * b, 128 * b + 128)
        small_ref[b, 0:8, :] = jnp.where(small_row == language, sums[4][:, cols], 0.0)
        piece = jnp.zeros((8, 128), wide)
        for k in range(4):
            piece = jnp.where(small_row == k, sums[k][:, cols], piece)
        small_ref[b, 8:16, :] = piece


def word_layer_kernel(pooled, words, cotangent, language, table, proj, weights, norms, head_masks):
    low, wide = jnp.bfloat16, jnp.float32
    length, model = words.shape
    width = pooled.shape[1]
    dp, mp, n = weights.shape[:3]
    hidden_width = (n * dp // model - 4) // 2 * 128 * mp
    blocks = length // 256
    heads = model // HEAD
    arrays = (pooled, words, cotangent, language, table, proj, weights, norms, head_masks)
    outs = (
        ((length, model), low),
        ((length, model), low),
        ((mp, dp, n, 128), low),
        ((width, model), wide),
        ((length, 1, width), wide),
        ((model // 128, 16, 128), wide),
    )
    return pl.pallas_call(
        word_kernel,
        grid=(1,),
        in_specs=[
            pl.BlockSpec(memory_space=pltpu.SMEM) if array is language else once(array.shape)
            for array in arrays
        ],
        out_specs=[once(shape) for shape, _ in outs],
        out_shape=[jax.ShapeDtypeStruct(shape, kind) for shape, kind in outs],
        scratch_shapes=[
            pltpu.VMEM((length, model), wide),
            pltpu.VMEM((length, model), low),
            pltpu.VMEM((3, length, model), low),
            pltpu.VMEM((heads, blocks * (blocks + 1) // 2 * 256, 256), low),
            pltpu.VMEM((length, model), low),
            pltpu.VMEM((length, model), wide),
            pltpu.VMEM((length, model), low),
            pltpu.VMEM((length, hidden_width), low),
            pltpu.VMEM((length, hidden_width), low),
            pltpu.VMEM((length, model), wide),
            pltpu.VMEM((length, 128), wide),
            pltpu.VMEM((length, 128), wide),
            pltpu.VMEM((5, 8, model), wide),
        ],
        compiler_params=pltpu.CompilerParams(vmem_limit_bytes=62 * 1024 * 1024),
        cost_estimate=pl.CostEstimate(
            flops=40 * 10**9, bytes_accessed=20 * 2**20, transcendentals=10**7
        ),
        name="word_layer",
    )(*arrays)


def attend_forward(queries, key_block, values, allowed):
    scores = low_sum("bqhd,bkhd->bhqk", queries, key_block) * HEAD ** (-0.5)
    scores = jnp.where(allowed, scores, NEG_FILL)
    row_max = jnp.max(scores, axis=-1, keepdims=True)
    powers = jnp.exp(scores - row_max)
    row_total = jnp.sum(powers, axis=-1, keepdims=True)
    attn_probs = (powers / row_total).astype(jnp.bfloat16)
    attn_mixed = low_sum("bhqk,bkhd->bqhd", attn_probs, values).astype(jnp.bfloat16)
    return (attn_mixed, row_max + jnp.log(row_total))


def attend_backward(queries, key_block, values, allowed, log_total, grad_mixed):
    scale = HEAD ** (-0.5)
    scores = low_sum("bqhd,bkhd->bhqk", queries, key_block) * scale
    attn_probs = jnp.where(allowed, jnp.exp(scores - log_total), 0.0)
    grad_probs = low_sum("bqhd,bkhd->bhqk", grad_mixed, values)
    grad_values = low_sum("bhqk,bqhd->bkhd", attn_probs.astype(jnp.bfloat16), grad_mixed)
    inner_sum = jnp.sum(grad_probs * attn_probs, axis=-1, keepdims=True)
    grad_scores = (attn_probs * (grad_probs - inner_sum)).astype(jnp.bfloat16)
    grad_queries = low_sum("bhqk,bkhd->bqhd", grad_scores, key_block) * scale
    grad_keys = low_sum("bhqk,bqhd->bkhd", grad_scores, queries) * scale
    return (grad_queries, grad_keys, grad_values)


def word_layer(residual, grad_rows, weights, norms, mp_size, mp_index):
    qkv, out_t, up, down_t = weights
    gain_one, bias_one, gain_two, bias_two = norms
    rows, width = residual.shape
    low = jnp.bfloat16
    sequences, length = max(1, rows // LEN), min(rows, LEN)
    share = LEN // length
    groups = [[a * share + b for b in range(share)] for a in range(mp_size // share)]
    unit_one, inverse_one, normed_one = apply_norm(residual, gain_one, bias_one)
    packed = low_sum("rd,tdc->trc", normed_one, qkv).astype(low)
    packed = packed.reshape(3, sequences, length, width // HEAD, HEAD)
    keys = packed[1:]
    start = 0
    if share > 1:
        keys = lax.all_gather(keys, "mp", axis=2, tiled=True, axis_index_groups=groups)
        start = lax.rem(mp_index, share) * length
    allowed = (
        lax.broadcasted_iota(jnp.int32, (length, LEN), 1)
        <= lax.broadcasted_iota(jnp.int32, (length, LEN), 0) + start
    )[None, None]
    mixed, log_total = attend_forward(packed[0], keys[0], keys[1], allowed)
    mixed_rows = mixed.reshape(rows, width)
    middle = residual + mm(mixed_rows, out_t, NT)
    unit_two, inverse_two, normed_two = apply_norm(middle, gain_two, bias_two)
    hidden, slope = gelu_pair(matmul(normed_two, up))
    hidden = hidden.astype(low)
    layer_output = (middle + mm(hidden, down_t, NT)).astype(low)
    grad_wide = grad_rows.astype(jnp.float32)
    grad_down_t = mm(grad_rows, hidden, TN)
    grad_pre = (matmul(grad_rows, down_t) * slope).astype(low)
    grad_up = mm(normed_two, grad_pre, TN)
    grad_normed = mm(grad_pre, up, NT)
    grad_gain_two = jnp.sum(grad_normed * unit_two, axis=0)
    grad_bias_two = jnp.sum(grad_normed, axis=0)
    grad_middle = grad_wide + norm_back(grad_normed, unit_two, inverse_two, gain_two)
    branch = grad_middle.astype(low)
    grad_out_t = mm(branch, mixed_rows, TN)
    grad_mixed = matmul(branch, out_t).astype(low).reshape(sequences, length, -1, HEAD)
    grad_queries, grad_keys, grad_values = attend_backward(
        packed[0], keys[0], keys[1], allowed, log_total, grad_mixed
    )
    grad_keys = jnp.stack((grad_keys, grad_values), axis=0)
    if share > 1:
        grad_keys = lax.psum_scatter(
            grad_keys, "mp", scatter_dimension=2, tiled=True, axis_index_groups=groups
        )
    grad_packed = jnp.concatenate((grad_queries[None], grad_keys), axis=0)
    grad_packed = grad_packed.reshape(3, rows, width).astype(low)
    grad_qkv = low_sum("rd,trc->tdc", normed_one, grad_packed)
    grad_normed = low_sum("trc,tdc->rd", grad_packed, qkv)
    grad_gain_one = jnp.sum(grad_normed * unit_one, axis=0)
    grad_bias_one = jnp.sum(grad_normed, axis=0)
    grad_residual = grad_middle + norm_back(grad_normed, unit_one, inverse_one, gain_one)
    return (
        layer_output,
        grad_residual,
        (grad_qkv, grad_out_t, grad_up, grad_down_t),
        (grad_gain_one, grad_bias_one, grad_gain_two, grad_bias_two),
    )


def mask_constants(width, chars):
    head, word = np.arange(width) // HEAD, np.arange(GROUP) // chars
    head_masks = head[None] == np.arange(8)[:, None]
    word_masks = word[None] == np.arange(GROUP // chars)[:, None]
    ones = head[:, None] == head[None]
    return tuple(jnp.asarray(mask.astype(ml_dtypes.bfloat16)) for mask in (head_masks, word_masks, ones))


def blocks_of(array, count):
    return array.reshape(count, -1)


def shards_general(
    char_states,
    word_states,
    char_counts,
    language_group,
    output_grad,
    char_norm_gain,
    char_norm_bias,
    char_qkv,
    char_out,
    char_mlp_gain,
    char_mlp_bias,
    char_up,
    char_down,
    pool_query,
    char_proj,
    language_table,
    word_norm_gain,
    word_norm_bias,
    word_qkv,
    word_out,
    word_mlp_gain,
    word_mlp_bias,
    word_up,
    word_down,
):
    low, wide = jnp.bfloat16, jnp.float32
    dp_size, mp_size = lax.axis_size("dp"), lax.axis_size("mp")
    mp_index = lax.axis_index("mp")
    devices = dp_size * mp_size
    word_count, chars, width = char_states.shape
    model = word_states.shape[1]
    langs = language_table.shape[0]

    char_parts = (
        char_qkv,
        char_out,
        char_up,
        char_down,
        char_proj,
        char_norm_gain,
        char_norm_bias,
        char_mlp_gain,
        char_mlp_bias,
        pool_query,
        word_norm_gain,
        word_norm_bias,
        word_mlp_gain,
        word_mlp_bias,
        language_table.T,
    )
    flat = jnp.concatenate([part.astype(low).reshape(-1) for part in char_parts])
    flat_size = flat.shape[0]
    flat = jnp.pad(flat, (0, -flat_size % 2048))
    full = lax.all_gather(flat, BOTH, axis=0, tiled=False)
    unpacked, start = [], 0
    for part in char_parts:
        stop = start + part.size
        piece = full[:, start:stop].reshape((devices * part.shape[0],) + part.shape[1:])
        unpacked.append(piece)
        start = stop
    (
        qkv_char,
        out_char,
        up_char,
        down_char,
        proj_char,
        gain_attn,
        bias_attn,
        gain_mlp,
        bias_mlp,
        query_pool,
        gain_one,
        bias_one,
        gain_two,
        bias_two,
        table_t,
    ) = unpacked

    word_parts = (word_qkv, word_out.T, word_up, word_down.T)
    word_flat = jnp.concatenate([part.astype(low).reshape(-1, 128) for part in word_parts])
    word_full = lax.all_gather(word_flat, BOTH, axis=0, tiled=False)
    word_full = word_full.reshape(dp_size, mp_size, word_flat.shape[0], 128)
    word_weights, start = [], 0
    for part in word_parts:
        stop = start + part.size // 128
        piece = word_full[:, :, start:stop].reshape((dp_size, mp_size) + part.shape)
        if part.ndim == 3:
            piece = piece.transpose(2, 0, 3, 1, 4).reshape(3, model, model)
        else:
            piece = piece.transpose(0, 2, 1, 3)
            piece = piece.reshape(dp_size * part.shape[0], mp_size * part.shape[1])
        word_weights.append(piece)
        start = stop

    rows = word_count * chars
    states = char_states.reshape(rows, width)
    counts = char_counts.reshape(-1, 128)
    head_masks, word_masks, ones = mask_constants(width, chars)
    zero = jnp.zeros_like(gain_attn)
    vecs = jnp.stack(
        (gain_attn, bias_attn, gain_mlp, bias_mlp, query_pool, zero, zero, zero)
    ).astype(wide)
    cp, probs, co, y1, hidden, slope, y2, pi, pooled = char_forward(
        states,
        counts,
        (qkv_char, out_char, up_char, down_char, ones, vecs, head_masks, word_masks),
        chars,
    )

    sequences = max(1, word_count // LEN)
    first = (mp_index * word_count) // LEN
    language = lax.dynamic_slice_in_dim(language_group, first, sequences)
    language_hot = (language[:, None] == jnp.arange(langs)[None]).astype(wide)
    language_rows = jnp.sum(language_hot[:, :, None] * table_t.T.astype(wide)[None], axis=1)
    residual = word_states.astype(wide) + matmul(pooled, proj_char)
    residual = (
        residual.reshape(sequences, -1, model) + language_rows[:, None, :]
    ).reshape(word_count, model)
    norms = tuple(value.astype(wide) for value in (gain_one, bias_one, gain_two, bias_two))
    layer_output, grad_residual, word_grads, word_norm_grads = word_layer(
        residual, output_grad, word_weights, norms, mp_size, mp_index
    )
    grad_words = grad_residual.astype(low)
    sequence_grads = jnp.sum(grad_residual.reshape(sequences, -1, model), axis=1)
    grad_table = jnp.sum(language_hot[:, :, None] * sequence_grads[:, None, :], axis=0)

    pieces = []
    for part, grad in zip(word_parts, word_grads):
        if part.ndim == 3:
            grad = grad.reshape(3, dp_size, part.shape[1], mp_size, part.shape[2])
            grad = grad.transpose(3, 1, 0, 2, 4)
        else:
            grad = grad.reshape(dp_size, part.shape[0], mp_size, part.shape[1])
            grad = grad.transpose(2, 0, 1, 3)
        pieces.append(grad.astype(low).reshape(mp_size, dp_size, -1, 128))
    word_terms = jnp.concatenate(pieces, axis=2)
    word_terms = lax.psum_scatter(word_terms, "mp", scatter_dimension=0, tiled=True)
    word_terms = lax.psum_scatter(word_terms[0], "dp", scatter_dimension=0, tiled=True)[0]
    word_shares, start = [], 0
    for part in word_parts:
        stop = start + part.size // 128
        word_shares.append(word_terms[start:stop].reshape(part.shape).astype(wide))
        start = stop

    grad_proj = mm(pooled, grad_words, TN)
    grad_pooled = mm(grad_words, proj_char, NT).reshape(word_count, 1, width)
    grad_y1, grad_up, grad_down_t, mlp_vecs = char_mlp_back(
        y1, y2, pi, grad_pooled, hidden, slope, (up_char.T, down_char.T, vecs, ones), chars
    )
    mlp_vecs = jnp.sum(mlp_vecs, axis=1)
    early = (
        grad_up,
        grad_down_t.T,
        grad_proj,
        mlp_vecs[0],
        mlp_vecs[1],
        mlp_vecs[2],
        word_norm_grads[0],
        word_norm_grads[1],
        word_norm_grads[2],
        word_norm_grads[3],
        grad_table.T,
    )
    early_terms = jnp.concatenate([blocks_of(part, devices) for part in early], axis=1)
    early_size = early_terms.shape[1]
    early_terms = jnp.pad(early_terms, ((0, 0), (0, -early_size % 1024)))
    early_terms = lax.psum_scatter(early_terms, BOTH, scatter_dimension=0, tiled=True)[0]
    grad_chars, grad_qkv, grad_out, attn_vecs = char_attn_back(
        states, cp, probs, co, grad_y1, (qkv_char.T, out_char.T, vecs, head_masks, word_masks), chars
    )
    attn_vecs = jnp.sum(attn_vecs, axis=1)
    late = (grad_qkv, grad_out, attn_vecs[0], attn_vecs[1])
    late_terms = jnp.concatenate([blocks_of(part, devices) for part in late], axis=1)
    late_terms = jnp.pad(late_terms, ((0, 0), (0, -late_terms.shape[1] % 1024)))
    late_terms = lax.psum_scatter(late_terms, BOTH, scatter_dimension=0, tiled=True)[0]

    def take(terms, parts):
        shares, start = [], 0
        for part in parts:
            stop = start + part.size // devices
            shape = (part.shape[0] // devices,) + part.shape[1:]
            shares.append(terms[start:stop].reshape(shape))
            start = stop
        return shares

    (
        g_up,
        g_down,
        g_proj,
        g_query,
        g_gain_mlp,
        g_bias_mlp,
        g_gain_one,
        g_bias_one,
        g_gain_two,
        g_bias_two,
        g_table_t,
    ) = take(early_terms, early)
    g_qkv, g_out, g_gain_attn, g_bias_attn = take(late_terms, late)
    return (
        layer_output,
        grad_chars.reshape(char_states.shape),
        grad_words,
        g_gain_attn,
        g_bias_attn,
        g_qkv,
        g_out,
        g_gain_mlp,
        g_bias_mlp,
        g_up,
        g_down,
        g_query,
        g_proj,
        g_table_t.T,
        g_gain_one,
        g_bias_one,
        word_shares[0],
        word_shares[1].T,
        g_gain_two,
        g_bias_two,
        word_shares[2],
        word_shares[3].T,
    )


def fits(dp, mp, words, model, width, chars, hidden_width, langs):
    count = dp * mp
    return (
        words == LEN
        and mp % 2 == 0
        and model == 128 * mp
        and model // dp % 16 == 0
        and width == 256
        and width == 8 * count
        and hidden_width % (16 * count) == 0
        and GROUP % chars == 0
        and langs == 8
    )


def shards(*arrays):
    char_states, word_states = arrays[:2]
    dp, mp = lax.axis_size("dp"), lax.axis_size("mp")
    words, chars, width = char_states.shape
    model, hidden_width = word_states.shape[1], arrays[11].shape[1]
    if not fits(dp, mp, words, model, width, chars, hidden_width, arrays[15].shape[0]):
        return shards_general(*arrays)
    return shards_whole(*arrays)


def shards_whole(
    char_states,
    word_states,
    char_counts,
    language_group,
    output_grad,
    char_norm_gain,
    char_norm_bias,
    char_qkv,
    char_out,
    char_mlp_gain,
    char_mlp_bias,
    char_up,
    char_down,
    pool_query,
    char_proj,
    language_table,
    word_norm_gain,
    word_norm_bias,
    word_qkv,
    word_out,
    word_mlp_gain,
    word_mlp_bias,
    word_up,
    word_down,
):
    low, wide = jnp.bfloat16, jnp.float32
    dp, mp = lax.axis_size("dp"), lax.axis_size("mp")
    count = dp * mp
    words, chars, width = char_states.shape
    model = word_states.shape[1]
    langs = language_table.shape[0]
    hidden_width = char_up.shape[1]
    small = (char_norm_gain, char_norm_bias, char_mlp_gain, char_mlp_bias, pool_query)
    small += (word_norm_gain, word_norm_bias, word_mlp_gain, word_mlp_bias)
    (
        qkv,
        qkv_t,
        out,
        out_t,
        up,
        up_t,
        down,
        down_t,
        proj,
        vecs,
        norms,
        table,
        word_share,
    ) = gather_weights(
        dp,
        mp,
        (char_qkv, char_out, char_up, char_down, char_proj),
        language_table,
        tuple(value[None] for value in small),
        (word_qkv, word_out.T, word_up, word_down.T),
    )
    word_weights = lax.all_gather(word_share, BOTH, axis=0, tiled=False)
    word_weights = word_weights.reshape(dp, mp, word_share.shape[0], 128)
    char_share, word_part = width // count, model // count

    rows = words * chars
    states = char_states.reshape(rows, width)
    counts = char_counts.reshape(-1, 128)
    head_masks, word_masks, ones = mask_constants(width, chars)
    cp, probs, co, y1, hidden, slope, y2, pi, pooled = char_forward(
        states,
        counts,
        (qkv, out, up, down, ones, vecs, head_masks, word_masks),
        chars,
    )

    language = lax.dynamic_slice_in_dim(language_group, lax.axis_index("mp"), 1)
    layer_output, grad_words, word_terms, grad_proj, grad_pooled, small_terms = word_layer_kernel(
        pooled,
        word_states,
        output_grad,
        language,
        table,
        proj,
        word_weights,
        norms,
        head_masks,
    )

    grad_y1, char_terms, g_word_qkv, g_word_out, g_word_up, g_word_down = char_mlp_back_exchange(
        y1, y2, pi, grad_pooled, hidden, slope, (up_t, down_t, vecs, ones), chars, (dp, mp),
        grad_proj, small_terms, word_terms,
    )
    grad_chars, g_qkv, g_out, g_up, g_down, g_proj, g_small, g_vecs = char_attn_back_exchange(
        states, cp, probs, co, grad_y1, (qkv_t, out_t, vecs, head_masks, word_masks), chars,
        (dp, mp), char_terms, hidden_width, model,
    )
    index = lax.axis_index("dp") * mp + lax.axis_index("mp")
    places = jnp.stack(((model - index * word_part) % model, (width - index * char_share) % width))
    shares = (
        g_qkv, g_out, g_up, g_down, g_proj, g_word_qkv, g_word_out, g_word_up, g_word_down,
    )
    grad_chars, *shares = hand_out(
        places, grad_chars, shares, g_small, g_vecs, word_part, char_share
    )
    g_qkv, g_out, g_up, g_down, g_proj, g_word_qkv, g_word_out, g_word_up, g_word_down = shares[:9]
    g_table, *small_shares = shares[9:]
    norm_shares = [value[0] for value in small_shares]
    return (
        layer_output,
        grad_chars.reshape(char_states.shape),
        grad_words,
        norm_shares[7],
        norm_shares[8],
        g_qkv,
        g_out,
        norm_shares[5],
        norm_shares[6],
        g_up,
        g_down,
        norm_shares[4],
        g_proj,
        g_table,
        norm_shares[0],
        norm_shares[1],
        g_word_qkv,
        g_word_out.T,
        norm_shares[2],
        norm_shares[3],
        g_word_up,
        g_word_down.T,
    )


def solution(mesh):
    vector, rows = P(BOTH), P(BOTH, None)
    cube = P(BOTH, None, None)
    table = P(None, BOTH)
    words = (P(None, "dp", "mp"), P("mp", "dp"), P("dp", "mp"), P("mp", "dp"))
    char_weights = (
        vector, vector, rows, rows, vector, vector, rows, rows, vector, rows, table,
    )
    weights = char_weights + (
        vector, vector, words[0], words[1], vector, vector, words[2], words[3],
    )
    return jax.shard_map(
        shards,
        mesh=mesh,
        in_specs=(cube, rows, vector, P("dp"), rows) + weights,
        out_specs=(rows, cube, rows) + weights,
        check_vma=False,
    )
```
